32 devices in a mesh: row: 4 (over x, core), col: 8 (over z, y).
Axes of the slice: x: 2, y: 2, z: 4, core: 2. Of those that a mesh axis runs over, the one named last changes fastest.
Arguments:
- start_columns: bfloat16 [16384, 4096], P('row', 'col'), may hold values from -6 to 6
- hamiltonian: bfloat16 [64, 2, 256, 256], P(('row', 'col')), may hold values from -0.09375 to 0.09375
- band_pattern: int32 [64], P(('row', 'col')), may hold values 0 or 1
- coefficients: float32 [4], replicated, may hold values from -1 to 1
- tile_peer: int32 [512, 1], P(('row', 'col')), may hold values from 0 to 7; in each aligned block of 16 rows (0 to 15, 16 to 31, ...) at most 2 rows name the same one
- tile_block: int32 [512], P(('row', 'col')), may hold values from 0 to 7
- tile_count: int32 [128], P(('row', 'col')), may hold values from 1 to 4
- basis_values: bfloat16 [512, 2, 512, 128], P(('row', 'col')), may hold values from -6 to 6
- core_density: float32 [128, 128], P(('row', 'col')), may hold values from 0.5 to 3
Outputs:
- density: float32 [128, 128], P(('row', 'col'))
- h_update: bfloat16 [16384, 4096], P('row', 'col')
The draws below stay inside these ranges and needn't reach their ends.
Inputs may be any that keep to these rules, and one draw needn't show every extreme that they name: `tile_peer`: the entries of one device name one col index at most 2 times, and on some device exactly 2 times.
All inputs are finite; a program needn't handle non-finite values. No bound on the sum of `band_pattern` on one device may be relied on, other than what follows from the above.
Results may differ from the reference program's by a relative error of at most 0.0059.
Values may be sent and summed in bfloat16 or wider, within the bound.
No kernel may reach another device: no remote copies, remote signals or barrier semaphores. Data moves between devices by JAX's collectives and lax.ppermute only.
A program may use at most 192 MiB of HBM per device.

```python
import math
import jax
import jax.numpy as jnp
import numpy as np
from jax import lax

W = 256
KB = 512
DEG = 3
TILES_DEV = 4
SLOTS = 4
CAP = 2
P_SIZE = 128
FUNCS = 16384
COLS = 4096
KROW = 8
NBLK = 64
TILES = 128
ENTRIES = 512
N_COL = 8


def set_ends(array, key, low, largest):
    spot = [jax.random.randint(jax.random.fold_in(key, axis), (), 0, length) for axis, length in enumerate(array.shape)]
    longest = array.shape.index(max(array.shape))
    beside = spot[:longest] + [(spot[longest] + 1) % array.shape[longest]] + spot[longest + 1:]
    return array.at[tuple(spot)].set(low).at[tuple(beside)].set(largest)


def block_levels(key, extent, split, smallest, top_value):
    factor_of = 1.0
    for position, parts in split:
        steps = jax.random.uniform(jax.random.fold_in(jax.random.fold_in(key, 6), position), (parts,), jnp.float32, smallest / len(split), top_value / len(split))
        factor_of = factor_of * jnp.repeat(jnp.exp(steps), extent[position] // parts).reshape((-1,) + (1,) * (len(extent) - 1 - position))
    return factor_of


def assign_block(key, own, number, rows, count, top, limit, lean):
    order = jax.random.permutation(key, count)
    heavy_load, common = shares(count, rows * top, limit, lean, True), shares(count, rows * top, limit, lean, False)
    places = jnp.arange(count)

    def named(sizes, offset_by):
        used = int((sizes > 0).sum())
        fixed = max(1, used // 4)
        moved = fixed + (places - fixed + offset_by * (used - fixed)) % max(1, count - fixed)
        return jnp.zeros((count,), jnp.int32).at[order[jnp.where(places < fixed, places, moved)]].set(jnp.asarray(sizes, jnp.int32))

    sizes = jnp.where(number % 4 == 0, named(heavy_load, number // 4), named(common, number - number // 4 - 1))
    mixed = jax.random.permutation(jax.random.fold_in(own, 3), count)
    source_of, sink = mixed[0:count // 2 * 2:2], mixed[1:count // 2 * 2:2]
    room = jnp.minimum(sizes[source_of] - 1, limit - sizes[sink]) // 2
    room = jnp.where((source_of == order[0]) | (sink == order[0]) | (sizes[sink] == 0), 0, jnp.maximum(room, 0))
    moved = jax.random.randint(jax.random.fold_in(own, 4), (count // 2,), 0, 1 << 20) % (room + 1)
    sizes = sizes.at[source_of].add(-moved).at[sink].add(moved)
    items = jnp.searchsorted(jnp.cumsum(sizes), jnp.arange(rows * top), side="right").astype(jnp.int32)
    table = items.reshape(top, rows).T
    table = table[jax.random.permutation(jax.random.fold_in(own, 1), rows)]
    offset_by = jax.random.randint(jax.random.fold_in(own, 2), (rows, 1), 0, top)
    return jnp.take_along_axis(table, (jnp.arange(top)[None, :] + offset_by) % top, axis=1)


def shares(number_of, total, reach, slope, full):
    weights = [(1 << 20) // math.isqrt(rank ** slope) + 1 for rank in range(1, number_of + 1)]
    largest = reach if full else min(reach, max(-(-total // number_of), total * weights[0] // sum(weights)))
    least = 1 if total - largest >= number_of - 1 else 0
    holding, surplus = [largest] + [least] * (number_of - 1), total - largest - least * (number_of - 1)
    while surplus > 0:
        candidates = [i for i in range(1, number_of) if holding[i] < largest] or [i for i in range(1, number_of) if holding[i] < reach]
        mass, left = sum([weights[i] for i in candidates]), surplus
        for i in candidates:
            extra = min(reach - holding[i], max(1, left * weights[i] // mass), surplus)
            holding[i] = holding[i] + extra
            surplus = surplus - extra
    return np.array(holding)


def centred(rng, extent, scale, bound, shards=(), kind=jnp.bfloat16):
    level = block_levels(rng, extent, shards, -0.22, 0.18) if shards else 1.0
    drawn = jax.random.normal(rng, extent, jnp.float32) * scale * level
    return jnp.minimum(jnp.maximum(drawn, -bound), bound).astype(kind)


def setup_inputs(seed: int = 0) -> dict:
    seeds = jax.random.split(jax.random.key(seed), 10)
    start_columns = centred(seeds[0], (FUNCS, COLS), 1.0, 6.0, ((0, 4), (1, 8)))
    hamiltonian = centred(seeds[1], (NBLK, 2, W, W), (16 * W) ** -0.5, 0.09375, ((0, 32),))
    band_pattern = set_ends((jax.random.randint(seeds[2], (NBLK,), 0, 4) < 3).astype(jnp.int32), jax.random.fold_in(seeds[2], 1), 0, 1)
    coefficients = jnp.clip(jax.random.uniform(seeds[3], (DEG + 1,), jnp.float32, -1.0, 1.0), -1.0, 1.0)
    tile_peer_keys = jax.random.split(jax.random.fold_in(seeds[4], 1), ENTRIES // (TILES_DEV * SLOTS))
    tile_peer_turns = jax.random.permutation(jax.random.fold_in(seeds[4], 3), ENTRIES // (TILES_DEV * SLOTS))
    tile_peer = jax.vmap(lambda own, number: assign_block(jax.random.fold_in(seeds[4], 2), own, number, TILES_DEV * SLOTS, N_COL, 1, CAP, 2))(tile_peer_keys, tile_peer_turns).reshape((ENTRIES, 1))
    tile_block = set_ends(jax.random.randint(seeds[5], (ENTRIES,), 0, KROW), jax.random.fold_in(seeds[5], 1), 0, KROW - 1).astype(jnp.int32)
    tile_count = set_ends(jax.random.randint(seeds[6], (TILES,), 1, SLOTS + 1), jax.random.fold_in(seeds[6], 1), 1, SLOTS).astype(jnp.int32)
    basis_values = centred(seeds[7], (ENTRIES, 2, KB, P_SIZE), 1.0, 6.0, ((0, 32),))
    core_density = jnp.clip(jnp.exp(math.log(3.0) - 1.7917595 * jax.random.uniform(seeds[8], (TILES, P_SIZE), jnp.float32) ** block_levels(seeds[8], (TILES, P_SIZE), ((0, 32),), -0.2, 0.2)), 0.5, 3.0)
    return {"start_columns": start_columns, "hamiltonian": hamiltonian, "band_pattern": band_pattern, "coefficients": coefficients, "tile_peer": tile_peer, "tile_block": tile_block, "tile_count": tile_count, "basis_values": basis_values, "core_density": core_density}


exchange_factor = (3.0 / math.pi) ** (1.0 / 3.0)

def band_apply(columns, diagonal_blocks, lower_band, upper_band):
    split_rows = columns.astype(jnp.float32).reshape(NBLK, W, columns.shape[1])
    zero_block = jnp.zeros_like(split_rows[:1])
    previous = jnp.concatenate([zero_block, split_rows[:-1]], axis=0)
    following = jnp.concatenate([split_rows[1:], zero_block], axis=0)
    product = jnp.einsum('nij,njc->nic', diagonal_blocks, split_rows)
    product = product + jnp.einsum('nij,njc->nic', lower_band, previous)
    product = product + jnp.einsum('nij,njc->nic', upper_band, following)
    return product.reshape(FUNCS, columns.shape[1])

def reference(start_columns, hamiltonian, band_pattern, coefficients, tile_peer, tile_block, tile_count, basis_values, core_density):
    band_values = hamiltonian.astype(jnp.float32)
    pattern = band_pattern.astype(jnp.float32)[:, None, None]
    diagonal_blocks = band_values[:, 0]
    coupling = band_values[:, 1]
    lower_band = jnp.triu(coupling) * pattern
    upper_band = jnp.tril(coupling, -1) * pattern

    def expand(columns):
        previous = columns.astype(jnp.float32)
        current = band_apply(columns, diagonal_blocks, lower_band, upper_band)
        kernel_sum = coefficients[0] * previous + coefficients[1] * current
        for degree in range(1, DEG):
            following = 2.0 * band_apply(current.astype(jnp.bfloat16), diagonal_blocks, lower_band, upper_band) - previous
            kernel_sum = kernel_sum + coefficients[degree + 1] * following
            previous, current = (current, following)
        return kernel_sum.astype(jnp.bfloat16)
    col_blocks = start_columns.reshape(FUNCS, N_COL, KB).transpose(1, 0, 2)
    kernel = lax.map(expand, col_blocks).transpose(1, 0, 2).reshape(FUNCS, COLS)
    entry_count = TILES_DEV * SLOTS
    entry_ids = jnp.arange(ENTRIES, dtype=jnp.int32)
    quadrature = 1.0 / math.sqrt(P_SIZE)

    def locate(entry):
        device = entry // entry_count
        row_index = device // N_COL
        row_start = ((row_index * KROW + tile_block[entry]) * KB).astype(jnp.int32)
        col_start = (tile_peer[entry, 0] * KB).astype(jnp.int32)
        is_live = (entry % SLOTS < tile_count[entry // SLOTS]).astype(jnp.float32)
        return (row_start, col_start, is_live)

    def contribute(entry):
        row_start, col_start, is_live = locate(entry)
        kernel_block = lax.dynamic_slice(kernel, (row_start, col_start), (KB, KB))
        basis_pair = basis_values[entry]
        projected = jnp.dot(kernel_block.T, basis_pair[0], preferred_element_type=jnp.float32)
        return lax.optimization_barrier(jnp.sum(projected * basis_pair[1].astype(jnp.float32), axis=0)) / KB * is_live
    contrib = lax.map(contribute, entry_ids)
    density = core_density + contrib.reshape(TILES, SLOTS, P_SIZE).sum(axis=1)
    potential = -exchange_factor * jnp.cbrt(jnp.maximum(density, 0.1))

    def accumulate(total, entry):
        row_start, col_start, is_live = locate(entry)
        basis_pair = basis_values[entry]
        weighted = (basis_pair[1].astype(jnp.float32) * potential[entry // SLOTS][None, :]).astype(jnp.bfloat16)
        update_block = jnp.dot(basis_pair[0], weighted.T, preferred_element_type=jnp.float32) * quadrature
        update_block = (update_block * is_live).astype(jnp.bfloat16).astype(jnp.float32)
        previous_sum = lax.dynamic_slice(total, (row_start, col_start), (KB, KB))
        total = lax.dynamic_update_slice(total, previous_sum + update_block, (row_start, col_start))
        return (total, None)
    total = lax.scan(accumulate, jnp.zeros((FUNCS, COLS), jnp.float32), entry_ids)[0]
    return (density, total.astype(jnp.bfloat16))
```

```python
import functools
import math

import jax
import jax.numpy as jnp
from jax import lax
from jax.experimental import pallas as pl
from jax.experimental.pallas import tpu as pltpu
from jax.sharding import PartitionSpec as P

W = 256
KB = 512
DEG = 3
SLOTS = 4
CAP = 2
P_SIZE = 128
MIB = 1 << 20

exchange_factor = (3.0 / math.pi) ** (1.0 / 3.0)
ANY = pl.BlockSpec(memory_space=pl.ANY)
SMEM = pl.BlockSpec(memory_space=pltpu.SMEM)
VMEM = pl.BlockSpec(memory_space=pltpu.VMEM)


def mask_kernel(pattern, ham, out):
    for i in range(ham.shape[0]):
        out[i, 0] = ham[i, 0]
        out[i, 1] = ham[i, 1] * pattern[i].astype(jnp.bfloat16)


def mask_couplings(hamiltonian, band_pattern):
    return pl.pallas_call(
        mask_kernel,
        out_shape=jax.ShapeDtypeStruct(hamiltonian.shape, hamiltonian.dtype),
        in_specs=[SMEM, VMEM],
        out_specs=VMEM,
        name="mask_couplings",
    )(band_pattern, hamiltonian)


def pack_kernel(entries, slots, peers, basis, out, owner, count, sems):
    for s in range(slots):
        owner[s] = 0
    for c in range(slots // CAP):
        count[c] = 0

    def place(e, carry):
        p = peers[e]
        k = count[p]
        count[p] = k + 1
        owner[p * CAP + k] = e
        return carry

    lax.fori_loop(0, entries, place, 0)

    def start(s, carry):
        pltpu.make_async_copy(basis.at[owner[s]], out.at[s], sems.at[s]).start()
        return carry

    def wait(s, carry):
        pltpu.make_async_copy(basis.at[0], out.at[s], sems.at[s]).wait()
        return carry

    lax.fori_loop(0, slots, start, 0)
    lax.fori_loop(0, slots, wait, 0)


def pack_basis(peers, basis, slots):
    entries = basis.shape[0]
    return pl.pallas_call(
        functools.partial(pack_kernel, entries, slots),
        out_shape=jax.ShapeDtypeStruct((slots,) + basis.shape[1:], basis.dtype),
        in_specs=[SMEM, ANY],
        out_specs=ANY,
        scratch_shapes=[
            pltpu.SMEM((slots,), jnp.int32),
            pltpu.SMEM((slots // CAP,), jnp.int32),
            pltpu.SemaphoreType.DMA((slots,)),
        ],
        name="pack_basis",
    )(peers, basis)


def cheb_kernel(
    blocks, coef, v_low, v_mid, v_high, h_low, h_mid, h_high, out,
    vext, hraw, hcat, cheb_1, cheb_2, total, sems,
):
    halo_v = DEG
    halo_h = DEG - 1
    copies = [
        pltpu.make_async_copy(h_low, hraw.at[pl.ds(0, halo_h)], sems.at[0]),
        pltpu.make_async_copy(h_mid, hraw.at[pl.ds(halo_h, blocks)], sems.at[1]),
        pltpu.make_async_copy(h_high, hraw.at[pl.ds(halo_h + blocks, halo_h)], sems.at[2]),
        pltpu.make_async_copy(v_low, vext.at[pl.ds(0, halo_v * W)], sems.at[3]),
        pltpu.make_async_copy(v_mid, vext.at[pl.ds(halo_v * W, blocks * W)], sems.at[4]),
        pltpu.make_async_copy(v_high, vext.at[pl.ds((halo_v + blocks) * W, halo_v * W)], sems.at[5]),
    ]
    for copy in copies:
        copy.start()
    for copy in copies:
        copy.wait()
    rows = lax.broadcasted_iota(jnp.int32, (W, W), 0)
    cols = lax.broadcasted_iota(jnp.int32, (W, W), 1)
    upper = rows <= cols

    def build(j, carry):
        coupling = hraw[j, 1].astype(jnp.float32)
        hcat[j, :, 0:W] = jnp.where(upper, coupling, 0.0).astype(jnp.bfloat16)
        hcat[j, :, W : 2 * W] = hraw[j, 0]
        hcat[j, :, 2 * W : 3 * W] = jnp.where(upper, 0.0, coupling).astype(jnp.bfloat16)
        return carry

    lax.fori_loop(0, blocks + 2 * halo_h, build, 0)

    def band(source, j):
        start = pl.multiple_of(j * W, W)
        return jnp.dot(
            hcat[j], source[pl.ds(start, 3 * W), :], preferred_element_type=jnp.float32
        )

    def rows_of(j):
        return pl.ds(pl.multiple_of(j * W, W), W)

    def first(j, carry):
        value = band(vext, j)
        cheb_1[rows_of(j), :] = value.astype(jnp.bfloat16)

        @pl.when((j >= 2) & (j < blocks + 2))
        def _():
            total[rows_of(j - 2), :] = value

        return carry

    lax.fori_loop(0, blocks + 4, first, 0)

    def second(j, carry):
        start = pl.multiple_of(j * W, W)
        value = 2.0 * jnp.dot(
            hcat[j + 1], cheb_1[pl.ds(start, 3 * W), :], preferred_element_type=jnp.float32
        )
        begin = vext[rows_of(j + 2), :].astype(jnp.float32)
        value = value - begin
        cheb_2[rows_of(j), :] = value.astype(jnp.bfloat16)

        @pl.when((j >= 1) & (j < blocks + 1))
        def _():
            total[rows_of(j - 1), :] = (
                coef[0] * begin + (coef[1] - coef[3]) * total[rows_of(j - 1), :] + coef[2] * value
            )

        return carry

    lax.fori_loop(0, blocks + 2, second, 0)

    def third(j, carry):
        for half in range(KB // W):
            i = j * (KB // W) + half
            start = pl.multiple_of(i * W, W)
            value = jnp.dot(
                hcat[i + 2], cheb_2[pl.ds(start, 3 * W), :], preferred_element_type=jnp.float32
            )
            value = total[rows_of(i), :] + (2.0 * coef[3]) * value
            out[j, :, half * W : (half + 1) * W] = value.T.astype(jnp.bfloat16)
        return carry

    lax.fori_loop(0, blocks // (KB // W), third, 0)


def chebyshev(coefficients, v_low, v_mid, v_high, h_low, h_mid, h_high):
    blocks = v_mid.shape[0] // W
    cols = v_mid.shape[1]
    ext = blocks + 2 * (DEG - 1)
    flops = 2 * W * 3 * W * cols * (3 * blocks + 6)
    return pl.pallas_call(
        functools.partial(cheb_kernel, blocks),
        out_shape=jax.ShapeDtypeStruct((blocks * W // KB, cols, KB), jnp.bfloat16),
        in_specs=[SMEM] + [ANY] * 6,
        out_specs=VMEM,
        scratch_shapes=[
            pltpu.VMEM(((blocks + 2 * DEG) * W, cols), jnp.bfloat16),
            pltpu.VMEM((ext, 2, W, W), jnp.bfloat16),
            pltpu.VMEM((ext, W, 3 * W), jnp.bfloat16),
            pltpu.VMEM((ext * W, cols), jnp.bfloat16),
            pltpu.VMEM(((blocks + 2) * W, cols), jnp.bfloat16),
            pltpu.VMEM((blocks * W, cols), jnp.float32),
            pltpu.SemaphoreType.DMA((6,)),
        ],
        compiler_params=pltpu.CompilerParams(vmem_limit_bytes=48 * MIB),
        cost_estimate=pl.CostEstimate(flops=flops, bytes_accessed=16 * MIB, transcendentals=0),
        name="chebyshev",
    )(coefficients, v_low, v_mid, v_high, h_low, h_mid, h_high)


def project_kernel(blocks, plan, order, kernel_t, basis, out, kern, pair, rows, ksem, bsems):
    slots = rows.shape[0]
    live = plan[slots + blocks]
    load = pltpu.make_async_copy(kernel_t, kern, ksem)
    load.start()

    def start(p, carry):
        n = order[p]
        pltpu.make_async_copy(basis.at[n], pair.at[p], bsems.at[p]).start()
        return carry

    lax.fori_loop(0, live, start, 0)
    rows[...] = jnp.zeros_like(rows)
    load.wait()

    def step(p, carry):
        n = order[p]
        pltpu.make_async_copy(basis.at[n], pair.at[p], bsems.at[p]).wait()
        projected = jnp.dot(kern[plan[n]], pair[p, 0], preferred_element_type=jnp.float32)
        product = projected * pair[p, 1].astype(jnp.float32)
        rows[pl.ds(n, 1), :] = jnp.sum(product, axis=0, keepdims=True) * (1.0 / KB)
        return carry

    lax.fori_loop(0, live, step, 0)
    for c in range(out.shape[0]):
        out[c] = rows[...]


def project(plan, order, kernel_t, basis, col_count):
    slots = basis.shape[0]
    blocks = kernel_t.shape[0]
    return pl.pallas_call(
        functools.partial(project_kernel, blocks),
        out_shape=jax.ShapeDtypeStruct((col_count, slots, P_SIZE), jnp.float32),
        in_specs=[SMEM, SMEM, ANY, ANY],
        out_specs=VMEM,
        scratch_shapes=[
            pltpu.VMEM(kernel_t.shape, jnp.bfloat16),
            pltpu.VMEM(basis.shape, jnp.bfloat16),
            pltpu.VMEM((slots, P_SIZE), jnp.float32),
            pltpu.SemaphoreType.DMA,
            pltpu.SemaphoreType.DMA((slots,)),
        ],
        compiler_params=pltpu.CompilerParams(vmem_limit_bytes=32 * MIB),
        name="project",
    )(plan, order, kernel_t, basis)


def update_kernel(
    blocks, tiles, plan, order, tile_of, contributions, collect, core, basis,
    density_out, update_out, pair, density, potential, acc, sems,
):
    slots = pair.shape[0]
    b = pl.program_id(0)
    live = plan[slots + blocks]
    me = plan[slots + blocks + 1]

    @pl.when(b == 0)
    def _():
        def start(p, carry):
            n = order[p]
            pltpu.make_async_copy(basis.at[n], pair.at[p], sems.at[p]).start()
            return carry

        lax.fori_loop(0, live, start, 0)
        density[...] = core[...] + jnp.dot(
            collect[...],
            contributions[...],
            preferred_element_type=jnp.float32,
            precision=lax.Precision.HIGHEST,
        )
        for t in range(tiles):
            density_out[pl.ds(t, 1), :] = density[pl.ds(me * tiles + t, 1), :]
        positive = jnp.maximum(density[...], 0.1)
        root = jnp.exp(jnp.log(positive) * (1.0 / 3.0))
        root = root - (root - positive / (root * root)) * (1.0 / 3.0)
        potential[...] = -exchange_factor * root

    first = plan[slots + b]
    last = plan[slots + b + 1]

    @pl.when(first == last)
    def _():
        update_out[...] = jnp.zeros_like(update_out)

    def step(p, carry):
        n = order[p]
        pltpu.make_async_copy(basis.at[n], pair.at[p], sems.at[p]).wait()
        weight = potential[pl.ds(tile_of[n], 1), :]
        weighted = (pair[p, 1].astype(jnp.float32) * weight).astype(jnp.bfloat16)
        block = lax.dot_general(
            pair[p, 0], weighted, (((1,), (1,)), ((), ())), preferred_element_type=jnp.float32
        )

        @pl.when(p == first)
        def _():
            acc[...] = block

        @pl.when(p != first)
        def _():
            acc[...] += block

        return carry

    lax.fori_loop(first, last, step, 0)

    @pl.when(first != last)
    def _():
        update_out[...] = (acc[...] * (1.0 / math.sqrt(P_SIZE))).astype(jnp.bfloat16)


def update(plan, order, tile_of, contributions, collect, core, basis, tiles, blocks, cols):
    slots = basis.shape[0]
    whole = lambda shape: pl.BlockSpec(shape, lambda b: (0,) * len(shape))
    return pl.pallas_call(
        functools.partial(update_kernel, blocks, tiles),
        grid=(blocks,),
        out_shape=(
            jax.ShapeDtypeStruct((tiles, P_SIZE), jnp.float32),
            jax.ShapeDtypeStruct((blocks * KB, cols), jnp.bfloat16),
        ),
        in_specs=[
            SMEM, SMEM, SMEM,
            whole(contributions.shape), whole(collect.shape), whole(core.shape), ANY,
        ],
        out_specs=(whole((tiles, P_SIZE)), pl.BlockSpec((KB, cols), lambda b: (b, 0))),
        scratch_shapes=[
            pltpu.VMEM(basis.shape, jnp.bfloat16),
            pltpu.VMEM(core.shape, jnp.float32),
            pltpu.VMEM(core.shape, jnp.float32),
            pltpu.VMEM((KB, cols), jnp.float32),
            pltpu.SemaphoreType.DMA((slots,)),
        ],
        compiler_params=pltpu.CompilerParams(vmem_limit_bytes=32 * MIB),
        name="update",
    )(plan, order, tile_of, contributions, collect, core, basis)


def shift(block, axis, step):
    count = lax.axis_size(axis)
    pairs = [(i, i + step) for i in range(count) if 0 <= i + step < count]
    return lax.ppermute(block, axis, pairs)


def make_plan(meta, me, entries, tiles, col_count, blocks):
    slots = col_count * CAP
    core = meta[:, :tiles].reshape(col_count * tiles, P_SIZE)
    lists = meta[:, tiles, : 2 * entries + tiles].astype(jnp.int32)
    peers, named, counts = lists[:, :entries], lists[:, entries : 2 * entries], lists[:, 2 * entries :]
    index = jnp.arange(entries, dtype=jnp.int32)
    home = jnp.arange(col_count, dtype=jnp.int32)[:, None]
    earlier = (peers[:, :, None] == peers[:, None, :]) & (index[None, :] < index[:, None])
    rank = jnp.sum(earlier.astype(jnp.int32), axis=2)
    live = (index % SLOTS)[None, :] < jnp.repeat(counts, SLOTS, axis=1)
    row = peers * slots + home * CAP + rank
    picked = (row[:, :, None] == jnp.arange(col_count * slots, dtype=jnp.int32)) & live[:, :, None]
    collect = jnp.sum(
        picked.astype(jnp.float32).reshape(col_count * tiles, SLOTS, col_count * slots), axis=1
    )
    hit = (
        (peers == me)[:, None, :]
        & (rank[:, None, :] == jnp.arange(CAP, dtype=jnp.int32)[None, :, None])
        & live[:, None, :]
    )
    wanted = (jnp.sum(jnp.where(hit, named[:, None, :] + 1, 0), axis=2) - 1).reshape(slots)
    tile = home * tiles + index[None, :] // SLOTS
    tile_of = jnp.sum(jnp.where(hit, tile[:, None, :], 0), axis=2).reshape(slots)
    key = jnp.where(wanted < 0, blocks, wanted)
    place = jnp.arange(slots, dtype=jnp.int32)
    before = (key[None, :] < key[:, None]) | (
        (key[None, :] == key[:, None]) & (place[None, :] < place[:, None])
    )
    spot = jnp.sum(before.astype(jnp.int32), axis=1)
    order = jnp.sum(jnp.where(spot[None, :] == place[:, None], place[None, :], 0), axis=1)
    starts = jnp.sum(
        (key[None, :] < jnp.arange(blocks + 1, dtype=jnp.int32)[:, None]).astype(jnp.int32), axis=1
    )
    plan = jnp.concatenate([wanted, starts, me[None]]).astype(jnp.int32)
    return core, collect, plan, order.astype(jnp.int32), tile_of.astype(jnp.int32)


def shards(
    start_columns,
    hamiltonian,
    band_pattern,
    coefficients,
    tile_peer,
    tile_block,
    tile_count,
    basis_values,
    core_density,
):
    col_count = lax.axis_size("col")
    slots = col_count * CAP
    entries = tile_peer.shape[0]
    tiles = core_density.shape[0]
    cols = start_columns.shape[1]
    blocks = start_columns.shape[0] // KB
    peers = tile_peer[:, 0]

    masked = mask_couplings(hamiltonian, band_pattern)
    gathered = lax.all_gather(masked, "col", axis=0, tiled=True)

    sent = pack_basis(peers, basis_values, slots)
    basis = lax.all_to_all(
        sent.reshape((col_count, CAP) + sent.shape[1:]), "col", split_axis=0, concat_axis=0, tiled=True
    ).reshape(sent.shape)

    v_low = shift(start_columns[-DEG * W :], "row", 1)
    v_high = shift(start_columns[: DEG * W], "row", -1)

    lists = jnp.concatenate([peers, tile_block, tile_count]).astype(jnp.float32)
    lists = jnp.pad(lists, (0, P_SIZE - lists.shape[0]))
    meta = jnp.concatenate([core_density, lists[None]], axis=0)
    meta = jnp.pad(meta, ((0, -meta.shape[0] % 8), (0, 0)))
    meta = lax.all_to_all(
        jnp.broadcast_to(meta[None], (col_count,) + meta.shape),
        "col", split_axis=0, concat_axis=0, tiled=True,
    )
    me = lax.axis_index("col").astype(jnp.int32)
    core, collect, plan, order, tile_of = make_plan(meta, me, entries, tiles, col_count, blocks)

    h_low = shift(gathered[-(DEG - 1) :], "row", 1)
    h_high = shift(gathered[: DEG - 1], "row", -1)
    kernel_t = chebyshev(coefficients, v_low, start_columns, v_high, h_low, gathered, h_high)

    partial = project(plan, order, kernel_t, basis, col_count)
    contributions = lax.all_to_all(partial, "col", split_axis=0, concat_axis=0, tiled=True)
    contributions = contributions.reshape(col_count * slots, P_SIZE)
    return update(
        plan, order, tile_of, contributions, collect, core, basis, tiles, blocks, cols
    )


def solution(mesh):
    return jax.shard_map(
        shards,
        mesh=mesh,
        in_specs=(
            P("row", "col"),
            P(("row", "col"), None, None, None),
            P(("row", "col")),
            P(),
            P(("row", "col"), None),
            P(("row", "col")),
            P(("row", "col")),
            P(("row", "col"), None, None, None),
            P(("row", "col"), None),
        ),
        out_specs=(P(("row", "col"), None), P("row", "col")),
        check_vma=False,
    )
```

```python
import functools
import math

import jax
import jax.numpy as jnp
from jax import lax
from jax.experimental import pallas as pl
from jax.experimental.pallas import tpu as pltpu
from jax.sharding import PartitionSpec as P

W = 256
KB = 512
DEG = 3
SLOTS = 4
CAP = 2
P_SIZE = 128
MIB = 1 << 20

exchange_factor = (3.0 / math.pi) ** (1.0 / 3.0)
ANY = pl.BlockSpec(memory_space=pl.ANY)
SMEM = pl.BlockSpec(memory_space=pltpu.SMEM)
VMEM = pl.BlockSpec(memory_space=pltpu.VMEM)


def mask_kernel(pattern, ham, out):
    for i in range(ham.shape[0]):
        out[i, 0] = ham[i, 0]
        out[i, 1] = ham[i, 1] * pattern[i].astype(jnp.bfloat16)


def mask_couplings(hamiltonian, band_pattern):
    return pl.pallas_call(
        mask_kernel,
        out_shape=jax.ShapeDtypeStruct(hamiltonian.shape, hamiltonian.dtype),
        in_specs=[SMEM, VMEM],
        out_specs=VMEM,
        name="mask_couplings",
    )(band_pattern, hamiltonian)


def pack_kernel(entries, slots, peers, basis, out_0, out_1, held, owner, count, in_sems, out_sems):
    def fetch(e):
        return pltpu.make_async_copy(basis.at[e], held.at[e], in_sems.at[e])

    def send(s, half):
        out = (out_0, out_1)[half]
        return pltpu.make_async_copy(held.at[owner[s], half], out.at[s], out_sems.at[half, s])

    for e in range(entries):
        fetch(e).start()
    for s in range(slots):
        owner[s] = 0
    for c in range(slots // CAP):
        count[c] = 0

    def place(e, carry):
        p = peers[e]
        k = count[p]
        count[p] = k + 1
        owner[p * CAP + k] = e
        return carry

    lax.fori_loop(0, entries, place, 0)
    for e in range(entries):
        fetch(e).wait()
    for half in range(2):
        for s in range(slots):
            send(s, half).start()
    for half in range(2):
        for s in range(slots):
            send(s, half).wait()


def pack_basis(peers, basis, slots):
    entries = basis.shape[0]
    half = jax.ShapeDtypeStruct((slots,) + basis.shape[2:], basis.dtype)
    return pl.pallas_call(
        functools.partial(pack_kernel, entries, slots),
        out_shape=(half, half),
        in_specs=[SMEM, ANY],
        out_specs=(ANY, ANY),
        scratch_shapes=[
            pltpu.VMEM(basis.shape, basis.dtype),
            pltpu.SMEM((slots,), jnp.int32),
            pltpu.SMEM((slots // CAP,), jnp.int32),
            pltpu.SemaphoreType.DMA((entries,)),
            pltpu.SemaphoreType.DMA((2, slots)),
        ],
        name="pack_basis",
    )(peers, basis)


def gather_pieces(own):
    count = lax.axis_size("col")
    outer = 4 if count % 4 == 0 else count
    inner = count // outer
    me = lax.axis_index("col").astype(jnp.int32)
    a, b = me // inner, me % inner

    def hop(block, pairs):
        return lax.ppermute(block, "col", pairs)

    def inside(i, size):
        return (i >= 0) & (i < size)

    lines = [(own, 0)]
    for way in (1, -1):
        block = own
        for step in range(1, outer):
            pairs = [
                (x * inner + y, (x + way) * inner + y)
                for x in range(outer) for y in range(inner)
                if 0 <= x + way < outer and 0 <= x - way * (step - 1) < outer
            ]
            block = hop(block, pairs)
            lines.append((block, -way * step))
    pieces, owners = [], []
    for line, shift_a in lines:
        pieces.append(line)
        owners.append(jnp.where(inside(a + shift_a, outer), (a + shift_a) * inner + b, -1))
        rows = [x for x in range(outer) if 0 <= x + shift_a < outer]
        if inner == 2:
            pairs = [(x * inner + y, x * inner + 1 - y) for x in rows for y in range(inner)]
            pieces.append(hop(line, pairs))
            owners.append(jnp.where(inside(a + shift_a, outer), (a + shift_a) * inner + 1 - b, -1))
            continue
        for way in (1, -1):
            block = line
            for step in range(1, inner):
                pairs = [
                    (x * inner + y, x * inner + y + way)
                    for x in rows for y in range(inner)
                    if 0 <= y + way < inner and 0 <= y - way * (step - 1) < inner
                ]
                block = hop(block, pairs)
                pieces.append(block)
                valid = inside(a + shift_a, outer) & inside(b - way * step, inner)
                owners.append(jnp.where(valid, (a + shift_a) * inner + b - way * step, -1))
    return pieces, jnp.stack(owners).astype(jnp.int32)


def edge_kernel(col_count, depth, owners, *refs):
    pieces, (first, last, sems) = refs[:-3], refs[-3:]
    held = pieces[0].shape[0]
    total = col_count * held

    def each(act):
        for i, piece in enumerate(pieces):
            for g in range(depth):
                for out, block, sem in ((first, g, 0), (last, total - depth + g, 1)):
                    copy = pltpu.make_async_copy(piece.at[block % held], out.at[g], sems.at[sem, g])

                    @pl.when(owners[i] == block // held)
                    def _():
                        act(copy)

    each(lambda copy: copy.start())
    each(lambda copy: copy.wait())


def edge_blocks(owners, pieces, col_count, depth):
    shape = jax.ShapeDtypeStruct((depth,) + pieces[0].shape[1:], pieces[0].dtype)
    return pl.pallas_call(
        functools.partial(edge_kernel, col_count, depth),
        out_shape=(shape, shape),
        in_specs=[SMEM] + [ANY] * len(pieces),
        out_specs=(VMEM, VMEM),
        scratch_shapes=[pltpu.SemaphoreType.DMA((2, depth))],
        name="edge_blocks",
    )(owners, *pieces)


def cheb_kernel(
    blocks, coef, owners, plan, order, v_low, v_mid, v_high, h_low, h_high, basis, *refs
):
    *pieces, out, vext, hraw, hcat, cheb_1, cheb_2, total, kern, pair, sems, psems, bsems = refs
    halo_v = DEG
    halo_h = DEG - 1
    held = pieces[0].shape[0]
    kern_blocks = kern.shape[0]
    slots = pair.shape[0]
    live = plan[slots + kern_blocks]
    copies = [
        pltpu.make_async_copy(h_low, hraw.at[pl.ds(0, halo_h)], sems.at[0]),
        pltpu.make_async_copy(h_high, hraw.at[pl.ds(halo_h + blocks, halo_h)], sems.at[1]),
        pltpu.make_async_copy(v_low, vext.at[pl.ds(0, halo_v * W)], sems.at[2]),
        pltpu.make_async_copy(v_mid, vext.at[pl.ds(halo_v * W, blocks * W)], sems.at[3]),
        pltpu.make_async_copy(v_high, vext.at[pl.ds((halo_v + blocks) * W, halo_v * W)], sems.at[4]),
    ]

    def each_piece(act):
        for i, piece in enumerate(pieces):
            @pl.when(owners[i] >= 0)
            def _():
                act(pltpu.make_async_copy(
                    piece, hraw.at[pl.ds(halo_h + owners[i] * held, held)], psems.at[i]
                ))

    each_piece(lambda copy: copy.start())
    for copy in copies:
        copy.start()

    def fetch(p, carry):
        pltpu.make_async_copy(basis.at[order[p]], pair.at[p], bsems.at[p]).start()
        return carry

    lax.fori_loop(0, live, fetch, 0)
    each_piece(lambda copy: copy.wait())
    for copy in copies:
        copy.wait()
    rows = lax.broadcasted_iota(jnp.int32, (W, W), 0)
    cols = lax.broadcasted_iota(jnp.int32, (W, W), 1)
    upper = rows <= cols

    def build(j, carry):
        coupling = hraw[j, 1].astype(jnp.float32)
        hcat[j, :, 0:W] = jnp.where(upper, coupling, 0.0).astype(jnp.bfloat16)
        hcat[j, :, W : 2 * W] = hraw[j, 0]
        hcat[j, :, 2 * W : 3 * W] = jnp.where(upper, 0.0, coupling).astype(jnp.bfloat16)
        return carry

    lax.fori_loop(0, blocks + 2 * halo_h, build, 0)

    def band(source, j):
        start = pl.multiple_of(j * W, W)
        return jnp.dot(
            hcat[j], source[pl.ds(start, 3 * W), :], preferred_element_type=jnp.float32
        )

    def rows_of(j):
        return pl.ds(pl.multiple_of(j * W, W), W)

    def first(j, carry):
        value = band(vext, j)
        cheb_1[rows_of(j), :] = value.astype(jnp.bfloat16)

        @pl.when((j >= 2) & (j < blocks + 2))
        def _():
            total[rows_of(j - 2), :] = value

        return carry

    lax.fori_loop(0, blocks + 4, first, 0)

    def second(j, carry):
        start = pl.multiple_of(j * W, W)
        value = 2.0 * jnp.dot(
            hcat[j + 1], cheb_1[pl.ds(start, 3 * W), :], preferred_element_type=jnp.float32
        )
        begin = vext[rows_of(j + 2), :].astype(jnp.float32)
        value = value - begin
        cheb_2[rows_of(j), :] = value.astype(jnp.bfloat16)

        @pl.when((j >= 1) & (j < blocks + 1))
        def _():
            total[rows_of(j - 1), :] = (
                coef[0] * begin + (coef[1] - coef[3]) * total[rows_of(j - 1), :] + coef[2] * value
            )

        return carry

    lax.fori_loop(0, blocks + 2, second, 0)

    def third(j, carry):
        for half in range(KB // W):
            i = j * (KB // W) + half
            start = pl.multiple_of(i * W, W)
            value = jnp.dot(
                hcat[i + 2], cheb_2[pl.ds(start, 3 * W), :], preferred_element_type=jnp.float32
            )
            value = total[rows_of(i), :] + (2.0 * coef[3]) * value
            kern[j, :, half * W : (half + 1) * W] = value.T.astype(jnp.bfloat16)
        return carry

    lax.fori_loop(0, blocks // (KB // W), third, 0)

    def project(p, carry):
        n = order[p]
        pltpu.make_async_copy(basis.at[n], pair.at[p], bsems.at[p]).wait()
        out[p] = jnp.dot(kern[plan[n]], pair[p], preferred_element_type=jnp.float32)
        return carry

    lax.fori_loop(0, live, project, 0)


def chebyshev(
    coefficients, owners, plan, order, v_low, v_mid, v_high, h_low, h_high, basis, pieces
):
    blocks = v_mid.shape[0] // W
    cols = v_mid.shape[1]
    slots = basis.shape[0]
    ext = blocks + 2 * (DEG - 1)
    flops = 2 * W * 3 * W * cols * (3 * blocks + 6)
    return pl.pallas_call(
        functools.partial(cheb_kernel, blocks),
        out_shape=jax.ShapeDtypeStruct((slots, cols, P_SIZE), jnp.float32),
        in_specs=[SMEM] * 4 + [ANY] * (6 + len(pieces)),
        out_specs=VMEM,
        scratch_shapes=[
            pltpu.VMEM(((blocks + 2 * DEG) * W, cols), jnp.bfloat16),
            pltpu.VMEM((ext, 2, W, W), jnp.bfloat16),
            pltpu.VMEM((ext, W, 3 * W), jnp.bfloat16),
            pltpu.VMEM((ext * W, cols), jnp.bfloat16),
            pltpu.VMEM(((blocks + 2) * W, cols), jnp.bfloat16),
            pltpu.VMEM((blocks * W, cols), jnp.float32),
            pltpu.VMEM((blocks * W // KB, cols, KB), jnp.bfloat16),
            pltpu.VMEM(basis.shape, jnp.bfloat16),
            pltpu.SemaphoreType.DMA((5,)),
            pltpu.SemaphoreType.DMA((len(pieces),)),
            pltpu.SemaphoreType.DMA((slots,)),
        ],
        compiler_params=pltpu.CompilerParams(vmem_limit_bytes=56 * MIB),
        cost_estimate=pl.CostEstimate(flops=flops, bytes_accessed=16 * MIB, transcendentals=0),
        name="chebyshev",
    )(coefficients, owners, plan, order, v_low, v_mid, v_high, h_low, h_high, basis, *pieces)


def contribute_kernel(blocks, plan, order, projected, basis, out, proj, pair, rows, psems, bsems):
    slots = rows.shape[0]
    live = plan[slots + blocks]

    def load(p):
        return (
            pltpu.make_async_copy(projected.at[p], proj.at[p], psems.at[p]),
            pltpu.make_async_copy(basis.at[order[p]], pair.at[p], bsems.at[p]),
        )

    def start(p, carry):
        for copy in load(p):
            copy.start()
        return carry

    lax.fori_loop(0, live, start, 0)
    rows[...] = jnp.zeros_like(rows)

    def step(p, carry):
        for copy in load(p):
            copy.wait()
        product = proj[p] * pair[p].astype(jnp.float32)
        rows[pl.ds(order[p], 1), :] = jnp.sum(product, axis=0, keepdims=True) * (1.0 / KB)
        return carry

    lax.fori_loop(0, live, step, 0)
    for c in range(out.shape[0]):
        out[c] = rows[...]


def contribute(plan, order, projected, basis, col_count, blocks):
    slots = basis.shape[0]
    return pl.pallas_call(
        functools.partial(contribute_kernel, blocks),
        out_shape=jax.ShapeDtypeStruct((col_count, slots, P_SIZE), jnp.float32),
        in_specs=[SMEM, SMEM, ANY, ANY],
        out_specs=VMEM,
        scratch_shapes=[
            pltpu.VMEM(projected.shape, jnp.float32),
            pltpu.VMEM(basis.shape, jnp.bfloat16),
            pltpu.VMEM((slots, P_SIZE), jnp.float32),
            pltpu.SemaphoreType.DMA((slots,)),
            pltpu.SemaphoreType.DMA((slots,)),
        ],
        compiler_params=pltpu.CompilerParams(vmem_limit_bytes=56 * MIB),
        name="contribute",
    )(plan, order, projected, basis)


def update_kernel(
    blocks, tiles, plan, order, tile_of, contributions, collect, core, basis_0, basis_1,
    density_out, update_out, pair, density, potential, acc, sems,
):
    slots = pair.shape[1]
    b = pl.program_id(0)
    live = plan[slots + blocks]
    me = plan[slots + blocks + 1]

    def load(p):
        n = order[p]
        return [
            pltpu.make_async_copy(basis.at[n], pair.at[half, p], sems.at[half, p])
            for half, basis in enumerate((basis_0, basis_1))
        ]

    @pl.when(b == 0)
    def _():
        def start(p, carry):
            for copy in load(p):
                copy.start()
            return carry

        lax.fori_loop(0, live, start, 0)
        density[...] = core[...] + jnp.dot(
            collect[...],
            contributions[...],
            preferred_element_type=jnp.float32,
            precision=lax.Precision.HIGHEST,
        )
        for t in range(tiles):
            density_out[pl.ds(t, 1), :] = density[pl.ds(me * tiles + t, 1), :]
        positive = jnp.maximum(density[...], 0.1)
        root = jnp.exp(jnp.log(positive) * (1.0 / 3.0))
        root = root - (root - positive / (root * root)) * (1.0 / 3.0)
        potential[...] = -exchange_factor * root

    first = plan[slots + b]
    last = plan[slots + b + 1]

    @pl.when(first == last)
    def _():
        update_out[...] = jnp.zeros_like(update_out)

    def step(p, carry):
        for copy in load(p):
            copy.wait()
        weight = potential[pl.ds(tile_of[order[p]], 1), :]
        weighted = (pair[1, p].astype(jnp.float32) * weight).astype(jnp.bfloat16)
        block = lax.dot_general(
            pair[0, p], weighted, (((1,), (1,)), ((), ())), preferred_element_type=jnp.float32
        )

        @pl.when(p == first)
        def _():
            acc[...] = block

        @pl.when(p != first)
        def _():
            acc[...] += block

        return carry

    lax.fori_loop(first, last, step, 0)

    @pl.when(first != last)
    def _():
        update_out[...] = (acc[...] * (1.0 / math.sqrt(P_SIZE))).astype(jnp.bfloat16)


def update(plan, order, tile_of, contributions, collect, core, basis_0, basis_1, tiles, blocks, cols):
    slots = basis_0.shape[0]
    whole = lambda shape: pl.BlockSpec(shape, lambda b: (0,) * len(shape))
    return pl.pallas_call(
        functools.partial(update_kernel, blocks, tiles),
        grid=(blocks,),
        out_shape=(
            jax.ShapeDtypeStruct((tiles, P_SIZE), jnp.float32),
            jax.ShapeDtypeStruct((blocks * KB, cols), jnp.bfloat16),
        ),
        in_specs=[
            SMEM, SMEM, SMEM,
            whole(contributions.shape), whole(collect.shape), whole(core.shape), ANY, ANY,
        ],
        out_specs=(whole((tiles, P_SIZE)), pl.BlockSpec((KB, cols), lambda b: (b, 0))),
        scratch_shapes=[
            pltpu.VMEM((2,) + basis_0.shape, jnp.bfloat16),
            pltpu.VMEM(core.shape, jnp.float32),
            pltpu.VMEM(core.shape, jnp.float32),
            pltpu.VMEM((KB, cols), jnp.float32),
            pltpu.SemaphoreType.DMA((2, slots)),
        ],
        compiler_params=pltpu.CompilerParams(vmem_limit_bytes=56 * MIB),
        name="update",
    )(plan, order, tile_of, contributions, collect, core, basis_0, basis_1)


def shift(block, axis, step):
    count = lax.axis_size(axis)
    pairs = [(i, i + step) for i in range(count) if 0 <= i + step < count]
    return lax.ppermute(block, axis, pairs)


def make_plan(meta, me, entries, tiles, col_count, blocks):
    slots = col_count * CAP
    core = meta[:, :tiles].reshape(col_count * tiles, P_SIZE)
    lists = meta[:, tiles, : 2 * entries + tiles].astype(jnp.int32)
    peers, named, counts = lists[:, :entries], lists[:, entries : 2 * entries], lists[:, 2 * entries :]
    index = jnp.arange(entries, dtype=jnp.int32)
    home = jnp.arange(col_count, dtype=jnp.int32)[:, None]
    earlier = (peers[:, :, None] == peers[:, None, :]) & (index[None, :] < index[:, None])
    rank = jnp.sum(earlier.astype(jnp.int32), axis=2)
    live = (index % SLOTS)[None, :] < jnp.repeat(counts, SLOTS, axis=1)
    row = peers * slots + home * CAP + rank
    picked = (row[:, :, None] == jnp.arange(col_count * slots, dtype=jnp.int32)) & live[:, :, None]
    collect = jnp.sum(
        picked.astype(jnp.float32).reshape(col_count * tiles, SLOTS, col_count * slots), axis=1
    )
    hit = (
        (peers == me)[:, None, :]
        & (rank[:, None, :] == jnp.arange(CAP, dtype=jnp.int32)[None, :, None])
        & live[:, None, :]
    )
    wanted = (jnp.sum(jnp.where(hit, named[:, None, :] + 1, 0), axis=2) - 1).reshape(slots)
    tile = home * tiles + index[None, :] // SLOTS
    tile_of = jnp.sum(jnp.where(hit, tile[:, None, :], 0), axis=2).reshape(slots)
    key = jnp.where(wanted < 0, blocks, wanted)
    place = jnp.arange(slots, dtype=jnp.int32)
    before = (key[None, :] < key[:, None]) | (
        (key[None, :] == key[:, None]) & (place[None, :] < place[:, None])
    )
    spot = jnp.sum(before.astype(jnp.int32), axis=1)
    order = jnp.sum(jnp.where(spot[None, :] == place[:, None], place[None, :], 0), axis=1)
    starts = jnp.sum(
        (key[None, :] < jnp.arange(blocks + 1, dtype=jnp.int32)[:, None]).astype(jnp.int32), axis=1
    )
    plan = jnp.concatenate([wanted, starts, me[None]]).astype(jnp.int32)
    return core, collect, plan, order.astype(jnp.int32), tile_of.astype(jnp.int32)


def shards(
    start_columns,
    hamiltonian,
    band_pattern,
    coefficients,
    tile_peer,
    tile_block,
    tile_count,
    basis_values,
    core_density,
):
    col_count = lax.axis_size("col")
    slots = col_count * CAP
    entries = tile_peer.shape[0]
    tiles = core_density.shape[0]
    cols = start_columns.shape[1]
    blocks = start_columns.shape[0] // KB
    peers = tile_peer[:, 0]

    masked = mask_couplings(hamiltonian, band_pattern)
    pieces, owners = gather_pieces(masked)

    def exchange(block):
        return lax.all_to_all(
            block.reshape((col_count, CAP) + block.shape[1:]),
            "col", split_axis=0, concat_axis=0, tiled=True,
        ).reshape(block.shape)

    sent_0, sent_1 = pack_basis(peers, basis_values, slots)
    basis_0, basis_1 = exchange(sent_0), exchange(sent_1)

    v_low = shift(start_columns[-DEG * W :], "row", 1)
    v_high = shift(start_columns[: DEG * W], "row", -1)

    lists = jnp.concatenate([peers, tile_block, tile_count]).astype(jnp.float32)
    lists = jnp.pad(lists, (0, P_SIZE - lists.shape[0]))
    meta = jnp.concatenate([core_density, lists[None]], axis=0)
    meta = jnp.pad(meta, ((0, -meta.shape[0] % 8), (0, 0)))
    meta = lax.all_to_all(
        jnp.broadcast_to(meta[None], (col_count,) + meta.shape),
        "col", split_axis=0, concat_axis=0, tiled=True,
    )
    me = lax.axis_index("col").astype(jnp.int32)
    core, collect, plan, order, tile_of = make_plan(meta, me, entries, tiles, col_count, blocks)

    first, last = edge_blocks(owners, pieces, col_count, DEG - 1)
    h_low = shift(last, "row", 1)
    h_high = shift(first, "row", -1)
    projected = chebyshev(
        coefficients, owners, plan, order, v_low, start_columns, v_high, h_low, h_high, basis_0, pieces
    )

    partial = contribute(plan, order, projected, basis_1, col_count, blocks)
    contributions = lax.all_to_all(partial, "col", split_axis=0, concat_axis=0, tiled=True)
    contributions = contributions.reshape(col_count * slots, P_SIZE)
    return update(
        plan, order, tile_of, contributions, collect, core, basis_0, basis_1, tiles, blocks, cols
    )


def solution(mesh):
    return jax.shard_map(
        shards,
        mesh=mesh,
        in_specs=(
            P("row", "col"),
            P(("row", "col"), None, None, None),
            P(("row", "col")),
            P(),
            P(("row", "col"), None),
            P(("row", "col")),
            P(("row", "col")),
            P(("row", "col"), None, None, None),
            P(("row", "col"), None),
        ),
        out_specs=(P(("row", "col"), None), P("row", "col")),
        check_vma=False,
    )
```

```python
import functools
import math

import jax
import jax.numpy as jnp
from jax import lax
from jax.experimental import pallas as pl
from jax.experimental.pallas import tpu as pltpu
from jax.sharding import PartitionSpec as P

W = 256
KB = 512
DEG = 3
SLOTS = 4
CAP = 2
P_SIZE = 128
MIB = 1 << 20

exchange_factor = (3.0 / math.pi) ** (1.0 / 3.0)
HBM = pl.BlockSpec(memory_space=pltpu.HBM)
SMEM = pl.BlockSpec(memory_space=pltpu.SMEM)
VMEM = pl.BlockSpec(memory_space=pltpu.VMEM)


def prepare_kernel(
    entries, slots, peers, pattern, basis, ham, sent, masked,
    held, blocks, count, in_sems, out_sems, ham_sems,
):
    def fetch(e):
        return pltpu.make_async_copy(basis.at[e], held.at[e], in_sems.at[e])

    def send(e, s):
        return pltpu.make_async_copy(held.at[e], sent.at[s], out_sems.at[s])

    load = pltpu.make_async_copy(ham, blocks, ham_sems.at[0])
    store = pltpu.make_async_copy(blocks, masked, ham_sems.at[1])
    load.start()
    for e in range(entries):
        fetch(e).start()
    for c in range(slots // CAP):
        count[c] = 0
    load.wait()
    for i in range(blocks.shape[0]):
        blocks[i, 1] = blocks[i, 1] * pattern[i].astype(jnp.bfloat16)
    store.start()
    for e in range(entries):
        p = peers[e]
        k = count[p]
        count[p] = k + 1
        fetch(e).wait()
        send(e, p * CAP + k).start()
    for c in range(slots // CAP):
        for k in range(CAP):
            @pl.when(count[c] <= k)
            def _():
                send(0, c * CAP + k).start()
    for s in range(slots):
        send(0, s).wait()
    store.wait()


def prepare(peers, pattern, basis, ham, slots):
    entries = basis.shape[0]
    return pl.pallas_call(
        functools.partial(prepare_kernel, entries, slots),
        out_shape=(
            jax.ShapeDtypeStruct((slots,) + basis.shape[1:], basis.dtype),
            jax.ShapeDtypeStruct(ham.shape, ham.dtype),
        ),
        in_specs=[SMEM, SMEM, HBM, HBM],
        out_specs=(HBM, HBM),
        scratch_shapes=[
            pltpu.VMEM(basis.shape, basis.dtype),
            pltpu.VMEM(ham.shape, ham.dtype),
            pltpu.SMEM((slots // CAP,), jnp.int32),
            pltpu.SemaphoreType.DMA((entries,)),
            pltpu.SemaphoreType.DMA((slots,)),
            pltpu.SemaphoreType.DMA((2,)),
        ],
        compiler_params=pltpu.CompilerParams(vmem_limit_bytes=16 * MIB),
        name="prepare",
    )(peers, pattern, basis, ham)


def gather_pieces(own):
    count = lax.axis_size("col")
    outer = 4 if count % 4 == 0 else count
    inner = count // outer
    me = lax.axis_index("col").astype(jnp.int32)
    a, b = me // inner, me % inner

    def hop(block, pairs):
        return lax.ppermute(block, "col", pairs)

    def inside(i, size):
        return (i >= 0) & (i < size)

    lines = [(own, 0)]
    for way in (1, -1):
        block = own
        for step in range(1, outer):
            pairs = [
                (x * inner + y, (x + way) * inner + y)
                for x in range(outer) for y in range(inner)
                if 0 <= x + way < outer and 0 <= x - way * (step - 1) < outer
            ]
            block = hop(block, pairs)
            lines.append((block, -way * step))
    pieces, owners = [], []
    for line, shift_a in lines:
        pieces.append(line)
        owners.append(jnp.where(inside(a + shift_a, outer), (a + shift_a) * inner + b, -1))
        rows = [x for x in range(outer) if 0 <= x + shift_a < outer]
        if inner == 2:
            pairs = [(x * inner + y, x * inner + 1 - y) for x in rows for y in range(inner)]
            pieces.append(hop(line, pairs))
            owners.append(jnp.where(inside(a + shift_a, outer), (a + shift_a) * inner + 1 - b, -1))
            continue
        for way in (1, -1):
            block = line
            for step in range(1, inner):
                pairs = [
                    (x * inner + y, x * inner + y + way)
                    for x in rows for y in range(inner)
                    if 0 <= y + way < inner and 0 <= y - way * (step - 1) < inner
                ]
                block = hop(block, pairs)
                pieces.append(block)
                valid = inside(a + shift_a, outer) & inside(b - way * step, inner)
                owners.append(jnp.where(valid, (a + shift_a) * inner + b - way * step, -1))
    return pieces, jnp.stack(owners).astype(jnp.int32)


def edge_kernel(col_count, depth, owners, *refs):
    pieces, (first, last, sems) = refs[:-3], refs[-3:]
    held = pieces[0].shape[0]
    total = col_count * held

    def each(act):
        for i, piece in enumerate(pieces):
            for g in range(depth):
                for out, block, sem in ((first, g, 0), (last, total - depth + g, 1)):
                    copy = pltpu.make_async_copy(piece.at[block % held], out.at[g], sems.at[sem, g])

                    @pl.when(owners[i] == block // held)
                    def _():
                        act(copy)

    each(lambda copy: copy.start())
    each(lambda copy: copy.wait())


def edge_blocks(owners, pieces, col_count, depth):
    shape = jax.ShapeDtypeStruct((depth,) + pieces[0].shape[1:], pieces[0].dtype)
    return pl.pallas_call(
        functools.partial(edge_kernel, col_count, depth),
        out_shape=(shape, shape),
        in_specs=[SMEM] + [HBM] * len(pieces),
        out_specs=(VMEM, VMEM),
        scratch_shapes=[pltpu.SemaphoreType.DMA((2, depth))],
        name="edge_blocks",
    )(owners, *pieces)


def cheb_kernel(blocks, coef, owners, v_low, v_mid, v_high, h_low, h_high, *refs):
    *pieces, out, vext, hraw, hcat, cheb_1, cheb_2, total, kern, sems, psems, osems = refs
    halo_v = DEG
    halo_h = DEG - 1
    held = pieces[0].shape[0]
    h_copies = [
        pltpu.make_async_copy(h_low, hraw.at[pl.ds(0, halo_h)], sems.at[0]),
        pltpu.make_async_copy(h_high, hraw.at[pl.ds(halo_h + blocks, halo_h)], sems.at[1]),
    ]
    v_copies = [
        pltpu.make_async_copy(v_low, vext.at[pl.ds(0, halo_v * W)], sems.at[2]),
        pltpu.make_async_copy(v_mid, vext.at[pl.ds(halo_v * W, blocks * W)], sems.at[3]),
        pltpu.make_async_copy(v_high, vext.at[pl.ds((halo_v + blocks) * W, halo_v * W)], sems.at[4]),
    ]

    def each_piece(act):
        for i, piece in enumerate(pieces):
            @pl.when(owners[i] >= 0)
            def _():
                act(pltpu.make_async_copy(
                    piece, hraw.at[pl.ds(halo_h + owners[i] * held, held)], psems.at[i]
                ))

    each_piece(lambda copy: copy.start())
    for copy in h_copies + v_copies:
        copy.start()
    each_piece(lambda copy: copy.wait())
    for copy in h_copies:
        copy.wait()
    rows = lax.broadcasted_iota(jnp.int32, (W, W), 0)
    cols = lax.broadcasted_iota(jnp.int32, (W, W), 1)
    upper = jnp.where(rows <= cols, 1.0, 0.0).astype(jnp.bfloat16)

    def build(j, carry):
        coupling = hraw[j, 1]
        lower_band = coupling * upper
        hcat[j, :, 0:W] = lower_band
        hcat[j, :, W : 2 * W] = hraw[j, 0]
        hcat[j, :, 2 * W : 3 * W] = coupling - lower_band
        return carry

    lax.fori_loop(0, blocks + 2 * halo_h, build, 0, unroll=2)
    for copy in v_copies:
        copy.wait()

    def rows_of(j, count=1):
        return pl.ds(pl.multiple_of(j * W, W), count * W)

    def band(source, j, row):
        return jnp.dot(hcat[j], source[rows_of(row, 3), :], preferred_element_type=jnp.float32)

    def first(j, carry):
        value = band(vext, j, j)
        cheb_1[rows_of(j), :] = value.astype(jnp.bfloat16)
        total[rows_of(j), :] = value
        return carry

    lax.fori_loop(0, blocks + 4, first, 0, unroll=2)

    def second(j, carry):
        begin = vext[rows_of(j + 2), :].astype(jnp.float32)
        value = 2.0 * band(cheb_1, j + 1, j) - begin
        cheb_2[rows_of(j), :] = value.astype(jnp.bfloat16)
        total[rows_of(j + 1), :] = (
            coef[0] * begin + (coef[1] - coef[3]) * total[rows_of(j + 1), :] + coef[2] * value
        )
        return carry

    lax.fori_loop(0, blocks + 2, second, 0, unroll=2)

    def store(j):
        return pltpu.make_async_copy(kern.at[j], out.at[j], osems.at[j])

    def third(j, carry):
        for half in range(KB // W):
            i = j * (KB // W) + half
            value = total[rows_of(i + 2), :] + (2.0 * coef[3]) * band(cheb_2, i + 2, i)
            kern[j, :, half * W : (half + 1) * W] = value.astype(jnp.bfloat16).T
        store(j).start()
        return carry

    lax.fori_loop(0, blocks // (KB // W), third, 0)
    for j in range(blocks // (KB // W)):
        store(j).wait()


def chebyshev(coefficients, owners, v_low, v_mid, v_high, h_low, h_high, pieces):
    blocks = v_mid.shape[0] // W
    cols = v_mid.shape[1]
    ext = blocks + 2 * (DEG - 1)
    flops = 2 * W * 3 * W * cols * (3 * blocks + 6)
    result = (blocks * W // KB, cols, KB)
    return pl.pallas_call(
        functools.partial(cheb_kernel, blocks),
        out_shape=jax.ShapeDtypeStruct(result, jnp.bfloat16),
        in_specs=[SMEM] * 2 + [HBM] * (5 + len(pieces)),
        out_specs=HBM,
        scratch_shapes=[
            pltpu.VMEM(((blocks + 2 * DEG) * W, cols), jnp.bfloat16),
            pltpu.VMEM((ext, 2, W, W), jnp.bfloat16),
            pltpu.VMEM((ext, W, 3 * W), jnp.bfloat16),
            pltpu.VMEM((ext * W, cols), jnp.bfloat16),
            pltpu.VMEM(((blocks + 2) * W, cols), jnp.bfloat16),
            pltpu.VMEM((ext * W, cols), jnp.float32),
            pltpu.VMEM(result, jnp.bfloat16),
            pltpu.SemaphoreType.DMA((5,)),
            pltpu.SemaphoreType.DMA((len(pieces),)),
            pltpu.SemaphoreType.DMA((result[0],)),
        ],
        compiler_params=pltpu.CompilerParams(vmem_limit_bytes=56 * MIB),
        cost_estimate=pl.CostEstimate(flops=flops, bytes_accessed=16 * MIB, transcendentals=0),
        name="chebyshev",
    )(coefficients, owners, v_low, v_mid, v_high, h_low, h_high, *pieces)


def entry_loads(order, basis, pair, sems):
    def load(p):
        return pltpu.make_async_copy(basis.at[order[p]], pair.at[p], sems.at[p])

    def start(p, carry):
        load(p).start()
        return carry

    return load, start


def by_twos(first, last, load, body):
    def step(i, carry):
        p = first + 2 * i
        q = jnp.minimum(p + 1, last - 1)
        load(p).wait()

        @pl.when(q > p)
        def _():
            load(q).wait()

        body(i, p, q)
        return carry

    lax.fori_loop(0, (last - first + 1) // 2, step, 0)


def project_kernel(blocks, plan, order, kernel_t, basis, out, kern, pair, rows, ksems, bsems):
    slots = rows.shape[0]
    load, start = entry_loads(order, basis, pair, bsems)

    def fetch(b):
        return pltpu.make_async_copy(kernel_t.at[b], kern.at[b], ksems.at[b])

    def begin(b, carry):
        first, last = plan[slots + b], plan[slots + b + 1]

        @pl.when(first < last)
        def _():
            fetch(b).start()

        return lax.fori_loop(first, last, start, carry)

    lax.fori_loop(0, blocks, begin, 0)
    rows[...] = jnp.zeros_like(rows)

    def step(b, carry):
        first, last = plan[slots + b], plan[slots + b + 1]

        @pl.when(first < last)
        def _():
            fetch(b).wait()

        def body(i, p, q):
            both = jnp.concatenate([pair[p, 0], pair[q, 0]], axis=1)
            projected = jnp.dot(kern[b], both, preferred_element_type=jnp.float32)
            other = jnp.concatenate([pair[p, 1], pair[q, 1]], axis=1).astype(jnp.float32)
            value = jnp.sum(projected * other, axis=0, keepdims=True) * (1.0 / KB)
            rows[pl.ds(order[p], 1), :] = value[:, :P_SIZE]
            rows[pl.ds(order[q], 1), :] = value[:, P_SIZE:]

        by_twos(first, last, load, body)
        return carry

    lax.fori_loop(0, blocks, step, 0)
    for c in range(out.shape[0]):
        out[c] = rows[...]


def project(plan, order, kernel_t, basis, col_count):
    slots = basis.shape[0]
    blocks = kernel_t.shape[0]
    return pl.pallas_call(
        functools.partial(project_kernel, blocks),
        out_shape=jax.ShapeDtypeStruct((col_count, slots, P_SIZE), jnp.float32),
        in_specs=[SMEM, SMEM, HBM, HBM],
        out_specs=VMEM,
        scratch_shapes=[
            pltpu.VMEM(kernel_t.shape, jnp.bfloat16),
            pltpu.VMEM(basis.shape, jnp.bfloat16),
            pltpu.VMEM((slots, P_SIZE), jnp.float32),
            pltpu.SemaphoreType.DMA((blocks,)),
            pltpu.SemaphoreType.DMA((slots,)),
        ],
        compiler_params=pltpu.CompilerParams(vmem_limit_bytes=56 * MIB),
        name="project",
    )(plan, order, kernel_t, basis)


def update_kernel(
    blocks, tiles, plan, order, tile_of, contributions, collect, core, basis,
    density_out, update_out, pair, density, potential, acc, stage, sems, osems,
):
    slots = pair.shape[0]
    live = plan[slots + blocks]
    me = plan[slots + blocks + 1]
    load, start = entry_loads(order, basis, pair, sems)
    lax.fori_loop(0, live, start, 0)
    density[...] = core[...] + jnp.dot(
        collect[...],
        contributions[...],
        preferred_element_type=jnp.float32,
        precision=lax.Precision.HIGHEST,
    )
    for t in range(tiles):
        density_out[pl.ds(t, 1), :] = density[pl.ds(me * tiles + t, 1), :]
    positive = jnp.maximum(density[...], 0.1)
    root = jnp.exp(jnp.log(positive) * (1.0 / 3.0))
    root = root - (root - positive / (root * root)) * (1.0 / 3.0)
    potential[...] = -exchange_factor * root
    scale = 1.0 / math.sqrt(P_SIZE)

    def store(b):
        rows = pl.ds(pl.multiple_of(b * KB, KB), KB)
        return pltpu.make_async_copy(stage.at[b], update_out.at[rows], osems.at[b])

    def step(b, carry):
        first, last = plan[slots + b], plan[slots + b + 1]

        @pl.when(first == last)
        def _():
            stage[b] = jnp.zeros(stage.shape[1:], jnp.bfloat16)

        def body(i, p, q):
            weight_p = potential[pl.ds(tile_of[order[p]], 1), :]
            weight_q = potential[pl.ds(tile_of[order[q]], 1), :] * (q - p).astype(jnp.float32)
            weighted = jnp.concatenate(
                [
                    (pair[p, 1].astype(jnp.float32) * weight_p).astype(jnp.bfloat16),
                    (pair[q, 1].astype(jnp.float32) * weight_q).astype(jnp.bfloat16),
                ],
                axis=1,
            )
            block = lax.dot_general(
                jnp.concatenate([pair[p, 0], pair[q, 0]], axis=1),
                weighted,
                (((1,), (1,)), ((), ())),
                preferred_element_type=jnp.float32,
            )

            @pl.when(last - first <= 2)
            def _():
                stage[b] = (block * scale).astype(jnp.bfloat16)

            @pl.when((last - first > 2) & (i == 0))
            def _():
                acc[...] = block

            @pl.when(i > 0)
            def _():
                acc[...] += block

        by_twos(first, last, load, body)

        @pl.when(last - first > 2)
        def _():
            stage[b] = (acc[...] * scale).astype(jnp.bfloat16)

        store(b).start()
        return carry

    lax.fori_loop(0, blocks, step, 0)
    for b in range(blocks):
        store(b).wait()


def update(plan, order, tile_of, contributions, collect, core, basis, tiles, blocks, cols):
    slots = basis.shape[0]
    return pl.pallas_call(
        functools.partial(update_kernel, blocks, tiles),
        out_shape=(
            jax.ShapeDtypeStruct((tiles, P_SIZE), jnp.float32),
            jax.ShapeDtypeStruct((blocks * KB, cols), jnp.bfloat16),
        ),
        in_specs=[SMEM] * 3 + [VMEM] * 3 + [HBM],
        out_specs=(VMEM, HBM),
        scratch_shapes=[
            pltpu.VMEM(basis.shape, jnp.bfloat16),
            pltpu.VMEM(core.shape, jnp.float32),
            pltpu.VMEM(core.shape, jnp.float32),
            pltpu.VMEM((KB, cols), jnp.float32),
            pltpu.VMEM((blocks, KB, cols), jnp.bfloat16),
            pltpu.SemaphoreType.DMA((slots,)),
            pltpu.SemaphoreType.DMA((blocks,)),
        ],
        compiler_params=pltpu.CompilerParams(vmem_limit_bytes=48 * MIB),
        name="update",
    )(plan, order, tile_of, contributions, collect, core, basis)


def shift(block, axis, step):
    count = lax.axis_size(axis)
    pairs = [(i, i + step) for i in range(count) if 0 <= i + step < count]
    return lax.ppermute(block, axis, pairs)


def make_plan(meta, me, entries, tiles, col_count, blocks):
    slots = col_count * CAP
    core = meta[:, :tiles].reshape(col_count * tiles, P_SIZE)
    lists = meta[:, tiles, : 2 * entries + tiles].astype(jnp.int32)
    peers, named, counts = lists[:, :entries], lists[:, entries : 2 * entries], lists[:, 2 * entries :]
    index = jnp.arange(entries, dtype=jnp.int32)
    home = jnp.arange(col_count, dtype=jnp.int32)[:, None]
    earlier = (peers[:, :, None] == peers[:, None, :]) & (index[None, :] < index[:, None])
    rank = jnp.sum(earlier.astype(jnp.int32), axis=2)
    live = (index % SLOTS)[None, :] < jnp.repeat(counts, SLOTS, axis=1)
    row = peers * slots + home * CAP + rank
    picked = (row[:, :, None] == jnp.arange(col_count * slots, dtype=jnp.int32)) & live[:, :, None]
    collect = jnp.sum(
        picked.astype(jnp.float32).reshape(col_count * tiles, SLOTS, col_count * slots), axis=1
    )
    hit = (
        (peers == me)[:, None, :]
        & (rank[:, None, :] == jnp.arange(CAP, dtype=jnp.int32)[None, :, None])
        & live[:, None, :]
    )
    wanted = (jnp.sum(jnp.where(hit, named[:, None, :] + 1, 0), axis=2) - 1).reshape(slots)
    tile = home * tiles + index[None, :] // SLOTS
    tile_of = jnp.sum(jnp.where(hit, tile[:, None, :], 0), axis=2).reshape(slots)
    key = jnp.where(wanted < 0, blocks, wanted)
    place = jnp.arange(slots, dtype=jnp.int32)
    before = (key[None, :] < key[:, None]) | (
        (key[None, :] == key[:, None]) & (place[None, :] < place[:, None])
    )
    spot = jnp.sum(before.astype(jnp.int32), axis=1)
    order = jnp.sum(jnp.where(spot[None, :] == place[:, None], place[None, :], 0), axis=1)
    starts = jnp.sum(
        (key[None, :] < jnp.arange(blocks + 1, dtype=jnp.int32)[:, None]).astype(jnp.int32), axis=1
    )
    plan = jnp.concatenate([wanted, starts, me[None]]).astype(jnp.int32)
    return core, collect, plan, order.astype(jnp.int32), tile_of.astype(jnp.int32)


def shards(
    start_columns,
    hamiltonian,
    band_pattern,
    coefficients,
    tile_peer,
    tile_block,
    tile_count,
    basis_values,
    core_density,
):
    col_count = lax.axis_size("col")
    slots = col_count * CAP
    entries = tile_peer.shape[0]
    tiles = core_density.shape[0]
    cols = start_columns.shape[1]
    blocks = start_columns.shape[0] // KB
    peers = tile_peer[:, 0]

    sent, masked = prepare(peers, band_pattern, basis_values, hamiltonian, slots)
    basis = lax.all_to_all(
        sent.reshape((col_count, CAP) + sent.shape[1:]), "col", split_axis=0, concat_axis=0, tiled=True
    ).reshape(sent.shape)
    pieces, owners = gather_pieces(masked)

    v_low = shift(start_columns[-DEG * W :], "row", 1)
    v_high = shift(start_columns[: DEG * W], "row", -1)

    lists = jnp.concatenate([peers, tile_block, tile_count]).astype(jnp.float32)
    lists = jnp.pad(lists, (0, P_SIZE - lists.shape[0]))
    meta = jnp.concatenate([core_density, lists[None]], axis=0)
    meta = jnp.pad(meta, ((0, -meta.shape[0] % 8), (0, 0)))
    meta = lax.all_gather(meta, "col", axis=0)
    me = lax.axis_index("col").astype(jnp.int32)
    core, collect, plan, order, tile_of = make_plan(meta, me, entries, tiles, col_count, blocks)

    first, last = edge_blocks(owners, pieces, col_count, DEG - 1)
    h_low = shift(last, "row", 1)
    h_high = shift(first, "row", -1)
    kernel_t = chebyshev(
        coefficients, owners, v_low, start_columns, v_high, h_low, h_high, pieces
    )
    partial = project(plan, order, kernel_t, basis, col_count)
    contributions = lax.all_to_all(partial, "col", split_axis=0, concat_axis=0, tiled=True)
    contributions = contributions.reshape(col_count * slots, P_SIZE)
    return update(
        plan, order, tile_of, contributions, collect, core, basis, tiles, blocks, cols
    )


def solution(mesh):
    return jax.shard_map(
        shards,
        mesh=mesh,
        in_specs=(
            P("row", "col"),
            P(("row", "col"), None, None, None),
            P(("row", "col")),
            P(),
            P(("row", "col"), None),
            P(("row", "col")),
            P(("row", "col")),
            P(("row", "col"), None, None, None),
            P(("row", "col"), None),
        ),
        out_specs=(P(("row", "col"), None), P("row", "col")),
        check_vma=False,
    )
```

```python
import functools
import math

import jax
import jax.numpy as jnp
from jax import lax
from jax.experimental import pallas as pl
from jax.experimental.pallas import tpu as pltpu
from jax.sharding import PartitionSpec as P

W = 256
KB = 512
DEG = 3
SLOTS = 4
CAP = 2
P_SIZE = 128
MIB = 1 << 20
LISTS = 16

exchange_factor = (3.0 / math.pi) ** (1.0 / 3.0)
HBM = pl.BlockSpec(memory_space=pltpu.HBM)
SMEM = pl.BlockSpec(memory_space=pltpu.SMEM)
VMEM = pl.BlockSpec(memory_space=pltpu.VMEM)


def prepare_kernel(
    entries, slots, peers, pattern, basis, ham, lists, sent, piece,
    held, blocks, count, in_sems, out_sems, ham_sems,
):
    def fetch(e):
        return pltpu.make_async_copy(basis.at[e], held.at[e], in_sems.at[e])

    def send(e, s):
        return pltpu.make_async_copy(held.at[e], sent.at[s], out_sems.at[s])

    rows = ham.shape[0]
    load = pltpu.make_async_copy(ham, blocks.at[pl.ds(0, rows)], ham_sems.at[0])
    store = pltpu.make_async_copy(blocks, piece, ham_sems.at[1])
    load.start()
    for e in range(entries):
        fetch(e).start()
    for c in range(slots // CAP):
        count[c] = 0
    blocks[rows:] = lists[...]
    load.wait()
    for i in range(rows // (2 * W)):
        coupling = slice((2 * i + 1) * W, (2 * i + 2) * W)
        blocks[coupling] = blocks[coupling] * pattern[i].astype(jnp.bfloat16)
    store.start()
    for e in range(entries):
        p = peers[e]
        k = count[p]
        count[p] = k + 1
        fetch(e).wait()
        send(e, p * CAP + k).start()
    for c in range(slots // CAP):
        for k in range(CAP):
            @pl.when(count[c] <= k)
            def _():
                send(0, c * CAP + k).start()
    for s in range(slots):
        send(0, s).wait()
    store.wait()


def prepare(peers, pattern, basis, ham, lists, slots):
    entries = basis.shape[0]
    piece = (ham.shape[0] + LISTS, W)
    return pl.pallas_call(
        functools.partial(prepare_kernel, entries, slots),
        out_shape=(
            jax.ShapeDtypeStruct((slots,) + basis.shape[1:], basis.dtype),
            jax.ShapeDtypeStruct(piece, ham.dtype),
        ),
        in_specs=[SMEM, SMEM, HBM, HBM, VMEM],
        out_specs=(HBM, HBM),
        scratch_shapes=[
            pltpu.VMEM(basis.shape, basis.dtype),
            pltpu.VMEM(piece, ham.dtype),
            pltpu.SMEM((slots // CAP,), jnp.int32),
            pltpu.SemaphoreType.DMA((entries,)),
            pltpu.SemaphoreType.DMA((slots,)),
            pltpu.SemaphoreType.DMA((2,)),
        ],
        compiler_params=pltpu.CompilerParams(vmem_limit_bytes=62 * MIB),
        name="prepare",
    )(peers, pattern, basis, ham, lists)


def gather_pieces(own):
    count = lax.axis_size("col")
    outer = 4 if count % 4 == 0 else count
    inner = count // outer
    me = lax.axis_index("col").astype(jnp.int32)
    a, b = me // inner, me % inner

    def hop(block, pairs):
        return lax.ppermute(block, "col", pairs)

    def inside(i, size):
        return (i >= 0) & (i < size)

    lines = [(own, 0)]
    for way in (1, -1):
        block = own
        for step in range(1, outer):
            pairs = [
                (x * inner + y, (x + way) * inner + y)
                for x in range(outer) for y in range(inner)
                if 0 <= x + way < outer and 0 <= x - way * (step - 1) < outer
            ]
            block = hop(block, pairs)
            lines.append((block, -way * step))
    pieces, owners = [], []
    for line, shift_a in lines:
        pieces.append(line)
        owners.append(jnp.where(inside(a + shift_a, outer), (a + shift_a) * inner + b, -1))
        rows = [x for x in range(outer) if 0 <= x + shift_a < outer]
        if inner == 2:
            pairs = [(x * inner + y, x * inner + 1 - y) for x in rows for y in range(inner)]
            pieces.append(hop(line, pairs))
            owners.append(jnp.where(inside(a + shift_a, outer), (a + shift_a) * inner + 1 - b, -1))
            continue
        for way in (1, -1):
            block = line
            for step in range(1, inner):
                pairs = [
                    (x * inner + y, x * inner + y + way)
                    for x in rows for y in range(inner)
                    if 0 <= y + way < inner and 0 <= y - way * (step - 1) < inner
                ]
                block = hop(block, pairs)
                pieces.append(block)
                valid = inside(a + shift_a, outer) & inside(b - way * step, inner)
                owners.append(jnp.where(valid, (a + shift_a) * inner + b - way * step, -1))
    return pieces, jnp.stack(owners).astype(jnp.int32)


def edge_kernel(col_count, depth, owners, *refs):
    pieces, (first, last, lists, sems, list_sems) = refs[:-5], refs[-5:]
    rows = pieces[0].shape[0] - LISTS
    held = rows // (2 * W)
    total = col_count * held

    def each(act):
        for i, piece in enumerate(pieces):
            for g in range(depth):
                for out, block, sem in ((first, g, 0), (last, total - depth + g, 1)):
                    source = piece.at[pl.ds(block % held * 2 * W, 2 * W)]
                    copy = pltpu.make_async_copy(source, out.at[g], sems.at[sem, g])

                    @pl.when(owners[i] == block // held)
                    def _():
                        act(copy)

            @pl.when(owners[i] >= 0)
            def _():
                act(pltpu.make_async_copy(
                    piece.at[pl.ds(rows, LISTS)], lists.at[owners[i]], list_sems.at[i]
                ))

    each(lambda copy: copy.start())
    each(lambda copy: copy.wait())


def edge_blocks(owners, pieces, col_count, depth):
    shape = jax.ShapeDtypeStruct((depth, 2 * W, W), pieces[0].dtype)
    return pl.pallas_call(
        functools.partial(edge_kernel, col_count, depth),
        out_shape=(shape, shape, jax.ShapeDtypeStruct((col_count, LISTS, W), pieces[0].dtype)),
        in_specs=[SMEM] + [HBM] * len(pieces),
        out_specs=(VMEM, VMEM, VMEM),
        scratch_shapes=[
            pltpu.SemaphoreType.DMA((2, depth)),
            pltpu.SemaphoreType.DMA((len(pieces),)),
        ],
        name="edge_blocks",
    )(owners, *pieces)


def cheb_kernel(blocks, coef, owners, v_low, v_mid, v_high, h_low, h_high, *refs):
    *pieces, out, vext, hraw, hcat, cheb_1, cheb_2, total, kern, sems, psems, osems = refs
    halo_v = DEG
    halo_h = DEG - 1
    held = (pieces[0].shape[0] - LISTS) // (2 * W)
    h_copies = [
        pltpu.make_async_copy(h_low, hraw.at[pl.ds(0, halo_h)], sems.at[0]),
        pltpu.make_async_copy(h_high, hraw.at[pl.ds(halo_h + blocks, halo_h)], sems.at[1]),
    ]
    v_copies = [
        pltpu.make_async_copy(v_low, vext.at[pl.ds(0, halo_v * W)], sems.at[2]),
        pltpu.make_async_copy(v_mid, vext.at[pl.ds(halo_v * W, blocks * W)], sems.at[3]),
        pltpu.make_async_copy(v_high, vext.at[pl.ds((halo_v + blocks) * W, halo_v * W)], sems.at[4]),
    ]

    def each_piece(act):
        for i, piece in enumerate(pieces):
            @pl.when(owners[i] >= 0)
            def _():
                for k in range(held):
                    act(pltpu.make_async_copy(
                        piece.at[pl.ds(k * 2 * W, 2 * W)],
                        hraw.at[halo_h + owners[i] * held + k],
                        psems.at[i, k],
                    ))

    each_piece(lambda copy: copy.start())
    for copy in h_copies + v_copies:
        copy.start()
    each_piece(lambda copy: copy.wait())
    for copy in h_copies:
        copy.wait()
    rows = lax.broadcasted_iota(jnp.int32, (W, W), 0)
    cols = lax.broadcasted_iota(jnp.int32, (W, W), 1)
    upper = jnp.where(rows <= cols, 1.0, 0.0).astype(jnp.bfloat16)

    def build(j, carry):
        coupling = hraw[j, W:]
        lower_band = coupling * upper
        hcat[j, :, 0:W] = lower_band
        hcat[j, :, W : 2 * W] = hraw[j, :W]
        hcat[j, :, 2 * W : 3 * W] = coupling - lower_band
        return carry

    lax.fori_loop(0, blocks + 2 * halo_h, build, 0, unroll=2)
    for copy in v_copies:
        copy.wait()

    def rows_of(j, count=1):
        return pl.ds(pl.multiple_of(j * W, W), count * W)

    def band(source, j, row):
        return jnp.dot(hcat[j], source[rows_of(row, 3), :], preferred_element_type=jnp.float32)

    def first(j, carry):
        value = band(vext, j, j)
        cheb_1[rows_of(j), :] = value.astype(jnp.bfloat16)
        total[rows_of(j), :] = value
        return carry

    lax.fori_loop(0, blocks + 4, first, 0, unroll=2)

    def second(j, carry):
        begin = vext[rows_of(j + 2), :].astype(jnp.float32)
        value = 2.0 * band(cheb_1, j + 1, j) - begin
        cheb_2[rows_of(j), :] = value.astype(jnp.bfloat16)
        total[rows_of(j + 1), :] = (
            coef[0] * begin + (coef[1] - coef[3]) * total[rows_of(j + 1), :] + coef[2] * value
        )
        return carry

    lax.fori_loop(0, blocks + 2, second, 0, unroll=2)

    def store(j):
        return pltpu.make_async_copy(kern.at[j], out.at[j], osems.at[j])

    def third(j, carry):
        for half in range(KB // W):
            i = j * (KB // W) + half
            value = total[rows_of(i + 2), :] + (2.0 * coef[3]) * band(cheb_2, i + 2, i)
            kern[j, :, half * W : (half + 1) * W] = value.astype(jnp.bfloat16).T
        store(j).start()
        return carry

    lax.fori_loop(0, blocks // (KB // W), third, 0)
    for j in range(blocks // (KB // W)):
        store(j).wait()


def chebyshev(coefficients, owners, v_low, v_mid, v_high, h_low, h_high, pieces):
    blocks = v_mid.shape[0] // W
    cols = v_mid.shape[1]
    ext = blocks + 2 * (DEG - 1)
    flops = 2 * W * 3 * W * cols * (3 * blocks + 6)
    result = (blocks * W // KB, cols, KB)
    held = (pieces[0].shape[0] - LISTS) // (2 * W)
    return pl.pallas_call(
        functools.partial(cheb_kernel, blocks),
        out_shape=jax.ShapeDtypeStruct(result, jnp.bfloat16),
        in_specs=[SMEM] * 2 + [HBM] * (5 + len(pieces)),
        out_specs=HBM,
        scratch_shapes=[
            pltpu.VMEM(((blocks + 2 * DEG) * W, cols), jnp.bfloat16),
            pltpu.VMEM((ext, 2 * W, W), jnp.bfloat16),
            pltpu.VMEM((ext, W, 3 * W), jnp.bfloat16),
            pltpu.VMEM((ext * W, cols), jnp.bfloat16),
            pltpu.VMEM(((blocks + 2) * W, cols), jnp.bfloat16),
            pltpu.VMEM((ext * W, cols), jnp.float32),
            pltpu.VMEM(result, jnp.bfloat16),
            pltpu.SemaphoreType.DMA((5,)),
            pltpu.SemaphoreType.DMA((len(pieces), held)),
            pltpu.SemaphoreType.DMA((result[0],)),
        ],
        compiler_params=pltpu.CompilerParams(vmem_limit_bytes=62 * MIB),
        cost_estimate=pl.CostEstimate(flops=flops, bytes_accessed=16 * MIB, transcendentals=0),
        name="chebyshev",
    )(coefficients, owners, v_low, v_mid, v_high, h_low, h_high, *pieces)


def entry_loads(order, basis, pair, sems):
    def load(p):
        return pltpu.make_async_copy(basis.at[order[p]], pair.at[p], sems.at[p])

    def start(p, carry):
        load(p).start()
        return carry

    return load, start


def by_twos(first, last, load, body):
    def step(i, carry):
        p = first + 2 * i
        q = jnp.minimum(p + 1, last - 1)
        load(p).wait()

        @pl.when(q > p)
        def _():
            load(q).wait()

        body(i, p, q)
        return carry

    lax.fori_loop(0, (last - first + 1) // 2, step, 0)


def sent_rows(slots, tiles):
    return slots + tiles + -(slots + tiles) % 8


def project_kernel(blocks, plan, order, kernel_t, basis, core, out, kern, pair, rows, ksems, bsems):
    slots = pair.shape[0]
    load, start = entry_loads(order, basis, pair, bsems)

    def fetch(b):
        return pltpu.make_async_copy(kernel_t.at[b], kern.at[b], ksems.at[b])

    def begin(b, carry):
        first, last = plan[slots + b], plan[slots + b + 1]

        @pl.when(first < last)
        def _():
            fetch(b).start()

        return lax.fori_loop(first, last, start, carry)

    lax.fori_loop(0, blocks, begin, 0)
    rows[...] = jnp.zeros_like(rows)
    rows[slots : slots + core.shape[0]] = core[...]

    def step(b, carry):
        first, last = plan[slots + b], plan[slots + b + 1]

        @pl.when(first < last)
        def _():
            fetch(b).wait()

        def body(i, p, q):
            both = jnp.concatenate([pair[p, 0], pair[q, 0]], axis=1)
            projected = jnp.dot(kern[b], both, preferred_element_type=jnp.float32)
            other = jnp.concatenate([pair[p, 1], pair[q, 1]], axis=1).astype(jnp.float32)
            value = jnp.sum(projected * other, axis=0, keepdims=True) * (1.0 / KB)
            rows[pl.ds(order[p], 1), :] = value[:, :P_SIZE]
            rows[pl.ds(order[q], 1), :] = value[:, P_SIZE:]

        by_twos(first, last, load, body)
        return carry

    lax.fori_loop(0, blocks, step, 0)
    for c in range(out.shape[0]):
        out[c] = rows[...]


def project(plan, order, kernel_t, basis, core, col_count):
    slots = basis.shape[0]
    sent = sent_rows(slots, core.shape[0])
    blocks = kernel_t.shape[0]
    return pl.pallas_call(
        functools.partial(project_kernel, blocks),
        out_shape=jax.ShapeDtypeStruct((col_count, sent, P_SIZE), jnp.float32),
        in_specs=[SMEM, SMEM, HBM, HBM, VMEM],
        out_specs=VMEM,
        scratch_shapes=[
            pltpu.VMEM(kernel_t.shape, jnp.bfloat16),
            pltpu.VMEM(basis.shape, jnp.bfloat16),
            pltpu.VMEM((sent, P_SIZE), jnp.float32),
            pltpu.SemaphoreType.DMA((blocks,)),
            pltpu.SemaphoreType.DMA((slots,)),
        ],
        compiler_params=pltpu.CompilerParams(vmem_limit_bytes=62 * MIB),
        name="project",
    )(plan, order, kernel_t, basis, core)


def update_kernel(
    blocks, tiles, plan, order, tile_of, contributions, collect, basis,
    density_out, update_out, pair, density, potential, acc, stage, sems, osems,
):
    slots = pair.shape[0]
    live = plan[slots + blocks]
    me = plan[slots + blocks + 1]
    load, start = entry_loads(order, basis, pair, sems)
    lax.fori_loop(0, live, start, 0)
    density[...] = jnp.dot(
        collect[...],
        contributions[...],
        preferred_element_type=jnp.float32,
        precision=lax.Precision.HIGHEST,
    )
    for t in range(tiles):
        density_out[pl.ds(t, 1), :] = density[pl.ds(me * tiles + t, 1), :]
    positive = jnp.maximum(density[...], 0.1)
    root = jnp.exp(jnp.log(positive) * (1.0 / 3.0))
    root = root - (root - positive / (root * root)) * (1.0 / 3.0)
    potential[...] = -exchange_factor * root
    scale = 1.0 / math.sqrt(P_SIZE)

    def store(b):
        rows = pl.ds(pl.multiple_of(b * KB, KB), KB)
        return pltpu.make_async_copy(stage.at[b], update_out.at[rows], osems.at[b])

    def step(b, carry):
        first, last = plan[slots + b], plan[slots + b + 1]

        @pl.when(first == last)
        def _():
            stage[b] = jnp.zeros(stage.shape[1:], jnp.bfloat16)

        def body(i, p, q):
            weight_p = potential[pl.ds(tile_of[order[p]], 1), :]
            weight_q = potential[pl.ds(tile_of[order[q]], 1), :] * (q - p).astype(jnp.float32)
            weighted = jnp.concatenate(
                [
                    (pair[p, 1].astype(jnp.float32) * weight_p).astype(jnp.bfloat16),
                    (pair[q, 1].astype(jnp.float32) * weight_q).astype(jnp.bfloat16),
                ],
                axis=1,
            )
            block = lax.dot_general(
                jnp.concatenate([pair[p, 0], pair[q, 0]], axis=1),
                weighted,
                (((1,), (1,)), ((), ())),
                preferred_element_type=jnp.float32,
            )

            @pl.when(last - first <= 2)
            def _():
                stage[b] = (block * scale).astype(jnp.bfloat16)

            @pl.when((last - first > 2) & (i == 0))
            def _():
                acc[...] = block

            @pl.when(i > 0)
            def _():
                acc[...] += block

        by_twos(first, last, load, body)

        @pl.when(last - first > 2)
        def _():
            stage[b] = (acc[...] * scale).astype(jnp.bfloat16)

        store(b).start()
        return carry

    lax.fori_loop(0, blocks, step, 0)
    for b in range(blocks):
        store(b).wait()


def update(plan, order, tile_of, contributions, collect, basis, tiles, blocks, cols):
    slots = basis.shape[0]
    all_tiles = (collect.shape[0], P_SIZE)
    return pl.pallas_call(
        functools.partial(update_kernel, blocks, tiles),
        out_shape=(
            jax.ShapeDtypeStruct((tiles, P_SIZE), jnp.float32),
            jax.ShapeDtypeStruct((blocks * KB, cols), jnp.bfloat16),
        ),
        in_specs=[SMEM] * 3 + [VMEM] * 2 + [HBM],
        out_specs=(VMEM, HBM),
        scratch_shapes=[
            pltpu.VMEM(basis.shape, jnp.bfloat16),
            pltpu.VMEM(all_tiles, jnp.float32),
            pltpu.VMEM(all_tiles, jnp.float32),
            pltpu.VMEM((KB, cols), jnp.float32),
            pltpu.VMEM((blocks, KB, cols), jnp.bfloat16),
            pltpu.SemaphoreType.DMA((slots,)),
            pltpu.SemaphoreType.DMA((blocks,)),
        ],
        compiler_params=pltpu.CompilerParams(vmem_limit_bytes=62 * MIB),
        name="update",
    )(plan, order, tile_of, contributions, collect, basis)


def shift(block, axis, step):
    count = lax.axis_size(axis)
    pairs = [(i, i + step) for i in range(count) if 0 <= i + step < count]
    return lax.ppermute(block, axis, pairs)


def make_plan(lists, me, entries, tiles, col_count, blocks):
    slots = col_count * CAP
    sent = sent_rows(slots, tiles)
    lists = lists[:, : 2 * entries + tiles].astype(jnp.int32)
    peers, named, counts = lists[:, :entries], lists[:, entries : 2 * entries], lists[:, 2 * entries :]
    index = jnp.arange(entries, dtype=jnp.int32)
    home = jnp.arange(col_count, dtype=jnp.int32)[:, None]
    earlier = (peers[:, :, None] == peers[:, None, :]) & (index[None, :] < index[:, None])
    rank = jnp.sum(earlier.astype(jnp.int32), axis=2)
    live = (index % SLOTS)[None, :] < jnp.repeat(counts, SLOTS, axis=1)
    row = jnp.where(live, peers * sent + home * CAP + rank, -1).reshape(col_count, tiles, SLOTS)
    core = (home * sent + slots + jnp.arange(tiles, dtype=jnp.int32))[:, :, None]
    row = jnp.concatenate([row, core], axis=2).reshape(col_count * tiles, SLOTS + 1, 1)
    picked = row == jnp.arange(col_count * sent, dtype=jnp.int32)
    collect = jnp.sum(picked.astype(jnp.float32), axis=1)
    hit = (
        (peers == me)[:, None, :]
        & (rank[:, None, :] == jnp.arange(CAP, dtype=jnp.int32)[None, :, None])
        & live[:, None, :]
    )
    wanted = (jnp.sum(jnp.where(hit, named[:, None, :] + 1, 0), axis=2) - 1).reshape(slots)
    tile = home * tiles + index[None, :] // SLOTS
    tile_of = jnp.sum(jnp.where(hit, tile[:, None, :], 0), axis=2).reshape(slots)
    key = jnp.where(wanted < 0, blocks, wanted)
    place = jnp.arange(slots, dtype=jnp.int32)
    before = (key[None, :] < key[:, None]) | (
        (key[None, :] == key[:, None]) & (place[None, :] < place[:, None])
    )
    spot = jnp.sum(before.astype(jnp.int32), axis=1)
    order = jnp.sum(jnp.where(spot[None, :] == place[:, None], place[None, :], 0), axis=1)
    starts = jnp.sum(
        (key[None, :] < jnp.arange(blocks + 1, dtype=jnp.int32)[:, None]).astype(jnp.int32), axis=1
    )
    plan = jnp.concatenate([wanted, starts, me[None]]).astype(jnp.int32)
    return collect, plan, order.astype(jnp.int32), tile_of.astype(jnp.int32)


def shards(
    start_columns,
    hamiltonian,
    band_pattern,
    coefficients,
    tile_peer,
    tile_block,
    tile_count,
    basis_values,
    core_density,
):
    col_count = lax.axis_size("col")
    slots = col_count * CAP
    entries = tile_peer.shape[0]
    tiles = core_density.shape[0]
    cols = start_columns.shape[1]
    blocks = start_columns.shape[0] // KB
    peers = tile_peer[:, 0]

    lists = jnp.concatenate([peers, tile_block, tile_count]).astype(jnp.bfloat16)
    lists = jnp.pad(lists[None], ((0, LISTS - 1), (0, W - lists.shape[0])))
    sent, own = prepare(
        peers, band_pattern, basis_values, hamiltonian.reshape(-1, W), lists, slots
    )
    basis = lax.all_to_all(
        sent.reshape((col_count, CAP) + sent.shape[1:]), "col", split_axis=0, concat_axis=0, tiled=True
    ).reshape(sent.shape)
    pieces, owners = gather_pieces(own)

    v_low = shift(start_columns[-DEG * W :], "row", 1)
    v_high = shift(start_columns[: DEG * W], "row", -1)

    first, last, lists = edge_blocks(owners, pieces, col_count, DEG - 1)
    h_low = shift(last, "row", 1)
    h_high = shift(first, "row", -1)
    kernel_t = chebyshev(
        coefficients, owners, v_low, start_columns, v_high, h_low, h_high, pieces
    )
    me = lax.axis_index("col").astype(jnp.int32)
    collect, plan, order, tile_of = make_plan(lists[:, 0], me, entries, tiles, col_count, blocks)
    partial = project(plan, order, kernel_t, basis, core_density, col_count)
    contributions = lax.all_to_all(partial, "col", split_axis=0, concat_axis=0, tiled=True)
    contributions = contributions.reshape(-1, P_SIZE)
    return update(
        plan, order, tile_of, contributions, collect, basis, tiles, blocks, cols
    )


def solution(mesh):
    return jax.shard_map(
        shards,
        mesh=mesh,
        in_specs=(
            P("row", "col"),
            P(("row", "col"), None, None, None),
            P(("row", "col")),
            P(),
            P(("row", "col"), None),
            P(("row", "col")),
            P(("row", "col")),
            P(("row", "col"), None, None, None),
            P(("row", "col"), None),
        ),
        out_specs=(P(("row", "col"), None), P("row", "col")),
        check_vma=False,
    )
```

```python
import functools
import math

import jax
import jax.numpy as jnp
from jax import lax
from jax.experimental import pallas as pl
from jax.experimental.pallas import tpu as pltpu
from jax.sharding import PartitionSpec as P

W = 256
KB = 512
DEG = 3
SLOTS = 4
CAP = 2
P_SIZE = 128
MIB = 1 << 20
LISTS = 16

exchange_factor = (3.0 / math.pi) ** (1.0 / 3.0)
HBM = pl.BlockSpec(memory_space=pltpu.HBM)
SMEM = pl.BlockSpec(memory_space=pltpu.SMEM)
VMEM = pl.BlockSpec(memory_space=pltpu.VMEM)


def partner(me, j, count):
    if count & (count - 1) == 0:
        return me ^ abs(j)
    return (me + j) % count


def piece_kernel(peers, named, counts, pattern, ham, piece, blocks, sems):
    rows = ham.shape[0]
    load = pltpu.make_async_copy(ham, blocks.at[pl.ds(0, rows)], sems.at[0])
    load.start()
    lane = lax.broadcasted_iota(jnp.int32, (LISTS, W), 1)
    lists = jnp.zeros((LISTS, W), jnp.int32)
    at = 0
    for ref in (peers, named, counts):
        for i in range(ref.shape[0]):
            lists = jnp.where(lane == at, ref[i], lists)
            at += 1
    blocks[rows:] = lists.astype(jnp.float32).astype(jnp.bfloat16)
    load.wait()
    for i in range(rows // (2 * W)):
        coupling = slice((2 * i + 1) * W, (2 * i + 2) * W)
        blocks[coupling] = blocks[coupling] * pattern[i].astype(jnp.bfloat16)
    store = pltpu.make_async_copy(blocks, piece, sems.at[1])
    store.start()
    store.wait()


def own_piece(peers, named, counts, pattern, ham):
    piece = (ham.shape[0] + LISTS, W)
    return pl.pallas_call(
        piece_kernel,
        out_shape=jax.ShapeDtypeStruct(piece, ham.dtype),
        in_specs=[SMEM] * 4 + [HBM],
        out_specs=HBM,
        scratch_shapes=[pltpu.VMEM(piece, ham.dtype), pltpu.SemaphoreType.DMA((2,))],
        compiler_params=pltpu.CompilerParams(vmem_limit_bytes=62 * MIB),
        name="own_piece",
    )(peers, named, counts, pattern, ham)


def pack_kernel(entries, col_count, me, peers, basis, *refs):
    *chunks, held, owner, count, in_sems, out_sems = refs

    def fetch(e):
        return pltpu.make_async_copy(basis.at[e], held.at[e], in_sems.at[e])

    def send(j, k, e):
        return pltpu.make_async_copy(held.at[e], chunks[j].at[k], out_sems.at[j, k])

    for e in range(entries):
        fetch(e).start()
    for c in range(col_count):
        count[c] = 0
        for k in range(CAP):
            owner[c * CAP + k] = 0
    for e in range(entries):
        p = peers[e]
        k = count[p]
        count[p] = k + 1
        owner[p * CAP + k] = e
    for e in range(entries):
        fetch(e).wait()
    for j in range(col_count):
        for k in range(CAP):
            send(j, k, owner[partner(me[0], j, col_count) * CAP + k]).start()
    for j in range(col_count):
        for k in range(CAP):
            send(j, k, 0).wait()


def pack(me, peers, basis, col_count):
    entries = basis.shape[0]
    chunk = jax.ShapeDtypeStruct((CAP,) + basis.shape[1:], basis.dtype)
    return pl.pallas_call(
        functools.partial(pack_kernel, entries, col_count),
        out_shape=(chunk,) * col_count,
        in_specs=[SMEM, SMEM, HBM],
        out_specs=(HBM,) * col_count,
        scratch_shapes=[
            pltpu.VMEM(basis.shape, basis.dtype),
            pltpu.SMEM((col_count * CAP,), jnp.int32),
            pltpu.SMEM((col_count,), jnp.int32),
            pltpu.SemaphoreType.DMA((entries,)),
            pltpu.SemaphoreType.DMA((col_count, CAP)),
        ],
        compiler_params=pltpu.CompilerParams(vmem_limit_bytes=62 * MIB),
        name="pack",
    )(me, peers, basis)


def after(block, *others):
    return lax.optimization_barrier((block,) + others)[0]


def gather_pieces(own):
    count = lax.axis_size("col")
    outer = 4 if count % 4 == 0 else count
    inner = count // outer
    me = lax.axis_index("col").astype(jnp.int32)
    a, b = me // inner, me % inner

    def hop(block, pairs):
        return lax.ppermute(block, "col", pairs)

    def inside(i, size):
        return (i >= 0) & (i < size)

    lines = [(own, 0)]
    steps = [[] for _ in range(outer - 1)]
    for way in (1, -1):
        block = own
        for step in range(1, outer):
            pairs = [
                (x * inner + y, (x + way) * inner + y)
                for x in range(outer) for y in range(inner)
                if 0 <= x + way < outer and 0 <= x - way * (step - 1) < outer
            ]
            block = hop(block, pairs)
            lines.append((block, -way * step))
            steps[step - 1].append(block)
    pieces, owners = [], []
    for line, shift_a in lines:
        pieces.append(line)
        owners.append(jnp.where(inside(a + shift_a, outer), (a + shift_a) * inner + b, -1))
        rows = [x for x in range(outer) if 0 <= x + shift_a < outer]
        if inner == 2:
            pairs = [(x * inner + y, x * inner + 1 - y) for x in rows for y in range(inner)]
            pieces.append(hop(line, pairs))
            if abs(shift_a) + 1 < outer - 1:
                steps[abs(shift_a) + 1].append(pieces[-1])
            owners.append(jnp.where(inside(a + shift_a, outer), (a + shift_a) * inner + 1 - b, -1))
            continue
        for way in (1, -1):
            block = line
            for step in range(1, inner):
                pairs = [
                    (x * inner + y, x * inner + y + way)
                    for x in rows for y in range(inner)
                    if 0 <= y + way < inner and 0 <= y - way * (step - 1) < inner
                ]
                block = hop(block, pairs)
                pieces.append(block)
                valid = inside(a + shift_a, outer) & inside(b - way * step, inner)
                owners.append(jnp.where(valid, (a + shift_a) * inner + b - way * step, -1))
    return pieces, jnp.stack(owners).astype(jnp.int32), steps


def edge_kernel(col_count, depth, owners, *refs):
    pieces, (first, last, lists, sems, list_sems) = refs[:-5], refs[-5:]
    rows = pieces[0].shape[0] - LISTS
    held = rows // (2 * W)
    total = col_count * held

    def each(act):
        for i, piece in enumerate(pieces):
            for g in range(depth):
                for out, block, sem in ((first, g, 0), (last, total - depth + g, 1)):
                    source = piece.at[pl.ds(block % held * 2 * W, 2 * W)]
                    copy = pltpu.make_async_copy(source, out.at[g], sems.at[sem, g])

                    @pl.when(owners[i] == block // held)
                    def _():
                        act(copy)

            @pl.when(owners[i] >= 0)
            def _():
                act(pltpu.make_async_copy(
                    piece.at[pl.ds(rows, LISTS)], lists.at[owners[i]], list_sems.at[i]
                ))

    each(lambda copy: copy.start())
    each(lambda copy: copy.wait())


def edge_blocks(owners, pieces, col_count, depth):
    shape = jax.ShapeDtypeStruct((depth, 2 * W, W), pieces[0].dtype)
    return pl.pallas_call(
        functools.partial(edge_kernel, col_count, depth),
        out_shape=(shape, shape, jax.ShapeDtypeStruct((col_count, LISTS, W), pieces[0].dtype)),
        in_specs=[SMEM] + [HBM] * len(pieces),
        out_specs=(VMEM, VMEM, VMEM),
        scratch_shapes=[
            pltpu.SemaphoreType.DMA((2, depth)),
            pltpu.SemaphoreType.DMA((len(pieces),)),
        ],
        name="edge_blocks",
    )(owners, *pieces)


def cheb_kernel(blocks, coef, owners, v_low, v_mid, v_high, h_low, h_high, *refs):
    *pieces, out, vext, hraw, hcat, cheb_1, cheb_2, total, kern, sems, psems, osems = refs
    halo_v = DEG
    halo_h = DEG - 1
    held = (pieces[0].shape[0] - LISTS) // (2 * W)
    h_copies = [
        pltpu.make_async_copy(h_low, hraw.at[pl.ds(0, halo_h)], sems.at[0]),
        pltpu.make_async_copy(h_high, hraw.at[pl.ds(halo_h + blocks, halo_h)], sems.at[1]),
    ]
    v_copies = [
        pltpu.make_async_copy(v_low, vext.at[pl.ds(0, halo_v * W)], sems.at[2]),
        pltpu.make_async_copy(v_mid, vext.at[pl.ds(halo_v * W, blocks * W)], sems.at[3]),
        pltpu.make_async_copy(v_high, vext.at[pl.ds((halo_v + blocks) * W, halo_v * W)], sems.at[4]),
    ]

    def each_piece(act):
        for i, piece in enumerate(pieces):
            @pl.when(owners[i] >= 0)
            def _():
                for k in range(held):
                    act(pltpu.make_async_copy(
                        piece.at[pl.ds(k * 2 * W, 2 * W)],
                        hraw.at[halo_h + owners[i] * held + k],
                        psems.at[i, k],
                    ))

    each_piece(lambda copy: copy.start())
    for copy in h_copies + v_copies:
        copy.start()
    each_piece(lambda copy: copy.wait())
    for copy in h_copies:
        copy.wait()
    rows = lax.broadcasted_iota(jnp.int32, (W, W), 0)
    cols = lax.broadcasted_iota(jnp.int32, (W, W), 1)
    upper = jnp.where(rows <= cols, 1.0, 0.0).astype(jnp.bfloat16)

    def build(j, carry):
        coupling = hraw[j, W:]
        lower_band = coupling * upper
        hcat[j, :, 0:W] = lower_band
        hcat[j, :, W : 2 * W] = hraw[j, :W]
        hcat[j, :, 2 * W : 3 * W] = coupling - lower_band
        return carry

    lax.fori_loop(0, blocks + 2 * halo_h, build, 0, unroll=2)
    for copy in v_copies:
        copy.wait()

    def rows_of(j, count=1):
        return pl.ds(pl.multiple_of(j * W, W), count * W)

    def band(source, j, row):
        return jnp.dot(hcat[j], source[rows_of(row, 3), :], preferred_element_type=jnp.float32)

    def first(j, carry):
        value = band(vext, j, j)
        cheb_1[rows_of(j), :] = value.astype(jnp.bfloat16)
        total[rows_of(j), :] = value
        return carry

    lax.fori_loop(0, blocks + 4, first, 0, unroll=2)

    def second(j, carry):
        begin = vext[rows_of(j + 2), :].astype(jnp.float32)
        value = 2.0 * band(cheb_1, j + 1, j) - begin
        cheb_2[rows_of(j), :] = value.astype(jnp.bfloat16)
        total[rows_of(j + 1), :] = (
            coef[0] * begin + (coef[1] - coef[3]) * total[rows_of(j + 1), :] + coef[2] * value
        )
        return carry

    lax.fori_loop(0, blocks + 2, second, 0, unroll=2)

    def store(j):
        return pltpu.make_async_copy(kern.at[j], out.at[j], osems.at[j])

    def third(j, carry):
        for half in range(KB // W):
            i = j * (KB // W) + half
            value = total[rows_of(i + 2), :] + (2.0 * coef[3]) * band(cheb_2, i + 2, i)
            kern[j, :, half * W : (half + 1) * W] = value.astype(jnp.bfloat16).T
        store(j).start()
        return carry

    lax.fori_loop(0, blocks // (KB // W), third, 0)
    for j in range(blocks // (KB // W)):
        store(j).wait()


def chebyshev(coefficients, owners, v_low, v_mid, v_high, h_low, h_high, pieces):
    blocks = v_mid.shape[0] // W
    cols = v_mid.shape[1]
    ext = blocks + 2 * (DEG - 1)
    flops = 2 * W * 3 * W * cols * (3 * blocks + 6)
    result = (blocks * W // KB, cols, KB)
    held = (pieces[0].shape[0] - LISTS) // (2 * W)
    return pl.pallas_call(
        functools.partial(cheb_kernel, blocks),
        out_shape=jax.ShapeDtypeStruct(result, jnp.bfloat16),
        in_specs=[SMEM] * 2 + [HBM] * (5 + len(pieces)),
        out_specs=HBM,
        scratch_shapes=[
            pltpu.VMEM(((blocks + 2 * DEG) * W, cols), jnp.bfloat16),
            pltpu.VMEM((ext, 2 * W, W), jnp.bfloat16),
            pltpu.VMEM((ext, W, 3 * W), jnp.bfloat16),
            pltpu.VMEM((ext * W, cols), jnp.bfloat16),
            pltpu.VMEM(((blocks + 2) * W, cols), jnp.bfloat16),
            pltpu.VMEM((ext * W, cols), jnp.float32),
            pltpu.VMEM(result, jnp.bfloat16),
            pltpu.SemaphoreType.DMA((5,)),
            pltpu.SemaphoreType.DMA((len(pieces), held)),
            pltpu.SemaphoreType.DMA((result[0],)),
        ],
        compiler_params=pltpu.CompilerParams(vmem_limit_bytes=62 * MIB),
        cost_estimate=pl.CostEstimate(flops=flops, bytes_accessed=16 * MIB, transcendentals=0),
        name="chebyshev",
    )(coefficients, owners, v_low, v_mid, v_high, h_low, h_high, *pieces)


def entry_loads(plan, spot, chunks, pair, sems):
    def start():
        for j, chunk in enumerate(chunks):
            for k in range(CAP):
                m = j * CAP + k

                @pl.when(plan[m] >= 0)
                def _():
                    pltpu.make_async_copy(chunk.at[k], pair.at[spot[m]], sems.at[spot[m]]).start()

    def load(p):
        return pltpu.make_async_copy(chunks[0].at[0], pair.at[p], sems.at[p])

    return start, load


def by_twos(first, last, load, body):
    def step(i, carry):
        p = first + 2 * i
        q = jnp.minimum(p + 1, last - 1)
        load(p).wait()

        @pl.when(q > p)
        def _():
            load(q).wait()

        body(i, p, q)
        return carry

    lax.fori_loop(0, (last - first + 1) // 2, step, 0)


def sent_rows(slots, tiles):
    return slots + tiles + -(slots + tiles) % 8


def project_kernel(blocks, plan, order, spot, kernel_t, core, *refs):
    *chunks, out, kern, pair, rows, ksems, bsems = refs
    slots = pair.shape[0]
    start, load = entry_loads(plan, spot, chunks, pair, bsems)

    def fetch(b):
        return pltpu.make_async_copy(kernel_t.at[b], kern.at[b], ksems.at[b])

    for b in range(blocks):
        @pl.when(plan[slots + b] < plan[slots + b + 1])
        def _():
            fetch(b).start()

    start()
    rows[...] = jnp.zeros_like(rows)
    rows[slots : slots + core.shape[0]] = core[...]

    def step(b, carry):
        first, last = plan[slots + b], plan[slots + b + 1]

        @pl.when(first < last)
        def _():
            fetch(b).wait()

        def body(i, p, q):
            both = jnp.concatenate([pair[p, 0], pair[q, 0]], axis=1)
            projected = jnp.dot(kern[b], both, preferred_element_type=jnp.float32)
            other = jnp.concatenate([pair[p, 1], pair[q, 1]], axis=1).astype(jnp.float32)
            value = jnp.sum(projected * other, axis=0, keepdims=True) * (1.0 / KB)
            rows[pl.ds(order[p], 1), :] = value[:, :P_SIZE]
            rows[pl.ds(order[q], 1), :] = value[:, P_SIZE:]

        by_twos(first, last, load, body)
        return carry

    lax.fori_loop(0, blocks, step, 0)
    for c in range(out.shape[0]):
        out[c] = rows[...]


def project(plan, order, spot, kernel_t, core, chunks):
    col_count = len(chunks)
    slots = col_count * CAP
    sent = sent_rows(slots, core.shape[0])
    blocks = kernel_t.shape[0]
    return pl.pallas_call(
        functools.partial(project_kernel, blocks),
        out_shape=jax.ShapeDtypeStruct((col_count, sent, P_SIZE), jnp.float32),
        in_specs=[SMEM, SMEM, SMEM, HBM, VMEM] + [HBM] * col_count,
        out_specs=VMEM,
        scratch_shapes=[
            pltpu.VMEM(kernel_t.shape, jnp.bfloat16),
            pltpu.VMEM((slots,) + chunks[0].shape[1:], jnp.bfloat16),
            pltpu.VMEM((sent, P_SIZE), jnp.float32),
            pltpu.SemaphoreType.DMA((blocks,)),
            pltpu.SemaphoreType.DMA((slots,)),
        ],
        compiler_params=pltpu.CompilerParams(vmem_limit_bytes=62 * MIB),
        name="project",
    )(plan, order, spot, kernel_t, core, *chunks)


def update_kernel(
    blocks, tiles, plan, order, spot, tile_of, contributions, collect, *refs
):
    (
        *chunks, density_out, update_out, pair, density, potential, acc, stage, sems, osems
    ) = refs
    slots = pair.shape[0]
    me = plan[slots + blocks + 1]
    start, load = entry_loads(plan, spot, chunks, pair, sems)
    start()
    density[...] = jnp.dot(
        collect[...],
        contributions[...],
        preferred_element_type=jnp.float32,
        precision=lax.Precision.HIGHEST,
    )
    for t in range(tiles):
        density_out[pl.ds(t, 1), :] = density[pl.ds(me * tiles + t, 1), :]
    positive = jnp.maximum(density[...], 0.1)
    root = jnp.exp(jnp.log(positive) * (1.0 / 3.0))
    root = root - (root - positive / (root * root)) * (1.0 / 3.0)
    potential[...] = -exchange_factor * root
    scale = 1.0 / math.sqrt(P_SIZE)

    def store(b):
        rows = pl.ds(pl.multiple_of(b * KB, KB), KB)
        return pltpu.make_async_copy(stage.at[b], update_out.at[rows], osems.at[b])

    def step(b, carry):
        first, last = plan[slots + b], plan[slots + b + 1]

        @pl.when(first == last)
        def _():
            stage[b] = jnp.zeros(stage.shape[1:], jnp.bfloat16)

        def body(i, p, q):
            weight_p = potential[pl.ds(tile_of[order[p]], 1), :]
            weight_q = potential[pl.ds(tile_of[order[q]], 1), :] * (q - p).astype(jnp.float32)
            weighted = jnp.concatenate(
                [
                    (pair[p, 1].astype(jnp.float32) * weight_p).astype(jnp.bfloat16),
                    (pair[q, 1].astype(jnp.float32) * weight_q).astype(jnp.bfloat16),
                ],
                axis=1,
            )
            block = lax.dot_general(
                jnp.concatenate([pair[p, 0], pair[q, 0]], axis=1),
                weighted,
                (((1,), (1,)), ((), ())),
                preferred_element_type=jnp.float32,
            )

            @pl.when(last - first <= 2)
            def _():
                stage[b] = (block * scale).astype(jnp.bfloat16)

            @pl.when((last - first > 2) & (i == 0))
            def _():
                acc[...] = block

            @pl.when(i > 0)
            def _():
                acc[...] += block

        by_twos(first, last, load, body)

        @pl.when(last - first > 2)
        def _():
            stage[b] = (acc[...] * scale).astype(jnp.bfloat16)

        store(b).start()
        return carry

    lax.fori_loop(0, blocks, step, 0)
    for b in range(blocks):
        store(b).wait()


def update(plan, order, spot, tile_of, contributions, collect, chunks, tiles, blocks, cols):
    slots = len(chunks) * CAP
    all_tiles = (collect.shape[0], P_SIZE)
    return pl.pallas_call(
        functools.partial(update_kernel, blocks, tiles),
        out_shape=(
            jax.ShapeDtypeStruct((tiles, P_SIZE), jnp.float32),
            jax.ShapeDtypeStruct((blocks * KB, cols), jnp.bfloat16),
        ),
        in_specs=[SMEM] * 4 + [VMEM] * 2 + [HBM] * len(chunks),
        out_specs=(VMEM, HBM),
        scratch_shapes=[
            pltpu.VMEM((slots,) + chunks[0].shape[1:], jnp.bfloat16),
            pltpu.VMEM(all_tiles, jnp.float32),
            pltpu.VMEM(all_tiles, jnp.float32),
            pltpu.VMEM((KB, cols), jnp.float32),
            pltpu.VMEM((blocks, KB, cols), jnp.bfloat16),
            pltpu.SemaphoreType.DMA((slots,)),
            pltpu.SemaphoreType.DMA((blocks,)),
        ],
        compiler_params=pltpu.CompilerParams(vmem_limit_bytes=62 * MIB),
        name="update",
    )(plan, order, spot, tile_of, contributions, collect, *chunks)


def shift(block, axis, step):
    count = lax.axis_size(axis)
    pairs = [(i, i + step) for i in range(count) if 0 <= i + step < count]
    return lax.ppermute(block, axis, pairs)


def chunk_of(home, owner, count):
    return home ^ owner if count & (count - 1) == 0 else (owner - home) % count


def make_plan(lists, me, entries, tiles, col_count, blocks):
    slots = col_count * CAP
    sent = sent_rows(slots, tiles)
    lists = lists[:, : 2 * entries + tiles].astype(jnp.int32)
    peers, named, counts = lists[:, :entries], lists[:, entries : 2 * entries], lists[:, 2 * entries :]
    index = jnp.arange(entries, dtype=jnp.int32)
    home = jnp.arange(col_count, dtype=jnp.int32)[:, None]
    earlier = (peers[:, :, None] == peers[:, None, :]) & (index[None, :] < index[:, None])
    rank = jnp.sum(earlier.astype(jnp.int32), axis=2)
    live = (index % SLOTS)[None, :] < jnp.repeat(counts, SLOTS, axis=1)
    row = jnp.where(live, peers * sent + chunk_of(home, peers, col_count) * CAP + rank, -1).reshape(col_count, tiles, SLOTS)
    core = (home * sent + slots + jnp.arange(tiles, dtype=jnp.int32))[:, :, None]
    row = jnp.concatenate([row, core], axis=2).reshape(col_count * tiles, SLOTS + 1, 1)
    picked = row == jnp.arange(col_count * sent, dtype=jnp.int32)
    collect = jnp.sum(picked.astype(jnp.float32), axis=1)
    hit = (
        (peers == me)[:, None, :]
        & (rank[:, None, :] == jnp.arange(CAP, dtype=jnp.int32)[None, :, None])
        & live[:, None, :]
    )
    at_me = chunk_of(home, me, col_count).reshape(1, col_count) == home
    tile = home * tiles + index[None, :] // SLOTS

    def of_slots(values):
        by_home = jnp.sum(jnp.where(hit, values[:, None, :], 0), axis=2)
        return jnp.sum(jnp.where(at_me[:, :, None], by_home[None], 0), axis=1).reshape(slots)

    wanted = of_slots(named + 1) - 1
    tile_of = of_slots(tile)
    key = jnp.where(wanted < 0, blocks, wanted)
    place = jnp.arange(slots, dtype=jnp.int32)
    before = (key[None, :] < key[:, None]) | (
        (key[None, :] == key[:, None]) & (place[None, :] < place[:, None])
    )
    spot = jnp.sum(before.astype(jnp.int32), axis=1)
    order = jnp.sum(jnp.where(spot[None, :] == place[:, None], place[None, :], 0), axis=1)
    starts = jnp.sum(
        (key[None, :] < jnp.arange(blocks + 1, dtype=jnp.int32)[:, None]).astype(jnp.int32), axis=1
    )
    plan = jnp.concatenate([wanted, starts, me[None]]).astype(jnp.int32)
    return collect, plan, order.astype(jnp.int32), spot.astype(jnp.int32), tile_of.astype(jnp.int32)


def shards(
    start_columns,
    hamiltonian,
    band_pattern,
    coefficients,
    tile_peer,
    tile_block,
    tile_count,
    basis_values,
    core_density,
):
    col_count = lax.axis_size("col")
    entries = tile_peer.shape[0]
    tiles = core_density.shape[0]
    cols = start_columns.shape[1]
    me = lax.axis_index("col").astype(jnp.int32)
    blocks = start_columns.shape[0] // KB
    peers = tile_peer[:, 0]

    own = own_piece(peers, tile_block, tile_count, band_pattern, hamiltonian.reshape(-1, W))
    pieces, owners, steps = gather_pieces(own)

    chunks = list(pack(me[None], peers, after(basis_values, own), col_count))
    half = col_count // 2
    stages = [(half,), (half + 1,)] if col_count > 2 else []
    waits = [steps[-2], steps[-1]] if len(steps) > 1 else [pieces, pieces]
    early = [j for stage in stages for j in stage]
    stages.append([j for j in range(col_count - 1, 0, -1) if j not in early])
    waits = waits[: len(stages) - 1] + [pieces]
    for stage, wait in zip(stages, waits):
        for j in stage:
            pairs = [(c, partner(c, j, col_count)) for c in range(col_count)]
            chunks[j] = lax.ppermute(after(chunks[j], *wait), "col", pairs)

    v_low = shift(start_columns[-DEG * W :], "row", 1)
    v_high = shift(start_columns[: DEG * W], "row", -1)

    first, last, lists = edge_blocks(owners, pieces, col_count, DEG - 1)
    h_low = shift(last, "row", 1)
    h_high = shift(first, "row", -1)
    kernel_t = chebyshev(
        coefficients, owners, v_low, start_columns, v_high, h_low, h_high, pieces
    )
    collect, plan, order, spot, tile_of = make_plan(lists[:, 0], me, entries, tiles, col_count, blocks)
    partial = project(plan, order, spot, kernel_t, core_density, chunks)
    contributions = lax.all_to_all(partial, "col", split_axis=0, concat_axis=0, tiled=True)
    contributions = contributions.reshape(-1, P_SIZE)
    return update(
        plan, order, spot, tile_of, contributions, collect, chunks, tiles, blocks, cols
    )


def solution(mesh):
    return jax.shard_map(
        shards,
        mesh=mesh,
        in_specs=(
            P("row", "col"),
            P(("row", "col"), None, None, None),
            P(("row", "col")),
            P(),
            P(("row", "col"), None),
            P(("row", "col")),
            P(("row", "col")),
            P(("row", "col"), None, None, None),
            P(("row", "col"), None),
        ),
        out_specs=(P(("row", "col"), None), P("row", "col")),
        check_vma=False,
    )
```

```python
import functools
import math

import jax
import jax.numpy as jnp
from jax import lax
from jax.experimental import pallas as pl
from jax.experimental.pallas import tpu as pltpu
from jax.sharding import PartitionSpec as P

W = 256
KB = 512
DEG = 3
SLOTS = 4
CAP = 2
P_SIZE = 128
MIB = 1 << 20
LISTS = 16

exchange_factor = (3.0 / math.pi) ** (1.0 / 3.0)
HBM = pl.BlockSpec(memory_space=pltpu.HBM)
SMEM = pl.BlockSpec(memory_space=pltpu.SMEM)
VMEM = pl.BlockSpec(memory_space=pltpu.VMEM)


def piece_kernel(peers, named, counts, pattern, ham, piece, blocks, sems):
    rows = ham.shape[0]
    load = pltpu.make_async_copy(ham, blocks.at[pl.ds(0, rows)], sems.at[0])
    load.start()
    lane = lax.broadcasted_iota(jnp.int32, (LISTS, W), 1)
    lists = jnp.zeros((LISTS, W), jnp.int32)
    at = 0
    for ref in (peers, named, counts):
        for i in range(ref.shape[0]):
            lists = jnp.where(lane == at, ref[i], lists)
            at += 1
    blocks[rows:] = lists.astype(jnp.float32).astype(jnp.bfloat16)
    load.wait()
    for i in range(rows // (2 * W)):
        coupling = slice((2 * i + 1) * W, (2 * i + 2) * W)
        blocks[coupling] = blocks[coupling] * pattern[i].astype(jnp.bfloat16)
    store = pltpu.make_async_copy(blocks, piece, sems.at[1])
    store.start()
    store.wait()


def own_piece(peers, named, counts, pattern, ham):
    piece = (ham.shape[0] + LISTS, W)
    return pl.pallas_call(
        piece_kernel,
        out_shape=jax.ShapeDtypeStruct(piece, ham.dtype),
        in_specs=[SMEM] * 4 + [HBM],
        out_specs=HBM,
        scratch_shapes=[pltpu.VMEM(piece, ham.dtype), pltpu.SemaphoreType.DMA((2,))],
        compiler_params=pltpu.CompilerParams(vmem_limit_bytes=62 * MIB),
        name="own_piece",
    )(peers, named, counts, pattern, ham)


def pack_kernel(entries, slots, peers, basis, sent, held, count, in_sems, out_sems):
    def fetch(e):
        return pltpu.make_async_copy(basis.at[e], held.at[e], in_sems.at[e])

    def send(e, s):
        return pltpu.make_async_copy(held.at[e], sent.at[s], out_sems.at[s])

    for e in range(entries):
        fetch(e).start()
    for c in range(slots // CAP):
        count[c] = 0
    for e in range(entries):
        p = peers[e]
        k = count[p]
        count[p] = k + 1
        fetch(e).wait()
        send(e, p * CAP + k).start()
    for c in range(slots // CAP):
        for k in range(CAP):
            @pl.when(count[c] <= k)
            def _():
                send(0, c * CAP + k).start()
    for s in range(slots):
        send(0, s).wait()


def pack(peers, basis, slots):
    entries = basis.shape[0]
    return pl.pallas_call(
        functools.partial(pack_kernel, entries, slots),
        out_shape=jax.ShapeDtypeStruct((slots,) + basis.shape[1:], basis.dtype),
        in_specs=[SMEM, HBM],
        out_specs=HBM,
        scratch_shapes=[
            pltpu.VMEM(basis.shape, basis.dtype),
            pltpu.SMEM((slots // CAP,), jnp.int32),
            pltpu.SemaphoreType.DMA((entries,)),
            pltpu.SemaphoreType.DMA((slots,)),
        ],
        compiler_params=pltpu.CompilerParams(vmem_limit_bytes=62 * MIB),
        name="pack",
    )(peers, basis)


def after(block, *others):
    return pl.pallas_call(
        lambda *refs: None,
        out_shape=jax.ShapeDtypeStruct(block.shape, block.dtype),
        in_specs=[HBM] * (1 + len(others)),
        out_specs=HBM,
        input_output_aliases={0: 0},
        name="after",
    )(block, *others)


def gather_pieces(own):
    count = lax.axis_size("col")
    outer = 4 if count % 4 == 0 else count
    inner = count // outer
    me = lax.axis_index("col").astype(jnp.int32)
    a, b = me // inner, me % inner

    def hop(block, pairs):
        return lax.ppermute(block, "col", pairs)

    def inside(i, size):
        return (i >= 0) & (i < size)

    lines = [(own, 0)]
    steps = [[] for _ in range(outer - 1)]
    for way in (1, -1):
        block = own
        for step in range(1, outer):
            pairs = [
                (x * inner + y, (x + way) * inner + y)
                for x in range(outer) for y in range(inner)
                if 0 <= x + way < outer and 0 <= x - way * (step - 1) < outer
            ]
            block = hop(block, pairs)
            lines.append((block, -way * step))
            steps[step - 1].append(block)
    pieces, owners = [], []
    for line, shift_a in lines:
        pieces.append(line)
        owners.append(jnp.where(inside(a + shift_a, outer), (a + shift_a) * inner + b, -1))
        rows = [x for x in range(outer) if 0 <= x + shift_a < outer]
        if inner == 2:
            pairs = [(x * inner + y, x * inner + 1 - y) for x in rows for y in range(inner)]
            pieces.append(hop(line, pairs))
            if abs(shift_a) + 1 < outer - 1:
                steps[abs(shift_a) + 1].append(pieces[-1])
            owners.append(jnp.where(inside(a + shift_a, outer), (a + shift_a) * inner + 1 - b, -1))
            continue
        for way in (1, -1):
            block = line
            for step in range(1, inner):
                pairs = [
                    (x * inner + y, x * inner + y + way)
                    for x in rows for y in range(inner)
                    if 0 <= y + way < inner and 0 <= y - way * (step - 1) < inner
                ]
                block = hop(block, pairs)
                pieces.append(block)
                valid = inside(a + shift_a, outer) & inside(b - way * step, inner)
                owners.append(jnp.where(valid, (a + shift_a) * inner + b - way * step, -1))
    return pieces, jnp.stack(owners).astype(jnp.int32), steps


def edge_kernel(col_count, depth, owners, *refs):
    pieces, (first, last, lists, sems, list_sems) = refs[:-5], refs[-5:]
    rows = pieces[0].shape[0] - LISTS
    held = rows // (2 * W)
    total = col_count * held

    def each(act):
        for i, piece in enumerate(pieces):
            for g in range(depth):
                for out, block, sem in ((first, g, 0), (last, total - depth + g, 1)):
                    source = piece.at[pl.ds(block % held * 2 * W, 2 * W)]
                    copy = pltpu.make_async_copy(source, out.at[g], sems.at[sem, g])

                    @pl.when(owners[i] == block // held)
                    def _():
                        act(copy)

            @pl.when(owners[i] >= 0)
            def _():
                act(pltpu.make_async_copy(
                    piece.at[pl.ds(rows, LISTS)], lists.at[owners[i]], list_sems.at[i]
                ))

    each(lambda copy: copy.start())
    each(lambda copy: copy.wait())


def edge_blocks(owners, pieces, col_count, depth):
    shape = jax.ShapeDtypeStruct((depth, 2 * W, W), pieces[0].dtype)
    return pl.pallas_call(
        functools.partial(edge_kernel, col_count, depth),
        out_shape=(shape, shape, jax.ShapeDtypeStruct((col_count, LISTS, W), pieces[0].dtype)),
        in_specs=[SMEM] + [HBM] * len(pieces),
        out_specs=(VMEM, VMEM, VMEM),
        scratch_shapes=[
            pltpu.SemaphoreType.DMA((2, depth)),
            pltpu.SemaphoreType.DMA((len(pieces),)),
        ],
        name="edge_blocks",
    )(owners, *pieces)


def cheb_kernel(blocks, coef, owners, v_low, v_mid, v_high, h_low, h_high, *refs):
    *pieces, out, vext, hraw, hcat, cheb_1, cheb_2, total, kern, sems, psems, osems = refs
    halo_v = DEG
    halo_h = DEG - 1
    held = (pieces[0].shape[0] - LISTS) // (2 * W)
    h_copies = [
        pltpu.make_async_copy(h_low, hraw.at[pl.ds(0, halo_h)], sems.at[0]),
        pltpu.make_async_copy(h_high, hraw.at[pl.ds(halo_h + blocks, halo_h)], sems.at[1]),
    ]
    v_copies = [
        pltpu.make_async_copy(v_low, vext.at[pl.ds(0, halo_v * W)], sems.at[2]),
        pltpu.make_async_copy(v_mid, vext.at[pl.ds(halo_v * W, blocks * W)], sems.at[3]),
        pltpu.make_async_copy(v_high, vext.at[pl.ds((halo_v + blocks) * W, halo_v * W)], sems.at[4]),
    ]

    def each_piece(act):
        for i, piece in enumerate(pieces):
            @pl.when(owners[i] >= 0)
            def _():
                for k in range(held):
                    act(pltpu.make_async_copy(
                        piece.at[pl.ds(k * 2 * W, 2 * W)],
                        hraw.at[halo_h + owners[i] * held + k],
                        psems.at[i, k],
                    ))

    each_piece(lambda copy: copy.start())
    for copy in h_copies + v_copies:
        copy.start()
    each_piece(lambda copy: copy.wait())
    for copy in h_copies:
        copy.wait()
    rows = lax.broadcasted_iota(jnp.int32, (W, W), 0)
    cols = lax.broadcasted_iota(jnp.int32, (W, W), 1)
    upper = jnp.where(rows <= cols, 1.0, 0.0).astype(jnp.bfloat16)

    def build(j, carry):
        coupling = hraw[j, W:]
        lower_band = coupling * upper
        hcat[j, :, 0:W] = lower_band
        hcat[j, :, W : 2 * W] = hraw[j, :W]
        hcat[j, :, 2 * W : 3 * W] = coupling - lower_band
        return carry

    lax.fori_loop(0, blocks + 2 * halo_h, build, 0, unroll=2)
    for copy in v_copies:
        copy.wait()

    def rows_of(j, count=1):
        return pl.ds(pl.multiple_of(j * W, W), count * W)

    def band(source, j, row):
        return jnp.dot(hcat[j], source[rows_of(row, 3), :], preferred_element_type=jnp.float32)

    def first(j, carry):
        value = band(vext, j, j)
        cheb_1[rows_of(j), :] = value.astype(jnp.bfloat16)
        total[rows_of(j), :] = value
        return carry

    lax.fori_loop(0, blocks + 4, first, 0, unroll=2)

    def second(j, carry):
        begin = vext[rows_of(j + 2), :].astype(jnp.float32)
        value = 2.0 * band(cheb_1, j + 1, j) - begin
        cheb_2[rows_of(j), :] = value.astype(jnp.bfloat16)
        total[rows_of(j + 1), :] = (
            coef[0] * begin + (coef[1] - coef[3]) * total[rows_of(j + 1), :] + coef[2] * value
        )
        return carry

    lax.fori_loop(0, blocks + 2, second, 0, unroll=2)

    def store(j):
        return pltpu.make_async_copy(kern.at[j], out.at[j], osems.at[j])

    def third(j, carry):
        for half in range(KB // W):
            i = j * (KB // W) + half
            value = total[rows_of(i + 2), :] + (2.0 * coef[3]) * band(cheb_2, i + 2, i)
            kern[j, :, half * W : (half + 1) * W] = value.astype(jnp.bfloat16).T
        store(j).start()
        return carry

    lax.fori_loop(0, blocks // (KB // W), third, 0)
    for j in range(blocks // (KB // W)):
        store(j).wait()


def chebyshev(coefficients, owners, v_low, v_mid, v_high, h_low, h_high, pieces):
    blocks = v_mid.shape[0] // W
    cols = v_mid.shape[1]
    ext = blocks + 2 * (DEG - 1)
    flops = 2 * W * 3 * W * cols * (3 * blocks + 6)
    result = (blocks * W // KB, cols, KB)
    held = (pieces[0].shape[0] - LISTS) // (2 * W)
    return pl.pallas_call(
        functools.partial(cheb_kernel, blocks),
        out_shape=jax.ShapeDtypeStruct(result, jnp.bfloat16),
        in_specs=[SMEM] * 2 + [HBM] * (5 + len(pieces)),
        out_specs=HBM,
        scratch_shapes=[
            pltpu.VMEM(((blocks + 2 * DEG) * W, cols), jnp.bfloat16),
            pltpu.VMEM((ext, 2 * W, W), jnp.bfloat16),
            pltpu.VMEM((ext, W, 3 * W), jnp.bfloat16),
            pltpu.VMEM((ext * W, cols), jnp.bfloat16),
            pltpu.VMEM(((blocks + 2) * W, cols), jnp.bfloat16),
            pltpu.VMEM((ext * W, cols), jnp.float32),
            pltpu.VMEM(result, jnp.bfloat16),
            pltpu.SemaphoreType.DMA((5,)),
            pltpu.SemaphoreType.DMA((len(pieces), held)),
            pltpu.SemaphoreType.DMA((result[0],)),
        ],
        compiler_params=pltpu.CompilerParams(vmem_limit_bytes=62 * MIB),
        cost_estimate=pl.CostEstimate(flops=flops, bytes_accessed=16 * MIB, transcendentals=0),
        name="chebyshev",
    )(coefficients, owners, v_low, v_mid, v_high, h_low, h_high, *pieces)


def entry_loads(order, basis, pair, sems):
    def load(p):
        return pltpu.make_async_copy(basis.at[order[p]], pair.at[p], sems.at[p])

    def start(p, carry):
        load(p).start()
        return carry

    return load, start


def by_twos(first, last, load, body):
    def step(i, carry):
        p = first + 2 * i
        q = jnp.minimum(p + 1, last - 1)
        load(p).wait()

        @pl.when(q > p)
        def _():
            load(q).wait()

        body(i, p, q)
        return carry

    lax.fori_loop(0, (last - first + 1) // 2, step, 0)


def sent_rows(slots, tiles):
    return slots + tiles + -(slots + tiles) % 8


def project_kernel(blocks, plan, order, kernel_t, basis, core, out, kern, pair, rows, ksems, bsems):
    slots = pair.shape[0]
    load, start = entry_loads(order, basis, pair, bsems)

    def fetch(b):
        return pltpu.make_async_copy(kernel_t.at[b], kern.at[b], ksems.at[b])

    def begin(b, carry):
        first, last = plan[slots + b], plan[slots + b + 1]

        @pl.when(first < last)
        def _():
            fetch(b).start()

        return lax.fori_loop(first, last, start, carry)

    lax.fori_loop(0, blocks, begin, 0)
    rows[...] = jnp.zeros_like(rows)
    rows[slots : slots + core.shape[0]] = core[...]

    def step(b, carry):
        first, last = plan[slots + b], plan[slots + b + 1]

        @pl.when(first < last)
        def _():
            fetch(b).wait()

        def body(i, p, q):
            both = jnp.concatenate([pair[p, 0], pair[q, 0]], axis=1)
            projected = jnp.dot(kern[b], both, preferred_element_type=jnp.float32)
            other = jnp.concatenate([pair[p, 1], pair[q, 1]], axis=1).astype(jnp.float32)
            value = jnp.sum(projected * other, axis=0, keepdims=True) * (1.0 / KB)
            rows[pl.ds(order[p], 1), :] = value[:, :P_SIZE]
            rows[pl.ds(order[q], 1), :] = value[:, P_SIZE:]

        by_twos(first, last, load, body)
        return carry

    lax.fori_loop(0, blocks, step, 0)
    for c in range(out.shape[0]):
        out[c] = rows[...]


def project(plan, order, kernel_t, basis, core, col_count):
    slots = basis.shape[0]
    sent = sent_rows(slots, core.shape[0])
    blocks = kernel_t.shape[0]
    return pl.pallas_call(
        functools.partial(project_kernel, blocks),
        out_shape=jax.ShapeDtypeStruct((col_count, sent, P_SIZE), jnp.float32),
        in_specs=[SMEM, SMEM, HBM, HBM, VMEM],
        out_specs=VMEM,
        scratch_shapes=[
            pltpu.VMEM(kernel_t.shape, jnp.bfloat16),
            pltpu.VMEM(basis.shape, jnp.bfloat16),
            pltpu.VMEM((sent, P_SIZE), jnp.float32),
            pltpu.SemaphoreType.DMA((blocks,)),
            pltpu.SemaphoreType.DMA((slots,)),
        ],
        compiler_params=pltpu.CompilerParams(vmem_limit_bytes=62 * MIB),
        name="project",
    )(plan, order, kernel_t, basis, core)


def update_kernel(
    blocks, tiles, plan, order, tile_of, contributions, collect, basis,
    density_out, update_out, pair, density, potential, acc, stage, sems, osems,
):
    slots = pair.shape[0]
    live = plan[slots + blocks]
    me = plan[slots + blocks + 1]
    load, start = entry_loads(order, basis, pair, sems)
    lax.fori_loop(0, live, start, 0)
    density[...] = jnp.dot(
        collect[...],
        contributions[...],
        preferred_element_type=jnp.float32,
        precision=lax.Precision.HIGHEST,
    )
    for t in range(tiles):
        density_out[pl.ds(t, 1), :] = density[pl.ds(me * tiles + t, 1), :]
    positive = jnp.maximum(density[...], 0.1)
    root = jnp.exp(jnp.log(positive) * (1.0 / 3.0))
    root = root - (root - positive / (root * root)) * (1.0 / 3.0)
    potential[...] = -exchange_factor * root
    scale = 1.0 / math.sqrt(P_SIZE)

    def store(b):
        rows = pl.ds(pl.multiple_of(b * KB, KB), KB)
        return pltpu.make_async_copy(stage.at[b], update_out.at[rows], osems.at[b])

    def step(b, carry):
        first, last = plan[slots + b], plan[slots + b + 1]

        @pl.when(first == last)
        def _():
            stage[b] = jnp.zeros(stage.shape[1:], jnp.bfloat16)

        def body(i, p, q):
            weight_p = potential[pl.ds(tile_of[order[p]], 1), :]
            weight_q = potential[pl.ds(tile_of[order[q]], 1), :] * (q - p).astype(jnp.float32)
            weighted = jnp.concatenate(
                [
                    (pair[p, 1].astype(jnp.float32) * weight_p).astype(jnp.bfloat16),
                    (pair[q, 1].astype(jnp.float32) * weight_q).astype(jnp.bfloat16),
                ],
                axis=1,
            )
            block = lax.dot_general(
                jnp.concatenate([pair[p, 0], pair[q, 0]], axis=1),
                weighted,
                (((1,), (1,)), ((), ())),
                preferred_element_type=jnp.float32,
            )

            @pl.when(last - first <= 2)
            def _():
                stage[b] = (block * scale).astype(jnp.bfloat16)

            @pl.when((last - first > 2) & (i == 0))
            def _():
                acc[...] = block

            @pl.when(i > 0)
            def _():
                acc[...] += block

        by_twos(first, last, load, body)

        @pl.when(last - first > 2)
        def _():
            stage[b] = (acc[...] * scale).astype(jnp.bfloat16)

        store(b).start()
        return carry

    lax.fori_loop(0, blocks, step, 0)
    for b in range(blocks):
        store(b).wait()


def update(plan, order, tile_of, contributions, collect, basis, tiles, blocks, cols):
    slots = basis.shape[0]
    all_tiles = (collect.shape[0], P_SIZE)
    return pl.pallas_call(
        functools.partial(update_kernel, blocks, tiles),
        out_shape=(
            jax.ShapeDtypeStruct((tiles, P_SIZE), jnp.float32),
            jax.ShapeDtypeStruct((blocks * KB, cols), jnp.bfloat16),
        ),
        in_specs=[SMEM] * 3 + [VMEM] * 2 + [HBM],
        out_specs=(VMEM, HBM),
        scratch_shapes=[
            pltpu.VMEM(basis.shape, jnp.bfloat16),
            pltpu.VMEM(all_tiles, jnp.float32),
            pltpu.VMEM(all_tiles, jnp.float32),
            pltpu.VMEM((KB, cols), jnp.float32),
            pltpu.VMEM((blocks, KB, cols), jnp.bfloat16),
            pltpu.SemaphoreType.DMA((slots,)),
            pltpu.SemaphoreType.DMA((blocks,)),
        ],
        compiler_params=pltpu.CompilerParams(vmem_limit_bytes=62 * MIB),
        name="update",
    )(plan, order, tile_of, contributions, collect, basis)


def shift(block, axis, step):
    count = lax.axis_size(axis)
    pairs = [(i, i + step) for i in range(count) if 0 <= i + step < count]
    return lax.ppermute(block, axis, pairs)


def make_plan(lists, me, entries, tiles, col_count, blocks):
    slots = col_count * CAP
    sent = sent_rows(slots, tiles)
    lists = lists[:, : 2 * entries + tiles].astype(jnp.int32)
    peers, named, counts = lists[:, :entries], lists[:, entries : 2 * entries], lists[:, 2 * entries :]
    index = jnp.arange(entries, dtype=jnp.int32)
    home = jnp.arange(col_count, dtype=jnp.int32)[:, None]
    earlier = (peers[:, :, None] == peers[:, None, :]) & (index[None, :] < index[:, None])
    rank = jnp.sum(earlier.astype(jnp.int32), axis=2)
    live = (index % SLOTS)[None, :] < jnp.repeat(counts, SLOTS, axis=1)
    row = jnp.where(live, peers * sent + home * CAP + rank, -1).reshape(col_count, tiles, SLOTS)
    core = (home * sent + slots + jnp.arange(tiles, dtype=jnp.int32))[:, :, None]
    row = jnp.concatenate([row, core], axis=2).reshape(col_count * tiles, SLOTS + 1, 1)
    picked = row == jnp.arange(col_count * sent, dtype=jnp.int32)
    collect = jnp.sum(picked.astype(jnp.float32), axis=1)
    hit = (
        (peers == me)[:, None, :]
        & (rank[:, None, :] == jnp.arange(CAP, dtype=jnp.int32)[None, :, None])
        & live[:, None, :]
    )
    wanted = (jnp.sum(jnp.where(hit, named[:, None, :] + 1, 0), axis=2) - 1).reshape(slots)
    tile = home * tiles + index[None, :] // SLOTS
    tile_of = jnp.sum(jnp.where(hit, tile[:, None, :], 0), axis=2).reshape(slots)
    key = jnp.where(wanted < 0, blocks, wanted)
    place = jnp.arange(slots, dtype=jnp.int32)
    before = (key[None, :] < key[:, None]) | (
        (key[None, :] == key[:, None]) & (place[None, :] < place[:, None])
    )
    spot = jnp.sum(before.astype(jnp.int32), axis=1)
    order = jnp.sum(jnp.where(spot[None, :] == place[:, None], place[None, :], 0), axis=1)
    starts = jnp.sum(
        (key[None, :] < jnp.arange(blocks + 1, dtype=jnp.int32)[:, None]).astype(jnp.int32), axis=1
    )
    plan = jnp.concatenate([wanted, starts, me[None]]).astype(jnp.int32)
    return collect, plan, order.astype(jnp.int32), tile_of.astype(jnp.int32)


def shards(
    start_columns,
    hamiltonian,
    band_pattern,
    coefficients,
    tile_peer,
    tile_block,
    tile_count,
    basis_values,
    core_density,
):
    col_count = lax.axis_size("col")
    slots = col_count * CAP
    entries = tile_peer.shape[0]
    tiles = core_density.shape[0]
    cols = start_columns.shape[1]
    blocks = start_columns.shape[0] // KB
    peers = tile_peer[:, 0]

    own = own_piece(peers, tile_block, tile_count, band_pattern, hamiltonian.reshape(-1, W))
    pieces, owners, steps = gather_pieces(own)
    sent = after(pack(peers, basis_values, slots), *steps[min(1, len(steps) - 1)][:2])
    basis = lax.all_to_all(
        sent.reshape((col_count, CAP) + sent.shape[1:]), "col", split_axis=0, concat_axis=0, tiled=True
    ).reshape(sent.shape)

    v_low = shift(start_columns[-DEG * W :], "row", 1)
    v_high = shift(start_columns[: DEG * W], "row", -1)

    first, last, lists = edge_blocks(owners, pieces, col_count, DEG - 1)
    h_low = shift(last, "row", 1)
    h_high = shift(first, "row", -1)
    kernel_t = chebyshev(
        coefficients, owners, v_low, start_columns, v_high, h_low, h_high, pieces
    )
    me = lax.axis_index("col").astype(jnp.int32)
    collect, plan, order, tile_of = make_plan(lists[:, 0], me, entries, tiles, col_count, blocks)
    partial = project(plan, order, kernel_t, basis, core_density, col_count)
    contributions = lax.all_to_all(partial, "col", split_axis=0, concat_axis=0, tiled=True)
    contributions = contributions.reshape(-1, P_SIZE)
    return update(
        plan, order, tile_of, contributions, collect, basis, tiles, blocks, cols
    )


def solution(mesh):
    return jax.shard_map(
        shards,
        mesh=mesh,
        in_specs=(
            P("row", "col"),
            P(("row", "col"), None, None, None),
            P(("row", "col")),
            P(),
            P(("row", "col"), None),
            P(("row", "col")),
            P(("row", "col")),
            P(("row", "col"), None, None, None),
            P(("row", "col"), None),
        ),
        out_specs=(P(("row", "col"), None), P("row", "col")),
        check_vma=False,
    )
```

```python
import functools
import math

import jax
import jax.numpy as jnp
from jax import lax
from jax.experimental import pallas as pl
from jax.experimental.pallas import tpu as pltpu
from jax.sharding import PartitionSpec as P

W = 256
KB = 512
DEG = 3
SLOTS = 4
CAP = 2
P_SIZE = 128
MIB = 1 << 20
LISTS = 16

exchange_factor = (3.0 / math.pi) ** (1.0 / 3.0)
HBM = pl.BlockSpec(memory_space=pltpu.HBM)
SMEM = pl.BlockSpec(memory_space=pltpu.SMEM)
VMEM = pl.BlockSpec(memory_space=pltpu.VMEM)


def partner(me, j, count):
    if count & (count - 1) == 0:
        return me ^ abs(j)
    return (me + j) % count


def piece_kernel(peers, named, counts, pattern, ham, piece, blocks, sems):
    rows = ham.shape[0]
    load = pltpu.make_async_copy(ham, blocks.at[pl.ds(0, rows)], sems.at[0])
    load.start()
    lane = lax.broadcasted_iota(jnp.int32, (LISTS, W), 1)
    lists = jnp.zeros((LISTS, W), jnp.int32)
    at = 0
    for ref in (peers, named, counts):
        for i in range(ref.shape[0]):
            lists = jnp.where(lane == at, ref[i], lists)
            at += 1
    blocks[rows:] = lists.astype(jnp.float32).astype(jnp.bfloat16)
    load.wait()
    for i in range(rows // (2 * W)):
        coupling = slice((2 * i + 1) * W, (2 * i + 2) * W)
        blocks[coupling] = blocks[coupling] * pattern[i].astype(jnp.bfloat16)
    store = pltpu.make_async_copy(blocks, piece, sems.at[1])
    store.start()
    store.wait()


def own_piece(peers, named, counts, pattern, ham):
    piece = (ham.shape[0] + LISTS, W)
    return pl.pallas_call(
        piece_kernel,
        out_shape=jax.ShapeDtypeStruct(piece, ham.dtype),
        in_specs=[SMEM] * 4 + [HBM],
        out_specs=HBM,
        scratch_shapes=[pltpu.VMEM(piece, ham.dtype), pltpu.SemaphoreType.DMA((2,))],
        compiler_params=pltpu.CompilerParams(vmem_limit_bytes=62 * MIB),
        name="own_piece",
    )(peers, named, counts, pattern, ham)


def pack_kernel(entries, col_count, me, peers, basis, *refs):
    *chunks, held, owner, count, in_sems, out_sems = refs

    def fetch(e):
        return pltpu.make_async_copy(basis.at[e], held.at[e], in_sems.at[e])

    def send(j, k, e):
        return pltpu.make_async_copy(held.at[e], chunks[j].at[k], out_sems.at[j, k])

    for e in range(entries):
        fetch(e).start()
    for c in range(col_count):
        count[c] = 0
        for k in range(CAP):
            owner[c * CAP + k] = 0
    for e in range(entries):
        p = peers[e]
        k = count[p]
        count[p] = k + 1
        owner[p * CAP + k] = e
    for e in range(entries):
        fetch(e).wait()
    for j in range(col_count):
        for k in range(CAP):
            send(j, k, owner[partner(me[0], j, col_count) * CAP + k]).start()
    for j in range(col_count):
        for k in range(CAP):
            send(j, k, 0).wait()


def pack(me, peers, basis, col_count):
    entries = basis.shape[0]
    chunk = jax.ShapeDtypeStruct((CAP,) + basis.shape[1:], basis.dtype)
    return pl.pallas_call(
        functools.partial(pack_kernel, entries, col_count),
        out_shape=(chunk,) * col_count,
        in_specs=[SMEM, SMEM, HBM],
        out_specs=(HBM,) * col_count,
        scratch_shapes=[
            pltpu.VMEM(basis.shape, basis.dtype),
            pltpu.SMEM((col_count * CAP,), jnp.int32),
            pltpu.SMEM((col_count,), jnp.int32),
            pltpu.SemaphoreType.DMA((entries,)),
            pltpu.SemaphoreType.DMA((col_count, CAP)),
        ],
        compiler_params=pltpu.CompilerParams(vmem_limit_bytes=62 * MIB),
        name="pack",
    )(me, peers, basis)


def gate(kept, awaited):
    return list(pl.pallas_call(
        lambda *refs: None,
        out_shape=tuple(jax.ShapeDtypeStruct(x.shape, x.dtype) for x in kept),
        in_specs=[HBM] * (len(kept) + len(awaited)),
        out_specs=(HBM,) * len(kept),
        input_output_aliases={i: i for i in range(len(kept))},
        compiler_params=pltpu.CompilerParams(vmem_limit_bytes=62 * MIB),
        name="gate",
    )(*kept, *awaited))


def gather_pieces(own, chunks, early):
    count = lax.axis_size("col")
    outer = 4 if count % 4 == 0 else count
    inner = count // outer
    me = lax.axis_index("col").astype(jnp.int32)
    a, b = me // inner, me % inner

    def inside(i, size):
        return (i >= 0) & (i < size)

    def along(block, way, step):
        pairs = [
            (x * inner + y, (x + way) * inner + y)
            for x in range(outer) for y in range(inner)
            if 0 <= x + way < outer and 0 <= x - way * (step - 1) < outer
        ]
        return lax.ppermute(block, "col", pairs)

    def across(line, shift_a):
        rows = [x for x in range(outer) if 0 <= x + shift_a < outer]
        there = inside(a + shift_a, outer)
        if inner == 2:
            pairs = [(x * inner + y, x * inner + 1 - y) for x in rows for y in range(inner)]
            block = lax.ppermute(line, "col", pairs)
            return [(block, jnp.where(there, (a + shift_a) * inner + 1 - b, -1))]
        found = []
        for way in (1, -1):
            block = line
            for step in range(1, inner):
                pairs = [
                    (x * inner + y, x * inner + y + way)
                    for x in rows for y in range(inner)
                    if 0 <= y + way < inner and 0 <= y - way * (step - 1) < inner
                ]
                block = lax.ppermute(block, "col", pairs)
                valid = there & inside(b - way * step, inner)
                found.append((block, jnp.where(valid, (a + shift_a) * inner + b - way * step, -1)))
        return found

    def send(j):
        pairs = [(c, partner(c, j, count)) for c in range(count)]
        chunks[j] = lax.ppermute(chunks[j], "col", pairs)

    found = [(own, me)] + across(own, 0)
    lines = [(own, 1), (own, -1)]
    waiting = [block for block, _ in found[1:]] + early
    order = sorted(range(1, count), key=lambda j: (j < count // 2, j))
    waiting.append(chunks[order[0]])
    staged = []
    for step in range(1, outer):
        lines = [(along(block, way, step), way) for block, way in lines]
        if step == 1:
            kept = gate([block for block, _ in lines], waiting)
            lines = [(block, way) for block, (_, way) in zip(kept, lines)]
            waiting = []
        elif step == 2:
            j = order[0]
            chunks[j] = gate([chunks[j]], [block for block, _ in lines])[0]
            send(j)
            staged.append(j)
        else:
            rest = [j for j in order if j not in staged]
            kept = gate(
                [block for block, _ in lines] + [chunks[j] for j in rest],
                waiting + [chunks[j] for j in staged],
            )
            lines = [(block, way) for block, (_, way) in zip(kept, lines)]
            for j, chunk in zip(rest, kept[len(lines):]):
                chunks[j] = chunk
        for block, way in lines:
            handed = across(block, -way * step)
            found.append((block, jnp.where(inside(a - way * step, outer), (a - way * step) * inner + b, -1)))
            found += handed
            if step == 1:
                waiting += [piece for piece, _ in handed]
    rest = [j for j in order if j not in staged]
    for j in [min(rest)] + [j for j in rest if j != min(rest)]:
        send(j)
    pieces = [block for block, _ in found]
    owners = jnp.stack([owner for _, owner in found]).astype(jnp.int32)
    return pieces, owners, chunks


def edge_kernel(col_count, depth, owners, *refs):
    pieces, (first, last, lists, sems, list_sems) = refs[:-5], refs[-5:]
    rows = pieces[0].shape[0] - LISTS
    held = rows // (2 * W)
    total = col_count * held

    def each(act):
        for i, piece in enumerate(pieces):
            for g in range(depth):
                for out, block, sem in ((first, g, 0), (last, total - depth + g, 1)):
                    source = piece.at[pl.ds(block % held * 2 * W, 2 * W)]
                    copy = pltpu.make_async_copy(source, out.at[g], sems.at[sem, g])

                    @pl.when(owners[i] == block // held)
                    def _():
                        act(copy)

            @pl.when(owners[i] >= 0)
            def _():
                act(pltpu.make_async_copy(
                    piece.at[pl.ds(rows, LISTS)], lists.at[owners[i]], list_sems.at[i]
                ))

    each(lambda copy: copy.start())
    each(lambda copy: copy.wait())


def edge_blocks(owners, pieces, col_count, depth):
    shape = jax.ShapeDtypeStruct((depth, 2 * W, W), pieces[0].dtype)
    return pl.pallas_call(
        functools.partial(edge_kernel, col_count, depth),
        out_shape=(shape, shape, jax.ShapeDtypeStruct((col_count, LISTS, W), pieces[0].dtype)),
        in_specs=[SMEM] + [HBM] * len(pieces),
        out_specs=(VMEM, VMEM, VMEM),
        scratch_shapes=[
            pltpu.SemaphoreType.DMA((2, depth)),
            pltpu.SemaphoreType.DMA((len(pieces),)),
        ],
        compiler_params=pltpu.CompilerParams(vmem_limit_bytes=62 * MIB),
        name="edge_blocks",
    )(owners, *pieces)


def cheb_kernel(blocks, coef, owners, v_low, v_mid, v_high, h_low, h_high, *refs):
    *pieces, out, vext, hraw, hcat, cheb_1, cheb_2, total, kern, sems, psems, osems = refs
    halo_v = DEG
    halo_h = DEG - 1
    held = (pieces[0].shape[0] - LISTS) // (2 * W)
    h_copies = [
        pltpu.make_async_copy(h_low, hraw.at[pl.ds(0, halo_h)], sems.at[0]),
        pltpu.make_async_copy(h_high, hraw.at[pl.ds(halo_h + blocks, halo_h)], sems.at[1]),
    ]
    v_copies = [
        pltpu.make_async_copy(v_low, vext.at[pl.ds(0, halo_v * W)], sems.at[2]),
        pltpu.make_async_copy(v_mid, vext.at[pl.ds(halo_v * W, blocks * W)], sems.at[3]),
        pltpu.make_async_copy(v_high, vext.at[pl.ds((halo_v + blocks) * W, halo_v * W)], sems.at[4]),
    ]

    def each_piece(act):
        for i, piece in enumerate(pieces):
            @pl.when(owners[i] >= 0)
            def _():
                for k in range(held):
                    act(pltpu.make_async_copy(
                        piece.at[pl.ds(k * 2 * W, 2 * W)],
                        hraw.at[halo_h + owners[i] * held + k],
                        psems.at[i, k],
                    ))

    each_piece(lambda copy: copy.start())
    for copy in h_copies + v_copies:
        copy.start()
    each_piece(lambda copy: copy.wait())
    for copy in h_copies:
        copy.wait()
    rows = lax.broadcasted_iota(jnp.int32, (W, W), 0)
    cols = lax.broadcasted_iota(jnp.int32, (W, W), 1)
    upper = jnp.where(rows <= cols, 1.0, 0.0).astype(jnp.bfloat16)

    def build(j, carry):
        coupling = hraw[j, W:]
        lower_band = coupling * upper
        hcat[j, :, 0:W] = lower_band
        hcat[j, :, W : 2 * W] = hraw[j, :W]
        hcat[j, :, 2 * W : 3 * W] = coupling - lower_band
        return carry

    lax.fori_loop(0, blocks + 2 * halo_h, build, 0, unroll=2)
    for copy in v_copies:
        copy.wait()

    def rows_of(j, count=1):
        return pl.ds(pl.multiple_of(j * W, W), count * W)

    def band(source, j, row):
        return jnp.dot(hcat[j], source[rows_of(row, 3), :], preferred_element_type=jnp.float32)

    def first(j, carry):
        value = band(vext, j, j)
        cheb_1[rows_of(j), :] = value.astype(jnp.bfloat16)
        total[rows_of(j), :] = value
        return carry

    lax.fori_loop(0, blocks + 4, first, 0, unroll=2)

    def second(j, carry):
        begin = vext[rows_of(j + 2), :].astype(jnp.float32)
        value = 2.0 * band(cheb_1, j + 1, j) - begin
        cheb_2[rows_of(j), :] = value.astype(jnp.bfloat16)
        total[rows_of(j + 1), :] = (
            coef[0] * begin + (coef[1] - coef[3]) * total[rows_of(j + 1), :] + coef[2] * value
        )
        return carry

    lax.fori_loop(0, blocks + 2, second, 0, unroll=2)

    def store(j):
        return pltpu.make_async_copy(kern.at[j], out.at[j], osems.at[j])

    def third(j, carry):
        for half in range(KB // W):
            i = j * (KB // W) + half
            value = total[rows_of(i + 2), :] + (2.0 * coef[3]) * band(cheb_2, i + 2, i)
            kern[j, :, half * W : (half + 1) * W] = value.astype(jnp.bfloat16).T
        store(j).start()
        return carry

    lax.fori_loop(0, blocks // (KB // W), third, 0)
    for j in range(blocks // (KB // W)):
        store(j).wait()


def chebyshev(coefficients, owners, v_low, v_mid, v_high, h_low, h_high, pieces):
    blocks = v_mid.shape[0] // W
    cols = v_mid.shape[1]
    ext = blocks + 2 * (DEG - 1)
    result = (blocks * W // KB, cols, KB)
    held = (pieces[0].shape[0] - LISTS) // (2 * W)
    return pl.pallas_call(
        functools.partial(cheb_kernel, blocks),
        out_shape=jax.ShapeDtypeStruct(result, jnp.bfloat16),
        in_specs=[SMEM] * 2 + [HBM] * (5 + len(pieces)),
        out_specs=HBM,
        scratch_shapes=[
            pltpu.VMEM(((blocks + 2 * DEG) * W, cols), jnp.bfloat16),
            pltpu.VMEM((ext, 2 * W, W), jnp.bfloat16),
            pltpu.VMEM((ext, W, 3 * W), jnp.bfloat16),
            pltpu.VMEM((ext * W, cols), jnp.bfloat16),
            pltpu.VMEM(((blocks + 2) * W, cols), jnp.bfloat16),
            pltpu.VMEM((ext * W, cols), jnp.float32),
            pltpu.VMEM(result, jnp.bfloat16),
            pltpu.SemaphoreType.DMA((5,)),
            pltpu.SemaphoreType.DMA((len(pieces), held)),
            pltpu.SemaphoreType.DMA((result[0],)),
        ],
        compiler_params=pltpu.CompilerParams(vmem_limit_bytes=62 * MIB),
        cost_estimate=pl.CostEstimate(flops=1, bytes_accessed=1, transcendentals=0),
        name="chebyshev",
    )(coefficients, owners, v_low, v_mid, v_high, h_low, h_high, *pieces)


def entry_loads(plan, spot, chunks, pair, sems):
    def start():
        for j, chunk in enumerate(chunks):
            for k in range(CAP):
                m = j * CAP + k

                @pl.when(plan[m] >= 0)
                def _():
                    pltpu.make_async_copy(chunk.at[k], pair.at[spot[m]], sems.at[spot[m]]).start()

    def load(p):
        return pltpu.make_async_copy(chunks[0].at[0], pair.at[p], sems.at[p])

    return start, load


def by_twos(first, last, load, body):
    def step(i, carry):
        p = first + 2 * i
        q = jnp.minimum(p + 1, last - 1)
        load(p).wait()

        @pl.when(q > p)
        def _():
            load(q).wait()

        body(i, p, q)
        return carry

    lax.fori_loop(0, (last - first + 1) // 2, step, 0)


def sent_rows(slots, tiles):
    return slots + tiles + -(slots + tiles) % 8


def project_kernel(blocks, plan, order, spot, kernel_t, core, *refs):
    *chunks, out, kern, pair, rows, ksems, bsems = refs
    slots = pair.shape[0]
    start, load = entry_loads(plan, spot, chunks, pair, bsems)

    def fetch(b):
        return pltpu.make_async_copy(kernel_t.at[b], kern.at[b], ksems.at[b])

    for b in range(blocks):
        @pl.when(plan[slots + b] < plan[slots + b + 1])
        def _():
            fetch(b).start()

    start()
    rows[...] = jnp.zeros_like(rows)
    rows[slots : slots + core.shape[0]] = core[...]

    def step(b, carry):
        first, last = plan[slots + b], plan[slots + b + 1]

        @pl.when(first < last)
        def _():
            fetch(b).wait()

        def body(i, p, q):
            both = jnp.concatenate([pair[p, 0], pair[q, 0]], axis=1)
            projected = jnp.dot(kern[b], both, preferred_element_type=jnp.float32)
            other = jnp.concatenate([pair[p, 1], pair[q, 1]], axis=1).astype(jnp.float32)
            value = jnp.sum(projected * other, axis=0, keepdims=True) * (1.0 / KB)
            rows[pl.ds(order[p], 1), :] = value[:, :P_SIZE]
            rows[pl.ds(order[q], 1), :] = value[:, P_SIZE:]

        by_twos(first, last, load, body)
        return carry

    lax.fori_loop(0, blocks, step, 0)
    for c in range(out.shape[0]):
        out[c] = rows[...]


def project(plan, order, spot, kernel_t, core, chunks):
    col_count = len(chunks)
    slots = col_count * CAP
    sent = sent_rows(slots, core.shape[0])
    blocks = kernel_t.shape[0]
    return pl.pallas_call(
        functools.partial(project_kernel, blocks),
        out_shape=jax.ShapeDtypeStruct((col_count, sent, P_SIZE), jnp.float32),
        in_specs=[SMEM, SMEM, SMEM, HBM, VMEM] + [HBM] * col_count,
        out_specs=VMEM,
        scratch_shapes=[
            pltpu.VMEM(kernel_t.shape, jnp.bfloat16),
            pltpu.VMEM((slots,) + chunks[0].shape[1:], jnp.bfloat16),
            pltpu.VMEM((sent, P_SIZE), jnp.float32),
            pltpu.SemaphoreType.DMA((blocks,)),
            pltpu.SemaphoreType.DMA((slots,)),
        ],
        compiler_params=pltpu.CompilerParams(vmem_limit_bytes=62 * MIB),
        name="project",
    )(plan, order, spot, kernel_t, core, *chunks)


def update_kernel(
    blocks, tiles, plan, order, spot, tile_of, contributions, collect, *refs
):
    (
        *chunks, density_out, update_out, pair, density, potential, acc, stage, sems, osems
    ) = refs
    slots = pair.shape[0]
    me = plan[slots + blocks + 1]
    start, load = entry_loads(plan, spot, chunks, pair, sems)
    start()
    density[...] = jnp.dot(
        collect[...],
        contributions[...],
        preferred_element_type=jnp.float32,
        precision=lax.Precision.HIGHEST,
    )
    for t in range(tiles):
        density_out[pl.ds(t, 1), :] = density[pl.ds(me * tiles + t, 1), :]
    positive = jnp.maximum(density[...], 0.1)
    root = jnp.exp(jnp.log(positive) * (1.0 / 3.0))
    root = root - (root - positive / (root * root)) * (1.0 / 3.0)
    potential[...] = -exchange_factor * root
    scale = 1.0 / math.sqrt(P_SIZE)

    def store(b):
        rows = pl.ds(pl.multiple_of(b * KB, KB), KB)
        return pltpu.make_async_copy(stage.at[b], update_out.at[rows], osems.at[b])

    def step(b, carry):
        first, last = plan[slots + b], plan[slots + b + 1]

        @pl.when(first == last)
        def _():
            stage[b] = jnp.zeros(stage.shape[1:], jnp.bfloat16)

        def body(i, p, q):
            weight_p = potential[pl.ds(tile_of[order[p]], 1), :]
            weight_q = potential[pl.ds(tile_of[order[q]], 1), :] * (q - p).astype(jnp.float32)
            weighted = jnp.concatenate(
                [
                    (pair[p, 1].astype(jnp.float32) * weight_p).astype(jnp.bfloat16),
                    (pair[q, 1].astype(jnp.float32) * weight_q).astype(jnp.bfloat16),
                ],
                axis=1,
            )
            block = lax.dot_general(
                jnp.concatenate([pair[p, 0], pair[q, 0]], axis=1),
                weighted,
                (((1,), (1,)), ((), ())),
                preferred_element_type=jnp.float32,
            )

            @pl.when(last - first <= 2)
            def _():
                stage[b] = (block * scale).astype(jnp.bfloat16)

            @pl.when((last - first > 2) & (i == 0))
            def _():
                acc[...] = block

            @pl.when(i > 0)
            def _():
                acc[...] += block

        by_twos(first, last, load, body)

        @pl.when(last - first > 2)
        def _():
            stage[b] = (acc[...] * scale).astype(jnp.bfloat16)

        store(b).start()
        return carry

    lax.fori_loop(0, blocks, step, 0)
    for b in range(blocks):
        store(b).wait()


def update(plan, order, spot, tile_of, contributions, collect, chunks, tiles, blocks, cols):
    slots = len(chunks) * CAP
    all_tiles = (collect.shape[0], P_SIZE)
    return pl.pallas_call(
        functools.partial(update_kernel, blocks, tiles),
        out_shape=(
            jax.ShapeDtypeStruct((tiles, P_SIZE), jnp.float32),
            jax.ShapeDtypeStruct((blocks * KB, cols), jnp.bfloat16),
        ),
        in_specs=[SMEM] * 4 + [VMEM] * 2 + [HBM] * len(chunks),
        out_specs=(VMEM, HBM),
        scratch_shapes=[
            pltpu.VMEM((slots,) + chunks[0].shape[1:], jnp.bfloat16),
            pltpu.VMEM(all_tiles, jnp.float32),
            pltpu.VMEM(all_tiles, jnp.float32),
            pltpu.VMEM((KB, cols), jnp.float32),
            pltpu.VMEM((blocks, KB, cols), jnp.bfloat16),
            pltpu.SemaphoreType.DMA((slots,)),
            pltpu.SemaphoreType.DMA((blocks,)),
        ],
        compiler_params=pltpu.CompilerParams(vmem_limit_bytes=62 * MIB),
        name="update",
    )(plan, order, spot, tile_of, contributions, collect, *chunks)


def shift(block, axis, step):
    count = lax.axis_size(axis)
    pairs = [(i, i + step) for i in range(count) if 0 <= i + step < count]
    return lax.ppermute(block, axis, pairs)


def chunk_of(home, owner, count):
    return home ^ owner if count & (count - 1) == 0 else (owner - home) % count


def make_plan(lists, me, entries, tiles, col_count, blocks):
    slots = col_count * CAP
    sent = sent_rows(slots, tiles)
    lists = lists[:, : 2 * entries + tiles].astype(jnp.int32)
    peers, named, counts = lists[:, :entries], lists[:, entries : 2 * entries], lists[:, 2 * entries :]
    index = jnp.arange(entries, dtype=jnp.int32)
    home = jnp.arange(col_count, dtype=jnp.int32)[:, None]
    earlier = (peers[:, :, None] == peers[:, None, :]) & (index[None, :] < index[:, None])
    rank = jnp.sum(earlier.astype(jnp.int32), axis=2)
    live = (index % SLOTS)[None, :] < jnp.repeat(counts, SLOTS, axis=1)
    row = jnp.where(live, peers * sent + chunk_of(home, peers, col_count) * CAP + rank, -1).reshape(col_count, tiles, SLOTS)
    core = (home * sent + slots + jnp.arange(tiles, dtype=jnp.int32))[:, :, None]
    row = jnp.concatenate([row, core], axis=2).reshape(col_count * tiles, SLOTS + 1, 1)
    picked = row == jnp.arange(col_count * sent, dtype=jnp.int32)
    collect = jnp.sum(picked.astype(jnp.float32), axis=1)
    hit = (
        (peers == me)[:, None, :]
        & (rank[:, None, :] == jnp.arange(CAP, dtype=jnp.int32)[None, :, None])
        & live[:, None, :]
    )
    at_me = chunk_of(home, me, col_count).reshape(1, col_count) == home
    tile = home * tiles + index[None, :] // SLOTS

    def of_slots(values):
        by_home = jnp.sum(jnp.where(hit, values[:, None, :], 0), axis=2)
        return jnp.sum(jnp.where(at_me[:, :, None], by_home[None], 0), axis=1).reshape(slots)

    wanted = of_slots(named + 1) - 1
    tile_of = of_slots(tile)
    key = jnp.where(wanted < 0, blocks, wanted)
    place = jnp.arange(slots, dtype=jnp.int32)
    before = (key[None, :] < key[:, None]) | (
        (key[None, :] == key[:, None]) & (place[None, :] < place[:, None])
    )
    spot = jnp.sum(before.astype(jnp.int32), axis=1)
    order = jnp.sum(jnp.where(spot[None, :] == place[:, None], place[None, :], 0), axis=1)
    starts = jnp.sum(
        (key[None, :] < jnp.arange(blocks + 1, dtype=jnp.int32)[:, None]).astype(jnp.int32), axis=1
    )
    plan = jnp.concatenate([wanted, starts, me[None]]).astype(jnp.int32)
    return collect, plan, order.astype(jnp.int32), spot.astype(jnp.int32), tile_of.astype(jnp.int32)


def shards(
    start_columns,
    hamiltonian,
    band_pattern,
    coefficients,
    tile_peer,
    tile_block,
    tile_count,
    basis_values,
    core_density,
):
    col_count = lax.axis_size("col")
    entries = tile_peer.shape[0]
    tiles = core_density.shape[0]
    cols = start_columns.shape[1]
    me = lax.axis_index("col").astype(jnp.int32)
    blocks = start_columns.shape[0] // KB
    peers = tile_peer[:, 0]

    own = own_piece(peers, tile_block, tile_count, band_pattern, hamiltonian.reshape(-1, W))
    v_low = shift(start_columns[-DEG * W :], "row", 1)
    v_high = shift(start_columns[: DEG * W], "row", -1)
    chunks = list(pack(me[None], peers, basis_values, col_count))
    pieces, owners, chunks = gather_pieces(own, chunks, [v_low, v_high])

    first, last, lists = edge_blocks(owners, pieces, col_count, DEG - 1)
    h_low = shift(last, "row", 1)
    h_high = shift(first, "row", -1)
    kernel_t = chebyshev(
        coefficients, owners, v_low, start_columns, v_high, h_low, h_high, pieces
    )
    collect, plan, order, spot, tile_of = make_plan(lists[:, 0], me, entries, tiles, col_count, blocks)
    partial = project(plan, order, spot, kernel_t, core_density, chunks)
    contributions = lax.all_to_all(partial, "col", split_axis=0, concat_axis=0, tiled=True)
    contributions = contributions.reshape(-1, P_SIZE)
    return update(
        plan, order, spot, tile_of, contributions, collect, chunks, tiles, blocks, cols
    )


def solution(mesh):
    return jax.shard_map(
        shards,
        mesh=mesh,
        in_specs=(
            P("row", "col"),
            P(("row", "col"), None, None, None),
            P(("row", "col")),
            P(),
            P(("row", "col"), None),
            P(("row", "col")),
            P(("row", "col")),
            P(("row", "col"), None, None, None),
            P(("row", "col"), None),
        ),
        out_specs=(P(("row", "col"), None), P("row", "col")),
        check_vma=False,
    )
```

```python
import functools
import math

import jax
import jax.numpy as jnp
from jax import lax
from jax.experimental import pallas as pl
from jax.experimental.pallas import tpu as pltpu
from jax.sharding import PartitionSpec as P

W = 256
KB = 512
DEG = 3
SLOTS = 4
CAP = 2
P_SIZE = 128
MIB = 1 << 20
LISTS = 16

exchange_factor = (3.0 / math.pi) ** (1.0 / 3.0)
HBM = pl.BlockSpec(memory_space=pltpu.HBM)
SMEM = pl.BlockSpec(memory_space=pltpu.SMEM)
VMEM = pl.BlockSpec(memory_space=pltpu.VMEM)


def piece_kernel(peers, named, counts, pattern, ham, piece, blocks, sems):
    rows = ham.shape[0]
    load = pltpu.make_async_copy(ham, blocks.at[pl.ds(0, rows)], sems.at[0])
    load.start()
    lane = lax.broadcasted_iota(jnp.int32, (LISTS, W), 1)
    lists = jnp.zeros((LISTS, W), jnp.int32)
    at = 0
    for ref in (peers, named, counts):
        for i in range(ref.shape[0]):
            lists = jnp.where(lane == at, ref[i], lists)
            at += 1
    blocks[rows:] = lists.astype(jnp.float32).astype(jnp.bfloat16)
    load.wait()
    for i in range(rows // (2 * W)):
        coupling = slice((2 * i + 1) * W, (2 * i + 2) * W)
        blocks[coupling] = blocks[coupling] * pattern[i].astype(jnp.bfloat16)
    store = pltpu.make_async_copy(blocks, piece, sems.at[1])
    store.start()
    store.wait()


def own_piece(peers, named, counts, pattern, ham):
    piece = (ham.shape[0] + LISTS, W)
    return pl.pallas_call(
        piece_kernel,
        out_shape=jax.ShapeDtypeStruct(piece, ham.dtype),
        in_specs=[SMEM] * 4 + [HBM],
        out_specs=HBM,
        scratch_shapes=[pltpu.VMEM(piece, ham.dtype), pltpu.SemaphoreType.DMA((2,))],
        compiler_params=pltpu.CompilerParams(vmem_limit_bytes=62 * MIB),
        name="own_piece",
    )(peers, named, counts, pattern, ham)


def pack_kernel(entries, slots, peers, basis, sent, held, count, in_sems, out_sems):
    def fetch(e):
        return pltpu.make_async_copy(basis.at[e], held.at[e], in_sems.at[e])

    def send(e, s):
        return pltpu.make_async_copy(held.at[e], sent.at[s], out_sems.at[s])

    for e in range(entries):
        fetch(e).start()
    for c in range(slots // CAP):
        count[c] = 0
    for e in range(entries):
        p = peers[e]
        k = count[p]
        count[p] = k + 1
        fetch(e).wait()
        send(e, p * CAP + k).start()
    for c in range(slots // CAP):
        for k in range(CAP):
            @pl.when(count[c] <= k)
            def _():
                send(0, c * CAP + k).start()
    for s in range(slots):
        send(0, s).wait()


def pack(peers, basis, slots):
    entries = basis.shape[0]
    return pl.pallas_call(
        functools.partial(pack_kernel, entries, slots),
        out_shape=jax.ShapeDtypeStruct((slots,) + basis.shape[1:], basis.dtype),
        in_specs=[SMEM, HBM],
        out_specs=HBM,
        scratch_shapes=[
            pltpu.VMEM(basis.shape, basis.dtype),
            pltpu.SMEM((slots // CAP,), jnp.int32),
            pltpu.SemaphoreType.DMA((entries,)),
            pltpu.SemaphoreType.DMA((slots,)),
        ],
        compiler_params=pltpu.CompilerParams(vmem_limit_bytes=62 * MIB),
        name="pack",
    )(peers, basis)


def after(block, *others):
    return pl.pallas_call(
        lambda *refs: None,
        out_shape=jax.ShapeDtypeStruct(block.shape, block.dtype),
        in_specs=[HBM] * (1 + len(others)),
        out_specs=HBM,
        input_output_aliases={0: 0},
        compiler_params=pltpu.CompilerParams(vmem_limit_bytes=62 * MIB),
        name="after",
    )(block, *others)


def gather_pieces(own):
    count = lax.axis_size("col")
    outer = 4 if count % 4 == 0 else count
    inner = count // outer
    me = lax.axis_index("col").astype(jnp.int32)
    a, b = me // inner, me % inner

    def hop(block, pairs):
        return lax.ppermute(block, "col", pairs)

    def inside(i, size):
        return (i >= 0) & (i < size)

    lines = [(own, 0)]
    steps = [[] for _ in range(outer - 1)]
    for way in (1, -1):
        block = own
        for step in range(1, outer):
            pairs = [
                (x * inner + y, (x + way) * inner + y)
                for x in range(outer) for y in range(inner)
                if 0 <= x + way < outer and 0 <= x - way * (step - 1) < outer
            ]
            block = hop(block, pairs)
            lines.append((block, -way * step))
            steps[step - 1].append(block)
    pieces, owners = [], []
    for line, shift_a in lines:
        pieces.append(line)
        owners.append(jnp.where(inside(a + shift_a, outer), (a + shift_a) * inner + b, -1))
        rows = [x for x in range(outer) if 0 <= x + shift_a < outer]
        if inner == 2:
            pairs = [(x * inner + y, x * inner + 1 - y) for x in rows for y in range(inner)]
            pieces.append(hop(line, pairs))
            if abs(shift_a) < outer - 2:
                steps[-2].append(pieces[-1])
            owners.append(jnp.where(inside(a + shift_a, outer), (a + shift_a) * inner + 1 - b, -1))
            continue
        for way in (1, -1):
            block = line
            for step in range(1, inner):
                pairs = [
                    (x * inner + y, x * inner + y + way)
                    for x in rows for y in range(inner)
                    if 0 <= y + way < inner and 0 <= y - way * (step - 1) < inner
                ]
                block = hop(block, pairs)
                pieces.append(block)
                valid = inside(a + shift_a, outer) & inside(b - way * step, inner)
                owners.append(jnp.where(valid, (a + shift_a) * inner + b - way * step, -1))
    return pieces, jnp.stack(owners).astype(jnp.int32), steps


def edge_kernel(col_count, depth, owners, *refs):
    pieces, (first, last, lists, sems, list_sems) = refs[:-5], refs[-5:]
    rows = pieces[0].shape[0] - LISTS
    held = rows // (2 * W)
    total = col_count * held

    def each(act):
        for i, piece in enumerate(pieces):
            for g in range(depth):
                for out, block, sem in ((first, g, 0), (last, total - depth + g, 1)):
                    source = piece.at[pl.ds(block % held * 2 * W, 2 * W)]
                    copy = pltpu.make_async_copy(source, out.at[g], sems.at[sem, g])

                    @pl.when(owners[i] == block // held)
                    def _():
                        act(copy)

            @pl.when(owners[i] >= 0)
            def _():
                act(pltpu.make_async_copy(
                    piece.at[pl.ds(rows, LISTS)], lists.at[owners[i]], list_sems.at[i]
                ))

    each(lambda copy: copy.start())
    each(lambda copy: copy.wait())


def edge_blocks(owners, pieces, col_count, depth):
    shape = jax.ShapeDtypeStruct((depth, 2 * W, W), pieces[0].dtype)
    return pl.pallas_call(
        functools.partial(edge_kernel, col_count, depth),
        out_shape=(shape, shape, jax.ShapeDtypeStruct((col_count, LISTS, W), pieces[0].dtype)),
        in_specs=[SMEM] + [HBM] * len(pieces),
        out_specs=(VMEM, VMEM, VMEM),
        scratch_shapes=[
            pltpu.SemaphoreType.DMA((2, depth)),
            pltpu.SemaphoreType.DMA((len(pieces),)),
        ],
        name="edge_blocks",
    )(owners, *pieces)


def cheb_kernel(blocks, coef, owners, v_low, v_mid, v_high, h_low, h_high, *refs):
    *pieces, out, vext, hraw, hcat, cheb_1, cheb_2, total, kern, sems, psems, osems = refs
    halo_v = DEG
    halo_h = DEG - 1
    held = (pieces[0].shape[0] - LISTS) // (2 * W)
    h_copies = [
        pltpu.make_async_copy(h_low, hraw.at[pl.ds(0, halo_h)], sems.at[0]),
        pltpu.make_async_copy(h_high, hraw.at[pl.ds(halo_h + blocks, halo_h)], sems.at[1]),
    ]
    v_copies = [
        pltpu.make_async_copy(v_low, vext.at[pl.ds(0, halo_v * W)], sems.at[2]),
        pltpu.make_async_copy(v_mid, vext.at[pl.ds(halo_v * W, blocks * W)], sems.at[3]),
        pltpu.make_async_copy(v_high, vext.at[pl.ds((halo_v + blocks) * W, halo_v * W)], sems.at[4]),
    ]

    def each_piece(act):
        for i, piece in enumerate(pieces):
            @pl.when(owners[i] >= 0)
            def _():
                for k in range(held):
                    act(pltpu.make_async_copy(
                        piece.at[pl.ds(k * 2 * W, 2 * W)],
                        hraw.at[halo_h + owners[i] * held + k],
                        psems.at[i, k],
                    ))

    each_piece(lambda copy: copy.start())
    for copy in h_copies + v_copies:
        copy.start()
    each_piece(lambda copy: copy.wait())
    for copy in h_copies:
        copy.wait()
    rows = lax.broadcasted_iota(jnp.int32, (W, W), 0)
    cols = lax.broadcasted_iota(jnp.int32, (W, W), 1)
    upper = jnp.where(rows <= cols, 1.0, 0.0).astype(jnp.bfloat16)

    def build(j, carry):
        coupling = hraw[j, W:]
        lower_band = coupling * upper
        hcat[j, :, 0:W] = lower_band
        hcat[j, :, W : 2 * W] = hraw[j, :W]
        hcat[j, :, 2 * W : 3 * W] = coupling - lower_band
        return carry

    lax.fori_loop(0, blocks + 2 * halo_h, build, 0, unroll=2)
    for copy in v_copies:
        copy.wait()

    def rows_of(j, count=1):
        return pl.ds(pl.multiple_of(j * W, W), count * W)

    def band(source, j, row):
        return jnp.dot(hcat[j], source[rows_of(row, 3), :], preferred_element_type=jnp.float32)

    def first(j, carry):
        value = band(vext, j, j)
        cheb_1[rows_of(j), :] = value.astype(jnp.bfloat16)
        total[rows_of(j), :] = value
        return carry

    lax.fori_loop(0, blocks + 4, first, 0, unroll=2)

    def second(j, carry):
        begin = vext[rows_of(j + 2), :].astype(jnp.float32)
        value = 2.0 * band(cheb_1, j + 1, j) - begin
        cheb_2[rows_of(j), :] = value.astype(jnp.bfloat16)
        total[rows_of(j + 1), :] = (
            coef[0] * begin + (coef[1] - coef[3]) * total[rows_of(j + 1), :] + coef[2] * value
        )
        return carry

    lax.fori_loop(0, blocks + 2, second, 0, unroll=2)

    def store(j):
        return pltpu.make_async_copy(kern.at[j], out.at[j], osems.at[j])

    def third(j, carry):
        for half in range(KB // W):
            i = j * (KB // W) + half
            value = total[rows_of(i + 2), :] + (2.0 * coef[3]) * band(cheb_2, i + 2, i)
            kern[j, :, half * W : (half + 1) * W] = value.astype(jnp.bfloat16).T
        store(j).start()
        return carry

    lax.fori_loop(0, blocks // (KB // W), third, 0)
    for j in range(blocks // (KB // W)):
        store(j).wait()


def chebyshev(coefficients, owners, v_low, v_mid, v_high, h_low, h_high, pieces):
    blocks = v_mid.shape[0] // W
    cols = v_mid.shape[1]
    ext = blocks + 2 * (DEG - 1)
    flops = 2 * W * 3 * W * cols * (3 * blocks + 6)
    result = (blocks * W // KB, cols, KB)
    held = (pieces[0].shape[0] - LISTS) // (2 * W)
    return pl.pallas_call(
        functools.partial(cheb_kernel, blocks),
        out_shape=jax.ShapeDtypeStruct(result, jnp.bfloat16),
        in_specs=[SMEM] * 2 + [HBM] * (5 + len(pieces)),
        out_specs=HBM,
        scratch_shapes=[
            pltpu.VMEM(((blocks + 2 * DEG) * W, cols), jnp.bfloat16),
            pltpu.VMEM((ext, 2 * W, W), jnp.bfloat16),
            pltpu.VMEM((ext, W, 3 * W), jnp.bfloat16),
            pltpu.VMEM((ext * W, cols), jnp.bfloat16),
            pltpu.VMEM(((blocks + 2) * W, cols), jnp.bfloat16),
            pltpu.VMEM((ext * W, cols), jnp.float32),
            pltpu.VMEM(result, jnp.bfloat16),
            pltpu.SemaphoreType.DMA((5,)),
            pltpu.SemaphoreType.DMA((len(pieces), held)),
            pltpu.SemaphoreType.DMA((result[0],)),
        ],
        compiler_params=pltpu.CompilerParams(vmem_limit_bytes=62 * MIB),
        cost_estimate=pl.CostEstimate(flops=flops, bytes_accessed=16 * MIB, transcendentals=0),
        name="chebyshev",
    )(coefficients, owners, v_low, v_mid, v_high, h_low, h_high, *pieces)


def entry_loads(order, basis, pair, sems):
    def load(p):
        return pltpu.make_async_copy(basis.at[order[p]], pair.at[p], sems.at[p])

    def start(p, carry):
        load(p).start()
        return carry

    return load, start


def by_twos(first, last, load, body):
    def step(i, carry):
        p = first + 2 * i
        q = jnp.minimum(p + 1, last - 1)
        load(p).wait()

        @pl.when(q > p)
        def _():
            load(q).wait()

        body(i, p, q)
        return carry

    lax.fori_loop(0, (last - first + 1) // 2, step, 0)


def sent_rows(slots, tiles):
    return slots + tiles + -(slots + tiles) % 8


def project_kernel(blocks, plan, order, kernel_t, basis, core, rows, kern, pair, ksems, bsems):
    slots = pair.shape[0]
    load, start = entry_loads(order, basis, pair, bsems)

    def fetch(b):
        return pltpu.make_async_copy(kernel_t.at[b], kern.at[b], ksems.at[b])

    def begin(b, carry):
        first, last = plan[slots + b], plan[slots + b + 1]

        @pl.when(first < last)
        def _():
            fetch(b).start()

        return lax.fori_loop(first, last, start, carry)

    lax.fori_loop(0, blocks, begin, 0)
    rows[...] = jnp.zeros_like(rows)
    rows[slots : slots + core.shape[0]] = core[...]

    def step(b, carry):
        first, last = plan[slots + b], plan[slots + b + 1]

        @pl.when(first < last)
        def _():
            fetch(b).wait()

        def body(i, p, q):
            both = jnp.concatenate([pair[p, 0], pair[q, 0]], axis=1)
            projected = jnp.dot(kern[b], both, preferred_element_type=jnp.float32)
            other = jnp.concatenate([pair[p, 1], pair[q, 1]], axis=1).astype(jnp.float32)
            value = jnp.sum(projected * other, axis=0, keepdims=True) * (1.0 / KB)
            rows[pl.ds(order[p], 1), :] = value[:, :P_SIZE]
            rows[pl.ds(order[q], 1), :] = value[:, P_SIZE:]

        by_twos(first, last, load, body)
        return carry

    lax.fori_loop(0, blocks, step, 0)


def project(plan, order, kernel_t, basis, core):
    slots = basis.shape[0]
    sent = sent_rows(slots, core.shape[0])
    blocks = kernel_t.shape[0]
    return pl.pallas_call(
        functools.partial(project_kernel, blocks),
        out_shape=jax.ShapeDtypeStruct((sent, P_SIZE), jnp.float32),
        in_specs=[SMEM, SMEM, HBM, HBM, VMEM],
        out_specs=VMEM,
        scratch_shapes=[
            pltpu.VMEM(kernel_t.shape, jnp.bfloat16),
            pltpu.VMEM(basis.shape, jnp.bfloat16),
            pltpu.SemaphoreType.DMA((blocks,)),
            pltpu.SemaphoreType.DMA((slots,)),
        ],
        compiler_params=pltpu.CompilerParams(vmem_limit_bytes=62 * MIB),
        name="project",
    )(plan, order, kernel_t, basis, core)


def update_kernel(
    blocks, tiles, plan, order, tile_of, contributions, collect, basis,
    density_out, update_out, pair, density, potential, acc, stage, sems, osems,
):
    slots = pair.shape[0]
    live = plan[slots + blocks]
    me = plan[slots + blocks + 1]
    load, start = entry_loads(order, basis, pair, sems)
    lax.fori_loop(0, live, start, 0)
    density[...] = jnp.dot(
        collect[...],
        contributions[...],
        preferred_element_type=jnp.float32,
        precision=lax.Precision.HIGHEST,
    )
    for t in range(tiles):
        density_out[pl.ds(t, 1), :] = density[pl.ds(me * tiles + t, 1), :]
    positive = jnp.maximum(density[...], 0.1)
    root = jnp.exp(jnp.log(positive) * (1.0 / 3.0))
    root = root - (root - positive / (root * root)) * (1.0 / 3.0)
    potential[...] = -exchange_factor * root
    scale = 1.0 / math.sqrt(P_SIZE)

    def store(b):
        rows = pl.ds(pl.multiple_of(b * KB, KB), KB)
        return pltpu.make_async_copy(stage.at[b], update_out.at[rows], osems.at[b])

    def step(b, carry):
        first, last = plan[slots + b], plan[slots + b + 1]

        @pl.when(first == last)
        def _():
            stage[b] = jnp.zeros(stage.shape[1:], jnp.bfloat16)

        def body(i, p, q):
            weight_p = potential[pl.ds(tile_of[order[p]], 1), :]
            weight_q = potential[pl.ds(tile_of[order[q]], 1), :] * (q - p).astype(jnp.float32)
            weighted = jnp.concatenate(
                [
                    (pair[p, 1].astype(jnp.float32) * weight_p).astype(jnp.bfloat16),
                    (pair[q, 1].astype(jnp.float32) * weight_q).astype(jnp.bfloat16),
                ],
                axis=1,
            )
            block = lax.dot_general(
                jnp.concatenate([pair[p, 0], pair[q, 0]], axis=1),
                weighted,
                (((1,), (1,)), ((), ())),
                preferred_element_type=jnp.float32,
            )

            @pl.when(last - first <= 2)
            def _():
                stage[b] = (block * scale).astype(jnp.bfloat16)

            @pl.when((last - first > 2) & (i == 0))
            def _():
                acc[...] = block

            @pl.when(i > 0)
            def _():
                acc[...] += block

        by_twos(first, last, load, body)

        @pl.when(last - first > 2)
        def _():
            stage[b] = (acc[...] * scale).astype(jnp.bfloat16)

        store(b).start()
        return carry

    lax.fori_loop(0, blocks, step, 0)
    for b in range(blocks):
        store(b).wait()


def update(plan, order, tile_of, contributions, collect, basis, tiles, blocks, cols):
    slots = basis.shape[0]
    all_tiles = (collect.shape[0], P_SIZE)
    return pl.pallas_call(
        functools.partial(update_kernel, blocks, tiles),
        out_shape=(
            jax.ShapeDtypeStruct((tiles, P_SIZE), jnp.float32),
            jax.ShapeDtypeStruct((blocks * KB, cols), jnp.bfloat16),
        ),
        in_specs=[SMEM] * 3 + [VMEM] * 2 + [HBM],
        out_specs=(VMEM, HBM),
        scratch_shapes=[
            pltpu.VMEM(basis.shape, jnp.bfloat16),
            pltpu.VMEM(all_tiles, jnp.float32),
            pltpu.VMEM(all_tiles, jnp.float32),
            pltpu.VMEM((KB, cols), jnp.float32),
            pltpu.VMEM((blocks, KB, cols), jnp.bfloat16),
            pltpu.SemaphoreType.DMA((slots,)),
            pltpu.SemaphoreType.DMA((blocks,)),
        ],
        compiler_params=pltpu.CompilerParams(vmem_limit_bytes=62 * MIB),
        name="update",
    )(plan, order, tile_of, contributions, collect, basis)


def shift(block, axis, step):
    count = lax.axis_size(axis)
    pairs = [(i, i + step) for i in range(count) if 0 <= i + step < count]
    return lax.ppermute(block, axis, pairs)


def make_plan(lists, me, entries, tiles, col_count, blocks):
    slots = col_count * CAP
    sent = sent_rows(slots, tiles)
    lists = lists[:, : 2 * entries + tiles].astype(jnp.int32)
    peers, named, counts = lists[:, :entries], lists[:, entries : 2 * entries], lists[:, 2 * entries :]
    index = jnp.arange(entries, dtype=jnp.int32)
    home = jnp.arange(col_count, dtype=jnp.int32)[:, None]
    earlier = (peers[:, :, None] == peers[:, None, :]) & (index[None, :] < index[:, None])
    rank = jnp.sum(earlier.astype(jnp.int32), axis=2)
    live = (index % SLOTS)[None, :] < jnp.repeat(counts, SLOTS, axis=1)
    row = jnp.where(live, peers * sent + home * CAP + rank, -1).reshape(col_count, tiles, SLOTS)
    core = (home * sent + slots + jnp.arange(tiles, dtype=jnp.int32))[:, :, None]
    row = jnp.concatenate([row, core], axis=2).reshape(col_count * tiles, SLOTS + 1, 1)
    picked = row == jnp.arange(col_count * sent, dtype=jnp.int32)
    collect = jnp.sum(picked.astype(jnp.float32), axis=1)
    hit = (
        (peers == me)[:, None, :]
        & (rank[:, None, :] == jnp.arange(CAP, dtype=jnp.int32)[None, :, None])
        & live[:, None, :]
    )
    wanted = (jnp.sum(jnp.where(hit, named[:, None, :] + 1, 0), axis=2) - 1).reshape(slots)
    tile = home * tiles + index[None, :] // SLOTS
    tile_of = jnp.sum(jnp.where(hit, tile[:, None, :], 0), axis=2).reshape(slots)
    key = jnp.where(wanted < 0, blocks, wanted)
    place = jnp.arange(slots, dtype=jnp.int32)
    before = (key[None, :] < key[:, None]) | (
        (key[None, :] == key[:, None]) & (place[None, :] < place[:, None])
    )
    spot = jnp.sum(before.astype(jnp.int32), axis=1)
    order = jnp.sum(jnp.where(spot[None, :] == place[:, None], place[None, :], 0), axis=1)
    starts = jnp.sum(
        (key[None, :] < jnp.arange(blocks + 1, dtype=jnp.int32)[:, None]).astype(jnp.int32), axis=1
    )
    plan = jnp.concatenate([wanted, starts, me[None]]).astype(jnp.int32)
    return collect, plan, order.astype(jnp.int32), tile_of.astype(jnp.int32)


def shards(
    start_columns,
    hamiltonian,
    band_pattern,
    coefficients,
    tile_peer,
    tile_block,
    tile_count,
    basis_values,
    core_density,
):
    col_count = lax.axis_size("col")
    slots = col_count * CAP
    entries = tile_peer.shape[0]
    tiles = core_density.shape[0]
    cols = start_columns.shape[1]
    blocks = start_columns.shape[0] // KB
    peers = tile_peer[:, 0]

    own = own_piece(peers, tile_block, tile_count, band_pattern, hamiltonian.reshape(-1, W))
    pieces, owners, steps = gather_pieces(own)
    sent = after(pack(peers, basis_values, slots), *steps[-1], *steps[-2][2:])
    basis = lax.all_to_all(
        sent.reshape((col_count, CAP) + sent.shape[1:]), "col", split_axis=0, concat_axis=0, tiled=True
    ).reshape(sent.shape)

    v_low = shift(start_columns[-DEG * W :], "row", 1)
    v_high = shift(start_columns[: DEG * W], "row", -1)

    first, last, lists = edge_blocks(owners, pieces, col_count, DEG - 1)
    h_low = shift(last, "row", 1)
    h_high = shift(first, "row", -1)
    kernel_t = chebyshev(
        coefficients, owners, v_low, start_columns, v_high, h_low, h_high, pieces
    )
    me = lax.axis_index("col").astype(jnp.int32)
    collect, plan, order, tile_of = make_plan(lists[:, 0], me, entries, tiles, col_count, blocks)
    partial = project(plan, order, kernel_t, basis, core_density)
    contributions = lax.all_gather(partial, "col", axis=0, tiled=True)
    return update(
        plan, order, tile_of, contributions, collect, basis, tiles, blocks, cols
    )


def solution(mesh):
    return jax.shard_map(
        shards,
        mesh=mesh,
        in_specs=(
            P("row", "col"),
            P(("row", "col"), None, None, None),
            P(("row", "col")),
            P(),
            P(("row", "col"), None),
            P(("row", "col")),
            P(("row", "col")),
            P(("row", "col"), None, None, None),
            P(("row", "col"), None),
        ),
        out_specs=(P(("row", "col"), None), P("row", "col")),
        check_vma=False,
    )
```

```python
import functools
import math

import jax
import jax.numpy as jnp
from jax import lax
from jax.experimental import pallas as pl
from jax.experimental.pallas import tpu as pltpu
from jax.sharding import PartitionSpec as P

W = 256
KB = 512
DEG = 3
SLOTS = 4
CAP = 2
P_SIZE = 128
MIB = 1 << 20
LISTS = 16

exchange_factor = (3.0 / math.pi) ** (1.0 / 3.0)
HBM = pl.BlockSpec(memory_space=pltpu.HBM)
SMEM = pl.BlockSpec(memory_space=pltpu.SMEM)
VMEM = pl.BlockSpec(memory_space=pltpu.VMEM)


def partner(me, j, count):
    if count & (count - 1) == 0:
        return me ^ abs(j)
    return (me + j) % count


def piece_kernel(peers, named, counts, pattern, ham, piece, blocks, sems):
    rows = ham.shape[0]
    load = pltpu.make_async_copy(ham, blocks.at[pl.ds(0, rows)], sems.at[0])
    load.start()
    lane = lax.broadcasted_iota(jnp.int32, (LISTS, W), 1)
    lists = jnp.zeros((LISTS, W), jnp.int32)
    at = 0
    for ref in (peers, named, counts):
        for i in range(ref.shape[0]):
            lists = jnp.where(lane == at, ref[i], lists)
            at += 1
    blocks[rows:] = lists.astype(jnp.float32).astype(jnp.bfloat16)
    load.wait()
    for i in range(rows // (2 * W)):
        coupling = slice((2 * i + 1) * W, (2 * i + 2) * W)
        blocks[coupling] = blocks[coupling] * pattern[i].astype(jnp.bfloat16)
    store = pltpu.make_async_copy(blocks, piece, sems.at[1])
    store.start()
    store.wait()


def own_piece(peers, named, counts, pattern, ham):
    piece = (ham.shape[0] + LISTS, W)
    return pl.pallas_call(
        piece_kernel,
        out_shape=jax.ShapeDtypeStruct(piece, ham.dtype),
        in_specs=[SMEM] * 4 + [HBM],
        out_specs=HBM,
        scratch_shapes=[pltpu.VMEM(piece, ham.dtype), pltpu.SemaphoreType.DMA((2,))],
        compiler_params=pltpu.CompilerParams(vmem_limit_bytes=62 * MIB),
        name="own_piece",
    )(peers, named, counts, pattern, ham)


def pack_kernel(entries, slots, peers, basis, sent, held, count, in_sems, out_sems):
    def fetch(e):
        return pltpu.make_async_copy(basis.at[e], held.at[e], in_sems.at[e])

    def send(e, s):
        return pltpu.make_async_copy(held.at[e], sent.at[s], out_sems.at[s])

    for e in range(entries):
        fetch(e).start()
    for c in range(slots // CAP):
        count[c] = 0
    for e in range(entries):
        p = peers[e]
        k = count[p]
        count[p] = k + 1
        fetch(e).wait()
        send(e, p * CAP + k).start()
    for c in range(slots // CAP):
        for k in range(CAP):
            @pl.when(count[c] <= k)
            def _():
                send(0, c * CAP + k).start()
    for s in range(slots):
        send(0, s).wait()


def pack(peers, basis, slots):
    entries = basis.shape[0]
    return pl.pallas_call(
        functools.partial(pack_kernel, entries, slots),
        out_shape=jax.ShapeDtypeStruct((slots,) + basis.shape[1:], basis.dtype),
        in_specs=[SMEM, HBM],
        out_specs=HBM,
        scratch_shapes=[
            pltpu.VMEM(basis.shape, basis.dtype),
            pltpu.SMEM((slots // CAP,), jnp.int32),
            pltpu.SemaphoreType.DMA((entries,)),
            pltpu.SemaphoreType.DMA((slots,)),
        ],
        compiler_params=pltpu.CompilerParams(vmem_limit_bytes=62 * MIB),
        name="pack",
    )(peers, basis)


def after(block, *others):
    return pl.pallas_call(
        lambda *refs: None,
        out_shape=jax.ShapeDtypeStruct(block.shape, block.dtype),
        in_specs=[HBM] * (1 + len(others)),
        out_specs=HBM,
        input_output_aliases={0: 0},
        compiler_params=pltpu.CompilerParams(vmem_limit_bytes=62 * MIB),
        name="after",
    )(block, *others)


def gather_pieces(own):
    count = lax.axis_size("col")
    straight = count & (count - 1) != 0
    inner = count if straight else max(count // 4, 1)

    def send(block, j):
        pairs = [(c, partner(c, j, count)) for c in range(count)]
        return lax.ppermute(block, "col", pairs)

    pieces = [own] + [None] * (count - 1)
    first = [j for j in range(1, count) if j % inner == 0 or j < inner]
    for j in sorted(first, reverse=True):
        pieces[j] = send(own, j)
    for j in range(count - 1, 0, -1):
        if pieces[j] is None:
            pieces[j] = send(pieces[j - j % inner], j % inner)
    return pieces, [pieces[j] for j in first]


def edge_kernel(col_count, depth, owners, *refs):
    pieces, (first, last, lists, sems, list_sems) = refs[:-5], refs[-5:]
    rows = pieces[0].shape[0] - LISTS
    held = rows // (2 * W)
    total = col_count * held

    def each(act):
        for i, piece in enumerate(pieces):
            for g in range(depth):
                for out, block, sem in ((first, g, 0), (last, total - depth + g, 1)):
                    source = piece.at[pl.ds(block % held * 2 * W, 2 * W)]
                    copy = pltpu.make_async_copy(source, out.at[g], sems.at[sem, g])

                    @pl.when(owners[i] == block // held)
                    def _():
                        act(copy)

            @pl.when(owners[i] >= 0)
            def _():
                act(pltpu.make_async_copy(
                    piece.at[pl.ds(rows, LISTS)], lists.at[owners[i]], list_sems.at[i]
                ))

    each(lambda copy: copy.start())
    each(lambda copy: copy.wait())


def edge_blocks(owners, pieces, col_count, depth):
    shape = jax.ShapeDtypeStruct((depth, 2 * W, W), pieces[0].dtype)
    return pl.pallas_call(
        functools.partial(edge_kernel, col_count, depth),
        out_shape=(shape, shape, jax.ShapeDtypeStruct((col_count, LISTS, W), pieces[0].dtype)),
        in_specs=[SMEM] + [HBM] * len(pieces),
        out_specs=(VMEM, VMEM, VMEM),
        scratch_shapes=[
            pltpu.SemaphoreType.DMA((2, depth)),
            pltpu.SemaphoreType.DMA((len(pieces),)),
        ],
        name="edge_blocks",
    )(owners, *pieces)


def cheb_kernel(blocks, coef, owners, v_low, v_mid, v_high, h_low, h_high, *refs):
    *pieces, out, vext, hraw, hcat, cheb_1, cheb_2, total, kern, sems, psems, osems = refs
    halo_v = DEG
    halo_h = DEG - 1
    held = (pieces[0].shape[0] - LISTS) // (2 * W)
    h_copies = [
        pltpu.make_async_copy(h_low, hraw.at[pl.ds(0, halo_h)], sems.at[0]),
        pltpu.make_async_copy(h_high, hraw.at[pl.ds(halo_h + blocks, halo_h)], sems.at[1]),
    ]
    v_copies = [
        pltpu.make_async_copy(v_low, vext.at[pl.ds(0, halo_v * W)], sems.at[2]),
        pltpu.make_async_copy(v_mid, vext.at[pl.ds(halo_v * W, blocks * W)], sems.at[3]),
        pltpu.make_async_copy(v_high, vext.at[pl.ds((halo_v + blocks) * W, halo_v * W)], sems.at[4]),
    ]

    def each_piece(act):
        for i, piece in enumerate(pieces):
            @pl.when(owners[i] >= 0)
            def _():
                for k in range(held):
                    act(pltpu.make_async_copy(
                        piece.at[pl.ds(k * 2 * W, 2 * W)],
                        hraw.at[halo_h + owners[i] * held + k],
                        psems.at[i, k],
                    ))

    each_piece(lambda copy: copy.start())
    for copy in h_copies + v_copies:
        copy.start()
    each_piece(lambda copy: copy.wait())
    for copy in h_copies:
        copy.wait()
    rows = lax.broadcasted_iota(jnp.int32, (W, W), 0)
    cols = lax.broadcasted_iota(jnp.int32, (W, W), 1)
    upper = jnp.where(rows <= cols, 1.0, 0.0).astype(jnp.bfloat16)

    def build(j, carry):
        coupling = hraw[j, W:]
        lower_band = coupling * upper
        hcat[j, :, 0:W] = lower_band
        hcat[j, :, W : 2 * W] = hraw[j, :W]
        hcat[j, :, 2 * W : 3 * W] = coupling - lower_band
        return carry

    lax.fori_loop(0, blocks + 2 * halo_h, build, 0, unroll=2)
    for copy in v_copies:
        copy.wait()

    def rows_of(j, count=1):
        return pl.ds(pl.multiple_of(j * W, W), count * W)

    def band(source, j, row):
        return jnp.dot(hcat[j], source[rows_of(row, 3), :], preferred_element_type=jnp.float32)

    def first(j, carry):
        value = band(vext, j, j)
        cheb_1[rows_of(j), :] = value.astype(jnp.bfloat16)
        total[rows_of(j), :] = value
        return carry

    lax.fori_loop(0, blocks + 4, first, 0, unroll=2)

    def second(j, carry):
        begin = vext[rows_of(j + 2), :].astype(jnp.float32)
        value = 2.0 * band(cheb_1, j + 1, j) - begin
        cheb_2[rows_of(j), :] = value.astype(jnp.bfloat16)
        total[rows_of(j + 1), :] = (
            coef[0] * begin + (coef[1] - coef[3]) * total[rows_of(j + 1), :] + coef[2] * value
        )
        return carry

    lax.fori_loop(0, blocks + 2, second, 0, unroll=2)

    def store(j):
        return pltpu.make_async_copy(kern.at[j], out.at[j], osems.at[j])

    def third(j, carry):
        for half in range(KB // W):
            i = j * (KB // W) + half
            value = total[rows_of(i + 2), :] + (2.0 * coef[3]) * band(cheb_2, i + 2, i)
            kern[j, :, half * W : (half + 1) * W] = value.astype(jnp.bfloat16).T
        store(j).start()
        return carry

    lax.fori_loop(0, blocks // (KB // W), third, 0)
    for j in range(blocks // (KB // W)):
        store(j).wait()


def chebyshev(coefficients, owners, v_low, v_mid, v_high, h_low, h_high, pieces):
    blocks = v_mid.shape[0] // W
    cols = v_mid.shape[1]
    ext = blocks + 2 * (DEG - 1)
    flops = 2 * W * 3 * W * cols * (3 * blocks + 6)
    result = (blocks * W // KB, cols, KB)
    held = (pieces[0].shape[0] - LISTS) // (2 * W)
    return pl.pallas_call(
        functools.partial(cheb_kernel, blocks),
        out_shape=jax.ShapeDtypeStruct(result, jnp.bfloat16),
        in_specs=[SMEM] * 2 + [HBM] * (5 + len(pieces)),
        out_specs=HBM,
        scratch_shapes=[
            pltpu.VMEM(((blocks + 2 * DEG) * W, cols), jnp.bfloat16),
            pltpu.VMEM((ext, 2 * W, W), jnp.bfloat16),
            pltpu.VMEM((ext, W, 3 * W), jnp.bfloat16),
            pltpu.VMEM((ext * W, cols), jnp.bfloat16),
            pltpu.VMEM(((blocks + 2) * W, cols), jnp.bfloat16),
            pltpu.VMEM((ext * W, cols), jnp.float32),
            pltpu.VMEM(result, jnp.bfloat16),
            pltpu.SemaphoreType.DMA((5,)),
            pltpu.SemaphoreType.DMA((len(pieces), held)),
            pltpu.SemaphoreType.DMA((result[0],)),
        ],
        compiler_params=pltpu.CompilerParams(vmem_limit_bytes=62 * MIB),
        cost_estimate=pl.CostEstimate(flops=flops, bytes_accessed=16 * MIB, transcendentals=0),
        name="chebyshev",
    )(coefficients, owners, v_low, v_mid, v_high, h_low, h_high, *pieces)


def entry_loads(order, basis, pair, sems):
    def load(p):
        return pltpu.make_async_copy(basis.at[order[p]], pair.at[p], sems.at[p])

    def start(p, carry):
        load(p).start()
        return carry

    return load, start


def by_twos(first, last, load, body):
    def step(i, carry):
        p = first + 2 * i
        q = jnp.minimum(p + 1, last - 1)
        load(p).wait()

        @pl.when(q > p)
        def _():
            load(q).wait()

        body(i, p, q)
        return carry

    lax.fori_loop(0, (last - first + 1) // 2, step, 0)


def sent_rows(slots, tiles):
    return slots + tiles + -(slots + tiles) % 8


def project_kernel(blocks, plan, order, kernel_t, basis, core, out, kern, pair, rows, ksems, bsems):
    slots = pair.shape[0]
    load, start = entry_loads(order, basis, pair, bsems)

    def fetch(b):
        return pltpu.make_async_copy(kernel_t.at[b], kern.at[b], ksems.at[b])

    def begin(b, carry):
        first, last = plan[slots + b], plan[slots + b + 1]

        @pl.when(first < last)
        def _():
            fetch(b).start()

        return lax.fori_loop(first, last, start, carry)

    lax.fori_loop(0, blocks, begin, 0)
    rows[...] = jnp.zeros_like(rows)
    rows[slots : slots + core.shape[0]] = core[...]

    def step(b, carry):
        first, last = plan[slots + b], plan[slots + b + 1]

        @pl.when(first < last)
        def _():
            fetch(b).wait()

        def body(i, p, q):
            both = jnp.concatenate([pair[p, 0], pair[q, 0]], axis=1)
            projected = jnp.dot(kern[b], both, preferred_element_type=jnp.float32)
            other = jnp.concatenate([pair[p, 1], pair[q, 1]], axis=1).astype(jnp.float32)
            value = jnp.sum(projected * other, axis=0, keepdims=True) * (1.0 / KB)
            rows[pl.ds(order[p], 1), :] = value[:, :P_SIZE]
            rows[pl.ds(order[q], 1), :] = value[:, P_SIZE:]

        by_twos(first, last, load, body)
        return carry

    lax.fori_loop(0, blocks, step, 0)
    for c in range(out.shape[0]):
        out[c] = rows[...]


def project(plan, order, kernel_t, basis, core, col_count):
    slots = basis.shape[0]
    sent = sent_rows(slots, core.shape[0])
    blocks = kernel_t.shape[0]
    return pl.pallas_call(
        functools.partial(project_kernel, blocks),
        out_shape=jax.ShapeDtypeStruct((col_count, sent, P_SIZE), jnp.float32),
        in_specs=[SMEM, SMEM, HBM, HBM, VMEM],
        out_specs=VMEM,
        scratch_shapes=[
            pltpu.VMEM(kernel_t.shape, jnp.bfloat16),
            pltpu.VMEM(basis.shape, jnp.bfloat16),
            pltpu.VMEM((sent, P_SIZE), jnp.float32),
            pltpu.SemaphoreType.DMA((blocks,)),
            pltpu.SemaphoreType.DMA((slots,)),
        ],
        compiler_params=pltpu.CompilerParams(vmem_limit_bytes=62 * MIB),
        name="project",
    )(plan, order, kernel_t, basis, core)


def update_kernel(
    blocks, tiles, plan, order, tile_of, contributions, collect, basis,
    density_out, update_out, pair, density, potential, acc, stage, sems, osems,
):
    slots = pair.shape[0]
    live = plan[slots + blocks]
    me = plan[slots + blocks + 1]
    load, start = entry_loads(order, basis, pair, sems)
    lax.fori_loop(0, live, start, 0)
    density[...] = jnp.dot(
        collect[...],
        contributions[...],
        preferred_element_type=jnp.float32,
        precision=lax.Precision.HIGHEST,
    )
    for t in range(tiles):
        density_out[pl.ds(t, 1), :] = density[pl.ds(me * tiles + t, 1), :]
    positive = jnp.maximum(density[...], 0.1)
    root = jnp.exp(jnp.log(positive) * (1.0 / 3.0))
    root = root - (root - positive / (root * root)) * (1.0 / 3.0)
    potential[...] = -exchange_factor * root
    scale = 1.0 / math.sqrt(P_SIZE)

    def store(b):
        rows = pl.ds(pl.multiple_of(b * KB, KB), KB)
        return pltpu.make_async_copy(stage.at[b], update_out.at[rows], osems.at[b])

    def step(b, carry):
        first, last = plan[slots + b], plan[slots + b + 1]

        @pl.when(first == last)
        def _():
            stage[b] = jnp.zeros(stage.shape[1:], jnp.bfloat16)

        def body(i, p, q):
            weight_p = potential[pl.ds(tile_of[order[p]], 1), :]
            weight_q = potential[pl.ds(tile_of[order[q]], 1), :] * (q - p).astype(jnp.float32)
            weighted = jnp.concatenate(
                [
                    (pair[p, 1].astype(jnp.float32) * weight_p).astype(jnp.bfloat16),
                    (pair[q, 1].astype(jnp.float32) * weight_q).astype(jnp.bfloat16),
                ],
                axis=1,
            )
            block = lax.dot_general(
                jnp.concatenate([pair[p, 0], pair[q, 0]], axis=1),
                weighted,
                (((1,), (1,)), ((), ())),
                preferred_element_type=jnp.float32,
            )

            @pl.when(last - first <= 2)
            def _():
                stage[b] = (block * scale).astype(jnp.bfloat16)

            @pl.when((last - first > 2) & (i == 0))
            def _():
                acc[...] = block

            @pl.when(i > 0)
            def _():
                acc[...] += block

        by_twos(first, last, load, body)

        @pl.when(last - first > 2)
        def _():
            stage[b] = (acc[...] * scale).astype(jnp.bfloat16)

        store(b).start()
        return carry

    lax.fori_loop(0, blocks, step, 0)
    for b in range(blocks):
        store(b).wait()


def update(plan, order, tile_of, contributions, collect, basis, tiles, blocks, cols):
    slots = basis.shape[0]
    all_tiles = (collect.shape[0], P_SIZE)
    return pl.pallas_call(
        functools.partial(update_kernel, blocks, tiles),
        out_shape=(
            jax.ShapeDtypeStruct((tiles, P_SIZE), jnp.float32),
            jax.ShapeDtypeStruct((blocks * KB, cols), jnp.bfloat16),
        ),
        in_specs=[SMEM] * 3 + [VMEM] * 2 + [HBM],
        out_specs=(VMEM, HBM),
        scratch_shapes=[
            pltpu.VMEM(basis.shape, jnp.bfloat16),
            pltpu.VMEM(all_tiles, jnp.float32),
            pltpu.VMEM(all_tiles, jnp.float32),
            pltpu.VMEM((KB, cols), jnp.float32),
            pltpu.VMEM((blocks, KB, cols), jnp.bfloat16),
            pltpu.SemaphoreType.DMA((slots,)),
            pltpu.SemaphoreType.DMA((blocks,)),
        ],
        compiler_params=pltpu.CompilerParams(vmem_limit_bytes=62 * MIB),
        name="update",
    )(plan, order, tile_of, contributions, collect, basis)


def shift(block, axis, step):
    count = lax.axis_size(axis)
    pairs = [(i, i + step) for i in range(count) if 0 <= i + step < count]
    return lax.ppermute(block, axis, pairs)


def make_plan(lists, me, entries, tiles, col_count, blocks):
    slots = col_count * CAP
    sent = sent_rows(slots, tiles)
    lists = lists[:, : 2 * entries + tiles].astype(jnp.int32)
    peers, named, counts = lists[:, :entries], lists[:, entries : 2 * entries], lists[:, 2 * entries :]
    index = jnp.arange(entries, dtype=jnp.int32)
    home = jnp.arange(col_count, dtype=jnp.int32)[:, None]
    earlier = (peers[:, :, None] == peers[:, None, :]) & (index[None, :] < index[:, None])
    rank = jnp.sum(earlier.astype(jnp.int32), axis=2)
    live = (index % SLOTS)[None, :] < jnp.repeat(counts, SLOTS, axis=1)
    row = jnp.where(live, peers * sent + home * CAP + rank, -1).reshape(col_count, tiles, SLOTS)
    core = (home * sent + slots + jnp.arange(tiles, dtype=jnp.int32))[:, :, None]
    row = jnp.concatenate([row, core], axis=2).reshape(col_count * tiles, SLOTS + 1, 1)
    picked = row == jnp.arange(col_count * sent, dtype=jnp.int32)
    collect = jnp.sum(picked.astype(jnp.float32), axis=1)
    hit = (
        (peers == me)[:, None, :]
        & (rank[:, None, :] == jnp.arange(CAP, dtype=jnp.int32)[None, :, None])
        & live[:, None, :]
    )
    wanted = (jnp.sum(jnp.where(hit, named[:, None, :] + 1, 0), axis=2) - 1).reshape(slots)
    tile = home * tiles + index[None, :] // SLOTS
    tile_of = jnp.sum(jnp.where(hit, tile[:, None, :], 0), axis=2).reshape(slots)
    key = jnp.where(wanted < 0, blocks, wanted)
    place = jnp.arange(slots, dtype=jnp.int32)
    before = (key[None, :] < key[:, None]) | (
        (key[None, :] == key[:, None]) & (place[None, :] < place[:, None])
    )
    spot = jnp.sum(before.astype(jnp.int32), axis=1)
    order = jnp.sum(jnp.where(spot[None, :] == place[:, None], place[None, :], 0), axis=1)
    starts = jnp.sum(
        (key[None, :] < jnp.arange(blocks + 1, dtype=jnp.int32)[:, None]).astype(jnp.int32), axis=1
    )
    plan = jnp.concatenate([wanted, starts, me[None]]).astype(jnp.int32)
    return collect, plan, order.astype(jnp.int32), tile_of.astype(jnp.int32)


def shards(
    start_columns,
    hamiltonian,
    band_pattern,
    coefficients,
    tile_peer,
    tile_block,
    tile_count,
    basis_values,
    core_density,
):
    col_count = lax.axis_size("col")
    slots = col_count * CAP
    entries = tile_peer.shape[0]
    tiles = core_density.shape[0]
    cols = start_columns.shape[1]
    blocks = start_columns.shape[0] // KB
    peers = tile_peer[:, 0]
    me = lax.axis_index("col").astype(jnp.int32)

    own = own_piece(peers, tile_block, tile_count, band_pattern, hamiltonian.reshape(-1, W))
    pieces, direct = gather_pieces(own)
    owners = jnp.stack([partner(me, -j, col_count) for j in range(col_count)])
    sent = after(pack(peers, basis_values, slots), *direct)
    basis = lax.all_to_all(
        sent.reshape((col_count, CAP) + sent.shape[1:]), "col", split_axis=0, concat_axis=0, tiled=True
    ).reshape(sent.shape)

    v_low = shift(start_columns[-DEG * W :], "row", 1)
    v_high = shift(start_columns[: DEG * W], "row", -1)

    first, last, lists = edge_blocks(owners, pieces, col_count, DEG - 1)
    h_low = shift(last, "row", 1)
    h_high = shift(first, "row", -1)
    kernel_t = chebyshev(
        coefficients, owners, v_low, start_columns, v_high, h_low, h_high, pieces
    )
    collect, plan, order, tile_of = make_plan(lists[:, 0], me, entries, tiles, col_count, blocks)
    partial = project(plan, order, kernel_t, basis, core_density, col_count)
    contributions = lax.all_to_all(partial, "col", split_axis=0, concat_axis=0, tiled=True)
    contributions = contributions.reshape(-1, P_SIZE)
    return update(
        plan, order, tile_of, contributions, collect, basis, tiles, blocks, cols
    )


def solution(mesh):
    return jax.shard_map(
        shards,
        mesh=mesh,
        in_specs=(
            P("row", "col"),
            P(("row", "col"), None, None, None),
            P(("row", "col")),
            P(),
            P(("row", "col"), None),
            P(("row", "col")),
            P(("row", "col")),
            P(("row", "col"), None, None, None),
            P(("row", "col"), None),
        ),
        out_specs=(P(("row", "col"), None), P("row", "col")),
        check_vma=False,
    )
```

```python
import functools
import math

import jax
import jax.numpy as jnp
from jax import lax
from jax.experimental import pallas as pl
from jax.experimental.pallas import tpu as pltpu
from jax.sharding import PartitionSpec as P

W = 256
KB = 512
DEG = 3
SLOTS = 4
CAP = 2
P_SIZE = 128
MIB = 1 << 20
LISTS = 16

exchange_factor = (3.0 / math.pi) ** (1.0 / 3.0)
HBM = pl.BlockSpec(memory_space=pltpu.HBM)
SMEM = pl.BlockSpec(memory_space=pltpu.SMEM)
VMEM = pl.BlockSpec(memory_space=pltpu.VMEM)


def partner(me, j, count):
    if count & (count - 1) == 0:
        return me ^ abs(j)
    return (me + j) % count


def piece_kernel(peers, named, counts, pattern, ham, piece, blocks, sems):
    rows = ham.shape[0]
    load = pltpu.make_async_copy(ham, blocks.at[pl.ds(0, rows)], sems.at[0])
    load.start()
    lane = lax.broadcasted_iota(jnp.int32, (LISTS, W), 1)
    lists = jnp.zeros((LISTS, W), jnp.int32)
    at = 0
    for ref in (peers, named, counts):
        for i in range(ref.shape[0]):
            lists = jnp.where(lane == at, ref[i], lists)
            at += 1
    blocks[rows:] = lists.astype(jnp.float32).astype(jnp.bfloat16)
    load.wait()
    for i in range(rows // (2 * W)):
        coupling = slice((2 * i + 1) * W, (2 * i + 2) * W)
        blocks[coupling] = blocks[coupling] * pattern[i].astype(jnp.bfloat16)
    store = pltpu.make_async_copy(blocks, piece, sems.at[1])
    store.start()
    store.wait()


def own_piece(peers, named, counts, pattern, ham):
    piece = (ham.shape[0] + LISTS, W)
    return pl.pallas_call(
        piece_kernel,
        out_shape=jax.ShapeDtypeStruct(piece, ham.dtype),
        in_specs=[SMEM] * 4 + [HBM],
        out_specs=HBM,
        scratch_shapes=[pltpu.VMEM(piece, ham.dtype), pltpu.SemaphoreType.DMA((2,))],
        compiler_params=pltpu.CompilerParams(vmem_limit_bytes=62 * MIB),
        name="own_piece",
    )(peers, named, counts, pattern, ham)


def pack_kernel(entries, slots, peers, basis, *refs):
    (*parts, held, count, in_sems, out_sems) = refs

    def fetch(e):
        return pltpu.make_async_copy(basis.at[e], held.at[e], in_sems.at[e])

    def send(e, p, k):
        return [
            pltpu.make_async_copy(held.at[e, half], part.at[p, place], out_sems.at[p, k])
            for part, place, half in places(parts, k)
        ]

    for e in range(entries):
        fetch(e).start()
    for c in range(slots // CAP):
        count[c] = 0
    for e in range(entries):
        p = peers[e]
        rank = count[p]
        count[p] = rank + 1
        fetch(e).wait()
        for k in range(CAP):
            @pl.when(rank == k)
            def _():
                for copy in send(e, p, k):
                    copy.start()
    for c in range(slots // CAP):
        for k in range(CAP):
            @pl.when(count[c] <= k)
            def _():
                for copy in send(0, c, k):
                    copy.start()
    for c in range(slots // CAP):
        for k in range(CAP):
            pltpu.make_async_copy(basis.at[0], held.at[0], out_sems.at[c, k]).wait()


def places(parts, k):
    found = []
    for half in range(2):
        unit = 2 * k + half
        for part in parts:
            if unit < part.shape[1]:
                found.append((part, unit, half))
                break
            unit -= part.shape[1]
    return found


def pack(peers, basis, col_count):
    entries = basis.shape[0]
    slots = col_count * CAP
    last = 1
    return pl.pallas_call(
        functools.partial(pack_kernel, entries, slots),
        out_shape=tuple(
            jax.ShapeDtypeStruct((col_count, units) + basis.shape[2:], basis.dtype)
            for units in (2 * CAP - last, last)
        ),
        in_specs=[SMEM, HBM],
        out_specs=(HBM, HBM),
        scratch_shapes=[
            pltpu.VMEM(basis.shape, basis.dtype),
            pltpu.SMEM((col_count,), jnp.int32),
            pltpu.SemaphoreType.DMA((entries,)),
            pltpu.SemaphoreType.DMA((col_count, CAP)),
        ],
        compiler_params=pltpu.CompilerParams(vmem_limit_bytes=62 * MIB),
        name="pack",
    )(peers, basis)


def after(block, *others):
    return pl.pallas_call(
        lambda *refs: None,
        out_shape=jax.ShapeDtypeStruct(block.shape, block.dtype),
        in_specs=[HBM] * (1 + len(others)),
        out_specs=HBM,
        input_output_aliases={0: 0},
        compiler_params=pltpu.CompilerParams(vmem_limit_bytes=62 * MIB),
        name="after",
    )(block, *others)


def gather_pieces(own):
    count = lax.axis_size("col")
    straight = count & (count - 1) != 0
    inner = count if straight else max(count // 4, 1)

    def send(block, j):
        pairs = [(c, partner(c, j, count)) for c in range(count)]
        return lax.ppermute(block, "col", pairs)

    pieces = [own] + [None] * (count - 1)
    first = [j for j in range(1, count) if j % inner == 0 or j < inner]
    for j in sorted(first, reverse=True):
        pieces[j] = send(own, j)
    for j in range(count - 1, 0, -1):
        if pieces[j] is None:
            pieces[j] = send(pieces[j - j % inner], j % inner)
    return pieces, [pieces[j] for j in first]


def edge_kernel(col_count, depth, owners, *refs):
    pieces, (first, last, lists, sems, list_sems) = refs[:-5], refs[-5:]
    rows = pieces[0].shape[0] - LISTS
    held = rows // (2 * W)
    total = col_count * held

    def each(act):
        for i, piece in enumerate(pieces):
            for g in range(depth):
                for out, block, sem in ((first, g, 0), (last, total - depth + g, 1)):
                    source = piece.at[pl.ds(block % held * 2 * W, 2 * W)]
                    copy = pltpu.make_async_copy(source, out.at[g], sems.at[sem, g])

                    @pl.when(owners[i] == block // held)
                    def _():
                        act(copy)

            @pl.when(owners[i] >= 0)
            def _():
                act(pltpu.make_async_copy(
                    piece.at[pl.ds(rows, LISTS)], lists.at[owners[i]], list_sems.at[i]
                ))

    each(lambda copy: copy.start())
    each(lambda copy: copy.wait())


def edge_blocks(owners, pieces, col_count, depth):
    shape = jax.ShapeDtypeStruct((depth, 2 * W, W), pieces[0].dtype)
    return pl.pallas_call(
        functools.partial(edge_kernel, col_count, depth),
        out_shape=(shape, shape, jax.ShapeDtypeStruct((col_count, LISTS, W), pieces[0].dtype)),
        in_specs=[SMEM] + [HBM] * len(pieces),
        out_specs=(VMEM, VMEM, VMEM),
        scratch_shapes=[
            pltpu.SemaphoreType.DMA((2, depth)),
            pltpu.SemaphoreType.DMA((len(pieces),)),
        ],
        name="edge_blocks",
    )(owners, *pieces)


def cheb_kernel(blocks, coef, owners, v_low, v_mid, v_high, h_low, h_high, *refs):
    *pieces, out, vext, hraw, hcat, cheb_1, cheb_2, total, kern, sems, psems, osems = refs
    halo_v = DEG
    halo_h = DEG - 1
    held = (pieces[0].shape[0] - LISTS) // (2 * W)
    h_copies = [
        pltpu.make_async_copy(h_low, hraw.at[pl.ds(0, halo_h)], sems.at[0]),
        pltpu.make_async_copy(h_high, hraw.at[pl.ds(halo_h + blocks, halo_h)], sems.at[1]),
    ]
    v_copies = [
        pltpu.make_async_copy(v_low, vext.at[pl.ds(0, halo_v * W)], sems.at[2]),
        pltpu.make_async_copy(v_mid, vext.at[pl.ds(halo_v * W, blocks * W)], sems.at[3]),
        pltpu.make_async_copy(v_high, vext.at[pl.ds((halo_v + blocks) * W, halo_v * W)], sems.at[4]),
    ]

    def each_piece(act):
        for i, piece in enumerate(pieces):
            @pl.when(owners[i] >= 0)
            def _():
                for k in range(held):
                    act(pltpu.make_async_copy(
                        piece.at[pl.ds(k * 2 * W, 2 * W)],
                        hraw.at[halo_h + owners[i] * held + k],
                        psems.at[i, k],
                    ))

    each_piece(lambda copy: copy.start())
    for copy in h_copies + v_copies:
        copy.start()
    each_piece(lambda copy: copy.wait())
    for copy in h_copies:
        copy.wait()
    rows = lax.broadcasted_iota(jnp.int32, (W, W), 0)
    cols = lax.broadcasted_iota(jnp.int32, (W, W), 1)
    upper = jnp.where(rows <= cols, 1.0, 0.0).astype(jnp.bfloat16)

    def build(j, carry):
        coupling = hraw[j, W:]
        lower_band = coupling * upper
        hcat[j, :, 0:W] = lower_band
        hcat[j, :, W : 2 * W] = hraw[j, :W]
        hcat[j, :, 2 * W : 3 * W] = coupling - lower_band
        return carry

    lax.fori_loop(0, blocks + 2 * halo_h, build, 0, unroll=2)
    for copy in v_copies:
        copy.wait()

    def rows_of(j, count=1):
        return pl.ds(pl.multiple_of(j * W, W), count * W)

    def band(source, j, row):
        return jnp.dot(hcat[j], source[rows_of(row, 3), :], preferred_element_type=jnp.float32)

    def first(j, carry):
        value = band(vext, j, j)
        cheb_1[rows_of(j), :] = value.astype(jnp.bfloat16)
        total[rows_of(j), :] = value
        return carry

    lax.fori_loop(0, blocks + 4, first, 0, unroll=2)

    def second(j, carry):
        begin = vext[rows_of(j + 2), :].astype(jnp.float32)
        value = 2.0 * band(cheb_1, j + 1, j) - begin
        cheb_2[rows_of(j), :] = value.astype(jnp.bfloat16)
        total[rows_of(j + 1), :] = (
            coef[0] * begin + (coef[1] - coef[3]) * total[rows_of(j + 1), :] + coef[2] * value
        )
        return carry

    lax.fori_loop(0, blocks + 2, second, 0, unroll=2)

    def store(j):
        return pltpu.make_async_copy(kern.at[j], out.at[j], osems.at[j])

    def third(j, carry):
        for half in range(KB // W):
            i = j * (KB // W) + half
            value = total[rows_of(i + 2), :] + (2.0 * coef[3]) * band(cheb_2, i + 2, i)
            kern[j, :, half * W : (half + 1) * W] = value.astype(jnp.bfloat16).T
        store(j).start()
        return carry

    lax.fori_loop(0, blocks // (KB // W), third, 0)
    for j in range(blocks // (KB // W)):
        store(j).wait()


def chebyshev(coefficients, owners, v_low, v_mid, v_high, h_low, h_high, pieces):
    blocks = v_mid.shape[0] // W
    cols = v_mid.shape[1]
    ext = blocks + 2 * (DEG - 1)
    flops = 2 * W * 3 * W * cols * (3 * blocks + 6)
    result = (blocks * W // KB, cols, KB)
    held = (pieces[0].shape[0] - LISTS) // (2 * W)
    return pl.pallas_call(
        functools.partial(cheb_kernel, blocks),
        out_shape=jax.ShapeDtypeStruct(result, jnp.bfloat16),
        in_specs=[SMEM] * 2 + [HBM] * (5 + len(pieces)),
        out_specs=HBM,
        scratch_shapes=[
            pltpu.VMEM(((blocks + 2 * DEG) * W, cols), jnp.bfloat16),
            pltpu.VMEM((ext, 2 * W, W), jnp.bfloat16),
            pltpu.VMEM((ext, W, 3 * W), jnp.bfloat16),
            pltpu.VMEM((ext * W, cols), jnp.bfloat16),
            pltpu.VMEM(((blocks + 2) * W, cols), jnp.bfloat16),
            pltpu.VMEM((ext * W, cols), jnp.float32),
            pltpu.VMEM(result, jnp.bfloat16),
            pltpu.SemaphoreType.DMA((5,)),
            pltpu.SemaphoreType.DMA((len(pieces), held)),
            pltpu.SemaphoreType.DMA((result[0],)),
        ],
        compiler_params=pltpu.CompilerParams(vmem_limit_bytes=62 * MIB),
        cost_estimate=pl.CostEstimate(flops=flops, bytes_accessed=16 * MIB, transcendentals=0),
        name="chebyshev",
    )(coefficients, owners, v_low, v_mid, v_high, h_low, h_high, *pieces)


def entry_loads(order, parts, pair, sems):
    def load(p):
        return pltpu.make_async_copy(pair.at[p], pair.at[p], sems.at[p])

    def start(p, carry):
        n = order[p]
        for k in range(CAP):
            @pl.when(lax.rem(n, CAP) == k)
            def _():
                for part, place, half in places(parts, k):
                    pltpu.make_async_copy(
                        part.at[lax.div(n, CAP), place], pair.at[p, half], sems.at[p]
                    ).start()

        return carry

    return load, start


def by_twos(first, last, load, body):
    def step(i, carry):
        p = first + 2 * i
        q = jnp.minimum(p + 1, last - 1)
        load(p).wait()

        @pl.when(q > p)
        def _():
            load(q).wait()

        body(i, p, q)
        return carry

    lax.fori_loop(0, (last - first + 1) // 2, step, 0)


def sent_rows(slots, tiles):
    return slots + tiles + -(slots + tiles) % 8


def project_kernel(blocks, plan, order, kernel_t, core, *refs):
    *parts, out, kern, pair, rows, ksems, bsems = refs
    slots = pair.shape[0]
    load, start = entry_loads(order, parts, pair, bsems)

    def fetch(b):
        return pltpu.make_async_copy(kernel_t.at[b], kern.at[b], ksems.at[b])

    def begin(b, carry):
        first, last = plan[slots + b], plan[slots + b + 1]

        @pl.when(first < last)
        def _():
            fetch(b).start()

        return lax.fori_loop(first, last, start, carry)

    lax.fori_loop(0, blocks, begin, 0)
    rows[...] = jnp.zeros_like(rows)
    rows[slots : slots + core.shape[0]] = core[...]

    def step(b, carry):
        first, last = plan[slots + b], plan[slots + b + 1]

        @pl.when(first < last)
        def _():
            fetch(b).wait()

        def body(i, p, q):
            both = jnp.concatenate([pair[p, 0], pair[q, 0]], axis=1)
            projected = jnp.dot(kern[b], both, preferred_element_type=jnp.float32)
            other = jnp.concatenate([pair[p, 1], pair[q, 1]], axis=1).astype(jnp.float32)
            value = jnp.sum(projected * other, axis=0, keepdims=True) * (1.0 / KB)
            rows[pl.ds(order[p], 1), :] = value[:, :P_SIZE]
            rows[pl.ds(order[q], 1), :] = value[:, P_SIZE:]

        by_twos(first, last, load, body)
        return carry

    lax.fori_loop(0, blocks, step, 0)
    for c in range(out.shape[0]):
        out[c] = rows[...]


def project(plan, order, kernel_t, core, parts):
    col_count = parts[0].shape[0]
    slots = col_count * CAP
    entry = (2,) + parts[0].shape[2:]
    sent = sent_rows(slots, core.shape[0])
    blocks = kernel_t.shape[0]
    return pl.pallas_call(
        functools.partial(project_kernel, blocks),
        out_shape=jax.ShapeDtypeStruct((col_count, sent, P_SIZE), jnp.float32),
        in_specs=[SMEM, SMEM, HBM, VMEM] + [HBM] * len(parts),
        out_specs=VMEM,
        scratch_shapes=[
            pltpu.VMEM(kernel_t.shape, jnp.bfloat16),
            pltpu.VMEM((slots,) + entry, jnp.bfloat16),
            pltpu.VMEM((sent, P_SIZE), jnp.float32),
            pltpu.SemaphoreType.DMA((blocks,)),
            pltpu.SemaphoreType.DMA((slots,)),
        ],
        compiler_params=pltpu.CompilerParams(vmem_limit_bytes=62 * MIB),
        name="project",
    )(plan, order, kernel_t, core, *parts)


def update_kernel(
    blocks, tiles, plan, order, tile_of, contributions, collect, *refs
):
    *parts, density_out, update_out, pair, density, potential, acc, stage, sems, osems = refs
    slots = pair.shape[0]
    live = plan[slots + blocks]
    me = plan[slots + blocks + 1]
    load, start = entry_loads(order, parts, pair, sems)
    lax.fori_loop(0, live, start, 0)
    density[...] = jnp.dot(
        collect[...],
        contributions[...],
        preferred_element_type=jnp.float32,
        precision=lax.Precision.HIGHEST,
    )
    for t in range(tiles):
        density_out[pl.ds(t, 1), :] = density[pl.ds(me * tiles + t, 1), :]
    positive = jnp.maximum(density[...], 0.1)
    root = jnp.exp(jnp.log(positive) * (1.0 / 3.0))
    root = root - (root - positive / (root * root)) * (1.0 / 3.0)
    potential[...] = -exchange_factor * root
    scale = 1.0 / math.sqrt(P_SIZE)

    def store(b):
        rows = pl.ds(pl.multiple_of(b * KB, KB), KB)
        return pltpu.make_async_copy(stage.at[b], update_out.at[rows], osems.at[b])

    def step(b, carry):
        first, last = plan[slots + b], plan[slots + b + 1]

        @pl.when(first == last)
        def _():
            stage[b] = jnp.zeros(stage.shape[1:], jnp.bfloat16)

        def body(i, p, q):
            weight_p = potential[pl.ds(tile_of[order[p]], 1), :]
            weight_q = potential[pl.ds(tile_of[order[q]], 1), :] * (q - p).astype(jnp.float32)
            weighted = jnp.concatenate(
                [
                    (pair[p, 1].astype(jnp.float32) * weight_p).astype(jnp.bfloat16),
                    (pair[q, 1].astype(jnp.float32) * weight_q).astype(jnp.bfloat16),
                ],
                axis=1,
            )
            block = lax.dot_general(
                jnp.concatenate([pair[p, 0], pair[q, 0]], axis=1),
                weighted,
                (((1,), (1,)), ((), ())),
                preferred_element_type=jnp.float32,
            )

            @pl.when(last - first <= 2)
            def _():
                stage[b] = (block * scale).astype(jnp.bfloat16)

            @pl.when((last - first > 2) & (i == 0))
            def _():
                acc[...] = block

            @pl.when(i > 0)
            def _():
                acc[...] += block

        by_twos(first, last, load, body)

        @pl.when(last - first > 2)
        def _():
            stage[b] = (acc[...] * scale).astype(jnp.bfloat16)

        store(b).start()
        return carry

    lax.fori_loop(0, blocks, step, 0)
    for b in range(blocks):
        store(b).wait()


def update(plan, order, tile_of, contributions, collect, parts, tiles, blocks, cols):
    slots = parts[0].shape[0] * CAP
    entry = (2,) + parts[0].shape[2:]
    all_tiles = (collect.shape[0], P_SIZE)
    return pl.pallas_call(
        functools.partial(update_kernel, blocks, tiles),
        out_shape=(
            jax.ShapeDtypeStruct((tiles, P_SIZE), jnp.float32),
            jax.ShapeDtypeStruct((blocks * KB, cols), jnp.bfloat16),
        ),
        in_specs=[SMEM] * 3 + [VMEM] * 2 + [HBM] * len(parts),
        out_specs=(VMEM, HBM),
        scratch_shapes=[
            pltpu.VMEM((slots,) + entry, jnp.bfloat16),
            pltpu.VMEM(all_tiles, jnp.float32),
            pltpu.VMEM(all_tiles, jnp.float32),
            pltpu.VMEM((KB, cols), jnp.float32),
            pltpu.VMEM((blocks, KB, cols), jnp.bfloat16),
            pltpu.SemaphoreType.DMA((slots,)),
            pltpu.SemaphoreType.DMA((blocks,)),
        ],
        compiler_params=pltpu.CompilerParams(vmem_limit_bytes=62 * MIB),
        name="update",
    )(plan, order, tile_of, contributions, collect, *parts)


def shift(block, axis, step):
    count = lax.axis_size(axis)
    pairs = [(i, i + step) for i in range(count) if 0 <= i + step < count]
    return lax.ppermute(block, axis, pairs)


def make_plan(lists, me, entries, tiles, col_count, blocks):
    slots = col_count * CAP
    sent = sent_rows(slots, tiles)
    lists = lists[:, : 2 * entries + tiles].astype(jnp.int32)
    peers, named, counts = lists[:, :entries], lists[:, entries : 2 * entries], lists[:, 2 * entries :]
    index = jnp.arange(entries, dtype=jnp.int32)
    home = jnp.arange(col_count, dtype=jnp.int32)[:, None]
    earlier = (peers[:, :, None] == peers[:, None, :]) & (index[None, :] < index[:, None])
    rank = jnp.sum(earlier.astype(jnp.int32), axis=2)
    live = (index % SLOTS)[None, :] < jnp.repeat(counts, SLOTS, axis=1)
    row = jnp.where(live, peers * sent + home * CAP + rank, -1).reshape(col_count, tiles, SLOTS)
    core = (home * sent + slots + jnp.arange(tiles, dtype=jnp.int32))[:, :, None]
    row = jnp.concatenate([row, core], axis=2).reshape(col_count * tiles, SLOTS + 1, 1)
    picked = row == jnp.arange(col_count * sent, dtype=jnp.int32)
    collect = jnp.sum(picked.astype(jnp.float32), axis=1)
    hit = (
        (peers == me)[:, None, :]
        & (rank[:, None, :] == jnp.arange(CAP, dtype=jnp.int32)[None, :, None])
        & live[:, None, :]
    )
    wanted = (jnp.sum(jnp.where(hit, named[:, None, :] + 1, 0), axis=2) - 1).reshape(slots)
    tile = home * tiles + index[None, :] // SLOTS
    tile_of = jnp.sum(jnp.where(hit, tile[:, None, :], 0), axis=2).reshape(slots)
    key = jnp.where(wanted < 0, blocks, wanted)
    place = jnp.arange(slots, dtype=jnp.int32)
    before = (key[None, :] < key[:, None]) | (
        (key[None, :] == key[:, None]) & (place[None, :] < place[:, None])
    )
    spot = jnp.sum(before.astype(jnp.int32), axis=1)
    order = jnp.sum(jnp.where(spot[None, :] == place[:, None], place[None, :], 0), axis=1)
    starts = jnp.sum(
        (key[None, :] < jnp.arange(blocks + 1, dtype=jnp.int32)[:, None]).astype(jnp.int32), axis=1
    )
    plan = jnp.concatenate([wanted, starts, me[None]]).astype(jnp.int32)
    return collect, plan, order.astype(jnp.int32), tile_of.astype(jnp.int32)


def shards(
    start_columns,
    hamiltonian,
    band_pattern,
    coefficients,
    tile_peer,
    tile_block,
    tile_count,
    basis_values,
    core_density,
):
    col_count = lax.axis_size("col")
    entries = tile_peer.shape[0]
    tiles = core_density.shape[0]
    cols = start_columns.shape[1]
    blocks = start_columns.shape[0] // KB
    peers = tile_peer[:, 0]
    me = lax.axis_index("col").astype(jnp.int32)

    own = own_piece(peers, tile_block, tile_count, band_pattern, hamiltonian.reshape(-1, W))
    pieces, direct = gather_pieces(own)
    owners = jnp.stack([partner(me, -j, col_count) for j in range(col_count)])
    most, last_part = pack(peers, basis_values, col_count)
    parts = [
        lax.all_to_all(part, "col", split_axis=0, concat_axis=0, tiled=True)
        for part in (after(most, *direct), after(last_part, *pieces))
    ]

    v_low = shift(start_columns[-DEG * W :], "row", 1)
    v_high = shift(start_columns[: DEG * W], "row", -1)

    first, last, lists = edge_blocks(owners, pieces, col_count, DEG - 1)
    h_low = shift(last, "row", 1)
    h_high = shift(first, "row", -1)
    kernel_t = chebyshev(
        coefficients, owners, v_low, start_columns, v_high, h_low, h_high, pieces
    )
    collect, plan, order, tile_of = make_plan(lists[:, 0], me, entries, tiles, col_count, blocks)
    partial = project(plan, order, kernel_t, core_density, parts)
    contributions = lax.all_to_all(partial, "col", split_axis=0, concat_axis=0, tiled=True)
    contributions = contributions.reshape(-1, P_SIZE)
    return update(
        plan, order, tile_of, contributions, collect, parts, tiles, blocks, cols
    )


def solution(mesh):
    return jax.shard_map(
        shards,
        mesh=mesh,
        in_specs=(
            P("row", "col"),
            P(("row", "col"), None, None, None),
            P(("row", "col")),
            P(),
            P(("row", "col"), None),
            P(("row", "col")),
            P(("row", "col")),
            P(("row", "col"), None, None, None),
            P(("row", "col"), None),
        ),
        out_specs=(P(("row", "col"), None), P("row", "col")),
        check_vma=False,
    )
```

```python
import functools
import math

import jax
import jax.numpy as jnp
from jax import lax
from jax.experimental import pallas as pl
from jax.experimental.pallas import tpu as pltpu
from jax.sharding import PartitionSpec as P

W = 256
KB = 512
DEG = 3
SLOTS = 4
CAP = 2
P_SIZE = 128
MIB = 1 << 20
LISTS = 16

exchange_factor = (3.0 / math.pi) ** (1.0 / 3.0)
HBM = pl.BlockSpec(memory_space=pltpu.HBM)
SMEM = pl.BlockSpec(memory_space=pltpu.SMEM)
VMEM = pl.BlockSpec(memory_space=pltpu.VMEM)


def partner(me, j, count):
    if count & (count - 1) == 0:
        return me ^ abs(j)
    return (me + j) % count


def piece_kernel(peers, named, counts, pattern, ham, piece, blocks, sems):
    rows = ham.shape[0]
    load = pltpu.make_async_copy(ham, blocks.at[pl.ds(0, rows)], sems.at[0])
    load.start()
    lane = lax.broadcasted_iota(jnp.int32, (LISTS, W), 1)
    lists = jnp.zeros((LISTS, W), jnp.int32)
    at = 0
    for ref in (peers, named, counts):
        for i in range(ref.shape[0]):
            lists = jnp.where(lane == at, ref[i], lists)
            at += 1
    blocks[rows:] = lists.astype(jnp.float32).astype(jnp.bfloat16)
    load.wait()
    for i in range(rows // (2 * W)):
        coupling = slice((2 * i + 1) * W, (2 * i + 2) * W)
        blocks[coupling] = blocks[coupling] * pattern[i].astype(jnp.bfloat16)
    store = pltpu.make_async_copy(blocks, piece, sems.at[1])
    store.start()
    store.wait()


def own_piece(peers, named, counts, pattern, ham):
    piece = (ham.shape[0] + LISTS, W)
    return pl.pallas_call(
        piece_kernel,
        out_shape=jax.ShapeDtypeStruct(piece, ham.dtype),
        in_specs=[SMEM] * 4 + [HBM],
        out_specs=HBM,
        scratch_shapes=[pltpu.VMEM(piece, ham.dtype), pltpu.SemaphoreType.DMA((2,))],
        compiler_params=pltpu.CompilerParams(vmem_limit_bytes=62 * MIB),
        name="own_piece",
    )(peers, named, counts, pattern, ham)


def pack_kernel(entries, slots, peers, basis, *refs):
    (*parts, held, count, in_sems, out_sems) = refs

    def fetch(e):
        return pltpu.make_async_copy(basis.at[e], held.at[e], in_sems.at[e])

    def send(e, p, k):
        return [
            pltpu.make_async_copy(held.at[e, half], part.at[p, place], out_sems.at[p, k])
            for part, place, half in places(parts, k)
        ]

    for e in range(entries):
        fetch(e).start()
    for c in range(slots // CAP):
        count[c] = 0
    for e in range(entries):
        p = peers[e]
        rank = count[p]
        count[p] = rank + 1
        fetch(e).wait()
        for k in range(CAP):
            @pl.when(rank == k)
            def _():
                for copy in send(e, p, k):
                    copy.start()
    for c in range(slots // CAP):
        for k in range(CAP):
            @pl.when(count[c] <= k)
            def _():
                for copy in send(0, c, k):
                    copy.start()
    for c in range(slots // CAP):
        for k in range(CAP):
            pltpu.make_async_copy(basis.at[0], held.at[0], out_sems.at[c, k]).wait()


def places(parts, k):
    found = []
    for half in range(2):
        unit = 2 * k + half
        for part in parts:
            if unit < part.shape[1]:
                found.append((part, unit, half))
                break
            unit -= part.shape[1]
    return found


def pack(peers, basis, col_count):
    entries = basis.shape[0]
    slots = col_count * CAP
    last = 1
    return pl.pallas_call(
        functools.partial(pack_kernel, entries, slots),
        out_shape=tuple(
            jax.ShapeDtypeStruct((col_count, units) + basis.shape[2:], basis.dtype)
            for units in (2 * CAP - last, last)
        ),
        in_specs=[SMEM, HBM],
        out_specs=(HBM, HBM),
        scratch_shapes=[
            pltpu.VMEM(basis.shape, basis.dtype),
            pltpu.SMEM((col_count,), jnp.int32),
            pltpu.SemaphoreType.DMA((entries,)),
            pltpu.SemaphoreType.DMA((col_count, CAP)),
        ],
        compiler_params=pltpu.CompilerParams(vmem_limit_bytes=62 * MIB),
        name="pack",
    )(peers, basis)


def after(block, *others):
    return pl.pallas_call(
        lambda *refs: None,
        out_shape=jax.ShapeDtypeStruct(block.shape, block.dtype),
        in_specs=[HBM] * (1 + len(others)),
        out_specs=HBM,
        input_output_aliases={0: 0},
        compiler_params=pltpu.CompilerParams(vmem_limit_bytes=62 * MIB),
        name="after",
    )(block, *others)


def gather_pieces(own):
    count = lax.axis_size("col")
    straight = count & (count - 1) != 0
    inner = count if straight else max(count // 4, 1)

    def send(block, j):
        pairs = [(c, partner(c, j, count)) for c in range(count)]
        return lax.ppermute(block, "col", pairs)

    pieces = [own] + [None] * (count - 1)
    first = [j for j in range(1, count) if j % inner == 0 or j < inner]
    for j in sorted(first, reverse=True):
        pieces[j] = send(own, j)
    for j in range(count - 1, 0, -1):
        if pieces[j] is None:
            pieces[j] = send(pieces[j - j % inner], j % inner)
    return pieces, [pieces[j] for j in first]


def edge_kernel(col_count, depth, owners, *refs):
    pieces, (first, last, lists, sems, list_sems) = refs[:-5], refs[-5:]
    rows = pieces[0].shape[0] - LISTS
    held = rows // (2 * W)
    total = col_count * held

    def each(act):
        for i, piece in enumerate(pieces):
            for g in range(depth):
                for out, block, sem in ((first, g, 0), (last, total - depth + g, 1)):
                    source = piece.at[pl.ds(block % held * 2 * W, 2 * W)]
                    copy = pltpu.make_async_copy(source, out.at[g], sems.at[sem, g])

                    @pl.when(owners[i] == block // held)
                    def _():
                        act(copy)

            @pl.when(owners[i] >= 0)
            def _():
                act(pltpu.make_async_copy(
                    piece.at[pl.ds(rows, LISTS)], lists.at[owners[i]], list_sems.at[i]
                ))

    each(lambda copy: copy.start())
    each(lambda copy: copy.wait())


def edge_blocks(owners, pieces, col_count, depth):
    shape = jax.ShapeDtypeStruct((depth, 2 * W, W), pieces[0].dtype)
    return pl.pallas_call(
        functools.partial(edge_kernel, col_count, depth),
        out_shape=(shape, shape, jax.ShapeDtypeStruct((col_count, LISTS, W), pieces[0].dtype)),
        in_specs=[SMEM] + [HBM] * len(pieces),
        out_specs=(VMEM, VMEM, VMEM),
        scratch_shapes=[
            pltpu.SemaphoreType.DMA((2, depth)),
            pltpu.SemaphoreType.DMA((len(pieces),)),
        ],
        name="edge_blocks",
    )(owners, *pieces)


def cheb_kernel(blocks, coef, owners, v_low, v_mid, v_high, h_low, h_high, *refs):
    *pieces, out, vext, hraw, hcat, cheb_1, cheb_2, total, kern, sems, psems, osems = refs
    halo_v = DEG
    halo_h = DEG - 1
    held = (pieces[0].shape[0] - LISTS) // (2 * W)
    h_copies = [
        pltpu.make_async_copy(h_low, hraw.at[pl.ds(0, halo_h)], sems.at[0]),
        pltpu.make_async_copy(h_high, hraw.at[pl.ds(halo_h + blocks, halo_h)], sems.at[1]),
    ]
    v_copies = [
        pltpu.make_async_copy(v_low, vext.at[pl.ds(0, halo_v * W)], sems.at[2]),
        pltpu.make_async_copy(v_mid, vext.at[pl.ds(halo_v * W, blocks * W)], sems.at[3]),
        pltpu.make_async_copy(v_high, vext.at[pl.ds((halo_v + blocks) * W, halo_v * W)], sems.at[4]),
    ]

    def each_piece(act):
        for i, piece in enumerate(pieces):
            @pl.when(owners[i] >= 0)
            def _():
                for k in range(held):
                    act(pltpu.make_async_copy(
                        piece.at[pl.ds(k * 2 * W, 2 * W)],
                        hraw.at[halo_h + owners[i] * held + k],
                        psems.at[i, k],
                    ))

    each_piece(lambda copy: copy.start())
    for copy in h_copies + v_copies:
        copy.start()
    each_piece(lambda copy: copy.wait())
    for copy in h_copies:
        copy.wait()
    rows = lax.broadcasted_iota(jnp.int32, (W, W), 0)
    cols = lax.broadcasted_iota(jnp.int32, (W, W), 1)
    upper = jnp.where(rows <= cols, 1.0, 0.0).astype(jnp.bfloat16)

    def build(j, carry):
        coupling = hraw[j, W:]
        lower_band = coupling * upper
        hcat[j, :, 0:W] = lower_band
        hcat[j, :, W : 2 * W] = hraw[j, :W]
        hcat[j, :, 2 * W : 3 * W] = coupling - lower_band
        return carry

    lax.fori_loop(0, blocks + 2 * halo_h, build, 0, unroll=2)
    for copy in v_copies:
        copy.wait()

    def rows_of(j, count=1):
        return pl.ds(pl.multiple_of(j * W, W), count * W)

    def band(source, j, row):
        return jnp.dot(hcat[j], source[rows_of(row, 3), :], preferred_element_type=jnp.float32)

    def first(j, carry):
        value = band(vext, j, j)
        cheb_1[rows_of(j), :] = value.astype(jnp.bfloat16)
        total[rows_of(j), :] = value
        return carry

    lax.fori_loop(0, blocks + 4, first, 0, unroll=2)

    def second(j, carry):
        begin = vext[rows_of(j + 2), :].astype(jnp.float32)
        value = 2.0 * band(cheb_1, j + 1, j) - begin
        cheb_2[rows_of(j), :] = value.astype(jnp.bfloat16)
        total[rows_of(j + 1), :] = (
            coef[0] * begin + (coef[1] - coef[3]) * total[rows_of(j + 1), :] + coef[2] * value
        )
        return carry

    lax.fori_loop(0, blocks + 2, second, 0, unroll=2)

    def store(j):
        return pltpu.make_async_copy(kern.at[j], out.at[j], osems.at[j])

    def third(j, carry):
        for half in range(KB // W):
            i = j * (KB // W) + half
            value = total[rows_of(i + 2), :] + (2.0 * coef[3]) * band(cheb_2, i + 2, i)
            kern[j, :, half * W : (half + 1) * W] = value.astype(jnp.bfloat16).T
        store(j).start()
        return carry

    lax.fori_loop(0, blocks // (KB // W), third, 0)
    for j in range(blocks // (KB // W)):
        store(j).wait()


def chebyshev(coefficients, owners, v_low, v_mid, v_high, h_low, h_high, pieces):
    blocks = v_mid.shape[0] // W
    cols = v_mid.shape[1]
    ext = blocks + 2 * (DEG - 1)
    flops = 2 * W * 3 * W * cols * (3 * blocks + 6)
    result = (blocks * W // KB, cols, KB)
    held = (pieces[0].shape[0] - LISTS) // (2 * W)
    return pl.pallas_call(
        functools.partial(cheb_kernel, blocks),
        out_shape=jax.ShapeDtypeStruct(result, jnp.bfloat16),
        in_specs=[SMEM] * 2 + [HBM] * (5 + len(pieces)),
        out_specs=HBM,
        scratch_shapes=[
            pltpu.VMEM(((blocks + 2 * DEG) * W, cols), jnp.bfloat16),
            pltpu.VMEM((ext, 2 * W, W), jnp.bfloat16),
            pltpu.VMEM((ext, W, 3 * W), jnp.bfloat16),
            pltpu.VMEM((ext * W, cols), jnp.bfloat16),
            pltpu.VMEM(((blocks + 2) * W, cols), jnp.bfloat16),
            pltpu.VMEM((ext * W, cols), jnp.float32),
            pltpu.VMEM(result, jnp.bfloat16),
            pltpu.SemaphoreType.DMA((5,)),
            pltpu.SemaphoreType.DMA((len(pieces), held)),
            pltpu.SemaphoreType.DMA((result[0],)),
        ],
        compiler_params=pltpu.CompilerParams(vmem_limit_bytes=62 * MIB),
        cost_estimate=pl.CostEstimate(flops=flops, bytes_accessed=16 * MIB, transcendentals=0),
        name="chebyshev",
    )(coefficients, owners, v_low, v_mid, v_high, h_low, h_high, *pieces)


def entry_loads(order, parts, pair, sems):
    def load(p):
        return pltpu.make_async_copy(pair.at[p], pair.at[p], sems.at[p])

    def start(p, carry):
        n = order[p]
        for k in range(CAP):
            @pl.when(lax.rem(n, CAP) == k)
            def _():
                for part, place, half in places(parts, k):
                    pltpu.make_async_copy(
                        part.at[lax.div(n, CAP), place], pair.at[p, half], sems.at[p]
                    ).start()

        return carry

    return load, start


def by_twos(first, last, load, body):
    def step(i, carry):
        p = first + 2 * i
        q = jnp.minimum(p + 1, last - 1)
        load(p).wait()

        @pl.when(q > p)
        def _():
            load(q).wait()

        body(i, p, q)
        return carry

    lax.fori_loop(0, (last - first + 1) // 2, step, 0)


def sent_rows(slots, tiles):
    return slots + tiles + -(slots + tiles) % 8


def project_kernel(blocks, plan, order, kernel_t, core, *refs):
    *parts, out, kern, pair, rows, ksems, bsems = refs
    slots = pair.shape[0]
    load, start = entry_loads(order, parts, pair, bsems)

    def fetch(b):
        return pltpu.make_async_copy(kernel_t.at[b], kern.at[b], ksems.at[b])

    def begin(b, carry):
        first, last = plan[slots + b], plan[slots + b + 1]

        @pl.when(first < last)
        def _():
            fetch(b).start()

        return lax.fori_loop(first, last, start, carry)

    lax.fori_loop(0, blocks, begin, 0)
    rows[...] = jnp.zeros_like(rows)
    rows[slots : slots + core.shape[0]] = core[...]

    def step(b, carry):
        first, last = plan[slots + b], plan[slots + b + 1]

        @pl.when(first < last)
        def _():
            fetch(b).wait()

        def body(i, p, q):
            both = jnp.concatenate([pair[p, 0], pair[q, 0]], axis=1)
            projected = jnp.dot(kern[b], both, preferred_element_type=jnp.float32)
            other = jnp.concatenate([pair[p, 1], pair[q, 1]], axis=1).astype(jnp.float32)
            value = jnp.sum(projected * other, axis=0, keepdims=True) * (1.0 / KB)
            rows[pl.ds(order[p], 1), :] = value[:, :P_SIZE]
            rows[pl.ds(order[q], 1), :] = value[:, P_SIZE:]

        by_twos(first, last, load, body)
        return carry

    lax.fori_loop(0, blocks, step, 0)
    for c in range(out.shape[0]):
        out[c] = rows[...]


def project(plan, order, kernel_t, core, parts):
    col_count = parts[0].shape[0]
    slots = col_count * CAP
    entry = (2,) + parts[0].shape[2:]
    sent = sent_rows(slots, core.shape[0])
    blocks = kernel_t.shape[0]
    return pl.pallas_call(
        functools.partial(project_kernel, blocks),
        out_shape=jax.ShapeDtypeStruct((col_count, sent, P_SIZE), jnp.float32),
        in_specs=[SMEM, SMEM, HBM, VMEM] + [HBM] * len(parts),
        out_specs=VMEM,
        scratch_shapes=[
            pltpu.VMEM(kernel_t.shape, jnp.bfloat16),
            pltpu.VMEM((slots,) + entry, jnp.bfloat16),
            pltpu.VMEM((sent, P_SIZE), jnp.float32),
            pltpu.SemaphoreType.DMA((blocks,)),
            pltpu.SemaphoreType.DMA((slots,)),
        ],
        compiler_params=pltpu.CompilerParams(vmem_limit_bytes=62 * MIB),
        name="project",
    )(plan, order, kernel_t, core, *parts)


def update_kernel(
    blocks, tiles, plan, order, tile_of, contributions, collect, *refs
):
    *parts, density_out, update_out, pair, density, potential, acc, stage, sems, osems = refs
    slots = pair.shape[0]
    live = plan[slots + blocks]
    me = plan[slots + blocks + 1]
    load, start = entry_loads(order, parts, pair, sems)
    lax.fori_loop(0, live, start, 0)
    density[...] = jnp.dot(
        collect[...],
        contributions[...],
        preferred_element_type=jnp.float32,
        precision=lax.Precision.HIGHEST,
    )
    for t in range(tiles):
        density_out[pl.ds(t, 1), :] = density[pl.ds(me * tiles + t, 1), :]
    positive = jnp.maximum(density[...], 0.1)
    root = jnp.exp(jnp.log(positive) * (1.0 / 3.0))
    root = root - (root - positive / (root * root)) * (1.0 / 3.0)
    potential[...] = -exchange_factor * root
    scale = 1.0 / math.sqrt(P_SIZE)

    def store(b):
        rows = pl.ds(pl.multiple_of(b * KB, KB), KB)
        return pltpu.make_async_copy(stage.at[b], update_out.at[rows], osems.at[b])

    def step(b, carry):
        first, last = plan[slots + b], plan[slots + b + 1]

        @pl.when(first == last)
        def _():
            stage[b] = jnp.zeros(stage.shape[1:], jnp.bfloat16)

        def body(i, p, q):
            weight_p = potential[pl.ds(tile_of[order[p]], 1), :]
            weight_q = potential[pl.ds(tile_of[order[q]], 1), :] * (q - p).astype(jnp.float32)
            weighted = jnp.concatenate(
                [
                    (pair[p, 1].astype(jnp.float32) * weight_p).astype(jnp.bfloat16),
                    (pair[q, 1].astype(jnp.float32) * weight_q).astype(jnp.bfloat16),
                ],
                axis=1,
            )
            block = lax.dot_general(
                jnp.concatenate([pair[p, 0], pair[q, 0]], axis=1),
                weighted,
                (((1,), (1,)), ((), ())),
                preferred_element_type=jnp.float32,
            )

            @pl.when(last - first <= 2)
            def _():
                stage[b] = (block * scale).astype(jnp.bfloat16)

            @pl.when((last - first > 2) & (i == 0))
            def _():
                acc[...] = block

            @pl.when(i > 0)
            def _():
                acc[...] += block

        by_twos(first, last, load, body)

        @pl.when(last - first > 2)
        def _():
            stage[b] = (acc[...] * scale).astype(jnp.bfloat16)

        store(b).start()
        return carry

    lax.fori_loop(0, blocks, step, 0)
    for b in range(blocks):
        store(b).wait()


def update(plan, order, tile_of, contributions, collect, parts, tiles, blocks, cols):
    slots = parts[0].shape[0] * CAP
    entry = (2,) + parts[0].shape[2:]
    all_tiles = (collect.shape[0], P_SIZE)
    return pl.pallas_call(
        functools.partial(update_kernel, blocks, tiles),
        out_shape=(
            jax.ShapeDtypeStruct((tiles, P_SIZE), jnp.float32),
            jax.ShapeDtypeStruct((blocks * KB, cols), jnp.bfloat16),
        ),
        in_specs=[SMEM] * 3 + [VMEM] * 2 + [HBM] * len(parts),
        out_specs=(VMEM, HBM),
        scratch_shapes=[
            pltpu.VMEM((slots,) + entry, jnp.bfloat16),
            pltpu.VMEM(all_tiles, jnp.float32),
            pltpu.VMEM(all_tiles, jnp.float32),
            pltpu.VMEM((KB, cols), jnp.float32),
            pltpu.VMEM((blocks, KB, cols), jnp.bfloat16),
            pltpu.SemaphoreType.DMA((slots,)),
            pltpu.SemaphoreType.DMA((blocks,)),
        ],
        compiler_params=pltpu.CompilerParams(vmem_limit_bytes=62 * MIB),
        name="update",
    )(plan, order, tile_of, contributions, collect, *parts)


def shift(block, axis, step):
    count = lax.axis_size(axis)
    pairs = [(i, i + step) for i in range(count) if 0 <= i + step < count]
    return lax.ppermute(block, axis, pairs)


def make_plan(lists, me, entries, tiles, col_count, blocks):
    slots = col_count * CAP
    sent = sent_rows(slots, tiles)
    lists = lists[:, : 2 * entries + tiles].astype(jnp.int32)
    peers, named, counts = lists[:, :entries], lists[:, entries : 2 * entries], lists[:, 2 * entries :]
    index = jnp.arange(entries, dtype=jnp.int32)
    home = jnp.arange(col_count, dtype=jnp.int32)[:, None]
    earlier = (peers[:, :, None] == peers[:, None, :]) & (index[None, :] < index[:, None])
    rank = jnp.sum(earlier.astype(jnp.int32), axis=2)
    live = (index % SLOTS)[None, :] < jnp.repeat(counts, SLOTS, axis=1)
    row = jnp.where(live, peers * sent + home * CAP + rank, -1).reshape(col_count, tiles, SLOTS)
    core = (home * sent + slots + jnp.arange(tiles, dtype=jnp.int32))[:, :, None]
    row = jnp.concatenate([row, core], axis=2).reshape(col_count * tiles, SLOTS + 1, 1)
    picked = row == jnp.arange(col_count * sent, dtype=jnp.int32)
    collect = jnp.sum(picked.astype(jnp.float32), axis=1)
    hit = (
        (peers == me)[:, None, :]
        & (rank[:, None, :] == jnp.arange(CAP, dtype=jnp.int32)[None, :, None])
        & live[:, None, :]
    )
    wanted = (jnp.sum(jnp.where(hit, named[:, None, :] + 1, 0), axis=2) - 1).reshape(slots)
    tile = home * tiles + index[None, :] // SLOTS
    tile_of = jnp.sum(jnp.where(hit, tile[:, None, :], 0), axis=2).reshape(slots)
    key = jnp.where(wanted < 0, blocks, wanted)
    place = jnp.arange(slots, dtype=jnp.int32)
    before = (key[None, :] < key[:, None]) | (
        (key[None, :] == key[:, None]) & (place[None, :] < place[:, None])
    )
    spot = jnp.sum(before.astype(jnp.int32), axis=1)
    order = jnp.sum(jnp.where(spot[None, :] == place[:, None], place[None, :], 0), axis=1)
    starts = jnp.sum(
        (key[None, :] < jnp.arange(blocks + 1, dtype=jnp.int32)[:, None]).astype(jnp.int32), axis=1
    )
    plan = jnp.concatenate([wanted, starts, me[None]]).astype(jnp.int32)
    return collect, plan, order.astype(jnp.int32), tile_of.astype(jnp.int32)


def shards(
    start_columns,
    hamiltonian,
    band_pattern,
    coefficients,
    tile_peer,
    tile_block,
    tile_count,
    basis_values,
    core_density,
):
    col_count = lax.axis_size("col")
    entries = tile_peer.shape[0]
    tiles = core_density.shape[0]
    cols = start_columns.shape[1]
    blocks = start_columns.shape[0] // KB
    peers = tile_peer[:, 0]
    me = lax.axis_index("col").astype(jnp.int32)

    own = own_piece(peers, tile_block, tile_count, band_pattern, hamiltonian.reshape(-1, W))
    pieces, direct = gather_pieces(own)
    owners = jnp.stack([partner(me, -j, col_count) for j in range(col_count)])
    most, last_part = pack(peers, basis_values, col_count)

    def exchange(part, *awaited):
        return lax.all_to_all(after(part, *awaited), "col", split_axis=0, concat_axis=0, tiled=True)

    parts = [exchange(most, *direct)]
    parts.append(exchange(last_part, *parts, *pieces))

    v_low = shift(start_columns[-DEG * W :], "row", 1)
    v_high = shift(start_columns[: DEG * W], "row", -1)

    first, last, lists = edge_blocks(owners, pieces, col_count, DEG - 1)
    h_low = shift(last, "row", 1)
    h_high = shift(first, "row", -1)
    kernel_t = chebyshev(
        coefficients, owners, v_low, start_columns, v_high, h_low, h_high, pieces
    )
    collect, plan, order, tile_of = make_plan(lists[:, 0], me, entries, tiles, col_count, blocks)
    partial = project(plan, order, kernel_t, core_density, parts)
    contributions = lax.all_to_all(partial, "col", split_axis=0, concat_axis=0, tiled=True)
    contributions = contributions.reshape(-1, P_SIZE)
    return update(
        plan, order, tile_of, contributions, collect, parts, tiles, blocks, cols
    )


def solution(mesh):
    return jax.shard_map(
        shards,
        mesh=mesh,
        in_specs=(
            P("row", "col"),
            P(("row", "col"), None, None, None),
            P(("row", "col")),
            P(),
            P(("row", "col"), None),
            P(("row", "col")),
            P(("row", "col")),
            P(("row", "col"), None, None, None),
            P(("row", "col"), None),
        ),
        out_specs=(P(("row", "col"), None), P("row", "col")),
        check_vma=False,
    )
```

```python
import functools
import math

import jax
import jax.numpy as jnp
from jax import lax
from jax.experimental import pallas as pl
from jax.experimental.pallas import tpu as pltpu
from jax.sharding import PartitionSpec as P

W = 256
KB = 512
DEG = 3
SLOTS = 4
CAP = 2
P_SIZE = 128
MIB = 1 << 20
LISTS = 16

exchange_factor = (3.0 / math.pi) ** (1.0 / 3.0)
HBM = pl.BlockSpec(memory_space=pltpu.HBM)
SMEM = pl.BlockSpec(memory_space=pltpu.SMEM)
VMEM = pl.BlockSpec(memory_space=pltpu.VMEM)


def partner(me, j, count):
    if count & (count - 1) == 0:
        return me ^ abs(j)
    return (me + j) % count


def piece_kernel(peers, named, counts, pattern, ham, piece, blocks, sems):
    rows = ham.shape[0]
    load = pltpu.make_async_copy(ham, blocks.at[pl.ds(0, rows)], sems.at[0])
    load.start()
    lane = lax.broadcasted_iota(jnp.int32, (LISTS, W), 1)
    lists = jnp.zeros((LISTS, W), jnp.int32)
    at = 0
    for ref in (peers, named, counts):
        for i in range(ref.shape[0]):
            lists = jnp.where(lane == at, ref[i], lists)
            at += 1
    blocks[rows:] = lists.astype(jnp.float32).astype(jnp.bfloat16)
    load.wait()
    for i in range(rows // (2 * W)):
        coupling = slice((2 * i + 1) * W, (2 * i + 2) * W)
        blocks[coupling] = blocks[coupling] * pattern[i].astype(jnp.bfloat16)
    store = pltpu.make_async_copy(blocks, piece, sems.at[1])
    store.start()
    store.wait()


def own_piece(peers, named, counts, pattern, ham):
    piece = (ham.shape[0] + LISTS, W)
    return pl.pallas_call(
        piece_kernel,
        out_shape=jax.ShapeDtypeStruct(piece, ham.dtype),
        in_specs=[SMEM] * 4 + [HBM],
        out_specs=HBM,
        scratch_shapes=[pltpu.VMEM(piece, ham.dtype), pltpu.SemaphoreType.DMA((2,))],
        compiler_params=pltpu.CompilerParams(vmem_limit_bytes=62 * MIB),
        name="own_piece",
    )(peers, named, counts, pattern, ham)


def lines_of(count):
    inner = max(count // 4, 1) if count & (count - 1) == 0 else 1
    return count // inner, inner


def chunk_of(home, owner, count):
    outer, inner = lines_of(count)
    return partner(home % inner, owner % inner, inner) * outer + home // inner


def pack_kernel(entries, col_count, me, peers, basis, *refs):
    outer, inner = lines_of(col_count)
    *sent, held, count, in_sems, out_sems = refs

    def fetch(e):
        return pltpu.make_async_copy(basis.at[e], held.at[e], in_sems.at[e])

    def send(e, p, k, act):
        line, place = lax.div(p, inner), lax.rem(p, inner)
        for t in range(inner):
            @pl.when(place == partner(lax.rem(me[0], inner), t, inner))
            def _():
                target = sent[0].at[line, k] if t == 0 else sent[1 + (t - 1) * CAP + k].at[line]
                act(pltpu.make_async_copy(held.at[e], target, out_sems.at[p, k]))

    for e in range(entries):
        fetch(e).start()
    for c in range(col_count):
        count[c] = 0
    for e in range(entries):
        p = peers[e]
        rank = count[p]
        count[p] = rank + 1
        fetch(e).wait()
        for k in range(CAP):
            @pl.when(rank == k)
            def _():
                send(e, p, k, lambda copy: copy.start())
    for c in range(col_count):
        for k in range(CAP):
            @pl.when(count[c] <= k)
            def _():
                send(0, jnp.int32(c), k, lambda copy: copy.start())
    for c in range(col_count):
        for k in range(CAP):
            pltpu.make_async_copy(basis.at[0], held.at[0], out_sems.at[c, k]).wait()


def pack(me, peers, basis, col_count):
    outer, inner = lines_of(col_count)
    entries = basis.shape[0]
    shapes = [(outer, CAP)] + [(outer,)] * ((inner - 1) * CAP)
    return pl.pallas_call(
        functools.partial(pack_kernel, entries, col_count),
        out_shape=tuple(
            jax.ShapeDtypeStruct(shape + basis.shape[1:], basis.dtype) for shape in shapes
        ),
        in_specs=[SMEM, SMEM, HBM],
        out_specs=(HBM,) * len(shapes),
        scratch_shapes=[
            pltpu.VMEM(basis.shape, basis.dtype),
            pltpu.SMEM((col_count,), jnp.int32),
            pltpu.SemaphoreType.DMA((entries,)),
            pltpu.SemaphoreType.DMA((col_count, CAP)),
        ],
        compiler_params=pltpu.CompilerParams(vmem_limit_bytes=62 * MIB),
        name="pack",
    )(me, peers, basis)


def exchange(sent, awaited):
    count = lax.axis_size("col")
    outer, inner = lines_of(count)
    groups = [[line * inner + place for line in range(outer)] for place in range(inner)]

    def swap(block, t):
        pairs = [
            (c, c - c % inner + partner(c % inner, t, inner)) for c in range(count)
        ]
        return lax.ppermute(block, "col", pairs)

    def between_lines(block, *others):
        return lax.all_to_all(
            after(block, *others), "col", split_axis=0, concat_axis=0,
            axis_index_groups=groups, tiled=True,
        )

    swapped = [
        [swap(sent[1 + (t - 1) * CAP + k], t) for k in range(CAP)] for t in range(1, inner)
    ]
    parts = [between_lines(sent[0], *awaited, *[blocks[0] for blocks in swapped])]
    for blocks in swapped:
        parts.append(between_lines(jnp.stack(blocks, axis=1), parts[-1]))
    return [part.reshape((outer * CAP,) + part.shape[2:]) for part in parts]


def after(block, *others):
    return pl.pallas_call(
        lambda *refs: None,
        out_shape=jax.ShapeDtypeStruct(block.shape, block.dtype),
        in_specs=[HBM] * (1 + len(others)),
        out_specs=HBM,
        input_output_aliases={0: 0},
        compiler_params=pltpu.CompilerParams(vmem_limit_bytes=62 * MIB),
        name="after",
    )(block, *others)


def gather_pieces(own):
    count = lax.axis_size("col")
    straight = count & (count - 1) != 0
    inner = count if straight else max(count // 4, 1)

    def send(block, j):
        pairs = [(c, partner(c, j, count)) for c in range(count)]
        return lax.ppermute(block, "col", pairs)

    pieces = [own] + [None] * (count - 1)
    first = [j for j in range(1, count) if j % inner == 0 or j < inner]
    for j in sorted(first, reverse=True):
        pieces[j] = send(own, j)
    for j in range(count - 1, 0, -1):
        if pieces[j] is None:
            pieces[j] = send(pieces[j - j % inner], j % inner)
    return pieces, [pieces[j] for j in first]


def edge_kernel(col_count, depth, owners, *refs):
    pieces, (first, last, lists, sems, list_sems) = refs[:-5], refs[-5:]
    rows = pieces[0].shape[0] - LISTS
    held = rows // (2 * W)
    total = col_count * held

    def each(act):
        for i, piece in enumerate(pieces):
            for g in range(depth):
                for out, block, sem in ((first, g, 0), (last, total - depth + g, 1)):
                    source = piece.at[pl.ds(block % held * 2 * W, 2 * W)]
                    copy = pltpu.make_async_copy(source, out.at[g], sems.at[sem, g])

                    @pl.when(owners[i] == block // held)
                    def _():
                        act(copy)

            @pl.when(owners[i] >= 0)
            def _():
                act(pltpu.make_async_copy(
                    piece.at[pl.ds(rows, LISTS)], lists.at[owners[i]], list_sems.at[i]
                ))

    each(lambda copy: copy.start())
    each(lambda copy: copy.wait())


def edge_blocks(owners, pieces, col_count, depth):
    shape = jax.ShapeDtypeStruct((depth, 2 * W, W), pieces[0].dtype)
    return pl.pallas_call(
        functools.partial(edge_kernel, col_count, depth),
        out_shape=(shape, shape, jax.ShapeDtypeStruct((col_count, LISTS, W), pieces[0].dtype)),
        in_specs=[SMEM] + [HBM] * len(pieces),
        out_specs=(VMEM, VMEM, VMEM),
        scratch_shapes=[
            pltpu.SemaphoreType.DMA((2, depth)),
            pltpu.SemaphoreType.DMA((len(pieces),)),
        ],
        name="edge_blocks",
    )(owners, *pieces)


def cheb_kernel(blocks, coef, owners, v_low, v_mid, v_high, h_low, h_high, *refs):
    *pieces, out, vext, hraw, hcat, cheb_1, cheb_2, total, kern, sems, psems, osems = refs
    halo_v = DEG
    halo_h = DEG - 1
    held = (pieces[0].shape[0] - LISTS) // (2 * W)
    h_copies = [
        pltpu.make_async_copy(h_low, hraw.at[pl.ds(0, halo_h)], sems.at[0]),
        pltpu.make_async_copy(h_high, hraw.at[pl.ds(halo_h + blocks, halo_h)], sems.at[1]),
    ]
    v_copies = [
        pltpu.make_async_copy(v_low, vext.at[pl.ds(0, halo_v * W)], sems.at[2]),
        pltpu.make_async_copy(v_mid, vext.at[pl.ds(halo_v * W, blocks * W)], sems.at[3]),
        pltpu.make_async_copy(v_high, vext.at[pl.ds((halo_v + blocks) * W, halo_v * W)], sems.at[4]),
    ]

    def each_piece(act):
        for i, piece in enumerate(pieces):
            @pl.when(owners[i] >= 0)
            def _():
                for k in range(held):
                    act(pltpu.make_async_copy(
                        piece.at[pl.ds(k * 2 * W, 2 * W)],
                        hraw.at[halo_h + owners[i] * held + k],
                        psems.at[i, k],
                    ))

    each_piece(lambda copy: copy.start())
    for copy in h_copies + v_copies:
        copy.start()
    each_piece(lambda copy: copy.wait())
    for copy in h_copies:
        copy.wait()
    rows = lax.broadcasted_iota(jnp.int32, (W, W), 0)
    cols = lax.broadcasted_iota(jnp.int32, (W, W), 1)
    upper = jnp.where(rows <= cols, 1.0, 0.0).astype(jnp.bfloat16)

    def build(j, carry):
        coupling = hraw[j, W:]
        lower_band = coupling * upper
        hcat[j, :, 0:W] = lower_band
        hcat[j, :, W : 2 * W] = hraw[j, :W]
        hcat[j, :, 2 * W : 3 * W] = coupling - lower_band
        return carry

    lax.fori_loop(0, blocks + 2 * halo_h, build, 0, unroll=2)
    for copy in v_copies:
        copy.wait()

    def rows_of(j, count=1):
        return pl.ds(pl.multiple_of(j * W, W), count * W)

    def band(source, j, row):
        return jnp.dot(hcat[j], source[rows_of(row, 3), :], preferred_element_type=jnp.float32)

    def first(j, carry):
        value = band(vext, j, j)
        cheb_1[rows_of(j), :] = value.astype(jnp.bfloat16)
        total[rows_of(j), :] = value
        return carry

    lax.fori_loop(0, blocks + 4, first, 0, unroll=2)

    def second(j, carry):
        begin = vext[rows_of(j + 2), :].astype(jnp.float32)
        value = 2.0 * band(cheb_1, j + 1, j) - begin
        cheb_2[rows_of(j), :] = value.astype(jnp.bfloat16)
        total[rows_of(j + 1), :] = (
            coef[0] * begin + (coef[1] - coef[3]) * total[rows_of(j + 1), :] + coef[2] * value
        )
        return carry

    lax.fori_loop(0, blocks + 2, second, 0, unroll=2)

    def store(j):
        return pltpu.make_async_copy(kern.at[j], out.at[j], osems.at[j])

    def third(j, carry):
        for half in range(KB // W):
            i = j * (KB // W) + half
            value = total[rows_of(i + 2), :] + (2.0 * coef[3]) * band(cheb_2, i + 2, i)
            kern[j, :, half * W : (half + 1) * W] = value.astype(jnp.bfloat16).T
        store(j).start()
        return carry

    lax.fori_loop(0, blocks // (KB // W), third, 0)
    for j in range(blocks // (KB // W)):
        store(j).wait()


def chebyshev(coefficients, owners, v_low, v_mid, v_high, h_low, h_high, pieces):
    blocks = v_mid.shape[0] // W
    cols = v_mid.shape[1]
    ext = blocks + 2 * (DEG - 1)
    flops = 2 * W * 3 * W * cols * (3 * blocks + 6)
    result = (blocks * W // KB, cols, KB)
    held = (pieces[0].shape[0] - LISTS) // (2 * W)
    return pl.pallas_call(
        functools.partial(cheb_kernel, blocks),
        out_shape=jax.ShapeDtypeStruct(result, jnp.bfloat16),
        in_specs=[SMEM] * 2 + [HBM] * (5 + len(pieces)),
        out_specs=HBM,
        scratch_shapes=[
            pltpu.VMEM(((blocks + 2 * DEG) * W, cols), jnp.bfloat16),
            pltpu.VMEM((ext, 2 * W, W), jnp.bfloat16),
            pltpu.VMEM((ext, W, 3 * W), jnp.bfloat16),
            pltpu.VMEM((ext * W, cols), jnp.bfloat16),
            pltpu.VMEM(((blocks + 2) * W, cols), jnp.bfloat16),
            pltpu.VMEM((ext * W, cols), jnp.float32),
            pltpu.VMEM(result, jnp.bfloat16),
            pltpu.SemaphoreType.DMA((5,)),
            pltpu.SemaphoreType.DMA((len(pieces), held)),
            pltpu.SemaphoreType.DMA((result[0],)),
        ],
        compiler_params=pltpu.CompilerParams(vmem_limit_bytes=62 * MIB),
        cost_estimate=pl.CostEstimate(flops=flops, bytes_accessed=16 * MIB, transcendentals=0),
        name="chebyshev",
    )(coefficients, owners, v_low, v_mid, v_high, h_low, h_high, *pieces)


def entry_loads(order, parts, pair, sems):
    size = parts[0].shape[0]

    def load(p):
        return pltpu.make_async_copy(parts[0].at[0], pair.at[p], sems.at[p])

    def start(p, carry):
        n = order[p]
        for t, part in enumerate(parts):
            @pl.when((n >= t * size) & (n < (t + 1) * size))
            def _():
                pltpu.make_async_copy(part.at[n - t * size], pair.at[p], sems.at[p]).start()

        return carry

    return load, start


def by_twos(first, last, load, body):
    def step(i, carry):
        p = first + 2 * i
        q = jnp.minimum(p + 1, last - 1)
        load(p).wait()

        @pl.when(q > p)
        def _():
            load(q).wait()

        body(i, p, q)
        return carry

    lax.fori_loop(0, (last - first + 1) // 2, step, 0)


def sent_rows(slots, tiles):
    return slots + tiles + -(slots + tiles) % 8


def project_kernel(blocks, plan, order, kernel_t, core, *refs):
    *parts, out, kern, pair, rows, ksems, bsems = refs
    slots = pair.shape[0]
    load, start = entry_loads(order, parts, pair, bsems)

    def fetch(b):
        return pltpu.make_async_copy(kernel_t.at[b], kern.at[b], ksems.at[b])

    def begin(b, carry):
        first, last = plan[slots + b], plan[slots + b + 1]

        @pl.when(first < last)
        def _():
            fetch(b).start()

        return lax.fori_loop(first, last, start, carry)

    lax.fori_loop(0, blocks, begin, 0)
    rows[...] = jnp.zeros_like(rows)
    rows[slots : slots + core.shape[0]] = core[...]

    def step(b, carry):
        first, last = plan[slots + b], plan[slots + b + 1]

        @pl.when(first < last)
        def _():
            fetch(b).wait()

        def body(i, p, q):
            both = jnp.concatenate([pair[p, 0], pair[q, 0]], axis=1)
            projected = jnp.dot(kern[b], both, preferred_element_type=jnp.float32)
            other = jnp.concatenate([pair[p, 1], pair[q, 1]], axis=1).astype(jnp.float32)
            value = jnp.sum(projected * other, axis=0, keepdims=True) * (1.0 / KB)
            rows[pl.ds(order[p], 1), :] = value[:, :P_SIZE]
            rows[pl.ds(order[q], 1), :] = value[:, P_SIZE:]

        by_twos(first, last, load, body)
        return carry

    lax.fori_loop(0, blocks, step, 0)
    for c in range(out.shape[0]):
        out[c] = rows[...]


def project(plan, order, kernel_t, core, parts, col_count):
    slots = col_count * CAP
    entry = parts[0].shape[1:]
    sent = sent_rows(slots, core.shape[0])
    blocks = kernel_t.shape[0]
    return pl.pallas_call(
        functools.partial(project_kernel, blocks),
        out_shape=jax.ShapeDtypeStruct((col_count, sent, P_SIZE), jnp.float32),
        in_specs=[SMEM, SMEM, HBM, VMEM] + [HBM] * len(parts),
        out_specs=VMEM,
        scratch_shapes=[
            pltpu.VMEM(kernel_t.shape, jnp.bfloat16),
            pltpu.VMEM((slots,) + entry, jnp.bfloat16),
            pltpu.VMEM((sent, P_SIZE), jnp.float32),
            pltpu.SemaphoreType.DMA((blocks,)),
            pltpu.SemaphoreType.DMA((slots,)),
        ],
        compiler_params=pltpu.CompilerParams(vmem_limit_bytes=62 * MIB),
        name="project",
    )(plan, order, kernel_t, core, *parts)


def update_kernel(
    blocks, tiles, plan, order, tile_of, contributions, collect, *refs
):
    *parts, density_out, update_out, pair, density, potential, acc, stage, sems, osems = refs
    slots = pair.shape[0]
    live = plan[slots + blocks]
    me = plan[slots + blocks + 1]
    load, start = entry_loads(order, parts, pair, sems)
    lax.fori_loop(0, live, start, 0)
    density[...] = jnp.dot(
        collect[...],
        contributions[...],
        preferred_element_type=jnp.float32,
        precision=lax.Precision.HIGHEST,
    )
    for t in range(tiles):
        density_out[pl.ds(t, 1), :] = density[pl.ds(me * tiles + t, 1), :]
    positive = jnp.maximum(density[...], 0.1)
    root = jnp.exp(jnp.log(positive) * (1.0 / 3.0))
    root = root - (root - positive / (root * root)) * (1.0 / 3.0)
    potential[...] = -exchange_factor * root
    scale = 1.0 / math.sqrt(P_SIZE)

    def store(b):
        rows = pl.ds(pl.multiple_of(b * KB, KB), KB)
        return pltpu.make_async_copy(stage.at[b], update_out.at[rows], osems.at[b])

    def step(b, carry):
        first, last = plan[slots + b], plan[slots + b + 1]

        @pl.when(first == last)
        def _():
            stage[b] = jnp.zeros(stage.shape[1:], jnp.bfloat16)

        def body(i, p, q):
            weight_p = potential[pl.ds(tile_of[order[p]], 1), :]
            weight_q = potential[pl.ds(tile_of[order[q]], 1), :] * (q - p).astype(jnp.float32)
            weighted = jnp.concatenate(
                [
                    (pair[p, 1].astype(jnp.float32) * weight_p).astype(jnp.bfloat16),
                    (pair[q, 1].astype(jnp.float32) * weight_q).astype(jnp.bfloat16),
                ],
                axis=1,
            )
            block = lax.dot_general(
                jnp.concatenate([pair[p, 0], pair[q, 0]], axis=1),
                weighted,
                (((1,), (1,)), ((), ())),
                preferred_element_type=jnp.float32,
            )

            @pl.when(last - first <= 2)
            def _():
                stage[b] = (block * scale).astype(jnp.bfloat16)

            @pl.when((last - first > 2) & (i == 0))
            def _():
                acc[...] = block

            @pl.when(i > 0)
            def _():
                acc[...] += block

        by_twos(first, last, load, body)

        @pl.when(last - first > 2)
        def _():
            stage[b] = (acc[...] * scale).astype(jnp.bfloat16)

        store(b).start()
        return carry

    lax.fori_loop(0, blocks, step, 0)
    for b in range(blocks):
        store(b).wait()


def update(plan, order, tile_of, contributions, collect, parts, tiles, blocks, cols):
    slots = len(parts) * parts[0].shape[0]
    entry = parts[0].shape[1:]
    all_tiles = (collect.shape[0], P_SIZE)
    return pl.pallas_call(
        functools.partial(update_kernel, blocks, tiles),
        out_shape=(
            jax.ShapeDtypeStruct((tiles, P_SIZE), jnp.float32),
            jax.ShapeDtypeStruct((blocks * KB, cols), jnp.bfloat16),
        ),
        in_specs=[SMEM] * 3 + [VMEM] * 2 + [HBM] * len(parts),
        out_specs=(VMEM, HBM),
        scratch_shapes=[
            pltpu.VMEM((slots,) + entry, jnp.bfloat16),
            pltpu.VMEM(all_tiles, jnp.float32),
            pltpu.VMEM(all_tiles, jnp.float32),
            pltpu.VMEM((KB, cols), jnp.float32),
            pltpu.VMEM((blocks, KB, cols), jnp.bfloat16),
            pltpu.SemaphoreType.DMA((slots,)),
            pltpu.SemaphoreType.DMA((blocks,)),
        ],
        compiler_params=pltpu.CompilerParams(vmem_limit_bytes=62 * MIB),
        name="update",
    )(plan, order, tile_of, contributions, collect, *parts)


def shift(block, axis, step):
    count = lax.axis_size(axis)
    pairs = [(i, i + step) for i in range(count) if 0 <= i + step < count]
    return lax.ppermute(block, axis, pairs)


def make_plan(lists, me, entries, tiles, col_count, blocks):
    slots = col_count * CAP
    sent = sent_rows(slots, tiles)
    lists = lists[:, : 2 * entries + tiles].astype(jnp.int32)
    peers, named, counts = lists[:, :entries], lists[:, entries : 2 * entries], lists[:, 2 * entries :]
    index = jnp.arange(entries, dtype=jnp.int32)
    home = jnp.arange(col_count, dtype=jnp.int32)[:, None]
    earlier = (peers[:, :, None] == peers[:, None, :]) & (index[None, :] < index[:, None])
    rank = jnp.sum(earlier.astype(jnp.int32), axis=2)
    live = (index % SLOTS)[None, :] < jnp.repeat(counts, SLOTS, axis=1)
    row = jnp.where(live, peers * sent + chunk_of(home, peers, col_count) * CAP + rank, -1).reshape(col_count, tiles, SLOTS)
    core = (home * sent + slots + jnp.arange(tiles, dtype=jnp.int32))[:, :, None]
    row = jnp.concatenate([row, core], axis=2).reshape(col_count * tiles, SLOTS + 1, 1)
    picked = row == jnp.arange(col_count * sent, dtype=jnp.int32)
    collect = jnp.sum(picked.astype(jnp.float32), axis=1)
    hit = (
        (peers == me)[:, None, :]
        & (rank[:, None, :] == jnp.arange(CAP, dtype=jnp.int32)[None, :, None])
        & live[:, None, :]
    )
    at_me = chunk_of(home, me, col_count).reshape(1, col_count) == home
    tile = home * tiles + index[None, :] // SLOTS

    def of_slots(values):
        by_home = jnp.sum(jnp.where(hit, values[:, None, :], 0), axis=2)
        return jnp.sum(jnp.where(at_me[:, :, None], by_home[None], 0), axis=1).reshape(slots)

    wanted = of_slots(named + 1) - 1
    tile_of = of_slots(tile)
    key = jnp.where(wanted < 0, blocks, wanted)
    place = jnp.arange(slots, dtype=jnp.int32)
    before = (key[None, :] < key[:, None]) | (
        (key[None, :] == key[:, None]) & (place[None, :] < place[:, None])
    )
    spot = jnp.sum(before.astype(jnp.int32), axis=1)
    order = jnp.sum(jnp.where(spot[None, :] == place[:, None], place[None, :], 0), axis=1)
    starts = jnp.sum(
        (key[None, :] < jnp.arange(blocks + 1, dtype=jnp.int32)[:, None]).astype(jnp.int32), axis=1
    )
    plan = jnp.concatenate([wanted, starts, me[None]]).astype(jnp.int32)
    return collect, plan, order.astype(jnp.int32), tile_of.astype(jnp.int32)


def shards(
    start_columns,
    hamiltonian,
    band_pattern,
    coefficients,
    tile_peer,
    tile_block,
    tile_count,
    basis_values,
    core_density,
):
    col_count = lax.axis_size("col")
    entries = tile_peer.shape[0]
    tiles = core_density.shape[0]
    cols = start_columns.shape[1]
    blocks = start_columns.shape[0] // KB
    peers = tile_peer[:, 0]
    me = lax.axis_index("col").astype(jnp.int32)

    own = own_piece(peers, tile_block, tile_count, band_pattern, hamiltonian.reshape(-1, W))
    pieces, direct = gather_pieces(own)
    owners = jnp.stack([partner(me, -j, col_count) for j in range(col_count)])
    parts = exchange(pack(me[None], peers, basis_values, col_count), direct)

    v_low = shift(start_columns[-DEG * W :], "row", 1)
    v_high = shift(start_columns[: DEG * W], "row", -1)

    first, last, lists = edge_blocks(owners, pieces, col_count, DEG - 1)
    h_low = shift(last, "row", 1)
    h_high = shift(first, "row", -1)
    kernel_t = chebyshev(
        coefficients, owners, v_low, start_columns, v_high, h_low, h_high, pieces
    )
    collect, plan, order, tile_of = make_plan(lists[:, 0], me, entries, tiles, col_count, blocks)
    partial = project(plan, order, kernel_t, core_density, parts, col_count)
    contributions = lax.all_to_all(partial, "col", split_axis=0, concat_axis=0, tiled=True)
    contributions = contributions.reshape(-1, P_SIZE)
    return update(
        plan, order, tile_of, contributions, collect, parts, tiles, blocks, cols
    )


def solution(mesh):
    return jax.shard_map(
        shards,
        mesh=mesh,
        in_specs=(
            P("row", "col"),
            P(("row", "col"), None, None, None),
            P(("row", "col")),
            P(),
            P(("row", "col"), None),
            P(("row", "col")),
            P(("row", "col")),
            P(("row", "col"), None, None, None),
            P(("row", "col"), None),
        ),
        out_specs=(P(("row", "col"), None), P("row", "col")),
        check_vma=False,
    )
```

```python
import functools
import math

import jax
import jax.numpy as jnp
from jax import lax
from jax.experimental import pallas as pl
from jax.experimental.pallas import tpu as pltpu
from jax.sharding import PartitionSpec as P

W = 256
KB = 512
DEG = 3
SLOTS = 4
CAP = 2
P_SIZE = 128
MIB = 1 << 20
LISTS = 16

exchange_factor = (3.0 / math.pi) ** (1.0 / 3.0)
HBM = pl.BlockSpec(memory_space=pltpu.HBM)
SMEM = pl.BlockSpec(memory_space=pltpu.SMEM)
VMEM = pl.BlockSpec(memory_space=pltpu.VMEM)


def partner(me, j, count):
    if count & (count - 1) == 0:
        return me ^ abs(j)
    return (me + j) % count


def piece_kernel(peers, named, counts, pattern, ham, piece, blocks, sems):
    rows = ham.shape[0]
    load = pltpu.make_async_copy(ham, blocks.at[pl.ds(0, rows)], sems.at[0])
    load.start()
    lane = lax.broadcasted_iota(jnp.int32, (LISTS, W), 1)
    lists = jnp.zeros((LISTS, W), jnp.int32)
    at = 0
    for ref in (peers, named, counts):
        for i in range(ref.shape[0]):
            lists = jnp.where(lane == at, ref[i], lists)
            at += 1
    blocks[rows:] = lists.astype(jnp.float32).astype(jnp.bfloat16)
    load.wait()
    for i in range(rows // (2 * W)):
        coupling = slice((2 * i + 1) * W, (2 * i + 2) * W)
        blocks[coupling] = blocks[coupling] * pattern[i].astype(jnp.bfloat16)
    store = pltpu.make_async_copy(blocks, piece, sems.at[1])
    store.start()
    store.wait()


def own_piece(peers, named, counts, pattern, ham):
    piece = (ham.shape[0] + LISTS, W)
    return pl.pallas_call(
        piece_kernel,
        out_shape=jax.ShapeDtypeStruct(piece, ham.dtype),
        in_specs=[SMEM] * 4 + [HBM],
        out_specs=HBM,
        scratch_shapes=[pltpu.VMEM(piece, ham.dtype), pltpu.SemaphoreType.DMA((2,))],
        compiler_params=pltpu.CompilerParams(vmem_limit_bytes=62 * MIB),
        name="own_piece",
    )(peers, named, counts, pattern, ham)


def lines_of(count):
    inner = max(count // 4, 1) if count & (count - 1) == 0 else 1
    return count // inner, inner


def swap_along(block, t):
    count = lax.axis_size("col")
    _, inner = lines_of(count)
    pairs = [(c, c - c % inner + partner(c % inner, t, inner)) for c in range(count)]
    return lax.ppermute(block, "col", pairs)


def chunk_of(home, owner, count):
    outer, inner = lines_of(count)
    return partner(home % inner, owner % inner, inner) * outer + home // inner


def pack_kernel(entries, col_count, me, peers, basis, first, *refs):
    outer, inner = lines_of(col_count)
    *sent, held, count, in_sems, out_sems = refs

    def fetch(e):
        return pltpu.make_async_copy(basis.at[e], held.at[e], in_sems.at[e])

    def send(e, p, k, act):
        line, place = lax.div(p, inner), lax.rem(p, inner)
        for t in range(inner):
            @pl.when(place == partner(lax.rem(me[0], inner), t, inner))
            def _():
                target = sent[0].at[line, k] if t == 0 else sent[1 + (t - 1) * CAP + k].at[line]
                act(pltpu.make_async_copy(held.at[e], target, out_sems.at[p, k]))

    for e in range(entries):
        fetch(e).start()
    for c in range(col_count):
        count[c] = 0
    for e in range(entries):
        p = peers[e]
        rank = count[p]
        count[p] = rank + 1
        fetch(e).wait()
        for k in range(CAP):
            @pl.when(rank == k)
            def _():
                send(e, p, k, lambda copy: copy.start())
    for c in range(col_count):
        for k in range(CAP):
            @pl.when(count[c] <= k)
            def _():
                send(0, jnp.int32(c), k, lambda copy: copy.start())
    for c in range(col_count):
        for k in range(CAP):
            pltpu.make_async_copy(basis.at[0], held.at[0], out_sems.at[c, k]).wait()


def pack(me, peers, basis, first, col_count):
    outer, inner = lines_of(col_count)
    entries = basis.shape[0]
    shapes = [(outer, CAP)] + [(outer,)] * ((inner - 1) * CAP)
    return pl.pallas_call(
        functools.partial(pack_kernel, entries, col_count),
        out_shape=tuple(
            jax.ShapeDtypeStruct(shape + basis.shape[1:], basis.dtype) for shape in shapes
        ),
        in_specs=[SMEM, SMEM, HBM, HBM],
        out_specs=(HBM,) * len(shapes),
        scratch_shapes=[
            pltpu.VMEM(basis.shape, basis.dtype),
            pltpu.SMEM((col_count,), jnp.int32),
            pltpu.SemaphoreType.DMA((entries,)),
            pltpu.SemaphoreType.DMA((col_count, CAP)),
        ],
        compiler_params=pltpu.CompilerParams(vmem_limit_bytes=62 * MIB),
        name="pack",
    )(me, peers, basis, first)


def exchange(sent, awaited):
    count = lax.axis_size("col")
    outer, inner = lines_of(count)
    groups = [[line * inner + place for line in range(outer)] for place in range(inner)]

    def between_lines(block, *others):
        return lax.all_to_all(
            after(block, *others), "col", split_axis=0, concat_axis=0,
            axis_index_groups=groups, tiled=True,
        )

    swapped = [
        [swap_along(sent[1 + (t - 1) * CAP + k], t) for k in range(CAP)] for t in range(1, inner)
    ]
    parts = [between_lines(sent[0], *awaited, *[blocks[0] for blocks in swapped])]
    for blocks in swapped:
        parts.append(between_lines(jnp.stack(blocks, axis=1), parts[-1]))
    return [part.reshape((outer * CAP,) + part.shape[2:]) for part in parts]


def after(block, *others):
    return pl.pallas_call(
        lambda *refs: None,
        out_shape=jax.ShapeDtypeStruct(block.shape, block.dtype),
        in_specs=[HBM] * (1 + len(others)),
        out_specs=HBM,
        input_output_aliases={0: 0},
        compiler_params=pltpu.CompilerParams(vmem_limit_bytes=62 * MIB),
        name="after",
    )(block, *others)


def gather_pieces(own):
    count = lax.axis_size("col")
    outer, inner = lines_of(count)
    me = lax.axis_index("col").astype(jnp.int32)
    a, b = me // inner, me % inner

    def move(block, ways):
        pairs = [(x * inner + y, z * inner + y) for x, z in ways for y in range(inner)]
        return lax.ppermute(block, "col", pairs)

    if outer == 4:
        middle, outwards = [(1, 2), (2, 1)], [(1, 0), (2, 3)]
        near = move(own, [(0, 1), (1, 0), (2, 3), (3, 2)])
        across = move(own, middle)
        far = move(near, middle)
        handed = move(across, outwards)
        last = move(far, outwards)
        within = (a == 1) | (a == 2)
        lines = [
            (own, a),
            (near, a ^ 1),
            (across + handed, jnp.where(within, a ^ 3, a ^ 2)),
            (far + last, jnp.where(within, a ^ 2, a ^ 3)),
        ]
        awaited = [far, handed]
    else:
        lines = [(own, a)] + [
            (move(own, [(x, partner(x, t, outer)) for x in range(outer)]), partner(a, -t, outer))
            for t in range(1, outer)
        ]
        awaited = [block for block, _ in lines[1:]]
    pieces, owners = [], []
    for block, line in lines:
        pieces.append(block)
        owners.append(line * inner + b)
        for t in range(1, inner):
            pieces.append(swap_along(block, t))
            owners.append(line * inner + partner(b, -t, inner))
    return pieces, jnp.stack(owners).astype(jnp.int32), awaited


def edge_kernel(col_count, depth, owners, *refs):
    pieces, (first, last, lists, sems, list_sems) = refs[:-5], refs[-5:]
    rows = pieces[0].shape[0] - LISTS
    held = rows // (2 * W)
    total = col_count * held

    def each(act):
        for i, piece in enumerate(pieces):
            for g in range(depth):
                for out, block, sem in ((first, g, 0), (last, total - depth + g, 1)):
                    source = piece.at[pl.ds(block % held * 2 * W, 2 * W)]
                    copy = pltpu.make_async_copy(source, out.at[g], sems.at[sem, g])

                    @pl.when(owners[i] == block // held)
                    def _():
                        act(copy)

            @pl.when(owners[i] >= 0)
            def _():
                act(pltpu.make_async_copy(
                    piece.at[pl.ds(rows, LISTS)], lists.at[owners[i]], list_sems.at[i]
                ))

    each(lambda copy: copy.start())
    each(lambda copy: copy.wait())


def edge_blocks(owners, pieces, col_count, depth):
    shape = jax.ShapeDtypeStruct((depth, 2 * W, W), pieces[0].dtype)
    return pl.pallas_call(
        functools.partial(edge_kernel, col_count, depth),
        out_shape=(shape, shape, jax.ShapeDtypeStruct((col_count, LISTS, W), pieces[0].dtype)),
        in_specs=[SMEM] + [HBM] * len(pieces),
        out_specs=(VMEM, VMEM, VMEM),
        scratch_shapes=[
            pltpu.SemaphoreType.DMA((2, depth)),
            pltpu.SemaphoreType.DMA((len(pieces),)),
        ],
        name="edge_blocks",
    )(owners, *pieces)


def cheb_kernel(blocks, coef, owners, v_low, v_mid, v_high, h_low, h_high, *refs):
    *pieces, out, vext, hraw, hcat, cheb_1, cheb_2, total, kern, sems, psems, osems = refs
    halo_v = DEG
    halo_h = DEG - 1
    held = (pieces[0].shape[0] - LISTS) // (2 * W)
    h_copies = [
        pltpu.make_async_copy(h_low, hraw.at[pl.ds(0, halo_h)], sems.at[0]),
        pltpu.make_async_copy(h_high, hraw.at[pl.ds(halo_h + blocks, halo_h)], sems.at[1]),
    ]
    v_copies = [
        pltpu.make_async_copy(v_low, vext.at[pl.ds(0, halo_v * W)], sems.at[2]),
        pltpu.make_async_copy(v_mid, vext.at[pl.ds(halo_v * W, blocks * W)], sems.at[3]),
        pltpu.make_async_copy(v_high, vext.at[pl.ds((halo_v + blocks) * W, halo_v * W)], sems.at[4]),
    ]

    def each_piece(act):
        for i, piece in enumerate(pieces):
            @pl.when(owners[i] >= 0)
            def _():
                for k in range(held):
                    act(pltpu.make_async_copy(
                        piece.at[pl.ds(k * 2 * W, 2 * W)],
                        hraw.at[halo_h + owners[i] * held + k],
                        psems.at[i, k],
                    ))

    each_piece(lambda copy: copy.start())
    for copy in h_copies + v_copies:
        copy.start()
    each_piece(lambda copy: copy.wait())
    for copy in h_copies:
        copy.wait()
    rows = lax.broadcasted_iota(jnp.int32, (W, W), 0)
    cols = lax.broadcasted_iota(jnp.int32, (W, W), 1)
    upper = jnp.where(rows <= cols, 1.0, 0.0).astype(jnp.bfloat16)

    def build(j, carry):
        coupling = hraw[j, W:]
        lower_band = coupling * upper
        hcat[j, :, 0:W] = lower_band
        hcat[j, :, W : 2 * W] = hraw[j, :W]
        hcat[j, :, 2 * W : 3 * W] = coupling - lower_band
        return carry

    lax.fori_loop(0, blocks + 2 * halo_h, build, 0, unroll=2)
    for copy in v_copies:
        copy.wait()

    def rows_of(j, count=1):
        return pl.ds(pl.multiple_of(j * W, W), count * W)

    def band(source, j, row):
        return jnp.dot(hcat[j], source[rows_of(row, 3), :], preferred_element_type=jnp.float32)

    def first(j, carry):
        value = band(vext, j, j)
        cheb_1[rows_of(j), :] = value.astype(jnp.bfloat16)
        total[rows_of(j), :] = value
        return carry

    lax.fori_loop(0, blocks + 4, first, 0, unroll=2)

    def second(j, carry):
        begin = vext[rows_of(j + 2), :].astype(jnp.float32)
        value = 2.0 * band(cheb_1, j + 1, j) - begin
        cheb_2[rows_of(j), :] = value.astype(jnp.bfloat16)
        total[rows_of(j + 1), :] = (
            coef[0] * begin + (coef[1] - coef[3]) * total[rows_of(j + 1), :] + coef[2] * value
        )
        return carry

    lax.fori_loop(0, blocks + 2, second, 0, unroll=2)

    def store(j):
        return pltpu.make_async_copy(kern.at[j], out.at[j], osems.at[j])

    def third(j, carry):
        for half in range(KB // W):
            i = j * (KB // W) + half
            value = total[rows_of(i + 2), :] + (2.0 * coef[3]) * band(cheb_2, i + 2, i)
            kern[j, :, half * W : (half + 1) * W] = value.astype(jnp.bfloat16).T
        store(j).start()
        return carry

    lax.fori_loop(0, blocks // (KB // W), third, 0)
    for j in range(blocks // (KB // W)):
        store(j).wait()


def chebyshev(coefficients, owners, v_low, v_mid, v_high, h_low, h_high, pieces):
    blocks = v_mid.shape[0] // W
    cols = v_mid.shape[1]
    ext = blocks + 2 * (DEG - 1)
    flops = 2 * W * 3 * W * cols * (3 * blocks + 6)
    result = (blocks * W // KB, cols, KB)
    held = (pieces[0].shape[0] - LISTS) // (2 * W)
    return pl.pallas_call(
        functools.partial(cheb_kernel, blocks),
        out_shape=jax.ShapeDtypeStruct(result, jnp.bfloat16),
        in_specs=[SMEM] * 2 + [HBM] * (5 + len(pieces)),
        out_specs=HBM,
        scratch_shapes=[
            pltpu.VMEM(((blocks + 2 * DEG) * W, cols), jnp.bfloat16),
            pltpu.VMEM((ext, 2 * W, W), jnp.bfloat16),
            pltpu.VMEM((ext, W, 3 * W), jnp.bfloat16),
            pltpu.VMEM((ext * W, cols), jnp.bfloat16),
            pltpu.VMEM(((blocks + 2) * W, cols), jnp.bfloat16),
            pltpu.VMEM((ext * W, cols), jnp.float32),
            pltpu.VMEM(result, jnp.bfloat16),
            pltpu.SemaphoreType.DMA((5,)),
            pltpu.SemaphoreType.DMA((len(pieces), held)),
            pltpu.SemaphoreType.DMA((result[0],)),
        ],
        compiler_params=pltpu.CompilerParams(vmem_limit_bytes=62 * MIB),
        cost_estimate=pl.CostEstimate(flops=flops, bytes_accessed=16 * MIB, transcendentals=0),
        name="chebyshev",
    )(coefficients, owners, v_low, v_mid, v_high, h_low, h_high, *pieces)


def entry_loads(order, parts, pair, sems):
    size = parts[0].shape[0]

    def load(p):
        return pltpu.make_async_copy(parts[0].at[0], pair.at[p], sems.at[p])

    def start(p, carry):
        n = order[p]
        for t, part in enumerate(parts):
            @pl.when((n >= t * size) & (n < (t + 1) * size))
            def _():
                pltpu.make_async_copy(part.at[n - t * size], pair.at[p], sems.at[p]).start()

        return carry

    return load, start


def by_twos(first, last, load, body):
    def step(i, carry):
        p = first + 2 * i
        q = jnp.minimum(p + 1, last - 1)
        load(p).wait()

        @pl.when(q > p)
        def _():
            load(q).wait()

        body(i, p, q)
        return carry

    lax.fori_loop(0, (last - first + 1) // 2, step, 0)


def sent_rows(slots, tiles):
    return slots + tiles + -(slots + tiles) % 8


def project_kernel(blocks, plan, order, kernel_t, core, *refs):
    *parts, out, kern, pair, rows, ksems, bsems = refs
    slots = pair.shape[0]
    load, start = entry_loads(order, parts, pair, bsems)

    def fetch(b):
        return pltpu.make_async_copy(kernel_t.at[b], kern.at[b], ksems.at[b])

    def begin(b, carry):
        first, last = plan[slots + b], plan[slots + b + 1]

        @pl.when(first < last)
        def _():
            fetch(b).start()

        return lax.fori_loop(first, last, start, carry)

    lax.fori_loop(0, blocks, begin, 0)
    rows[...] = jnp.zeros_like(rows)
    rows[slots : slots + core.shape[0]] = core[...]

    def step(b, carry):
        first, last = plan[slots + b], plan[slots + b + 1]

        @pl.when(first < last)
        def _():
            fetch(b).wait()

        def body(i, p, q):
            both = jnp.concatenate([pair[p, 0], pair[q, 0]], axis=1)
            projected = jnp.dot(kern[b], both, preferred_element_type=jnp.float32)
            other = jnp.concatenate([pair[p, 1], pair[q, 1]], axis=1).astype(jnp.float32)
            value = jnp.sum(projected * other, axis=0, keepdims=True) * (1.0 / KB)
            rows[pl.ds(order[p], 1), :] = value[:, :P_SIZE]
            rows[pl.ds(order[q], 1), :] = value[:, P_SIZE:]

        by_twos(first, last, load, body)
        return carry

    lax.fori_loop(0, blocks, step, 0)
    for c in range(out.shape[0]):
        out[c] = rows[...]


def project(plan, order, kernel_t, core, parts, col_count):
    slots = col_count * CAP
    entry = parts[0].shape[1:]
    sent = sent_rows(slots, core.shape[0])
    blocks = kernel_t.shape[0]
    return pl.pallas_call(
        functools.partial(project_kernel, blocks),
        out_shape=jax.ShapeDtypeStruct((col_count, sent, P_SIZE), jnp.float32),
        in_specs=[SMEM, SMEM, HBM, VMEM] + [HBM] * len(parts),
        out_specs=VMEM,
        scratch_shapes=[
            pltpu.VMEM(kernel_t.shape, jnp.bfloat16),
            pltpu.VMEM((slots,) + entry, jnp.bfloat16),
            pltpu.VMEM((sent, P_SIZE), jnp.float32),
            pltpu.SemaphoreType.DMA((blocks,)),
            pltpu.SemaphoreType.DMA((slots,)),
        ],
        compiler_params=pltpu.CompilerParams(vmem_limit_bytes=62 * MIB),
        name="project",
    )(plan, order, kernel_t, core, *parts)


def update_kernel(
    blocks, tiles, plan, order, tile_of, contributions, collect, *refs
):
    *parts, density_out, update_out, pair, density, potential, acc, stage, sems, osems = refs
    slots = pair.shape[0]
    live = plan[slots + blocks]
    me = plan[slots + blocks + 1]
    load, start = entry_loads(order, parts, pair, sems)
    lax.fori_loop(0, live, start, 0)
    density[...] = jnp.dot(
        collect[...],
        contributions[...],
        preferred_element_type=jnp.float32,
        precision=lax.Precision.HIGHEST,
    )
    for t in range(tiles):
        density_out[pl.ds(t, 1), :] = density[pl.ds(me * tiles + t, 1), :]
    positive = jnp.maximum(density[...], 0.1)
    root = jnp.exp(jnp.log(positive) * (1.0 / 3.0))
    root = root - (root - positive / (root * root)) * (1.0 / 3.0)
    potential[...] = -exchange_factor * root
    scale = 1.0 / math.sqrt(P_SIZE)

    def store(b):
        rows = pl.ds(pl.multiple_of(b * KB, KB), KB)
        return pltpu.make_async_copy(stage.at[b], update_out.at[rows], osems.at[b])

    def step(b, carry):
        first, last = plan[slots + b], plan[slots + b + 1]

        @pl.when(first == last)
        def _():
            stage[b] = jnp.zeros(stage.shape[1:], jnp.bfloat16)

        def body(i, p, q):
            weight_p = potential[pl.ds(tile_of[order[p]], 1), :]
            weight_q = potential[pl.ds(tile_of[order[q]], 1), :] * (q - p).astype(jnp.float32)
            weighted = jnp.concatenate(
                [
                    (pair[p, 1].astype(jnp.float32) * weight_p).astype(jnp.bfloat16),
                    (pair[q, 1].astype(jnp.float32) * weight_q).astype(jnp.bfloat16),
                ],
                axis=1,
            )
            block = lax.dot_general(
                jnp.concatenate([pair[p, 0], pair[q, 0]], axis=1),
                weighted,
                (((1,), (1,)), ((), ())),
                preferred_element_type=jnp.float32,
            )

            @pl.when(last - first <= 2)
            def _():
                stage[b] = (block * scale).astype(jnp.bfloat16)

            @pl.when((last - first > 2) & (i == 0))
            def _():
                acc[...] = block

            @pl.when(i > 0)
            def _():
                acc[...] += block

        by_twos(first, last, load, body)

        @pl.when(last - first > 2)
        def _():
            stage[b] = (acc[...] * scale).astype(jnp.bfloat16)

        store(b).start()
        return carry

    lax.fori_loop(0, blocks, step, 0)
    for b in range(blocks):
        store(b).wait()


def update(plan, order, tile_of, contributions, collect, parts, tiles, blocks, cols):
    slots = len(parts) * parts[0].shape[0]
    entry = parts[0].shape[1:]
    all_tiles = (collect.shape[0], P_SIZE)
    return pl.pallas_call(
        functools.partial(update_kernel, blocks, tiles),
        out_shape=(
            jax.ShapeDtypeStruct((tiles, P_SIZE), jnp.float32),
            jax.ShapeDtypeStruct((blocks * KB, cols), jnp.bfloat16),
        ),
        in_specs=[SMEM] * 3 + [VMEM] * 2 + [HBM] * len(parts),
        out_specs=(VMEM, HBM),
        scratch_shapes=[
            pltpu.VMEM((slots,) + entry, jnp.bfloat16),
            pltpu.VMEM(all_tiles, jnp.float32),
            pltpu.VMEM(all_tiles, jnp.float32),
            pltpu.VMEM((KB, cols), jnp.float32),
            pltpu.VMEM((blocks, KB, cols), jnp.bfloat16),
            pltpu.SemaphoreType.DMA((slots,)),
            pltpu.SemaphoreType.DMA((blocks,)),
        ],
        compiler_params=pltpu.CompilerParams(vmem_limit_bytes=62 * MIB),
        name="update",
    )(plan, order, tile_of, contributions, collect, *parts)


def shift(block, axis, step):
    count = lax.axis_size(axis)
    pairs = [(i, i + step) for i in range(count) if 0 <= i + step < count]
    return lax.ppermute(block, axis, pairs)


def make_plan(lists, me, entries, tiles, col_count, blocks):
    slots = col_count * CAP
    sent = sent_rows(slots, tiles)
    lists = lists[:, : 2 * entries + tiles].astype(jnp.int32)
    peers, named, counts = lists[:, :entries], lists[:, entries : 2 * entries], lists[:, 2 * entries :]
    index = jnp.arange(entries, dtype=jnp.int32)
    home = jnp.arange(col_count, dtype=jnp.int32)[:, None]
    earlier = (peers[:, :, None] == peers[:, None, :]) & (index[None, :] < index[:, None])
    rank = jnp.sum(earlier.astype(jnp.int32), axis=2)
    live = (index % SLOTS)[None, :] < jnp.repeat(counts, SLOTS, axis=1)
    row = jnp.where(live, peers * sent + chunk_of(home, peers, col_count) * CAP + rank, -1).reshape(col_count, tiles, SLOTS)
    core = (home * sent + slots + jnp.arange(tiles, dtype=jnp.int32))[:, :, None]
    row = jnp.concatenate([row, core], axis=2).reshape(col_count * tiles, SLOTS + 1, 1)
    picked = row == jnp.arange(col_count * sent, dtype=jnp.int32)
    collect = jnp.sum(picked.astype(jnp.float32), axis=1)
    hit = (
        (peers == me)[:, None, :]
        & (rank[:, None, :] == jnp.arange(CAP, dtype=jnp.int32)[None, :, None])
        & live[:, None, :]
    )
    at_me = chunk_of(home, me, col_count).reshape(1, col_count) == home
    tile = home * tiles + index[None, :] // SLOTS

    def of_slots(values):
        by_home = jnp.sum(jnp.where(hit, values[:, None, :], 0), axis=2)
        return jnp.sum(jnp.where(at_me[:, :, None], by_home[None], 0), axis=1).reshape(slots)

    wanted = of_slots(named + 1) - 1
    tile_of = of_slots(tile)
    key = jnp.where(wanted < 0, blocks, wanted)
    place = jnp.arange(slots, dtype=jnp.int32)
    before = (key[None, :] < key[:, None]) | (
        (key[None, :] == key[:, None]) & (place[None, :] < place[:, None])
    )
    spot = jnp.sum(before.astype(jnp.int32), axis=1)
    order = jnp.sum(jnp.where(spot[None, :] == place[:, None], place[None, :], 0), axis=1)
    starts = jnp.sum(
        (key[None, :] < jnp.arange(blocks + 1, dtype=jnp.int32)[:, None]).astype(jnp.int32), axis=1
    )
    plan = jnp.concatenate([wanted, starts, me[None]]).astype(jnp.int32)
    return collect, plan, order.astype(jnp.int32), tile_of.astype(jnp.int32)


def shards(
    start_columns,
    hamiltonian,
    band_pattern,
    coefficients,
    tile_peer,
    tile_block,
    tile_count,
    basis_values,
    core_density,
):
    col_count = lax.axis_size("col")
    entries = tile_peer.shape[0]
    tiles = core_density.shape[0]
    cols = start_columns.shape[1]
    blocks = start_columns.shape[0] // KB
    peers = tile_peer[:, 0]
    me = lax.axis_index("col").astype(jnp.int32)

    own = own_piece(peers, tile_block, tile_count, band_pattern, hamiltonian.reshape(-1, W))
    pieces, owners, awaited = gather_pieces(own)
    parts = exchange(pack(me[None], peers, basis_values, own, col_count), awaited)

    v_low = shift(start_columns[-DEG * W :], "row", 1)
    v_high = shift(start_columns[: DEG * W], "row", -1)

    first, last, lists = edge_blocks(owners, pieces, col_count, DEG - 1)
    h_low = shift(last, "row", 1)
    h_high = shift(first, "row", -1)
    kernel_t = chebyshev(
        coefficients, owners, v_low, start_columns, v_high, h_low, h_high, pieces
    )
    collect, plan, order, tile_of = make_plan(lists[:, 0], me, entries, tiles, col_count, blocks)
    partial = project(plan, order, kernel_t, core_density, parts, col_count)
    contributions = lax.all_to_all(partial, "col", split_axis=0, concat_axis=0, tiled=True)
    contributions = contributions.reshape(-1, P_SIZE)
    return update(
        plan, order, tile_of, contributions, collect, parts, tiles, blocks, cols
    )


def solution(mesh):
    return jax.shard_map(
        shards,
        mesh=mesh,
        in_specs=(
            P("row", "col"),
            P(("row", "col"), None, None, None),
            P(("row", "col")),
            P(),
            P(("row", "col"), None),
            P(("row", "col")),
            P(("row", "col")),
            P(("row", "col"), None, None, None),
            P(("row", "col"), None),
        ),
        out_specs=(P(("row", "col"), None), P("row", "col")),
        check_vma=False,
    )
```

```python
import functools
import math

import jax
import jax.numpy as jnp
from jax import lax
from jax.experimental import pallas as pl
from jax.experimental.pallas import tpu as pltpu
from jax.sharding import PartitionSpec as P

W = 256
KB = 512
DEG = 3
SLOTS = 4
CAP = 2
P_SIZE = 128
MIB = 1 << 20
LISTS = 16

exchange_factor = (3.0 / math.pi) ** (1.0 / 3.0)
HBM = pl.BlockSpec(memory_space=pltpu.HBM)
ANY = pl.BlockSpec(memory_space=pl.ANY)
SMEM = pl.BlockSpec(memory_space=pltpu.SMEM)
VMEM = pl.BlockSpec(memory_space=pltpu.VMEM)


def partner(me, j, count):
    if count & (count - 1) == 0:
        return me ^ abs(j)
    return (me + j) % count


def piece_kernel(peers, named, counts, pattern, ham, piece, blocks, sems):
    rows = ham.shape[0]
    load = pltpu.make_async_copy(ham, blocks.at[pl.ds(0, rows)], sems.at[0])
    load.start()
    lane = lax.broadcasted_iota(jnp.int32, (LISTS, W), 1)
    lists = jnp.zeros((LISTS, W), jnp.int32)
    at = 0
    for ref in (peers, named, counts):
        for i in range(ref.shape[0]):
            lists = jnp.where(lane == at, ref[i], lists)
            at += 1
    blocks[rows:] = lists.astype(jnp.float32).astype(jnp.bfloat16)
    load.wait()
    for i in range(rows // (2 * W)):
        coupling = slice((2 * i + 1) * W, (2 * i + 2) * W)
        blocks[coupling] = blocks[coupling] * pattern[i].astype(jnp.bfloat16)
    store = pltpu.make_async_copy(blocks, piece, sems.at[1])
    store.start()
    store.wait()


def own_piece(peers, named, counts, pattern, ham):
    piece = (ham.shape[0] + LISTS, W)
    return pl.pallas_call(
        piece_kernel,
        out_shape=jax.ShapeDtypeStruct(piece, ham.dtype),
        in_specs=[SMEM] * 4 + [HBM],
        out_specs=HBM,
        scratch_shapes=[pltpu.VMEM(piece, ham.dtype), pltpu.SemaphoreType.DMA((2,))],
        compiler_params=pltpu.CompilerParams(vmem_limit_bytes=62 * MIB),
        name="own_piece",
    )(peers, named, counts, pattern, ham)


def lines_of(count):
    inner = max(count // 4, 1) if count & (count - 1) == 0 else 1
    return count // inner, inner


def swap_along(block, t):
    count = lax.axis_size("col")
    _, inner = lines_of(count)
    pairs = [(c, c - c % inner + partner(c % inner, t, inner)) for c in range(count)]
    return lax.ppermute(block, "col", pairs)


def chunk_of(home, owner, count):
    outer, inner = lines_of(count)
    return partner(home % inner, owner % inner, inner) * outer + home // inner


def pack_kernel(entries, col_count, wanted, me, peers, basis, first, *refs):
    outer, inner = lines_of(col_count)
    sent, (held, owner, count, in_sems, out_sems) = refs[: len(wanted)], refs[len(wanted) :]
    for c in range(col_count):
        count[c] = 0
        for k in range(CAP):
            owner[c * CAP + k] = 0
    for e in range(entries):
        p = peers[e]
        k = count[p]
        count[p] = k + 1
        owner[p * CAP + k] = e
    place = lax.rem(me[0], inner)
    tasks = []
    for target, group in zip(sent, wanted):
        for line in range(outer):
            for i, (t, k) in enumerate(group):
                n = len(tasks)
                e = owner[(line * inner + partner(place, t, inner)) * CAP + k]
                fetch = pltpu.make_async_copy(basis.at[e], held.at[n], in_sems.at[n])
                store = pltpu.make_async_copy(held.at[n], target.at[line, i], out_sems.at[n])
                tasks.append((fetch, store))
    for fetch, _ in tasks:
        fetch.start()
    for fetch, store in tasks:
        fetch.wait()
        store.start()
    for _, store in tasks:
        store.wait()


def pack(me, peers, basis, first, col_count, wanted):
    outer, _ = lines_of(col_count)
    entries = basis.shape[0]
    number = sum(len(group) for group in wanted) * outer
    return list(pl.pallas_call(
        functools.partial(pack_kernel, entries, col_count, wanted),
        out_shape=tuple(
            jax.ShapeDtypeStruct((outer, len(group)) + basis.shape[1:], basis.dtype)
            for group in wanted
        ),
        in_specs=[SMEM, SMEM, HBM, HBM],
        out_specs=(HBM,) * len(wanted),
        scratch_shapes=[
            pltpu.VMEM((number,) + basis.shape[1:], basis.dtype),
            pltpu.SMEM((col_count * CAP,), jnp.int32),
            pltpu.SMEM((col_count,), jnp.int32),
            pltpu.SemaphoreType.DMA((number,)),
            pltpu.SemaphoreType.DMA((number,)),
        ],
        compiler_params=pltpu.CompilerParams(vmem_limit_bytes=62 * MIB),
        name="pack",
    )(me, peers, basis, first))


def after(block, *others):
    return pl.pallas_call(
        lambda *refs: None,
        out_shape=jax.ShapeDtypeStruct(block.shape, block.dtype),
        in_specs=[HBM] + [ANY] * len(others),
        out_specs=HBM,
        input_output_aliases={0: 0},
        compiler_params=pltpu.CompilerParams(vmem_limit_bytes=MIB),
        name="after",
    )(block, *others)


def exchange(me, peers, basis, own, awaited):
    count = lax.axis_size("col")
    outer, inner = lines_of(count)
    groups = [[line * inner + place for line in range(outer)] for place in range(inner)]

    def between_lines(blocks, *others):
        block = jnp.concatenate(blocks, axis=1)
        return lax.all_to_all(
            after(block, *others), "col", split_axis=0, concat_axis=0,
            axis_index_groups=groups, tiled=True,
        )

    here = [(0, k) for k in range(CAP)]
    ahead = [[(t, 0)] for t in range(1, inner)]
    rest = [[(t, k)] for k in range(1, CAP) for t in range(1, inner)]
    sent = pack(me, peers, basis, own, count, ahead) if ahead else []
    to_lines, *later = pack(me, peers, basis, sent[0] if ahead else own, count, [here] + rest)
    swapped = {
        group[0]: swap_along(block, group[0][0]) for block, group in zip(sent + later, ahead + rest)
    }
    parts = [between_lines([to_lines], *awaited, *[swapped[group[0]] for group in ahead])]
    for t in range(1, inner):
        parts.append(between_lines([swapped[t, k] for k in range(CAP)], parts[-1]))
    return [part.reshape((outer * CAP,) + part.shape[2:]) for part in parts]


def gather_pieces(own):
    count = lax.axis_size("col")
    outer, inner = lines_of(count)
    me = lax.axis_index("col").astype(jnp.int32)
    a, b = me // inner, me % inner

    def move(block, ways):
        pairs = [(x * inner + y, z * inner + y) for x, z in ways for y in range(inner)]
        return lax.ppermute(block, "col", pairs)

    if outer == 4:
        middle, outwards = [(1, 2), (2, 1)], [(1, 0), (2, 3)]
        near = move(own, [(0, 1), (1, 0), (2, 3), (3, 2)])
        across = move(own, middle)
        far = move(near, middle)
        handed = move(across, outwards)
        last = move(far, outwards)
        within = (a == 1) | (a == 2)
        lines = [
            (own, a),
            (near, a ^ 1),
            (across + handed, jnp.where(within, a ^ 3, a ^ 2)),
            (far + last, jnp.where(within, a ^ 2, a ^ 3)),
        ]
        awaited = [far, handed]
    else:
        lines = [(own, a)] + [
            (move(own, [(x, partner(x, t, outer)) for x in range(outer)]), partner(a, -t, outer))
            for t in range(1, outer)
        ]
        awaited = [block for block, _ in lines[1:]]
    pieces, owners = [], []
    for block, line in lines:
        pieces.append(block)
        owners.append(line * inner + b)
        for t in range(1, inner):
            pieces.append(swap_along(block, t))
            owners.append(line * inner + partner(b, -t, inner))
    return pieces, jnp.stack(owners).astype(jnp.int32), awaited


def edge_kernel(col_count, depth, owners, *refs):
    pieces, (first, last, lists, sems, list_sems) = refs[:-5], refs[-5:]
    rows = pieces[0].shape[0] - LISTS
    held = rows // (2 * W)
    total = col_count * held

    def each(act):
        for i, piece in enumerate(pieces):
            for g in range(depth):
                for out, block, sem in ((first, g, 0), (last, total - depth + g, 1)):
                    source = piece.at[pl.ds(block % held * 2 * W, 2 * W)]
                    copy = pltpu.make_async_copy(source, out.at[g], sems.at[sem, g])

                    @pl.when(owners[i] == block // held)
                    def _():
                        act(copy)

            @pl.when(owners[i] >= 0)
            def _():
                act(pltpu.make_async_copy(
                    piece.at[pl.ds(rows, LISTS)], lists.at[owners[i]], list_sems.at[i]
                ))

    each(lambda copy: copy.start())
    each(lambda copy: copy.wait())


def edge_blocks(owners, pieces, col_count, depth):
    shape = jax.ShapeDtypeStruct((depth, 2 * W, W), pieces[0].dtype)
    return pl.pallas_call(
        functools.partial(edge_kernel, col_count, depth),
        out_shape=(shape, shape, jax.ShapeDtypeStruct((col_count, LISTS, W), pieces[0].dtype)),
        in_specs=[SMEM] + [HBM] * len(pieces),
        out_specs=(VMEM, VMEM, VMEM),
        scratch_shapes=[
            pltpu.SemaphoreType.DMA((2, depth)),
            pltpu.SemaphoreType.DMA((len(pieces),)),
        ],
        name="edge_blocks",
    )(owners, *pieces)


def cheb_kernel(blocks, coef, owners, v_low, v_mid, v_high, h_low, h_high, *refs):
    *pieces, out, vext, hraw, hcat, cheb_1, cheb_2, total, kern, sems, psems, osems = refs
    halo_v = DEG
    halo_h = DEG - 1
    held = (pieces[0].shape[0] - LISTS) // (2 * W)
    h_copies = [
        pltpu.make_async_copy(h_low, hraw.at[pl.ds(0, halo_h)], sems.at[0]),
        pltpu.make_async_copy(h_high, hraw.at[pl.ds(halo_h + blocks, halo_h)], sems.at[1]),
    ]
    v_copies = [
        pltpu.make_async_copy(v_low, vext.at[pl.ds(0, halo_v * W)], sems.at[2]),
        pltpu.make_async_copy(v_mid, vext.at[pl.ds(halo_v * W, blocks * W)], sems.at[3]),
        pltpu.make_async_copy(v_high, vext.at[pl.ds((halo_v + blocks) * W, halo_v * W)], sems.at[4]),
    ]

    def each_piece(act):
        for i, piece in enumerate(pieces):
            @pl.when(owners[i] >= 0)
            def _():
                for k in range(held):
                    act(pltpu.make_async_copy(
                        piece.at[pl.ds(k * 2 * W, 2 * W)],
                        hraw.at[halo_h + owners[i] * held + k],
                        psems.at[i, k],
                    ))

    each_piece(lambda copy: copy.start())
    for copy in h_copies + v_copies:
        copy.start()
    each_piece(lambda copy: copy.wait())
    for copy in h_copies:
        copy.wait()
    rows = lax.broadcasted_iota(jnp.int32, (W, W), 0)
    cols = lax.broadcasted_iota(jnp.int32, (W, W), 1)
    upper = jnp.where(rows <= cols, 1.0, 0.0).astype(jnp.bfloat16)

    def build(j, carry):
        coupling = hraw[j, W:]
        lower_band = coupling * upper
        hcat[j, :, 0:W] = lower_band
        hcat[j, :, W : 2 * W] = hraw[j, :W]
        hcat[j, :, 2 * W : 3 * W] = coupling - lower_band
        return carry

    lax.fori_loop(0, blocks + 2 * halo_h, build, 0, unroll=2)
    for copy in v_copies:
        copy.wait()

    def rows_of(j, count=1):
        return pl.ds(pl.multiple_of(j * W, W), count * W)

    def band(source, j, row):
        return jnp.dot(hcat[j], source[rows_of(row, 3), :], preferred_element_type=jnp.float32)

    def first(j, carry):
        value = band(vext, j, j)
        cheb_1[rows_of(j), :] = value.astype(jnp.bfloat16)
        total[rows_of(j), :] = value
        return carry

    lax.fori_loop(0, blocks + 4, first, 0, unroll=2)

    def second(j, carry):
        begin = vext[rows_of(j + 2), :].astype(jnp.float32)
        value = 2.0 * band(cheb_1, j + 1, j) - begin
        cheb_2[rows_of(j), :] = value.astype(jnp.bfloat16)
        total[rows_of(j + 1), :] = (
            coef[0] * begin + (coef[1] - coef[3]) * total[rows_of(j + 1), :] + coef[2] * value
        )
        return carry

    lax.fori_loop(0, blocks + 2, second, 0, unroll=2)

    def store(j):
        return pltpu.make_async_copy(kern.at[j], out.at[j], osems.at[j])

    def third(j, carry):
        for half in range(KB // W):
            i = j * (KB // W) + half
            value = total[rows_of(i + 2), :] + (2.0 * coef[3]) * band(cheb_2, i + 2, i)
            kern[j, :, half * W : (half + 1) * W] = value.astype(jnp.bfloat16).T
        store(j).start()
        return carry

    lax.fori_loop(0, blocks // (KB // W), third, 0)
    for j in range(blocks // (KB // W)):
        store(j).wait()


def chebyshev(coefficients, owners, v_low, v_mid, v_high, h_low, h_high, pieces):
    blocks = v_mid.shape[0] // W
    cols = v_mid.shape[1]
    ext = blocks + 2 * (DEG - 1)
    flops = 2 * W * 3 * W * cols * (3 * blocks + 6)
    result = (blocks * W // KB, cols, KB)
    held = (pieces[0].shape[0] - LISTS) // (2 * W)
    return pl.pallas_call(
        functools.partial(cheb_kernel, blocks),
        out_shape=jax.ShapeDtypeStruct(result, jnp.bfloat16),
        in_specs=[SMEM] * 2 + [ANY] * (5 + len(pieces)),
        out_specs=HBM,
        scratch_shapes=[
            pltpu.VMEM(((blocks + 2 * DEG) * W, cols), jnp.bfloat16),
            pltpu.VMEM((ext, 2 * W, W), jnp.bfloat16),
            pltpu.VMEM((ext, W, 3 * W), jnp.bfloat16),
            pltpu.VMEM((ext * W, cols), jnp.bfloat16),
            pltpu.VMEM(((blocks + 2) * W, cols), jnp.bfloat16),
            pltpu.VMEM((ext * W, cols), jnp.float32),
            pltpu.VMEM(result, jnp.bfloat16),
            pltpu.SemaphoreType.DMA((5,)),
            pltpu.SemaphoreType.DMA((len(pieces), held)),
            pltpu.SemaphoreType.DMA((result[0],)),
        ],
        compiler_params=pltpu.CompilerParams(vmem_limit_bytes=48 * MIB),
        cost_estimate=pl.CostEstimate(flops=flops, bytes_accessed=16 * MIB, transcendentals=0),
        name="chebyshev",
    )(coefficients, owners, v_low, v_mid, v_high, h_low, h_high, *pieces)


def entry_loads(order, parts, pair, sems):
    size = parts[0].shape[0]

    def load(p):
        return pltpu.make_async_copy(parts[0].at[0], pair.at[p], sems.at[p])

    def start(p, carry):
        n = order[p]
        for t, part in enumerate(parts):
            @pl.when((n >= t * size) & (n < (t + 1) * size))
            def _():
                pltpu.make_async_copy(part.at[n - t * size], pair.at[p], sems.at[p]).start()

        return carry

    return load, start


def by_twos(first, last, load, body):
    def step(i, carry):
        p = first + 2 * i
        q = jnp.minimum(p + 1, last - 1)
        load(p).wait()

        @pl.when(q > p)
        def _():
            load(q).wait()

        body(i, p, q)
        return carry

    lax.fori_loop(0, (last - first + 1) // 2, step, 0)


def sent_rows(slots, tiles):
    return slots + tiles + -(slots + tiles) % 8


def project_kernel(blocks, plan, order, kernel_t, core, *refs):
    *parts, out, kern, pair, rows, ksems, bsems = refs
    slots = pair.shape[0]
    load, start = entry_loads(order, parts, pair, bsems)

    def fetch(b):
        return pltpu.make_async_copy(kernel_t.at[b], kern.at[b], ksems.at[b])

    def begin(b, carry):
        first, last = plan[slots + b], plan[slots + b + 1]

        @pl.when(first < last)
        def _():
            fetch(b).start()

        return lax.fori_loop(first, last, start, carry)

    lax.fori_loop(0, blocks, begin, 0)
    rows[...] = jnp.zeros_like(rows)
    rows[slots : slots + core.shape[0]] = core[...]

    def step(b, carry):
        first, last = plan[slots + b], plan[slots + b + 1]

        @pl.when(first < last)
        def _():
            fetch(b).wait()

        def body(i, p, q):
            both = jnp.concatenate([pair[p, 0], pair[q, 0]], axis=1)
            projected = jnp.dot(kern[b], both, preferred_element_type=jnp.float32)
            other = jnp.concatenate([pair[p, 1], pair[q, 1]], axis=1).astype(jnp.float32)
            value = jnp.sum(projected * other, axis=0, keepdims=True) * (1.0 / KB)
            rows[pl.ds(order[p], 1), :] = value[:, :P_SIZE]
            rows[pl.ds(order[q], 1), :] = value[:, P_SIZE:]

        by_twos(first, last, load, body)
        return carry

    lax.fori_loop(0, blocks, step, 0)
    for c in range(out.shape[0]):
        out[c] = rows[...]


def project(plan, order, kernel_t, core, parts, col_count):
    slots = col_count * CAP
    entry = parts[0].shape[1:]
    sent = sent_rows(slots, core.shape[0])
    blocks = kernel_t.shape[0]
    return pl.pallas_call(
        functools.partial(project_kernel, blocks),
        out_shape=jax.ShapeDtypeStruct((col_count, sent, P_SIZE), jnp.float32),
        in_specs=[SMEM, SMEM, HBM, VMEM] + [HBM] * len(parts),
        out_specs=VMEM,
        scratch_shapes=[
            pltpu.VMEM(kernel_t.shape, jnp.bfloat16),
            pltpu.VMEM((slots,) + entry, jnp.bfloat16),
            pltpu.VMEM((sent, P_SIZE), jnp.float32),
            pltpu.SemaphoreType.DMA((blocks,)),
            pltpu.SemaphoreType.DMA((slots,)),
        ],
        compiler_params=pltpu.CompilerParams(vmem_limit_bytes=20 * MIB),
        name="project",
    )(plan, order, kernel_t, core, *parts)


def update_kernel(
    blocks, tiles, plan, order, tile_of, contributions, collect, *refs
):
    *parts, density_out, update_out, pair, density, potential, acc, stage, sems, osems = refs
    slots = pair.shape[0]
    live = plan[slots + blocks]
    me = plan[slots + blocks + 1]
    load, start = entry_loads(order, parts, pair, sems)
    lax.fori_loop(0, live, start, 0)
    density[...] = jnp.dot(
        collect[...],
        contributions[...],
        preferred_element_type=jnp.float32,
        precision=lax.Precision.HIGHEST,
    )
    for t in range(tiles):
        density_out[pl.ds(t, 1), :] = density[pl.ds(me * tiles + t, 1), :]
    positive = jnp.maximum(density[...], 0.1)
    root = jnp.exp(jnp.log(positive) * (1.0 / 3.0))
    root = root - (root - positive / (root * root)) * (1.0 / 3.0)
    potential[...] = -exchange_factor * root
    scale = 1.0 / math.sqrt(P_SIZE)

    def store(b):
        rows = pl.ds(pl.multiple_of(b * KB, KB), KB)
        return pltpu.make_async_copy(stage.at[b], update_out.at[rows], osems.at[b])

    def step(b, carry):
        first, last = plan[slots + b], plan[slots + b + 1]

        @pl.when(first == last)
        def _():
            stage[b] = jnp.zeros(stage.shape[1:], jnp.bfloat16)

        def body(i, p, q):
            weight_p = potential[pl.ds(tile_of[order[p]], 1), :]
            weight_q = potential[pl.ds(tile_of[order[q]], 1), :] * (q - p).astype(jnp.float32)
            weighted = jnp.concatenate(
                [
                    (pair[p, 1].astype(jnp.float32) * weight_p).astype(jnp.bfloat16),
                    (pair[q, 1].astype(jnp.float32) * weight_q).astype(jnp.bfloat16),
                ],
                axis=1,
            )
            block = lax.dot_general(
                jnp.concatenate([pair[p, 0], pair[q, 0]], axis=1),
                weighted,
                (((1,), (1,)), ((), ())),
                preferred_element_type=jnp.float32,
            )

            @pl.when(last - first <= 2)
            def _():
                stage[b] = (block * scale).astype(jnp.bfloat16)

            @pl.when((last - first > 2) & (i == 0))
            def _():
                acc[...] = block

            @pl.when(i > 0)
            def _():
                acc[...] += block

        by_twos(first, last, load, body)

        @pl.when(last - first > 2)
        def _():
            stage[b] = (acc[...] * scale).astype(jnp.bfloat16)

        store(b).start()
        return carry

    lax.fori_loop(0, blocks, step, 0)
    for b in range(blocks):
        store(b).wait()


def update(plan, order, tile_of, contributions, collect, parts, tiles, blocks, cols):
    slots = len(parts) * parts[0].shape[0]
    entry = parts[0].shape[1:]
    all_tiles = (collect.shape[0], P_SIZE)
    return pl.pallas_call(
        functools.partial(update_kernel, blocks, tiles),
        out_shape=(
            jax.ShapeDtypeStruct((tiles, P_SIZE), jnp.float32),
            jax.ShapeDtypeStruct((blocks * KB, cols), jnp.bfloat16),
        ),
        in_specs=[SMEM] * 3 + [VMEM] * 2 + [HBM] * len(parts),
        out_specs=(VMEM, HBM),
        scratch_shapes=[
            pltpu.VMEM((slots,) + entry, jnp.bfloat16),
            pltpu.VMEM(all_tiles, jnp.float32),
            pltpu.VMEM(all_tiles, jnp.float32),
            pltpu.VMEM((KB, cols), jnp.float32),
            pltpu.VMEM((blocks, KB, cols), jnp.bfloat16),
            pltpu.SemaphoreType.DMA((slots,)),
            pltpu.SemaphoreType.DMA((blocks,)),
        ],
        compiler_params=pltpu.CompilerParams(vmem_limit_bytes=24 * MIB),
        name="update",
    )(plan, order, tile_of, contributions, collect, *parts)


def shift(block, axis, step):
    count = lax.axis_size(axis)
    pairs = [(i, i + step) for i in range(count) if 0 <= i + step < count]
    return lax.ppermute(block, axis, pairs)


def make_plan(lists, me, entries, tiles, col_count, blocks):
    slots = col_count * CAP
    sent = sent_rows(slots, tiles)
    lists = lists[:, : 2 * entries + tiles].astype(jnp.int32)
    peers, named, counts = lists[:, :entries], lists[:, entries : 2 * entries], lists[:, 2 * entries :]
    index = jnp.arange(entries, dtype=jnp.int32)
    home = jnp.arange(col_count, dtype=jnp.int32)[:, None]
    earlier = (peers[:, :, None] == peers[:, None, :]) & (index[None, :] < index[:, None])
    rank = jnp.sum(earlier.astype(jnp.int32), axis=2)
    live = (index % SLOTS)[None, :] < jnp.repeat(counts, SLOTS, axis=1)
    row = jnp.where(live, peers * sent + chunk_of(home, peers, col_count) * CAP + rank, -1).reshape(col_count, tiles, SLOTS)
    core = (home * sent + slots + jnp.arange(tiles, dtype=jnp.int32))[:, :, None]
    row = jnp.concatenate([row, core], axis=2).reshape(col_count * tiles, SLOTS + 1, 1)
    picked = row == jnp.arange(col_count * sent, dtype=jnp.int32)
    collect = jnp.sum(picked.astype(jnp.float32), axis=1)
    hit = (
        (peers == me)[:, None, :]
        & (rank[:, None, :] == jnp.arange(CAP, dtype=jnp.int32)[None, :, None])
        & live[:, None, :]
    )
    at_me = chunk_of(home, me, col_count).reshape(1, col_count) == home
    tile = home * tiles + index[None, :] // SLOTS

    def of_slots(values):
        by_home = jnp.sum(jnp.where(hit, values[:, None, :], 0), axis=2)
        return jnp.sum(jnp.where(at_me[:, :, None], by_home[None], 0), axis=1).reshape(slots)

    wanted = of_slots(named + 1) - 1
    tile_of = of_slots(tile)
    key = jnp.where(wanted < 0, blocks, wanted)
    place = jnp.arange(slots, dtype=jnp.int32)
    before = (key[None, :] < key[:, None]) | (
        (key[None, :] == key[:, None]) & (place[None, :] < place[:, None])
    )
    spot = jnp.sum(before.astype(jnp.int32), axis=1)
    order = jnp.sum(jnp.where(spot[None, :] == place[:, None], place[None, :], 0), axis=1)
    starts = jnp.sum(
        (key[None, :] < jnp.arange(blocks + 1, dtype=jnp.int32)[:, None]).astype(jnp.int32), axis=1
    )
    plan = jnp.concatenate([wanted, starts, me[None]]).astype(jnp.int32)
    return collect, plan, order.astype(jnp.int32), tile_of.astype(jnp.int32)


def shards(
    start_columns,
    hamiltonian,
    band_pattern,
    coefficients,
    tile_peer,
    tile_block,
    tile_count,
    basis_values,
    core_density,
):
    col_count = lax.axis_size("col")
    entries = tile_peer.shape[0]
    tiles = core_density.shape[0]
    cols = start_columns.shape[1]
    blocks = start_columns.shape[0] // KB
    peers = tile_peer[:, 0]
    me = lax.axis_index("col").astype(jnp.int32)

    own = own_piece(peers, tile_block, tile_count, band_pattern, hamiltonian.reshape(-1, W))
    pieces, owners, awaited = gather_pieces(own)
    v_low = shift(start_columns[-DEG * W :], "row", 1)
    v_high = shift(start_columns[: DEG * W], "row", -1)
    parts = exchange(me[None], peers, basis_values, own, awaited + [v_low, v_high])

    first, last, lists = edge_blocks(owners, pieces, col_count, DEG - 1)
    h_low = shift(last, "row", 1)
    h_high = shift(first, "row", -1)
    kernel_t = chebyshev(
        coefficients, owners, v_low, start_columns, v_high, h_low, h_high, pieces
    )
    collect, plan, order, tile_of = make_plan(lists[:, 0], me, entries, tiles, col_count, blocks)
    partial = project(plan, order, kernel_t, core_density, parts, col_count)
    contributions = lax.all_to_all(partial, "col", split_axis=0, concat_axis=0, tiled=True)
    contributions = contributions.reshape(-1, P_SIZE)
    return update(
        plan, order, tile_of, contributions, collect, parts, tiles, blocks, cols
    )


def solution(mesh):
    return jax.shard_map(
        shards,
        mesh=mesh,
        in_specs=(
            P("row", "col"),
            P(("row", "col"), None, None, None),
            P(("row", "col")),
            P(),
            P(("row", "col"), None),
            P(("row", "col")),
            P(("row", "col")),
            P(("row", "col"), None, None, None),
            P(("row", "col"), None),
        ),
        out_specs=(P(("row", "col"), None), P("row", "col")),
        check_vma=False,
    )
```

```python
import functools
import math

import jax
import jax.numpy as jnp
from jax import lax
from jax.experimental import pallas as pl
from jax.experimental.pallas import tpu as pltpu
from jax.sharding import PartitionSpec as P

W = 256
KB = 512
DEG = 3
SLOTS = 4
CAP = 2
P_SIZE = 128
MIB = 1 << 20
LISTS = 16

exchange_factor = (3.0 / math.pi) ** (1.0 / 3.0)
HBM = pl.BlockSpec(memory_space=pltpu.HBM)
ANY = pl.BlockSpec(memory_space=pl.ANY)
SMEM = pl.BlockSpec(memory_space=pltpu.SMEM)
VMEM = pl.BlockSpec(memory_space=pltpu.VMEM)


def partner(me, j, count):
    if count & (count - 1) == 0:
        return me ^ abs(j)
    return (me + j) % count


def piece_kernel(peers, named, counts, pattern, ham, piece, blocks, sems):
    rows = ham.shape[0]
    load = pltpu.make_async_copy(ham, blocks.at[pl.ds(0, rows)], sems.at[0])
    load.start()
    lane = lax.broadcasted_iota(jnp.int32, (LISTS, W), 1)
    lists = jnp.zeros((LISTS, W), jnp.int32)
    at = 0
    for ref in (peers, named, counts):
        for i in range(ref.shape[0]):
            lists = jnp.where(lane == at, ref[i], lists)
            at += 1
    blocks[rows:] = lists.astype(jnp.float32).astype(jnp.bfloat16)
    load.wait()
    for i in range(rows // (2 * W)):
        coupling = slice((2 * i + 1) * W, (2 * i + 2) * W)
        blocks[coupling] = blocks[coupling] * pattern[i].astype(jnp.bfloat16)
    store = pltpu.make_async_copy(blocks, piece, sems.at[1])
    store.start()
    store.wait()


def own_piece(peers, named, counts, pattern, ham):
    piece = (ham.shape[0] + LISTS, W)
    return pl.pallas_call(
        piece_kernel,
        out_shape=jax.ShapeDtypeStruct(piece, ham.dtype),
        in_specs=[SMEM] * 4 + [HBM],
        out_specs=HBM,
        scratch_shapes=[pltpu.VMEM(piece, ham.dtype), pltpu.SemaphoreType.DMA((2,))],
        compiler_params=pltpu.CompilerParams(vmem_limit_bytes=62 * MIB),
        name="own_piece",
    )(peers, named, counts, pattern, ham)


def lines_of(count):
    inner = max(count // 4, 1) if count & (count - 1) == 0 else 1
    return count // inner, inner


def swap_along(block, t):
    count = lax.axis_size("col")
    _, inner = lines_of(count)
    pairs = [(c, c - c % inner + partner(c % inner, t, inner)) for c in range(count)]
    return lax.ppermute(block, "col", pairs)


def chunk_of(home, owner, count):
    outer, inner = lines_of(count)
    return partner(home % inner, owner % inner, inner) * outer + home // inner


def pack_kernel(entries, col_count, wanted, me, peers, basis, first, *refs):
    outer, inner = lines_of(col_count)
    sent, (held, owner, count, in_sems, out_sems) = refs[: len(wanted)], refs[len(wanted) :]
    for c in range(col_count):
        count[c] = 0
        for k in range(CAP):
            owner[c * CAP + k] = 0
    for e in range(entries):
        p = peers[e]
        k = count[p]
        count[p] = k + 1
        owner[p * CAP + k] = e
    place = lax.rem(me[0], inner)
    tasks = []
    for target, group in zip(sent, wanted):
        for line in range(outer):
            for i, (t, k) in enumerate(group):
                n = len(tasks)
                e = owner[(line * inner + partner(place, t, inner)) * CAP + k]
                fetch = pltpu.make_async_copy(basis.at[e], held.at[n], in_sems.at[n])
                store = pltpu.make_async_copy(held.at[n], target.at[line, i], out_sems.at[n])
                tasks.append((fetch, store))
    for fetch, _ in tasks:
        fetch.start()
    for fetch, store in tasks:
        fetch.wait()
        store.start()
    for _, store in tasks:
        store.wait()


def pack(me, peers, basis, first, col_count, wanted, spare=0):
    outer, _ = lines_of(col_count)
    entries = basis.shape[0]
    number = sum(len(group) for group in wanted) * outer
    return list(pl.pallas_call(
        functools.partial(pack_kernel, entries, col_count, wanted),
        out_shape=tuple(
            jax.ShapeDtypeStruct(
                (outer, len(group) + (spare if i == 0 else 0)) + basis.shape[1:], basis.dtype
            )
            for i, group in enumerate(wanted)
        ),
        in_specs=[SMEM, SMEM, HBM, HBM],
        out_specs=(HBM,) * len(wanted),
        scratch_shapes=[
            pltpu.VMEM((number,) + basis.shape[1:], basis.dtype),
            pltpu.SMEM((col_count * CAP,), jnp.int32),
            pltpu.SMEM((col_count,), jnp.int32),
            pltpu.SemaphoreType.DMA((number,)),
            pltpu.SemaphoreType.DMA((number,)),
        ],
        compiler_params=pltpu.CompilerParams(vmem_limit_bytes=62 * MIB),
        name="pack",
    )(me, peers, basis, first))


def join_kernel(fills, block, *refs):
    sources, (out, held, in_sems, out_sems) = refs[:fills], refs[-4:]
    units = out.shape[1]
    loads = [pltpu.make_async_copy(sources[i], held.at[i], in_sems.at[i]) for i in range(fills)]
    stores = [
        pltpu.make_async_copy(held.at[i], out.at[:, pl.ds(units - fills + i, 1)], out_sems.at[i])
        for i in range(fills)
    ]
    for load in loads:
        load.start()
    for load, store in zip(loads, stores):
        load.wait()
        store.start()
    for store in stores:
        store.wait()


def join(block, fills, *others):
    return pl.pallas_call(
        functools.partial(join_kernel, len(fills)),
        out_shape=jax.ShapeDtypeStruct(block.shape, block.dtype),
        in_specs=[HBM] + [ANY] * (len(fills) + len(others)),
        out_specs=HBM,
        input_output_aliases={0: 0},
        scratch_shapes=[
            pltpu.VMEM((max(len(fills), 1), block.shape[0], 1) + block.shape[2:], block.dtype),
            pltpu.SemaphoreType.DMA((max(len(fills), 1),)),
            pltpu.SemaphoreType.DMA((max(len(fills), 1),)),
        ],
        compiler_params=pltpu.CompilerParams(vmem_limit_bytes=62 * MIB),
        name="join",
    )(block, *fills, *others)


def unit_of(t, k, inner):
    if t == 0:
        return 0, k
    return (0, CAP + t - 1) if k == 0 else (1, (k - 1) * (inner - 1) + t - 1)


def exchange(me, peers, basis, own, awaited, handed):
    count = lax.axis_size("col")
    outer, inner = lines_of(count)
    groups = [[line * inner + place for line in range(outer)] for place in range(inner)]

    def between_lines(block):
        return lax.all_to_all(
            block, "col", split_axis=0, concat_axis=0, axis_index_groups=groups, tiled=True
        )

    here = [(0, k) for k in range(CAP)]
    ahead = [[(t, 0)] for t in range(1, inner)]
    rest = [[(t, k)] for k in range(1, CAP) for t in range(1, inner)]
    sent = pack(me, peers, basis, own, count, ahead) if ahead else []
    first, *later = pack(
        me, peers, basis, sent[0] if ahead else own, count, [here] + rest, spare=len(ahead)
    )
    swapped = [swap_along(block, group[0][0]) for block, group in zip(sent, ahead)]
    parts = [between_lines(join(first, swapped, *awaited))]
    if rest:
        swapped = [
            swap_along(join(block, [], *handed), group[0][0]) for block, group in zip(later, rest)
        ]
        last = swapped[0] if len(swapped) == 1 else jnp.concatenate(swapped, axis=1)
        parts.append(between_lines(join(last, [], parts[0])))
    return parts


def gather_pieces(own):
    count = lax.axis_size("col")
    outer, inner = lines_of(count)
    me = lax.axis_index("col").astype(jnp.int32)
    a, b = me // inner, me % inner

    def move(block, ways):
        pairs = [(x * inner + y, z * inner + y) for x, z in ways for y in range(inner)]
        return lax.ppermute(block, "col", pairs)

    if outer == 4:
        middle, outwards = [(1, 2), (2, 1)], [(1, 0), (2, 3)]
        near = move(own, [(0, 1), (1, 0), (2, 3), (3, 2)])
        across = move(own, middle)
        far = move(near, middle)
        handed = move(across, outwards)
        last = move(far, outwards)
        within = (a == 1) | (a == 2)
        lines = [
            (own, a),
            (near, a ^ 1),
            (across + handed, jnp.where(within, a ^ 3, a ^ 2)),
            (far + last, jnp.where(within, a ^ 2, a ^ 3)),
        ]
        awaited, end = [far, handed], [last]
    else:
        lines = [(own, a)] + [
            (move(own, [(x, partner(x, t, outer)) for x in range(outer)]), partner(a, -t, outer))
            for t in range(1, outer)
        ]
        awaited, end = [block for block, _ in lines[1:]], []
    pieces, owners = [], []
    for block, line in lines:
        pieces.append(block)
        owners.append(line * inner + b)
        for t in range(1, inner):
            pieces.append(swap_along(block, t))
            owners.append(line * inner + partner(b, -t, inner))
    return pieces, jnp.stack(owners).astype(jnp.int32), awaited, end


def edge_kernel(col_count, depth, owners, *refs):
    pieces, (first, last, lists, sems, list_sems) = refs[:-5], refs[-5:]
    rows = pieces[0].shape[0] - LISTS
    held = rows // (2 * W)
    total = col_count * held

    def each(act):
        for i, piece in enumerate(pieces):
            for g in range(depth):
                for out, block, sem in ((first, g, 0), (last, total - depth + g, 1)):
                    source = piece.at[pl.ds(block % held * 2 * W, 2 * W)]
                    copy = pltpu.make_async_copy(source, out.at[g], sems.at[sem, g])

                    @pl.when(owners[i] == block // held)
                    def _():
                        act(copy)

            @pl.when(owners[i] >= 0)
            def _():
                act(pltpu.make_async_copy(
                    piece.at[pl.ds(rows, LISTS)], lists.at[owners[i]], list_sems.at[i]
                ))

    each(lambda copy: copy.start())
    each(lambda copy: copy.wait())


def edge_blocks(owners, pieces, col_count, depth):
    shape = jax.ShapeDtypeStruct((depth, 2 * W, W), pieces[0].dtype)
    return pl.pallas_call(
        functools.partial(edge_kernel, col_count, depth),
        out_shape=(shape, shape, jax.ShapeDtypeStruct((col_count, LISTS, W), pieces[0].dtype)),
        in_specs=[SMEM] + [HBM] * len(pieces),
        out_specs=(VMEM, VMEM, VMEM),
        scratch_shapes=[
            pltpu.SemaphoreType.DMA((2, depth)),
            pltpu.SemaphoreType.DMA((len(pieces),)),
        ],
        name="edge_blocks",
    )(owners, *pieces)


def cheb_kernel(blocks, coef, owners, v_low, v_mid, v_high, h_low, h_high, *refs):
    *pieces, out, vext, hraw, hcat, cheb_1, cheb_2, total, kern, sems, psems, osems = refs
    halo_v = DEG
    halo_h = DEG - 1
    held = (pieces[0].shape[0] - LISTS) // (2 * W)
    h_copies = [
        pltpu.make_async_copy(h_low, hraw.at[pl.ds(0, halo_h)], sems.at[0]),
        pltpu.make_async_copy(h_high, hraw.at[pl.ds(halo_h + blocks, halo_h)], sems.at[1]),
    ]
    v_copies = [
        pltpu.make_async_copy(v_low, vext.at[pl.ds(0, halo_v * W)], sems.at[2]),
        pltpu.make_async_copy(v_mid, vext.at[pl.ds(halo_v * W, blocks * W)], sems.at[3]),
        pltpu.make_async_copy(v_high, vext.at[pl.ds((halo_v + blocks) * W, halo_v * W)], sems.at[4]),
    ]

    def each_piece(act):
        for i, piece in enumerate(pieces):
            @pl.when(owners[i] >= 0)
            def _():
                for k in range(held):
                    act(pltpu.make_async_copy(
                        piece.at[pl.ds(k * 2 * W, 2 * W)],
                        hraw.at[halo_h + owners[i] * held + k],
                        psems.at[i, k],
                    ))

    each_piece(lambda copy: copy.start())
    for copy in h_copies + v_copies:
        copy.start()
    each_piece(lambda copy: copy.wait())
    for copy in h_copies:
        copy.wait()
    rows = lax.broadcasted_iota(jnp.int32, (W, W), 0)
    cols = lax.broadcasted_iota(jnp.int32, (W, W), 1)
    upper = jnp.where(rows <= cols, 1.0, 0.0).astype(jnp.bfloat16)

    def build(j, carry):
        coupling = hraw[j, W:]
        lower_band = coupling * upper
        hcat[j, :, 0:W] = lower_band
        hcat[j, :, W : 2 * W] = hraw[j, :W]
        hcat[j, :, 2 * W : 3 * W] = coupling - lower_band
        return carry

    lax.fori_loop(0, blocks + 2 * halo_h, build, 0, unroll=2)
    for copy in v_copies:
        copy.wait()

    def rows_of(j, count=1):
        return pl.ds(pl.multiple_of(j * W, W), count * W)

    def band(source, j, row):
        return jnp.dot(hcat[j], source[rows_of(row, 3), :], preferred_element_type=jnp.float32)

    def first(j, carry):
        value = band(vext, j, j)
        cheb_1[rows_of(j), :] = value.astype(jnp.bfloat16)
        total[rows_of(j), :] = value
        return carry

    lax.fori_loop(0, blocks + 4, first, 0, unroll=2)

    def second(j, carry):
        begin = vext[rows_of(j + 2), :].astype(jnp.float32)
        value = 2.0 * band(cheb_1, j + 1, j) - begin
        cheb_2[rows_of(j), :] = value.astype(jnp.bfloat16)
        total[rows_of(j + 1), :] = (
            coef[0] * begin + (coef[1] - coef[3]) * total[rows_of(j + 1), :] + coef[2] * value
        )
        return carry

    lax.fori_loop(0, blocks + 2, second, 0, unroll=2)

    def store(j):
        return pltpu.make_async_copy(kern.at[j], out.at[j], osems.at[j])

    def third(j, carry):
        for half in range(KB // W):
            i = j * (KB // W) + half
            value = total[rows_of(i + 2), :] + (2.0 * coef[3]) * band(cheb_2, i + 2, i)
            kern[j, :, half * W : (half + 1) * W] = value.astype(jnp.bfloat16).T
        store(j).start()
        return carry

    lax.fori_loop(0, blocks // (KB // W), third, 0)
    for j in range(blocks // (KB // W)):
        store(j).wait()


def chebyshev(coefficients, owners, v_low, v_mid, v_high, h_low, h_high, pieces):
    blocks = v_mid.shape[0] // W
    cols = v_mid.shape[1]
    ext = blocks + 2 * (DEG - 1)
    flops = 2 * W * 3 * W * cols * (3 * blocks + 6)
    result = (blocks * W // KB, cols, KB)
    held = (pieces[0].shape[0] - LISTS) // (2 * W)
    return pl.pallas_call(
        functools.partial(cheb_kernel, blocks),
        out_shape=jax.ShapeDtypeStruct(result, jnp.bfloat16),
        in_specs=[SMEM] * 2 + [ANY] * (5 + len(pieces)),
        out_specs=HBM,
        scratch_shapes=[
            pltpu.VMEM(((blocks + 2 * DEG) * W, cols), jnp.bfloat16),
            pltpu.VMEM((ext, 2 * W, W), jnp.bfloat16),
            pltpu.VMEM((ext, W, 3 * W), jnp.bfloat16),
            pltpu.VMEM((ext * W, cols), jnp.bfloat16),
            pltpu.VMEM(((blocks + 2) * W, cols), jnp.bfloat16),
            pltpu.VMEM((ext * W, cols), jnp.float32),
            pltpu.VMEM(result, jnp.bfloat16),
            pltpu.SemaphoreType.DMA((5,)),
            pltpu.SemaphoreType.DMA((len(pieces), held)),
            pltpu.SemaphoreType.DMA((result[0],)),
        ],
        compiler_params=pltpu.CompilerParams(vmem_limit_bytes=48 * MIB),
        cost_estimate=pl.CostEstimate(flops=flops, bytes_accessed=16 * MIB, transcendentals=0),
        name="chebyshev",
    )(coefficients, owners, v_low, v_mid, v_high, h_low, h_high, *pieces)


def entry_loads(order, parts, pair, sems):
    outer, units = parts[0].shape[:2]
    inner = units - CAP + 1

    def load(p):
        return pltpu.make_async_copy(parts[0].at[0, 0], pair.at[p], sems.at[p])

    def start(p, carry):
        n = order[p]
        line = lax.rem(lax.div(n, CAP), outer)
        for t in range(inner):
            for k in range(CAP):
                part, unit = unit_of(t, k, inner)

                @pl.when((lax.div(n, CAP * outer) == t) & (lax.rem(n, CAP) == k))
                def _():
                    source = parts[part].at[line, unit]
                    pltpu.make_async_copy(source, pair.at[p], sems.at[p]).start()

        return carry

    return load, start


def by_twos(first, last, load, body):
    def step(i, carry):
        p = first + 2 * i
        q = jnp.minimum(p + 1, last - 1)
        load(p).wait()

        @pl.when(q > p)
        def _():
            load(q).wait()

        body(i, p, q)
        return carry

    lax.fori_loop(0, (last - first + 1) // 2, step, 0)


def sent_rows(slots, tiles):
    return slots + tiles + -(slots + tiles) % 8


def project_kernel(blocks, plan, order, kernel_t, core, *refs):
    *parts, out, kern, pair, rows, ksems, bsems = refs
    slots = pair.shape[0]
    load, start = entry_loads(order, parts, pair, bsems)

    def fetch(b):
        return pltpu.make_async_copy(kernel_t.at[b], kern.at[b], ksems.at[b])

    def begin(b, carry):
        first, last = plan[slots + b], plan[slots + b + 1]

        @pl.when(first < last)
        def _():
            fetch(b).start()

        return lax.fori_loop(first, last, start, carry)

    lax.fori_loop(0, blocks, begin, 0)
    rows[...] = jnp.zeros_like(rows)
    rows[slots : slots + core.shape[0]] = core[...]

    def step(b, carry):
        first, last = plan[slots + b], plan[slots + b + 1]

        @pl.when(first < last)
        def _():
            fetch(b).wait()

        def body(i, p, q):
            both = jnp.concatenate([pair[p, 0], pair[q, 0]], axis=1)
            projected = jnp.dot(kern[b], both, preferred_element_type=jnp.float32)
            other = jnp.concatenate([pair[p, 1], pair[q, 1]], axis=1).astype(jnp.float32)
            value = jnp.sum(projected * other, axis=0, keepdims=True) * (1.0 / KB)
            rows[pl.ds(order[p], 1), :] = value[:, :P_SIZE]
            rows[pl.ds(order[q], 1), :] = value[:, P_SIZE:]

        by_twos(first, last, load, body)
        return carry

    lax.fori_loop(0, blocks, step, 0)
    for c in range(out.shape[0]):
        out[c] = rows[...]


def project(plan, order, kernel_t, core, parts, col_count):
    slots = col_count * CAP
    entry = parts[0].shape[2:]
    sent = sent_rows(slots, core.shape[0])
    blocks = kernel_t.shape[0]
    return pl.pallas_call(
        functools.partial(project_kernel, blocks),
        out_shape=jax.ShapeDtypeStruct((col_count, sent, P_SIZE), jnp.float32),
        in_specs=[SMEM, SMEM, HBM, VMEM] + [HBM] * len(parts),
        out_specs=VMEM,
        scratch_shapes=[
            pltpu.VMEM(kernel_t.shape, jnp.bfloat16),
            pltpu.VMEM((slots,) + entry, jnp.bfloat16),
            pltpu.VMEM((sent, P_SIZE), jnp.float32),
            pltpu.SemaphoreType.DMA((blocks,)),
            pltpu.SemaphoreType.DMA((slots,)),
        ],
        compiler_params=pltpu.CompilerParams(vmem_limit_bytes=62 * MIB),
        name="project",
    )(plan, order, kernel_t, core, *parts)


def update_kernel(
    blocks, tiles, plan, order, tile_of, contributions, collect, *refs
):
    *parts, density_out, update_out, pair, density, potential, acc, stage, sems, osems = refs
    slots = pair.shape[0]
    live = plan[slots + blocks]
    me = plan[slots + blocks + 1]
    load, start = entry_loads(order, parts, pair, sems)
    lax.fori_loop(0, live, start, 0)
    density[...] = jnp.dot(
        collect[...],
        contributions[...],
        preferred_element_type=jnp.float32,
        precision=lax.Precision.HIGHEST,
    )
    for t in range(tiles):
        density_out[pl.ds(t, 1), :] = density[pl.ds(me * tiles + t, 1), :]
    positive = jnp.maximum(density[...], 0.1)
    root = jnp.exp(jnp.log(positive) * (1.0 / 3.0))
    root = root - (root - positive / (root * root)) * (1.0 / 3.0)
    potential[...] = -exchange_factor * root
    scale = 1.0 / math.sqrt(P_SIZE)

    def store(b):
        rows = pl.ds(pl.multiple_of(b * KB, KB), KB)
        return pltpu.make_async_copy(stage.at[b], update_out.at[rows], osems.at[b])

    def step(b, carry):
        first, last = plan[slots + b], plan[slots + b + 1]

        @pl.when(first == last)
        def _():
            stage[b] = jnp.zeros(stage.shape[1:], jnp.bfloat16)

        def body(i, p, q):
            weight_p = potential[pl.ds(tile_of[order[p]], 1), :]
            weight_q = potential[pl.ds(tile_of[order[q]], 1), :] * (q - p).astype(jnp.float32)
            weighted = jnp.concatenate(
                [
                    (pair[p, 1].astype(jnp.float32) * weight_p).astype(jnp.bfloat16),
                    (pair[q, 1].astype(jnp.float32) * weight_q).astype(jnp.bfloat16),
                ],
                axis=1,
            )
            block = lax.dot_general(
                jnp.concatenate([pair[p, 0], pair[q, 0]], axis=1),
                weighted,
                (((1,), (1,)), ((), ())),
                preferred_element_type=jnp.float32,
            )

            @pl.when(last - first <= 2)
            def _():
                stage[b] = (block * scale).astype(jnp.bfloat16)

            @pl.when((last - first > 2) & (i == 0))
            def _():
                acc[...] = block

            @pl.when(i > 0)
            def _():
                acc[...] += block

        by_twos(first, last, load, body)

        @pl.when(last - first > 2)
        def _():
            stage[b] = (acc[...] * scale).astype(jnp.bfloat16)

        store(b).start()
        return carry

    lax.fori_loop(0, blocks, step, 0)
    for b in range(blocks):
        store(b).wait()


def update(plan, order, tile_of, contributions, collect, parts, col_count, tiles, blocks, cols):
    slots = col_count * CAP
    entry = parts[0].shape[2:]
    all_tiles = (collect.shape[0], P_SIZE)
    return pl.pallas_call(
        functools.partial(update_kernel, blocks, tiles),
        out_shape=(
            jax.ShapeDtypeStruct((tiles, P_SIZE), jnp.float32),
            jax.ShapeDtypeStruct((blocks * KB, cols), jnp.bfloat16),
        ),
        in_specs=[SMEM] * 3 + [VMEM] * 2 + [HBM] * len(parts),
        out_specs=(VMEM, HBM),
        scratch_shapes=[
            pltpu.VMEM((slots,) + entry, jnp.bfloat16),
            pltpu.VMEM(all_tiles, jnp.float32),
            pltpu.VMEM(all_tiles, jnp.float32),
            pltpu.VMEM((KB, cols), jnp.float32),
            pltpu.VMEM((blocks, KB, cols), jnp.bfloat16),
            pltpu.SemaphoreType.DMA((slots,)),
            pltpu.SemaphoreType.DMA((blocks,)),
        ],
        compiler_params=pltpu.CompilerParams(vmem_limit_bytes=62 * MIB),
        name="update",
    )(plan, order, tile_of, contributions, collect, *parts)


def shift(block, axis, step):
    count = lax.axis_size(axis)
    pairs = [(i, i + step) for i in range(count) if 0 <= i + step < count]
    return lax.ppermute(block, axis, pairs)


def make_plan(lists, me, entries, tiles, col_count, blocks):
    slots = col_count * CAP
    sent = sent_rows(slots, tiles)
    lists = lists[:, : 2 * entries + tiles].astype(jnp.int32)
    peers, named, counts = lists[:, :entries], lists[:, entries : 2 * entries], lists[:, 2 * entries :]
    index = jnp.arange(entries, dtype=jnp.int32)
    home = jnp.arange(col_count, dtype=jnp.int32)[:, None]
    earlier = (peers[:, :, None] == peers[:, None, :]) & (index[None, :] < index[:, None])
    rank = jnp.sum(earlier.astype(jnp.int32), axis=2)
    live = (index % SLOTS)[None, :] < jnp.repeat(counts, SLOTS, axis=1)
    row = jnp.where(live, peers * sent + chunk_of(home, peers, col_count) * CAP + rank, -1).reshape(col_count, tiles, SLOTS)
    core = (home * sent + slots + jnp.arange(tiles, dtype=jnp.int32))[:, :, None]
    row = jnp.concatenate([row, core], axis=2).reshape(col_count * tiles, SLOTS + 1, 1)
    picked = row == jnp.arange(col_count * sent, dtype=jnp.int32)
    collect = jnp.sum(picked.astype(jnp.float32), axis=1)
    hit = (
        (peers == me)[:, None, :]
        & (rank[:, None, :] == jnp.arange(CAP, dtype=jnp.int32)[None, :, None])
        & live[:, None, :]
    )
    at_me = chunk_of(home, me, col_count).reshape(1, col_count) == home
    tile = home * tiles + index[None, :] // SLOTS

    def of_slots(values):
        by_home = jnp.sum(jnp.where(hit, values[:, None, :], 0), axis=2)
        return jnp.sum(jnp.where(at_me[:, :, None], by_home[None], 0), axis=1).reshape(slots)

    wanted = of_slots(named + 1) - 1
    tile_of = of_slots(tile)
    key = jnp.where(wanted < 0, blocks, wanted)
    place = jnp.arange(slots, dtype=jnp.int32)
    before = (key[None, :] < key[:, None]) | (
        (key[None, :] == key[:, None]) & (place[None, :] < place[:, None])
    )
    spot = jnp.sum(before.astype(jnp.int32), axis=1)
    order = jnp.sum(jnp.where(spot[None, :] == place[:, None], place[None, :], 0), axis=1)
    starts = jnp.sum(
        (key[None, :] < jnp.arange(blocks + 1, dtype=jnp.int32)[:, None]).astype(jnp.int32), axis=1
    )
    plan = jnp.concatenate([wanted, starts, me[None]]).astype(jnp.int32)
    return collect, plan, order.astype(jnp.int32), tile_of.astype(jnp.int32)


def shards(
    start_columns,
    hamiltonian,
    band_pattern,
    coefficients,
    tile_peer,
    tile_block,
    tile_count,
    basis_values,
    core_density,
):
    col_count = lax.axis_size("col")
    entries = tile_peer.shape[0]
    tiles = core_density.shape[0]
    cols = start_columns.shape[1]
    blocks = start_columns.shape[0] // KB
    peers = tile_peer[:, 0]
    me = lax.axis_index("col").astype(jnp.int32)

    own = own_piece(peers, tile_block, tile_count, band_pattern, hamiltonian.reshape(-1, W))
    pieces, owners, awaited, end = gather_pieces(own)
    v_low = shift(start_columns[-DEG * W :], "row", 1)
    v_high = shift(start_columns[: DEG * W], "row", -1)
    parts = exchange(me[None], peers, basis_values, own, awaited + [v_low, v_high], end)

    first, last, lists = edge_blocks(owners, pieces, col_count, DEG - 1)
    h_low = shift(last, "row", 1)
    h_high = shift(first, "row", -1)
    kernel_t = chebyshev(
        coefficients, owners, v_low, start_columns, v_high, h_low, h_high, pieces
    )
    collect, plan, order, tile_of = make_plan(lists[:, 0], me, entries, tiles, col_count, blocks)
    partial = project(plan, order, kernel_t, core_density, parts, col_count)
    contributions = lax.all_to_all(partial, "col", split_axis=0, concat_axis=0, tiled=True)
    contributions = contributions.reshape(-1, P_SIZE)
    return update(
        plan, order, tile_of, contributions, collect, parts, col_count, tiles, blocks, cols
    )


def solution(mesh):
    return jax.shard_map(
        shards,
        mesh=mesh,
        in_specs=(
            P("row", "col"),
            P(("row", "col"), None, None, None),
            P(("row", "col")),
            P(),
            P(("row", "col"), None),
            P(("row", "col")),
            P(("row", "col")),
            P(("row", "col"), None, None, None),
            P(("row", "col"), None),
        ),
        out_specs=(P(("row", "col"), None), P("row", "col")),
        check_vma=False,
    )
```

```python
import functools
import math

import jax
import jax.numpy as jnp
from jax import lax
from jax.experimental import pallas as pl
from jax.experimental.pallas import tpu as pltpu
from jax.sharding import PartitionSpec as P

W = 256
KB = 512
DEG = 3
SLOTS = 4
CAP = 2
P_SIZE = 128
MIB = 1 << 20
LISTS = 16

exchange_factor = (3.0 / math.pi) ** (1.0 / 3.0)
HBM = pl.BlockSpec(memory_space=pltpu.HBM)
ANY = pl.BlockSpec(memory_space=pl.ANY)
SMEM = pl.BlockSpec(memory_space=pltpu.SMEM)
VMEM = pl.BlockSpec(memory_space=pltpu.VMEM)


def partner(me, j, count):
    if count & (count - 1) == 0:
        return me ^ abs(j)
    return (me + j) % count


def piece_kernel(peers, named, counts, pattern, ham, piece, blocks, sems):
    rows = ham.shape[0]
    load = pltpu.make_async_copy(ham, blocks.at[pl.ds(0, rows)], sems.at[0])
    load.start()
    lane = lax.broadcasted_iota(jnp.int32, (LISTS, W), 1)
    lists = jnp.zeros((LISTS, W), jnp.int32)
    at = 0
    for ref in (peers, named, counts):
        for i in range(ref.shape[0]):
            lists = jnp.where(lane == at, ref[i], lists)
            at += 1
    blocks[rows:] = lists.astype(jnp.float32).astype(jnp.bfloat16)
    load.wait()
    for i in range(rows // (2 * W)):
        coupling = slice((2 * i + 1) * W, (2 * i + 2) * W)
        blocks[coupling] = blocks[coupling] * pattern[i].astype(jnp.bfloat16)
    store = pltpu.make_async_copy(blocks, piece, sems.at[1])
    store.start()
    store.wait()


def own_piece(peers, named, counts, pattern, ham):
    piece = (ham.shape[0] + LISTS, W)
    return pl.pallas_call(
        piece_kernel,
        out_shape=jax.ShapeDtypeStruct(piece, ham.dtype),
        in_specs=[SMEM] * 4 + [HBM],
        out_specs=HBM,
        scratch_shapes=[pltpu.VMEM(piece, ham.dtype), pltpu.SemaphoreType.DMA((2,))],
        compiler_params=pltpu.CompilerParams(vmem_limit_bytes=62 * MIB),
        name="own_piece",
    )(peers, named, counts, pattern, ham)


def lines_of(count):
    inner = max(count // 4, 1) if count & (count - 1) == 0 else 1
    return count // inner, inner


def swap_along(block, t):
    count = lax.axis_size("col")
    _, inner = lines_of(count)
    pairs = [(c, c - c % inner + partner(c % inner, t, inner)) for c in range(count)]
    return lax.ppermute(block, "col", pairs)


def chunk_of(home, owner, count):
    outer, inner = lines_of(count)
    return partner(home % inner, owner % inner, inner) * outer + home // inner


def pack_kernel(entries, col_count, wanted, me, peers, basis, first, *refs):
    outer, inner = lines_of(col_count)
    sent, (held, owner, count, in_sems, out_sems) = refs[: len(wanted)], refs[len(wanted) :]
    for c in range(col_count):
        count[c] = 0
        for k in range(CAP):
            owner[c * CAP + k] = 0
    for e in range(entries):
        p = peers[e]
        k = count[p]
        count[p] = k + 1
        owner[p * CAP + k] = e
    place = lax.rem(me[0], inner)
    tasks = []
    for target, group in zip(sent, wanted):
        for line in range(outer):
            for i, (t, k) in enumerate(group):
                n = len(tasks)
                e = owner[(line * inner + partner(place, t, inner)) * CAP + k]
                fetch = pltpu.make_async_copy(basis.at[e], held.at[n], in_sems.at[n])
                store = pltpu.make_async_copy(held.at[n], target.at[line, i], out_sems.at[n])
                tasks.append((fetch, store))
    for fetch, _ in tasks:
        fetch.start()
    for fetch, store in tasks:
        fetch.wait()
        store.start()
    for _, store in tasks:
        store.wait()


def pack(me, peers, basis, first, col_count, wanted, spare=0):
    outer, _ = lines_of(col_count)
    entries = basis.shape[0]
    number = sum(len(group) for group in wanted) * outer
    return list(pl.pallas_call(
        functools.partial(pack_kernel, entries, col_count, wanted),
        out_shape=tuple(
            jax.ShapeDtypeStruct(
                (outer, len(group) + (spare if i == 0 else 0)) + basis.shape[1:], basis.dtype
            )
            for i, group in enumerate(wanted)
        ),
        in_specs=[SMEM, SMEM, HBM, HBM],
        out_specs=(HBM,) * len(wanted),
        scratch_shapes=[
            pltpu.VMEM((number,) + basis.shape[1:], basis.dtype),
            pltpu.SMEM((col_count * CAP,), jnp.int32),
            pltpu.SMEM((col_count,), jnp.int32),
            pltpu.SemaphoreType.DMA((number,)),
            pltpu.SemaphoreType.DMA((number,)),
        ],
        compiler_params=pltpu.CompilerParams(vmem_limit_bytes=62 * MIB),
        name="pack",
    )(me, peers, basis, first))


def join_kernel(fills, block, *refs):
    sources, (out, held, in_sems, out_sems) = refs[:fills], refs[-4:]
    units = out.shape[1]
    loads = [pltpu.make_async_copy(sources[i], held.at[i], in_sems.at[i]) for i in range(fills)]
    stores = [
        pltpu.make_async_copy(held.at[i], out.at[:, pl.ds(units - fills + i, 1)], out_sems.at[i])
        for i in range(fills)
    ]
    for load in loads:
        load.start()
    for load, store in zip(loads, stores):
        load.wait()
        store.start()
    for store in stores:
        store.wait()


def join(block, fills, *others):
    return pl.pallas_call(
        functools.partial(join_kernel, len(fills)),
        out_shape=jax.ShapeDtypeStruct(block.shape, block.dtype),
        in_specs=[HBM] + [ANY] * (len(fills) + len(others)),
        out_specs=HBM,
        input_output_aliases={0: 0},
        scratch_shapes=[
            pltpu.VMEM((max(len(fills), 1), block.shape[0], 1) + block.shape[2:], block.dtype),
            pltpu.SemaphoreType.DMA((max(len(fills), 1),)),
            pltpu.SemaphoreType.DMA((max(len(fills), 1),)),
        ],
        compiler_params=pltpu.CompilerParams(vmem_limit_bytes=62 * MIB),
        name="join",
    )(block, *fills, *others)


def unit_of(t, k, inner):
    if t == 0:
        return 0, k
    return (0, CAP + t - 1) if k == 0 else (1, (k - 1) * (inner - 1) + t - 1)


def exchange(me, peers, basis, own, awaited):
    count = lax.axis_size("col")
    outer, inner = lines_of(count)
    groups = [[line * inner + place for line in range(outer)] for place in range(inner)]

    def between_lines(block):
        return lax.all_to_all(
            block, "col", split_axis=0, concat_axis=0, axis_index_groups=groups, tiled=True
        )

    here = [(0, k) for k in range(CAP)]
    ahead = [[(t, 0)] for t in range(1, inner)]
    rest = [[(t, k)] for k in range(1, CAP) for t in range(1, inner)]
    sent = pack(me, peers, basis, own, count, ahead) if ahead else []
    first, *later = pack(
        me, peers, basis, sent[0] if ahead else own, count, [here] + rest, spare=len(ahead)
    )
    swapped = [swap_along(block, group[0][0]) for block, group in zip(sent, ahead)]
    parts = [between_lines(join(first, swapped, *awaited))]
    if rest:
        swapped = [swap_along(block, group[0][0]) for block, group in zip(later, rest)]
        last = swapped[0] if len(swapped) == 1 else jnp.concatenate(swapped, axis=1)
        parts.append(between_lines(join(last, [], parts[0])))
    return parts


def gather_pieces(own):
    count = lax.axis_size("col")
    outer, inner = lines_of(count)
    me = lax.axis_index("col").astype(jnp.int32)
    a, b = me // inner, me % inner

    def move(block, ways):
        pairs = [(x * inner + y, z * inner + y) for x, z in ways for y in range(inner)]
        return lax.ppermute(block, "col", pairs)

    if outer == 4:
        middle, outwards = [(1, 2), (2, 1)], [(1, 0), (2, 3)]
        near = move(own, [(0, 1), (1, 0), (2, 3), (3, 2)])
        across = move(own, middle)
        far = move(near, middle)
        handed = move(across, outwards)
        last = move(far, outwards)
        within = (a == 1) | (a == 2)
        lines = [
            (own, a),
            (near, a ^ 1),
            (across + handed, jnp.where(within, a ^ 3, a ^ 2)),
            (far + last, jnp.where(within, a ^ 2, a ^ 3)),
        ]
        awaited = [far, handed]
    else:
        lines = [(own, a)] + [
            (move(own, [(x, partner(x, t, outer)) for x in range(outer)]), partner(a, -t, outer))
            for t in range(1, outer)
        ]
        awaited = [block for block, _ in lines[1:]]
    pieces, owners = [], []
    for block, line in lines:
        pieces.append(block)
        owners.append(line * inner + b)
        for t in range(1, inner):
            pieces.append(swap_along(block, t))
            owners.append(line * inner + partner(b, -t, inner))
    return pieces, jnp.stack(owners).astype(jnp.int32), awaited


def edge_kernel(col_count, depth, owners, *refs):
    pieces, (first, last, lists, sems, list_sems) = refs[:-5], refs[-5:]
    rows = pieces[0].shape[0] - LISTS
    held = rows // (2 * W)
    total = col_count * held

    def each(act):
        for i, piece in enumerate(pieces):
            for g in range(depth):
                for out, block, sem in ((first, g, 0), (last, total - depth + g, 1)):
                    source = piece.at[pl.ds(block % held * 2 * W, 2 * W)]
                    copy = pltpu.make_async_copy(source, out.at[g], sems.at[sem, g])

                    @pl.when(owners[i] == block // held)
                    def _():
                        act(copy)

            @pl.when(owners[i] >= 0)
            def _():
                act(pltpu.make_async_copy(
                    piece.at[pl.ds(rows, LISTS)], lists.at[owners[i]], list_sems.at[i]
                ))

    each(lambda copy: copy.start())
    each(lambda copy: copy.wait())


def edge_blocks(owners, pieces, col_count, depth):
    shape = jax.ShapeDtypeStruct((depth, 2 * W, W), pieces[0].dtype)
    return pl.pallas_call(
        functools.partial(edge_kernel, col_count, depth),
        out_shape=(shape, shape, jax.ShapeDtypeStruct((col_count, LISTS, W), pieces[0].dtype)),
        in_specs=[SMEM] + [HBM] * len(pieces),
        out_specs=(VMEM, VMEM, VMEM),
        scratch_shapes=[
            pltpu.SemaphoreType.DMA((2, depth)),
            pltpu.SemaphoreType.DMA((len(pieces),)),
        ],
        name="edge_blocks",
    )(owners, *pieces)


def cheb_kernel(blocks, coef, owners, v_low, v_mid, v_high, h_low, h_high, *refs):
    *pieces, out, vext, hraw, hcat, cheb_1, cheb_2, total, kern, sems, psems, osems = refs
    halo_v = DEG
    halo_h = DEG - 1
    held = (pieces[0].shape[0] - LISTS) // (2 * W)
    h_copies = [
        pltpu.make_async_copy(h_low, hraw.at[pl.ds(0, halo_h)], sems.at[0]),
        pltpu.make_async_copy(h_high, hraw.at[pl.ds(halo_h + blocks, halo_h)], sems.at[1]),
    ]
    v_copies = [
        pltpu.make_async_copy(v_low, vext.at[pl.ds(0, halo_v * W)], sems.at[2]),
        pltpu.make_async_copy(v_mid, vext.at[pl.ds(halo_v * W, blocks * W)], sems.at[3]),
        pltpu.make_async_copy(v_high, vext.at[pl.ds((halo_v + blocks) * W, halo_v * W)], sems.at[4]),
    ]

    def each_piece(act):
        for i, piece in enumerate(pieces):
            @pl.when(owners[i] >= 0)
            def _():
                for k in range(held):
                    act(pltpu.make_async_copy(
                        piece.at[pl.ds(k * 2 * W, 2 * W)],
                        hraw.at[halo_h + owners[i] * held + k],
                        psems.at[i, k],
                    ))

    each_piece(lambda copy: copy.start())
    for copy in h_copies + v_copies:
        copy.start()
    each_piece(lambda copy: copy.wait())
    for copy in h_copies:
        copy.wait()
    rows = lax.broadcasted_iota(jnp.int32, (W, W), 0)
    cols = lax.broadcasted_iota(jnp.int32, (W, W), 1)
    upper = jnp.where(rows <= cols, 1.0, 0.0).astype(jnp.bfloat16)

    def build(j, carry):
        coupling = hraw[j, W:]
        lower_band = coupling * upper
        hcat[j, :, 0:W] = lower_band
        hcat[j, :, W : 2 * W] = hraw[j, :W]
        hcat[j, :, 2 * W : 3 * W] = coupling - lower_band
        return carry

    lax.fori_loop(0, blocks + 2 * halo_h, build, 0, unroll=2)
    for copy in v_copies:
        copy.wait()

    def rows_of(j, count=1):
        return pl.ds(pl.multiple_of(j * W, W), count * W)

    def band(source, j, row):
        return jnp.dot(hcat[j], source[rows_of(row, 3), :], preferred_element_type=jnp.float32)

    def first(j, carry):
        value = band(vext, j, j)
        cheb_1[rows_of(j), :] = value.astype(jnp.bfloat16)
        total[rows_of(j), :] = value
        return carry

    lax.fori_loop(0, blocks + 4, first, 0, unroll=2)

    def second(j, carry):
        begin = vext[rows_of(j + 2), :].astype(jnp.float32)
        value = 2.0 * band(cheb_1, j + 1, j) - begin
        cheb_2[rows_of(j), :] = value.astype(jnp.bfloat16)
        total[rows_of(j + 1), :] = (
            coef[0] * begin + (coef[1] - coef[3]) * total[rows_of(j + 1), :] + coef[2] * value
        )
        return carry

    lax.fori_loop(0, blocks + 2, second, 0, unroll=2)

    def store(j):
        return pltpu.make_async_copy(kern.at[j], out.at[j], osems.at[j])

    def third(j, carry):
        for half in range(KB // W):
            i = j * (KB // W) + half
            value = total[rows_of(i + 2), :] + (2.0 * coef[3]) * band(cheb_2, i + 2, i)
            kern[j, :, half * W : (half + 1) * W] = value.astype(jnp.bfloat16).T
        store(j).start()
        return carry

    lax.fori_loop(0, blocks // (KB // W), third, 0)
    for j in range(blocks // (KB // W)):
        store(j).wait()


def chebyshev(coefficients, owners, v_low, v_mid, v_high, h_low, h_high, pieces):
    blocks = v_mid.shape[0] // W
    cols = v_mid.shape[1]
    ext = blocks + 2 * (DEG - 1)
    flops = 2 * W * 3 * W * cols * (3 * blocks + 6)
    result = (blocks * W // KB, cols, KB)
    held = (pieces[0].shape[0] - LISTS) // (2 * W)
    return pl.pallas_call(
        functools.partial(cheb_kernel, blocks),
        out_shape=jax.ShapeDtypeStruct(result, jnp.bfloat16),
        in_specs=[SMEM] * 2 + [ANY] * (5 + len(pieces)),
        out_specs=HBM,
        scratch_shapes=[
            pltpu.VMEM(((blocks + 2 * DEG) * W, cols), jnp.bfloat16),
            pltpu.VMEM((ext, 2 * W, W), jnp.bfloat16),
            pltpu.VMEM((ext, W, 3 * W), jnp.bfloat16),
            pltpu.VMEM((ext * W, cols), jnp.bfloat16),
            pltpu.VMEM(((blocks + 2) * W, cols), jnp.bfloat16),
            pltpu.VMEM((ext * W, cols), jnp.float32),
            pltpu.VMEM(result, jnp.bfloat16),
            pltpu.SemaphoreType.DMA((5,)),
            pltpu.SemaphoreType.DMA((len(pieces), held)),
            pltpu.SemaphoreType.DMA((result[0],)),
        ],
        compiler_params=pltpu.CompilerParams(vmem_limit_bytes=48 * MIB),
        cost_estimate=pl.CostEstimate(flops=flops, bytes_accessed=16 * MIB, transcendentals=0),
        name="chebyshev",
    )(coefficients, owners, v_low, v_mid, v_high, h_low, h_high, *pieces)


def entry_loads(order, parts, pair, sems):
    outer, units = parts[0].shape[:2]
    inner = units - CAP + 1

    def load(p):
        return pltpu.make_async_copy(parts[0].at[0, 0], pair.at[p], sems.at[p])

    def start(p, carry):
        n = order[p]
        line = lax.rem(lax.div(n, CAP), outer)
        for t in range(inner):
            for k in range(CAP):
                part, unit = unit_of(t, k, inner)

                @pl.when((lax.div(n, CAP * outer) == t) & (lax.rem(n, CAP) == k))
                def _():
                    source = parts[part].at[line, unit]
                    pltpu.make_async_copy(source, pair.at[p], sems.at[p]).start()

        return carry

    return load, start


def by_twos(first, last, load, body):
    def step(i, carry):
        p = first + 2 * i
        q = jnp.minimum(p + 1, last - 1)
        load(p).wait()

        @pl.when(q > p)
        def _():
            load(q).wait()

        body(i, p, q)
        return carry

    lax.fori_loop(0, (last - first + 1) // 2, step, 0)


def sent_rows(slots, tiles):
    return slots + tiles + -(slots + tiles) % 8


def project_kernel(blocks, plan, order, kernel_t, core, *refs):
    *parts, out, kern, pair, rows, ksems, bsems = refs
    slots = pair.shape[0]
    load, start = entry_loads(order, parts, pair, bsems)

    def fetch(b):
        return pltpu.make_async_copy(kernel_t.at[b], kern.at[b], ksems.at[b])

    def begin(b, carry):
        first, last = plan[slots + b], plan[slots + b + 1]

        @pl.when(first < last)
        def _():
            fetch(b).start()

        return lax.fori_loop(first, last, start, carry)

    lax.fori_loop(0, blocks, begin, 0)
    rows[...] = jnp.zeros_like(rows)
    rows[slots : slots + core.shape[0]] = core[...]

    def step(b, carry):
        first, last = plan[slots + b], plan[slots + b + 1]

        @pl.when(first < last)
        def _():
            fetch(b).wait()

        def body(i, p, q):
            both = jnp.concatenate([pair[p, 0], pair[q, 0]], axis=1)
            projected = jnp.dot(kern[b], both, preferred_element_type=jnp.float32)
            other = jnp.concatenate([pair[p, 1], pair[q, 1]], axis=1).astype(jnp.float32)
            value = jnp.sum(projected * other, axis=0, keepdims=True) * (1.0 / KB)
            rows[pl.ds(order[p], 1), :] = value[:, :P_SIZE]
            rows[pl.ds(order[q], 1), :] = value[:, P_SIZE:]

        by_twos(first, last, load, body)
        return carry

    lax.fori_loop(0, blocks, step, 0)
    for c in range(out.shape[0]):
        out[c] = rows[...]


def project(plan, order, kernel_t, core, parts, col_count):
    slots = col_count * CAP
    entry = parts[0].shape[2:]
    sent = sent_rows(slots, core.shape[0])
    blocks = kernel_t.shape[0]
    return pl.pallas_call(
        functools.partial(project_kernel, blocks),
        out_shape=jax.ShapeDtypeStruct((col_count, sent, P_SIZE), jnp.float32),
        in_specs=[SMEM, SMEM, HBM, VMEM] + [HBM] * len(parts),
        out_specs=VMEM,
        scratch_shapes=[
            pltpu.VMEM(kernel_t.shape, jnp.bfloat16),
            pltpu.VMEM((slots,) + entry, jnp.bfloat16),
            pltpu.VMEM((sent, P_SIZE), jnp.float32),
            pltpu.SemaphoreType.DMA((blocks,)),
            pltpu.SemaphoreType.DMA((slots,)),
        ],
        compiler_params=pltpu.CompilerParams(vmem_limit_bytes=62 * MIB),
        name="project",
    )(plan, order, kernel_t, core, *parts)


def update_kernel(
    blocks, tiles, plan, order, tile_of, contributions, collect, *refs
):
    *parts, density_out, update_out, pair, density, potential, acc, stage, sems, osems = refs
    slots = pair.shape[0]
    live = plan[slots + blocks]
    me = plan[slots + blocks + 1]
    load, start = entry_loads(order, parts, pair, sems)
    lax.fori_loop(0, live, start, 0)
    density[...] = jnp.dot(
        collect[...],
        contributions[...],
        preferred_element_type=jnp.float32,
        precision=lax.Precision.HIGHEST,
    )
    for t in range(tiles):
        density_out[pl.ds(t, 1), :] = density[pl.ds(me * tiles + t, 1), :]
    positive = jnp.maximum(density[...], 0.1)
    root = jnp.exp(jnp.log(positive) * (1.0 / 3.0))
    root = root - (root - positive / (root * root)) * (1.0 / 3.0)
    potential[...] = -exchange_factor * root
    scale = 1.0 / math.sqrt(P_SIZE)

    def store(b):
        rows = pl.ds(pl.multiple_of(b * KB, KB), KB)
        return pltpu.make_async_copy(stage.at[b], update_out.at[rows], osems.at[b])

    def step(b, carry):
        first, last = plan[slots + b], plan[slots + b + 1]

        @pl.when(first == last)
        def _():
            stage[b] = jnp.zeros(stage.shape[1:], jnp.bfloat16)

        def body(i, p, q):
            weight_p = potential[pl.ds(tile_of[order[p]], 1), :]
            weight_q = potential[pl.ds(tile_of[order[q]], 1), :] * (q - p).astype(jnp.float32)
            weighted = jnp.concatenate(
                [
                    (pair[p, 1].astype(jnp.float32) * weight_p).astype(jnp.bfloat16),
                    (pair[q, 1].astype(jnp.float32) * weight_q).astype(jnp.bfloat16),
                ],
                axis=1,
            )
            block = lax.dot_general(
                jnp.concatenate([pair[p, 0], pair[q, 0]], axis=1),
                weighted,
                (((1,), (1,)), ((), ())),
                preferred_element_type=jnp.float32,
            )

            @pl.when(last - first <= 2)
            def _():
                stage[b] = (block * scale).astype(jnp.bfloat16)

            @pl.when((last - first > 2) & (i == 0))
            def _():
                acc[...] = block

            @pl.when(i > 0)
            def _():
                acc[...] += block

        by_twos(first, last, load, body)

        @pl.when(last - first > 2)
        def _():
            stage[b] = (acc[...] * scale).astype(jnp.bfloat16)

        store(b).start()
        return carry

    lax.fori_loop(0, blocks, step, 0)
    for b in range(blocks):
        store(b).wait()


def update(plan, order, tile_of, contributions, collect, parts, col_count, tiles, blocks, cols):
    slots = col_count * CAP
    entry = parts[0].shape[2:]
    all_tiles = (collect.shape[0], P_SIZE)
    return pl.pallas_call(
        functools.partial(update_kernel, blocks, tiles),
        out_shape=(
            jax.ShapeDtypeStruct((tiles, P_SIZE), jnp.float32),
            jax.ShapeDtypeStruct((blocks * KB, cols), jnp.bfloat16),
        ),
        in_specs=[SMEM] * 3 + [VMEM] * 2 + [HBM] * len(parts),
        out_specs=(VMEM, HBM),
        scratch_shapes=[
            pltpu.VMEM((slots,) + entry, jnp.bfloat16),
            pltpu.VMEM(all_tiles, jnp.float32),
            pltpu.VMEM(all_tiles, jnp.float32),
            pltpu.VMEM((KB, cols), jnp.float32),
            pltpu.VMEM((blocks, KB, cols), jnp.bfloat16),
            pltpu.SemaphoreType.DMA((slots,)),
            pltpu.SemaphoreType.DMA((blocks,)),
        ],
        compiler_params=pltpu.CompilerParams(vmem_limit_bytes=62 * MIB),
        name="update",
    )(plan, order, tile_of, contributions, collect, *parts)


def shift(block, axis, step):
    count = lax.axis_size(axis)
    pairs = [(i, i + step) for i in range(count) if 0 <= i + step < count]
    return lax.ppermute(block, axis, pairs)


def make_plan(lists, me, entries, tiles, col_count, blocks):
    slots = col_count * CAP
    sent = sent_rows(slots, tiles)
    lists = lists[:, : 2 * entries + tiles].astype(jnp.int32)
    peers, named, counts = lists[:, :entries], lists[:, entries : 2 * entries], lists[:, 2 * entries :]
    index = jnp.arange(entries, dtype=jnp.int32)
    home = jnp.arange(col_count, dtype=jnp.int32)[:, None]
    earlier = (peers[:, :, None] == peers[:, None, :]) & (index[None, :] < index[:, None])
    rank = jnp.sum(earlier.astype(jnp.int32), axis=2)
    live = (index % SLOTS)[None, :] < jnp.repeat(counts, SLOTS, axis=1)
    row = jnp.where(live, peers * sent + chunk_of(home, peers, col_count) * CAP + rank, -1).reshape(col_count, tiles, SLOTS)
    core = (home * sent + slots + jnp.arange(tiles, dtype=jnp.int32))[:, :, None]
    row = jnp.concatenate([row, core], axis=2).reshape(col_count * tiles, SLOTS + 1, 1)
    picked = row == jnp.arange(col_count * sent, dtype=jnp.int32)
    collect = jnp.sum(picked.astype(jnp.float32), axis=1)
    hit = (
        (peers == me)[:, None, :]
        & (rank[:, None, :] == jnp.arange(CAP, dtype=jnp.int32)[None, :, None])
        & live[:, None, :]
    )
    at_me = chunk_of(home, me, col_count).reshape(1, col_count) == home
    tile = home * tiles + index[None, :] // SLOTS

    def of_slots(values):
        by_home = jnp.sum(jnp.where(hit, values[:, None, :], 0), axis=2)
        return jnp.sum(jnp.where(at_me[:, :, None], by_home[None], 0), axis=1).reshape(slots)

    wanted = of_slots(named + 1) - 1
    tile_of = of_slots(tile)
    key = jnp.where(wanted < 0, blocks, wanted)
    place = jnp.arange(slots, dtype=jnp.int32)
    before = (key[None, :] < key[:, None]) | (
        (key[None, :] == key[:, None]) & (place[None, :] < place[:, None])
    )
    spot = jnp.sum(before.astype(jnp.int32), axis=1)
    order = jnp.sum(jnp.where(spot[None, :] == place[:, None], place[None, :], 0), axis=1)
    starts = jnp.sum(
        (key[None, :] < jnp.arange(blocks + 1, dtype=jnp.int32)[:, None]).astype(jnp.int32), axis=1
    )
    plan = jnp.concatenate([wanted, starts, me[None]]).astype(jnp.int32)
    return collect, plan, order.astype(jnp.int32), tile_of.astype(jnp.int32)


def shards(
    start_columns,
    hamiltonian,
    band_pattern,
    coefficients,
    tile_peer,
    tile_block,
    tile_count,
    basis_values,
    core_density,
):
    col_count = lax.axis_size("col")
    entries = tile_peer.shape[0]
    tiles = core_density.shape[0]
    cols = start_columns.shape[1]
    blocks = start_columns.shape[0] // KB
    peers = tile_peer[:, 0]
    me = lax.axis_index("col").astype(jnp.int32)

    own = own_piece(peers, tile_block, tile_count, band_pattern, hamiltonian.reshape(-1, W))
    pieces, owners, awaited = gather_pieces(own)
    v_low = shift(start_columns[-DEG * W :], "row", 1)
    v_high = shift(start_columns[: DEG * W], "row", -1)
    parts = exchange(me[None], peers, basis_values, own, awaited + [v_low, v_high])

    first, last, lists = edge_blocks(owners, pieces, col_count, DEG - 1)
    h_low = shift(last, "row", 1)
    h_high = shift(first, "row", -1)
    kernel_t = chebyshev(
        coefficients, owners, v_low, start_columns, v_high, h_low, h_high, pieces
    )
    collect, plan, order, tile_of = make_plan(lists[:, 0], me, entries, tiles, col_count, blocks)
    partial = project(plan, order, kernel_t, core_density, parts, col_count)
    contributions = lax.all_to_all(partial, "col", split_axis=0, concat_axis=0, tiled=True)
    contributions = contributions.reshape(-1, P_SIZE)
    return update(
        plan, order, tile_of, contributions, collect, parts, col_count, tiles, blocks, cols
    )


def solution(mesh):
    return jax.shard_map(
        shards,
        mesh=mesh,
        in_specs=(
            P("row", "col"),
            P(("row", "col"), None, None, None),
            P(("row", "col")),
            P(),
            P(("row", "col"), None),
            P(("row", "col")),
            P(("row", "col")),
            P(("row", "col"), None, None, None),
            P(("row", "col"), None),
        ),
        out_specs=(P(("row", "col"), None), P("row", "col")),
        check_vma=False,
    )
```

```python
import functools
import math

import jax
import jax.numpy as jnp
from jax import lax
from jax.experimental import pallas as pl
from jax.experimental.pallas import tpu as pltpu
from jax.sharding import PartitionSpec as P

W = 256
KB = 512
DEG = 3
SLOTS = 4
CAP = 2
P_SIZE = 128
MIB = 1 << 20
LISTS = 16

exchange_factor = (3.0 / math.pi) ** (1.0 / 3.0)
HBM = pl.BlockSpec(memory_space=pltpu.HBM)
ANY = pl.BlockSpec(memory_space=pl.ANY)
SMEM = pl.BlockSpec(memory_space=pltpu.SMEM)
VMEM = pl.BlockSpec(memory_space=pltpu.VMEM)


def partner(me, j, count):
    if count & (count - 1) == 0:
        return me ^ abs(j)
    return (me + j) % count


def piece_kernel(peers, named, counts, pattern, ham, piece, blocks, sems):
    rows = ham.shape[0]
    load = pltpu.make_async_copy(ham, blocks.at[pl.ds(0, rows)], sems.at[0])
    load.start()
    lane = lax.broadcasted_iota(jnp.int32, (LISTS, W), 1)
    lists = jnp.zeros((LISTS, W), jnp.int32)
    at = 0
    for ref in (peers, named, counts):
        for i in range(ref.shape[0]):
            lists = jnp.where(lane == at, ref[i], lists)
            at += 1
    blocks[rows:] = lists.astype(jnp.float32).astype(jnp.bfloat16)
    load.wait()
    for i in range(rows // (2 * W)):
        coupling = slice((2 * i + 1) * W, (2 * i + 2) * W)
        blocks[coupling] = blocks[coupling] * pattern[i].astype(jnp.bfloat16)
    store = pltpu.make_async_copy(blocks, piece, sems.at[1])
    store.start()
    store.wait()


def own_piece(peers, named, counts, pattern, ham):
    piece = (ham.shape[0] + LISTS, W)
    return pl.pallas_call(
        piece_kernel,
        out_shape=jax.ShapeDtypeStruct(piece, ham.dtype),
        in_specs=[SMEM] * 4 + [HBM],
        out_specs=HBM,
        scratch_shapes=[pltpu.VMEM(piece, ham.dtype), pltpu.SemaphoreType.DMA((2,))],
        compiler_params=pltpu.CompilerParams(vmem_limit_bytes=62 * MIB),
        name="own_piece",
    )(peers, named, counts, pattern, ham)


def lines_of(count):
    inner = max(count // 4, 1) if count & (count - 1) == 0 else 1
    return count // inner, inner


def swap_along(block, t):
    count = lax.axis_size("col")
    _, inner = lines_of(count)
    pairs = [(c, c - c % inner + partner(c % inner, t, inner)) for c in range(count)]
    return lax.ppermute(block, "col", pairs)


def chunk_of(home, owner, count):
    outer, inner = lines_of(count)
    return partner(home % inner, owner % inner, inner) * outer + home // inner


def pack_kernel(entries, col_count, wanted, me, peers, basis, first, *refs):
    outer, inner = lines_of(col_count)
    sent, (held, owner, count, in_sems, out_sems) = refs[: len(wanted)], refs[len(wanted) :]
    for c in range(col_count):
        count[c] = 0
        for k in range(CAP):
            owner[c * CAP + k] = 0
    for e in range(entries):
        p = peers[e]
        k = count[p]
        count[p] = k + 1
        owner[p * CAP + k] = e
    place = lax.rem(me[0], inner)
    tasks = []
    for target, group in zip(sent, wanted):
        for line in range(outer):
            for i, (t, k) in enumerate(group):
                n = len(tasks)
                e = owner[(line * inner + partner(place, t, inner)) * CAP + k]
                fetch = pltpu.make_async_copy(basis.at[e], held.at[n], in_sems.at[n])
                store = pltpu.make_async_copy(held.at[n], target.at[line, i], out_sems.at[n])
                tasks.append((fetch, store))
    for fetch, _ in tasks:
        fetch.start()
    for fetch, store in tasks:
        fetch.wait()
        store.start()
    for _, store in tasks:
        store.wait()


def pack(me, peers, basis, first, col_count, wanted):
    outer, _ = lines_of(col_count)
    entries = basis.shape[0]
    number = sum(len(group) for group in wanted) * outer
    return list(pl.pallas_call(
        functools.partial(pack_kernel, entries, col_count, wanted),
        out_shape=tuple(
            jax.ShapeDtypeStruct((outer, len(group)) + basis.shape[1:], basis.dtype)
            for group in wanted
        ),
        in_specs=[SMEM, SMEM, HBM, HBM],
        out_specs=(HBM,) * len(wanted),
        scratch_shapes=[
            pltpu.VMEM((number,) + basis.shape[1:], basis.dtype),
            pltpu.SMEM((col_count * CAP,), jnp.int32),
            pltpu.SMEM((col_count,), jnp.int32),
            pltpu.SemaphoreType.DMA((number,)),
            pltpu.SemaphoreType.DMA((number,)),
        ],
        compiler_params=pltpu.CompilerParams(vmem_limit_bytes=62 * MIB),
        name="pack",
    )(me, peers, basis, first))


def after(block, *others):
    return pl.pallas_call(
        lambda *refs: None,
        out_shape=jax.ShapeDtypeStruct(block.shape, block.dtype),
        in_specs=[HBM] + [ANY] * len(others),
        out_specs=HBM,
        input_output_aliases={0: 0},
        compiler_params=pltpu.CompilerParams(vmem_limit_bytes=62 * MIB),
        name="after",
    )(block, *others)


def exchange(me, peers, basis, own, awaited):
    count = lax.axis_size("col")
    outer, inner = lines_of(count)
    groups = [[line * inner + place for line in range(outer)] for place in range(inner)]

    def between_lines(blocks, *others):
        block = jnp.concatenate(blocks, axis=1)
        return lax.all_to_all(
            after(block, *others), "col", split_axis=0, concat_axis=0,
            axis_index_groups=groups, tiled=True,
        )

    here = [(0, k) for k in range(CAP)]
    ahead = [[(t, 0)] for t in range(1, inner)]
    rest = [[(t, k)] for k in range(1, CAP) for t in range(1, inner)]
    sent = pack(me, peers, basis, own, count, ahead) if ahead else []
    to_lines, *later = pack(me, peers, basis, sent[0] if ahead else own, count, [here] + rest)
    swapped = {
        group[0]: swap_along(block, group[0][0]) for block, group in zip(sent + later, ahead + rest)
    }
    parts = [between_lines([to_lines], *awaited, *[swapped[group[0]] for group in ahead])]
    for t in range(1, inner):
        parts.append(between_lines([swapped[t, k] for k in range(CAP)], parts[-1]))
    return [part.reshape((outer * CAP,) + part.shape[2:]) for part in parts]


def gather_pieces(own):
    count = lax.axis_size("col")
    outer, inner = lines_of(count)
    me = lax.axis_index("col").astype(jnp.int32)
    a, b = me // inner, me % inner

    def move(block, ways):
        pairs = [(x * inner + y, z * inner + y) for x, z in ways for y in range(inner)]
        return lax.ppermute(block, "col", pairs)

    if outer == 4:
        middle, outwards = [(1, 2), (2, 1)], [(1, 0), (2, 3)]
        near = move(own, [(0, 1), (1, 0), (2, 3), (3, 2)])
        across = move(own, middle)
        far = move(near, middle)
        handed = move(across, outwards)
        last = move(far, outwards)
        within = (a == 1) | (a == 2)
        lines = [
            (own, a),
            (near, a ^ 1),
            (across + handed, jnp.where(within, a ^ 3, a ^ 2)),
            (far + last, jnp.where(within, a ^ 2, a ^ 3)),
        ]
        awaited = [far, handed]
    else:
        lines = [(own, a)] + [
            (move(own, [(x, partner(x, t, outer)) for x in range(outer)]), partner(a, -t, outer))
            for t in range(1, outer)
        ]
        awaited = [block for block, _ in lines[1:]]
    pieces, owners = [], []
    for block, line in lines:
        pieces.append(block)
        owners.append(line * inner + b)
        for t in range(1, inner):
            pieces.append(swap_along(block, t))
            owners.append(line * inner + partner(b, -t, inner))
    return pieces, jnp.stack(owners).astype(jnp.int32), awaited


def edge_kernel(col_count, depth, owners, *refs):
    pieces, (first, last, lists, sems, list_sems) = refs[:-5], refs[-5:]
    rows = pieces[0].shape[0] - LISTS
    held = rows // (2 * W)
    total = col_count * held

    def each(act):
        for i, piece in enumerate(pieces):
            for g in range(depth):
                for out, block, sem in ((first, g, 0), (last, total - depth + g, 1)):
                    source = piece.at[pl.ds(block % held * 2 * W, 2 * W)]
                    copy = pltpu.make_async_copy(source, out.at[g], sems.at[sem, g])

                    @pl.when(owners[i] == block // held)
                    def _():
                        act(copy)

            @pl.when(owners[i] >= 0)
            def _():
                act(pltpu.make_async_copy(
                    piece.at[pl.ds(rows, LISTS)], lists.at[owners[i]], list_sems.at[i]
                ))

    each(lambda copy: copy.start())
    each(lambda copy: copy.wait())


def edge_blocks(owners, pieces, col_count, depth):
    shape = jax.ShapeDtypeStruct((depth, 2 * W, W), pieces[0].dtype)
    return pl.pallas_call(
        functools.partial(edge_kernel, col_count, depth),
        out_shape=(shape, shape, jax.ShapeDtypeStruct((col_count, LISTS, W), pieces[0].dtype)),
        in_specs=[SMEM] + [HBM] * len(pieces),
        out_specs=(VMEM, VMEM, VMEM),
        scratch_shapes=[
            pltpu.SemaphoreType.DMA((2, depth)),
            pltpu.SemaphoreType.DMA((len(pieces),)),
        ],
        name="edge_blocks",
    )(owners, *pieces)


def rows_of(j, count=1):
    return pl.ds(j * W if isinstance(j, int) else pl.multiple_of(j * W, W), count * W)


def band_builder(source, target):
    rows = lax.broadcasted_iota(jnp.int32, (W, W), 0)
    cols = lax.broadcasted_iota(jnp.int32, (W, W), 1)
    upper = jnp.where(rows <= cols, 1.0, 0.0).astype(jnp.bfloat16)

    def build(j, carry):
        coupling = source[j, W:]
        lower_band = coupling * upper
        target[j, :, 0:W] = lower_band
        target[j, :, W : 2 * W] = source[j, :W]
        target[j, :, 2 * W : 3 * W] = coupling - lower_band
        return carry

    return build


def inner_kernel(blocks, coef, owners, v_low, v_mid, v_high, *refs):
    (
        *pieces, out, edge_1, edge_2, edge_total,
        vext, hraw, hcat, cheb_1, cheb_2, total, kern, sems, psems, osems, esems,
    ) = refs
    held = (pieces[0].shape[0] - LISTS) // (2 * W)
    v_copies = [
        pltpu.make_async_copy(v_low.at[rows_of(DEG - 1)], vext.at[rows_of(0)], sems.at[0]),
        pltpu.make_async_copy(v_mid, vext.at[rows_of(1, blocks)], sems.at[1]),
        pltpu.make_async_copy(v_high.at[rows_of(0)], vext.at[rows_of(blocks + 1)], sems.at[2]),
    ]

    def each_piece(act):
        for i, piece in enumerate(pieces):
            for k in range(held):
                act(pltpu.make_async_copy(
                    piece.at[pl.ds(k * 2 * W, 2 * W)],
                    hraw.at[owners[i] * held + k],
                    psems.at[i, k],
                ))

    each_piece(lambda copy: copy.start())
    for copy in v_copies:
        copy.start()
    each_piece(lambda copy: copy.wait())
    lax.fori_loop(0, blocks, band_builder(hraw, hcat), 0, unroll=2)
    for copy in v_copies:
        copy.wait()

    def band(source, j, row):
        return jnp.dot(hcat[j], source[rows_of(row, 3), :], preferred_element_type=jnp.float32)

    def edges(source, target, at):
        size = source.shape[0] // W
        return [
            pltpu.make_async_copy(
                source.at[rows_of(place, 2)], target.at[rows_of(2 * i, 2)], esems.at[at, i]
            )
            for i, place in enumerate((0, size - 2))
        ]

    def first(j, carry):
        value = band(vext, j, j)
        cheb_1[rows_of(j), :] = value.astype(jnp.bfloat16)
        total[rows_of(j), :] = value
        return carry

    lax.fori_loop(0, blocks, first, 0, unroll=2)

    def second(j, carry):
        begin = vext[rows_of(j + 2), :].astype(jnp.float32)
        value = 2.0 * band(cheb_1, j + 1, j) - begin
        cheb_2[rows_of(j), :] = value.astype(jnp.bfloat16)
        total[rows_of(j + 1), :] = (
            coef[0] * begin + (coef[1] - coef[3]) * total[rows_of(j + 1), :] + coef[2] * value
        )
        return carry

    lax.fori_loop(0, blocks - 2, second, 0, unroll=2)
    outgoing = (
        edges(cheb_1, edge_1, 0) + edges(cheb_2, edge_2, 1) + edges(total, edge_total, 2)
    )
    for copy in outgoing:
        copy.start()

    def store(j):
        return pltpu.make_async_copy(kern.at[j], out.at[j], osems.at[j])

    def third(j, carry):
        for half in range(KB // W):
            i = j * (KB // W) + half
            value = total[rows_of(i), :] + (2.0 * coef[3]) * band(cheb_2, i, i - 2)
            kern[j, :, half * W : (half + 1) * W] = value.astype(jnp.bfloat16).T
        store(j).start()
        return carry

    last = blocks // (KB // W) - 1
    lax.fori_loop(1, last, third, 0)
    for j in range(1, last):
        store(j).wait()
    for copy in outgoing:
        copy.wait()


def chebyshev_inner(coefficients, owners, v_low, v_mid, v_high, pieces):
    blocks = v_mid.shape[0] // W
    cols = v_mid.shape[1]
    flops = 2 * W * 3 * W * cols * (3 * blocks - 6)
    result = (blocks * W // KB, cols, KB)
    held = (pieces[0].shape[0] - LISTS) // (2 * W)
    return pl.pallas_call(
        functools.partial(inner_kernel, blocks),
        out_shape=(
            jax.ShapeDtypeStruct(result, jnp.bfloat16),
            jax.ShapeDtypeStruct((4 * W, cols), jnp.bfloat16),
            jax.ShapeDtypeStruct((4 * W, cols), jnp.bfloat16),
            jax.ShapeDtypeStruct((4 * W, cols), jnp.float32),
        ),
        in_specs=[SMEM] * 2 + [HBM] * (3 + len(pieces)),
        out_specs=(HBM,) * 4,
        scratch_shapes=[
            pltpu.VMEM(((blocks + 2) * W, cols), jnp.bfloat16),
            pltpu.VMEM((blocks, 2 * W, W), jnp.bfloat16),
            pltpu.VMEM((blocks, W, 3 * W), jnp.bfloat16),
            pltpu.VMEM((blocks * W, cols), jnp.bfloat16),
            pltpu.VMEM(((blocks - 2) * W, cols), jnp.bfloat16),
            pltpu.VMEM((blocks * W, cols), jnp.float32),
            pltpu.VMEM(result, jnp.bfloat16),
            pltpu.SemaphoreType.DMA((3,)),
            pltpu.SemaphoreType.DMA((len(pieces), held)),
            pltpu.SemaphoreType.DMA((result[0],)),
            pltpu.SemaphoreType.DMA((3, 2)),
        ],
        compiler_params=pltpu.CompilerParams(vmem_limit_bytes=62 * MIB),
        cost_estimate=pl.CostEstimate(flops=flops, bytes_accessed=16 * MIB, transcendentals=0),
        name="chebyshev_inner",
    )(coefficients, owners, v_low, v_mid, v_high, *pieces)


def outer_kernel(
    blocks, coef, kernel_in, v_low, v_mid, v_high, h_low, h_first, h_last, h_high,
    edge_1, edge_2, edge_total, out,
    v, hraw, hcat, cheb_1, cheb_2, total, kern, sems, osems,
):
    last = kern.shape[0] - 1
    end = out.shape[0] - 1
    copies = [
        (h_low, hraw.at[pl.ds(0, 2)]),
        (h_first, hraw.at[pl.ds(2, 2)]),
        (h_last, hraw.at[pl.ds(4, 2)]),
        (h_high, hraw.at[pl.ds(6, 2)]),
        (v_low, v.at[0, rows_of(0, 3)]),
        (v_mid.at[rows_of(0)], v.at[0, rows_of(3)]),
        (v_mid.at[rows_of(blocks - 1)], v.at[1, rows_of(0)]),
        (v_high, v.at[1, rows_of(1, 3)]),
        (edge_1.at[rows_of(0, 2)], cheb_1.at[0, rows_of(2, 2)]),
        (edge_1.at[rows_of(2, 2)], cheb_1.at[1, rows_of(0, 2)]),
        (edge_2.at[rows_of(0, 2)], cheb_2.at[0, rows_of(2, 2)]),
        (edge_2.at[rows_of(2, 2)], cheb_2.at[1, rows_of(0, 2)]),
        (edge_total.at[rows_of(0, 2)], total.at[0]),
        (edge_total.at[rows_of(2, 2)], total.at[1]),
    ]
    copies = [
        pltpu.make_async_copy(source, target, sems.at[i])
        for i, (source, target) in enumerate(copies)
    ]
    for copy in copies:
        copy.start()
    for copy in copies:
        copy.wait()
    lax.fori_loop(0, 8, band_builder(hraw, hcat), 0, unroll=2)

    def band(side, j, source, row):
        return jnp.dot(
            hcat[4 * side + j], source[side, rows_of(row, 3), :], preferred_element_type=jnp.float32
        )

    for side, places in ((0, (0, 1)), (1, (2, 3))):
        for j in places:
            value = band(side, j, v, j - 2 * side)
            cheb_1[side, rows_of(j), :] = value.astype(jnp.bfloat16)
    for side, places in ((0, ((1, 0), (2, 1))), (1, ((2, 3), (1, 2)))):
        for j, place in places:
            begin = v[side, rows_of(place + 2 - 4 * side), :].astype(jnp.float32)
            value = 2.0 * band(side, j, cheb_1, j - 1) - begin
            cheb_2[side, rows_of(place), :] = value.astype(jnp.bfloat16)
            if (j, place) == places[1]:
                within = rows_of(side)
                total[side, within, :] = (
                    coef[0] * begin + (coef[1] - coef[3]) * total[side, within, :] + coef[2] * value
                )
    for side in range(2):
        for half in range(2):
            j = 2 + half if side == 0 else half
            value = total[side, rows_of(half), :] + (2.0 * coef[3]) * band(side, j, cheb_2, half)
            kern[side, :, half * W : (half + 1) * W] = value.astype(jnp.bfloat16).T
    stores = [
        pltpu.make_async_copy(kern.at[0], out.at[0], osems.at[0]),
        pltpu.make_async_copy(kern.at[last], out.at[end], osems.at[1]),
    ]
    for store in stores:
        store.start()
    for store in stores:
        store.wait()


def chebyshev_outer(coefficients, inner, v_low, v_mid, v_high, h_low, h_first, h_last, h_high):
    kernel_t, edge_1, edge_2, edge_total = inner
    blocks = v_mid.shape[0] // W
    cols = v_mid.shape[1]
    return pl.pallas_call(
        functools.partial(outer_kernel, blocks),
        out_shape=jax.ShapeDtypeStruct(kernel_t.shape, kernel_t.dtype),
        in_specs=[SMEM] + [HBM] * 11,
        out_specs=HBM,
        input_output_aliases={1: 0},
        scratch_shapes=[
            pltpu.VMEM((2, 4 * W, cols), jnp.bfloat16),
            pltpu.VMEM((8, 2 * W, W), jnp.bfloat16),
            pltpu.VMEM((8, W, 3 * W), jnp.bfloat16),
            pltpu.VMEM((2, 4 * W, cols), jnp.bfloat16),
            pltpu.VMEM((2, 4 * W, cols), jnp.bfloat16),
            pltpu.VMEM((2, 2 * W, cols), jnp.float32),
            pltpu.VMEM((2, cols, KB), jnp.bfloat16),
            pltpu.SemaphoreType.DMA((14,)),
            pltpu.SemaphoreType.DMA((2,)),
        ],
        compiler_params=pltpu.CompilerParams(vmem_limit_bytes=62 * MIB),
        name="chebyshev_outer",
    )(
        coefficients, kernel_t, v_low, v_mid, v_high, h_low, h_first, h_last, h_high,
        edge_1, edge_2, edge_total,
    )


def entry_loads(order, parts, pair, sems):
    size = parts[0].shape[0]

    def load(p):
        return pltpu.make_async_copy(parts[0].at[0], pair.at[p], sems.at[p])

    def start(p, carry):
        n = order[p]
        for t, part in enumerate(parts):
            @pl.when((n >= t * size) & (n < (t + 1) * size))
            def _():
                pltpu.make_async_copy(part.at[n - t * size], pair.at[p], sems.at[p]).start()

        return carry

    return load, start


def by_twos(first, last, load, body):
    def step(i, carry):
        p = first + 2 * i
        q = jnp.minimum(p + 1, last - 1)
        load(p).wait()

        @pl.when(q > p)
        def _():
            load(q).wait()

        body(i, p, q)
        return carry

    lax.fori_loop(0, (last - first + 1) // 2, step, 0)


def sent_rows(slots, tiles):
    return slots + tiles + -(slots + tiles) % 8


def project_kernel(blocks, plan, order, kernel_t, core, *refs):
    *parts, out, kern, pair, rows, ksems, bsems = refs
    slots = pair.shape[0]
    load, start = entry_loads(order, parts, pair, bsems)

    def fetch(b):
        return pltpu.make_async_copy(kernel_t.at[b], kern.at[b], ksems.at[b])

    def begin(b, carry):
        first, last = plan[slots + b], plan[slots + b + 1]

        @pl.when(first < last)
        def _():
            fetch(b).start()

        return lax.fori_loop(first, last, start, carry)

    lax.fori_loop(0, blocks, begin, 0)
    rows[...] = jnp.zeros_like(rows)
    rows[slots : slots + core.shape[0]] = core[...]

    def step(b, carry):
        first, last = plan[slots + b], plan[slots + b + 1]

        @pl.when(first < last)
        def _():
            fetch(b).wait()

        def body(i, p, q):
            both = jnp.concatenate([pair[p, 0], pair[q, 0]], axis=1)
            projected = jnp.dot(kern[b], both, preferred_element_type=jnp.float32)
            other = jnp.concatenate([pair[p, 1], pair[q, 1]], axis=1).astype(jnp.float32)
            value = jnp.sum(projected * other, axis=0, keepdims=True) * (1.0 / KB)
            rows[pl.ds(order[p], 1), :] = value[:, :P_SIZE]
            rows[pl.ds(order[q], 1), :] = value[:, P_SIZE:]

        by_twos(first, last, load, body)
        return carry

    lax.fori_loop(0, blocks, step, 0)
    for c in range(out.shape[0]):
        out[c] = rows[...]


def project(plan, order, kernel_t, core, parts, col_count):
    slots = col_count * CAP
    entry = parts[0].shape[1:]
    sent = sent_rows(slots, core.shape[0])
    blocks = kernel_t.shape[0]
    return pl.pallas_call(
        functools.partial(project_kernel, blocks),
        out_shape=jax.ShapeDtypeStruct((col_count, sent, P_SIZE), jnp.float32),
        in_specs=[SMEM, SMEM, HBM, VMEM] + [HBM] * len(parts),
        out_specs=VMEM,
        scratch_shapes=[
            pltpu.VMEM(kernel_t.shape, jnp.bfloat16),
            pltpu.VMEM((slots,) + entry, jnp.bfloat16),
            pltpu.VMEM((sent, P_SIZE), jnp.float32),
            pltpu.SemaphoreType.DMA((blocks,)),
            pltpu.SemaphoreType.DMA((slots,)),
        ],
        compiler_params=pltpu.CompilerParams(vmem_limit_bytes=62 * MIB),
        name="project",
    )(plan, order, kernel_t, core, *parts)


def update_kernel(
    blocks, tiles, plan, order, tile_of, contributions, collect, *refs
):
    *parts, density_out, update_out, pair, density, potential, acc, stage, sems, osems = refs
    slots = pair.shape[0]
    live = plan[slots + blocks]
    me = plan[slots + blocks + 1]
    load, start = entry_loads(order, parts, pair, sems)
    lax.fori_loop(0, live, start, 0)
    density[...] = jnp.dot(
        collect[...],
        contributions[...],
        preferred_element_type=jnp.float32,
        precision=lax.Precision.HIGHEST,
    )
    for t in range(tiles):
        density_out[pl.ds(t, 1), :] = density[pl.ds(me * tiles + t, 1), :]
    positive = jnp.maximum(density[...], 0.1)
    root = jnp.exp(jnp.log(positive) * (1.0 / 3.0))
    root = root - (root - positive / (root * root)) * (1.0 / 3.0)
    potential[...] = -exchange_factor * root
    scale = 1.0 / math.sqrt(P_SIZE)

    def store(b):
        rows = pl.ds(pl.multiple_of(b * KB, KB), KB)
        return pltpu.make_async_copy(stage.at[b], update_out.at[rows], osems.at[b])

    def step(b, carry):
        first, last = plan[slots + b], plan[slots + b + 1]

        @pl.when(first == last)
        def _():
            stage[b] = jnp.zeros(stage.shape[1:], jnp.bfloat16)

        def body(i, p, q):
            weight_p = potential[pl.ds(tile_of[order[p]], 1), :]
            weight_q = potential[pl.ds(tile_of[order[q]], 1), :] * (q - p).astype(jnp.float32)
            weighted = jnp.concatenate(
                [
                    (pair[p, 1].astype(jnp.float32) * weight_p).astype(jnp.bfloat16),
                    (pair[q, 1].astype(jnp.float32) * weight_q).astype(jnp.bfloat16),
                ],
                axis=1,
            )
            block = lax.dot_general(
                jnp.concatenate([pair[p, 0], pair[q, 0]], axis=1),
                weighted,
                (((1,), (1,)), ((), ())),
                preferred_element_type=jnp.float32,
            )

            @pl.when(last - first <= 2)
            def _():
                stage[b] = (block * scale).astype(jnp.bfloat16)

            @pl.when((last - first > 2) & (i == 0))
            def _():
                acc[...] = block

            @pl.when(i > 0)
            def _():
                acc[...] += block

        by_twos(first, last, load, body)

        @pl.when(last - first > 2)
        def _():
            stage[b] = (acc[...] * scale).astype(jnp.bfloat16)

        store(b).start()
        return carry

    lax.fori_loop(0, blocks, step, 0)
    for b in range(blocks):
        store(b).wait()


def update(plan, order, tile_of, contributions, collect, parts, tiles, blocks, cols):
    slots = len(parts) * parts[0].shape[0]
    entry = parts[0].shape[1:]
    all_tiles = (collect.shape[0], P_SIZE)
    return pl.pallas_call(
        functools.partial(update_kernel, blocks, tiles),
        out_shape=(
            jax.ShapeDtypeStruct((tiles, P_SIZE), jnp.float32),
            jax.ShapeDtypeStruct((blocks * KB, cols), jnp.bfloat16),
        ),
        in_specs=[SMEM] * 3 + [VMEM] * 2 + [HBM] * len(parts),
        out_specs=(VMEM, HBM),
        scratch_shapes=[
            pltpu.VMEM((slots,) + entry, jnp.bfloat16),
            pltpu.VMEM(all_tiles, jnp.float32),
            pltpu.VMEM(all_tiles, jnp.float32),
            pltpu.VMEM((KB, cols), jnp.float32),
            pltpu.VMEM((blocks, KB, cols), jnp.bfloat16),
            pltpu.SemaphoreType.DMA((slots,)),
            pltpu.SemaphoreType.DMA((blocks,)),
        ],
        compiler_params=pltpu.CompilerParams(vmem_limit_bytes=62 * MIB),
        name="update",
    )(plan, order, tile_of, contributions, collect, *parts)


def shift(block, axis, step):
    count = lax.axis_size(axis)
    pairs = [(i, i + step) for i in range(count) if 0 <= i + step < count]
    return lax.ppermute(block, axis, pairs)


def make_plan(lists, me, entries, tiles, col_count, blocks):
    slots = col_count * CAP
    sent = sent_rows(slots, tiles)
    lists = lists[:, : 2 * entries + tiles].astype(jnp.int32)
    peers, named, counts = lists[:, :entries], lists[:, entries : 2 * entries], lists[:, 2 * entries :]
    index = jnp.arange(entries, dtype=jnp.int32)
    home = jnp.arange(col_count, dtype=jnp.int32)[:, None]
    earlier = (peers[:, :, None] == peers[:, None, :]) & (index[None, :] < index[:, None])
    rank = jnp.sum(earlier.astype(jnp.int32), axis=2)
    live = (index % SLOTS)[None, :] < jnp.repeat(counts, SLOTS, axis=1)
    row = jnp.where(live, peers * sent + chunk_of(home, peers, col_count) * CAP + rank, -1).reshape(col_count, tiles, SLOTS)
    core = (home * sent + slots + jnp.arange(tiles, dtype=jnp.int32))[:, :, None]
    row = jnp.concatenate([row, core], axis=2).reshape(col_count * tiles, SLOTS + 1, 1)
    picked = row == jnp.arange(col_count * sent, dtype=jnp.int32)
    collect = jnp.sum(picked.astype(jnp.float32), axis=1)
    hit = (
        (peers == me)[:, None, :]
        & (rank[:, None, :] == jnp.arange(CAP, dtype=jnp.int32)[None, :, None])
        & live[:, None, :]
    )
    at_me = chunk_of(home, me, col_count).reshape(1, col_count) == home
    tile = home * tiles + index[None, :] // SLOTS

    def of_slots(values):
        by_home = jnp.sum(jnp.where(hit, values[:, None, :], 0), axis=2)
        return jnp.sum(jnp.where(at_me[:, :, None], by_home[None], 0), axis=1).reshape(slots)

    wanted = of_slots(named + 1) - 1
    tile_of = of_slots(tile)
    key = jnp.where(wanted < 0, blocks, wanted)
    place = jnp.arange(slots, dtype=jnp.int32)
    before = (key[None, :] < key[:, None]) | (
        (key[None, :] == key[:, None]) & (place[None, :] < place[:, None])
    )
    spot = jnp.sum(before.astype(jnp.int32), axis=1)
    order = jnp.sum(jnp.where(spot[None, :] == place[:, None], place[None, :], 0), axis=1)
    starts = jnp.sum(
        (key[None, :] < jnp.arange(blocks + 1, dtype=jnp.int32)[:, None]).astype(jnp.int32), axis=1
    )
    plan = jnp.concatenate([wanted, starts, me[None]]).astype(jnp.int32)
    return collect, plan, order.astype(jnp.int32), tile_of.astype(jnp.int32)


def shards(
    start_columns,
    hamiltonian,
    band_pattern,
    coefficients,
    tile_peer,
    tile_block,
    tile_count,
    basis_values,
    core_density,
):
    col_count = lax.axis_size("col")
    entries = tile_peer.shape[0]
    tiles = core_density.shape[0]
    cols = start_columns.shape[1]
    blocks = start_columns.shape[0] // KB
    peers = tile_peer[:, 0]
    me = lax.axis_index("col").astype(jnp.int32)

    own = own_piece(peers, tile_block, tile_count, band_pattern, hamiltonian.reshape(-1, W))
    pieces, owners, awaited = gather_pieces(own)
    v_low = shift(start_columns[-DEG * W :], "row", 1)
    v_high = shift(start_columns[: DEG * W], "row", -1)
    parts = exchange(me[None], peers, basis_values, own, awaited + [v_low, v_high])

    first, last, lists = edge_blocks(owners, pieces, col_count, DEG - 1)
    h_low = shift(last, "row", 1)
    h_high = shift(first, "row", -1)
    inner = chebyshev_inner(coefficients, owners, v_low, start_columns, v_high, pieces)
    kernel_t = chebyshev_outer(
        coefficients, inner, v_low, start_columns, v_high, h_low, first, last, h_high
    )
    collect, plan, order, tile_of = make_plan(lists[:, 0], me, entries, tiles, col_count, blocks)
    partial = project(plan, order, kernel_t, core_density, parts, col_count)
    contributions = lax.all_to_all(partial, "col", split_axis=0, concat_axis=0, tiled=True)
    contributions = contributions.reshape(-1, P_SIZE)
    return update(
        plan, order, tile_of, contributions, collect, parts, tiles, blocks, cols
    )


def solution(mesh):
    return jax.shard_map(
        shards,
        mesh=mesh,
        in_specs=(
            P("row", "col"),
            P(("row", "col"), None, None, None),
            P(("row", "col")),
            P(),
            P(("row", "col"), None),
            P(("row", "col")),
            P(("row", "col")),
            P(("row", "col"), None, None, None),
            P(("row", "col"), None),
        ),
        out_specs=(P(("row", "col"), None), P("row", "col")),
        check_vma=False,
    )
```

```python
import functools
import math

import jax
import jax.numpy as jnp
from jax import lax
from jax.experimental import pallas as pl
from jax.experimental.pallas import tpu as pltpu
from jax.sharding import PartitionSpec as P

W = 256
KB = 512
DEG = 3
SLOTS = 4
CAP = 2
P_SIZE = 128
MIB = 1 << 20
LISTS = 8

exchange_factor = (3.0 / math.pi) ** (1.0 / 3.0)
HBM = pl.BlockSpec(memory_space=pltpu.HBM)
ANY = pl.BlockSpec(memory_space=pl.ANY)
SMEM = pl.BlockSpec(memory_space=pltpu.SMEM)
VMEM = pl.BlockSpec(memory_space=pltpu.VMEM)


def partner(me, j, count):
    if count & (count - 1) == 0:
        return me ^ abs(j)
    return (me + j) % count


def piece_kernel(peers, named, counts, pattern, ham, piece, lists, blocks, sems):
    load = pltpu.make_async_copy(ham, blocks, sems.at[0])
    load.start()
    lane = lax.broadcasted_iota(jnp.int32, (LISTS, P_SIZE), 1)
    row = jnp.zeros((LISTS, P_SIZE), jnp.int32)
    at = 0
    for ref in (peers, named, counts):
        for i in range(ref.shape[0]):
            row = jnp.where(lane == at, ref[i], row)
            at += 1
    for c in range(lists.shape[0]):
        lists[c] = row
    load.wait()
    for i in range(ham.shape[0] // (2 * W)):
        coupling = slice((2 * i + 1) * W, (2 * i + 2) * W)
        blocks[coupling] = blocks[coupling] * pattern[i].astype(jnp.bfloat16)
    store = pltpu.make_async_copy(blocks, piece, sems.at[1])
    store.start()
    store.wait()


def own_piece(peers, named, counts, pattern, ham, col_count):
    return pl.pallas_call(
        piece_kernel,
        out_shape=(
            jax.ShapeDtypeStruct(ham.shape, ham.dtype),
            jax.ShapeDtypeStruct((col_count, LISTS, P_SIZE), jnp.int32),
        ),
        in_specs=[SMEM] * 4 + [HBM],
        out_specs=(HBM, VMEM),
        scratch_shapes=[pltpu.VMEM(ham.shape, ham.dtype), pltpu.SemaphoreType.DMA((2,))],
        compiler_params=pltpu.CompilerParams(vmem_limit_bytes=62 * MIB),
        name="own_piece",
    )(peers, named, counts, pattern, ham)


def lines_of(count):
    inner = max(count // 4, 1) if count & (count - 1) == 0 else 1
    return count // inner, inner


def swap_along(block, t):
    count = lax.axis_size("col")
    _, inner = lines_of(count)
    pairs = [(c, c - c % inner + partner(c % inner, t, inner)) for c in range(count)]
    return lax.ppermute(block, "col", pairs)


def chunk_of(home, owner, count):
    outer, inner = lines_of(count)
    return partner(home % inner, owner % inner, inner) * outer + home // inner


def pack_kernel(entries, col_count, wanted, me, peers, basis, first, *refs):
    outer, inner = lines_of(col_count)
    sent, (held, owner, count, in_sems, out_sems) = refs[: len(wanted)], refs[len(wanted) :]
    for c in range(col_count):
        count[c] = 0
        for k in range(CAP):
            owner[c * CAP + k] = 0
    for e in range(entries):
        p = peers[e]
        k = count[p]
        count[p] = k + 1
        owner[p * CAP + k] = e
    place = lax.rem(me[0], inner)
    tasks = []
    for target, group in zip(sent, wanted):
        for line in range(outer):
            for i, (t, k) in enumerate(group):
                n = len(tasks)
                e = owner[(line * inner + partner(place, t, inner)) * CAP + k]
                fetch = pltpu.make_async_copy(basis.at[e], held.at[n], in_sems.at[n])
                store = pltpu.make_async_copy(held.at[n], target.at[line, i], out_sems.at[n])
                tasks.append((fetch, store))
    for fetch, _ in tasks:
        fetch.start()
    for fetch, store in tasks:
        fetch.wait()
        store.start()
    for _, store in tasks:
        store.wait()


def pack(me, peers, basis, first, col_count, wanted):
    outer, _ = lines_of(col_count)
    entries = basis.shape[0]
    number = sum(len(group) for group in wanted) * outer
    return list(pl.pallas_call(
        functools.partial(pack_kernel, entries, col_count, wanted),
        out_shape=tuple(
            jax.ShapeDtypeStruct((outer, len(group)) + basis.shape[1:], basis.dtype)
            for group in wanted
        ),
        in_specs=[SMEM, SMEM, HBM, HBM],
        out_specs=(HBM,) * len(wanted),
        scratch_shapes=[
            pltpu.VMEM((number,) + basis.shape[1:], basis.dtype),
            pltpu.SMEM((col_count * CAP,), jnp.int32),
            pltpu.SMEM((col_count,), jnp.int32),
            pltpu.SemaphoreType.DMA((number,)),
            pltpu.SemaphoreType.DMA((number,)),
        ],
        compiler_params=pltpu.CompilerParams(vmem_limit_bytes=62 * MIB),
        name="pack",
    )(me, peers, basis, first))


def after(block, *others):
    return pl.pallas_call(
        lambda *refs: None,
        out_shape=jax.ShapeDtypeStruct(block.shape, block.dtype),
        in_specs=[HBM] + [ANY] * len(others),
        out_specs=HBM,
        input_output_aliases={0: 0},
        compiler_params=pltpu.CompilerParams(vmem_limit_bytes=62 * MIB),
        name="after",
    )(block, *others)


def exchange(me, peers, basis, own, awaited):
    count = lax.axis_size("col")
    outer, inner = lines_of(count)
    groups = [[line * inner + place for line in range(outer)] for place in range(inner)]

    def between_lines(blocks, *others):
        block = jnp.concatenate(blocks, axis=1)
        return lax.all_to_all(
            after(block, *others), "col", split_axis=0, concat_axis=0,
            axis_index_groups=groups, tiled=True,
        )

    here = [(0, k) for k in range(CAP)]
    ahead = [[(t, 0)] for t in range(1, inner)]
    rest = [[(t, k)] for k in range(1, CAP) for t in range(1, inner)]
    sent = pack(me, peers, basis, own, count, ahead) if ahead else []
    to_lines, *later = pack(me, peers, basis, sent[0] if ahead else own, count, [here] + rest)
    swapped = {
        group[0]: swap_along(block, group[0][0]) for block, group in zip(sent + later, ahead + rest)
    }
    parts = [between_lines([to_lines], *awaited, *[swapped[group[0]] for group in ahead])]
    for t in range(1, inner):
        parts.append(between_lines([swapped[t, k] for k in range(CAP)], parts[-1]))
    return [part.reshape((outer * CAP,) + part.shape[2:]) for part in parts]


def gather_pieces(own):
    count = lax.axis_size("col")
    outer, inner = lines_of(count)
    me = lax.axis_index("col").astype(jnp.int32)
    a, b = me // inner, me % inner

    def move(block, ways):
        pairs = [(x * inner + y, z * inner + y) for x, z in ways for y in range(inner)]
        return lax.ppermute(block, "col", pairs)

    if outer == 4:
        middle, outwards = [(1, 2), (2, 1)], [(1, 0), (2, 3)]
        near = move(own, [(0, 1), (1, 0), (2, 3), (3, 2)])
        across = move(own, middle)
        far = move(near, middle)
        handed = move(across, outwards)
        last = move(far, outwards)
        within = (a == 1) | (a == 2)
        lines = [
            (own, a),
            (near, a ^ 1),
            (across + handed, jnp.where(within, a ^ 3, a ^ 2)),
            (far + last, jnp.where(within, a ^ 2, a ^ 3)),
        ]
        awaited = [far, handed]
    else:
        lines = [(own, a)] + [
            (move(own, [(x, partner(x, t, outer)) for x in range(outer)]), partner(a, -t, outer))
            for t in range(1, outer)
        ]
        awaited = [block for block, _ in lines[1:]]
    pieces, owners = [], []
    for block, line in lines:
        pieces.append(block)
        owners.append(line * inner + b)
        for t in range(1, inner):
            pieces.append(swap_along(block, t))
            owners.append(line * inner + partner(b, -t, inner))
    return pieces, jnp.stack(owners).astype(jnp.int32), awaited


def edge_kernel(col_count, depth, owners, *refs):
    pieces, (first, last, sems) = refs[:-3], refs[-3:]
    held = pieces[0].shape[0] // (2 * W)
    total = col_count * held

    def each(act):
        for i, piece in enumerate(pieces):
            for g in range(depth):
                for out, block, sem in ((first, g, 0), (last, total - depth + g, 1)):
                    source = piece.at[pl.ds(block % held * 2 * W, 2 * W)]
                    copy = pltpu.make_async_copy(source, out.at[g], sems.at[sem, g])

                    @pl.when(owners[i] == block // held)
                    def _():
                        act(copy)

    each(lambda copy: copy.start())
    each(lambda copy: copy.wait())


def edge_blocks(owners, pieces, col_count, depth):
    shape = jax.ShapeDtypeStruct((depth, 2 * W, W), pieces[0].dtype)
    return pl.pallas_call(
        functools.partial(edge_kernel, col_count, depth),
        out_shape=(shape, shape),
        in_specs=[SMEM] + [HBM] * len(pieces),
        out_specs=(VMEM, VMEM),
        scratch_shapes=[pltpu.SemaphoreType.DMA((2, depth))],
        compiler_params=pltpu.CompilerParams(vmem_limit_bytes=62 * MIB),
        name="edge_blocks",
    )(owners, *pieces)


def rows_of(j, count=1):
    return pl.ds(j * W if isinstance(j, int) else pl.multiple_of(j * W, W), count * W)


def band_builder(source, target):
    rows = lax.broadcasted_iota(jnp.int32, (W, W), 0)
    cols = lax.broadcasted_iota(jnp.int32, (W, W), 1)
    upper = jnp.where(rows <= cols, 1.0, 0.0).astype(jnp.bfloat16)

    def build(j, carry):
        coupling = source[j, W:]
        lower_band = coupling * upper
        target[j, :, 0:W] = lower_band
        target[j, :, W : 2 * W] = source[j, :W]
        target[j, :, 2 * W : 3 * W] = coupling - lower_band
        return carry

    return build


def inner_kernel(blocks, coef, owners, v_low, v_mid, v_high, *refs):
    (
        *pieces, out, edge_1, edge_2, edge_total,
        vext, hraw, hcat, cheb_1, cheb_2, total, kern, sems, psems, osems, esems,
    ) = refs
    held = pieces[0].shape[0] // (2 * W)
    v_copies = [
        pltpu.make_async_copy(v_low.at[rows_of(DEG - 1)], vext.at[rows_of(0)], sems.at[0]),
        pltpu.make_async_copy(v_mid, vext.at[rows_of(1, blocks)], sems.at[1]),
        pltpu.make_async_copy(v_high.at[rows_of(0)], vext.at[rows_of(blocks + 1)], sems.at[2]),
    ]

    def each_piece(act):
        for i, piece in enumerate(pieces):
            for k in range(held):
                act(pltpu.make_async_copy(
                    piece.at[pl.ds(k * 2 * W, 2 * W)],
                    hraw.at[owners[i] * held + k],
                    psems.at[i, k],
                ))

    each_piece(lambda copy: copy.start())
    for copy in v_copies:
        copy.start()
    each_piece(lambda copy: copy.wait())
    build = band_builder(hraw, hcat)
    build(0, 0)
    for copy in v_copies:
        copy.wait()

    def band(source, j, row):
        return jnp.dot(hcat[j], source[rows_of(row, 3), :], preferred_element_type=jnp.float32)

    def edges(source, target, at):
        size = source.shape[0] // W
        return [
            pltpu.make_async_copy(
                source.at[rows_of(place, 2)], target.at[rows_of(2 * i, 2)], esems.at[at, i]
            )
            for i, place in enumerate((0, size - 2))
        ]

    def first(j, carry):
        value = band(vext, j, j)
        build(jnp.minimum(j + 1, blocks - 1), 0)
        cheb_1[rows_of(j), :] = value.astype(jnp.bfloat16)
        total[rows_of(j), :] = value
        return carry

    lax.fori_loop(0, blocks, first, 0, unroll=4)

    def second(j, carry):
        begin = vext[rows_of(j + 2), :].astype(jnp.float32)
        value = 2.0 * band(cheb_1, j + 1, j) - begin
        cheb_2[rows_of(j), :] = value.astype(jnp.bfloat16)
        total[rows_of(j + 1), :] = (
            coef[0] * begin + (coef[1] - coef[3]) * total[rows_of(j + 1), :] + coef[2] * value
        )
        return carry

    lax.fori_loop(0, blocks - 2, second, 0, unroll=4)
    outgoing = (
        edges(cheb_1, edge_1, 0) + edges(cheb_2, edge_2, 1) + edges(total, edge_total, 2)
    )
    for copy in outgoing:
        copy.start()

    def store(j):
        return pltpu.make_async_copy(kern.at[j], out.at[j], osems.at[j])

    def third(j, carry):
        for half in range(KB // W):
            i = j * (KB // W) + half
            value = total[rows_of(i), :] + (2.0 * coef[3]) * band(cheb_2, i, i - 2)
            kern[j, :, half * W : (half + 1) * W] = value.astype(jnp.bfloat16).T
        store(j).start()
        return carry

    last = blocks // (KB // W) - 1
    lax.fori_loop(1, last, third, 0, unroll=2)
    for j in range(1, last):
        store(j).wait()
    for copy in outgoing:
        copy.wait()


def chebyshev_inner(coefficients, owners, v_low, v_mid, v_high, pieces):
    blocks = v_mid.shape[0] // W
    cols = v_mid.shape[1]
    flops = 2 * W * 3 * W * cols * (3 * blocks - 6)
    result = (blocks * W // KB, cols, KB)
    held = pieces[0].shape[0] // (2 * W)
    return pl.pallas_call(
        functools.partial(inner_kernel, blocks),
        out_shape=(
            jax.ShapeDtypeStruct(result, jnp.bfloat16),
            jax.ShapeDtypeStruct((4 * W, cols), jnp.bfloat16),
            jax.ShapeDtypeStruct((4 * W, cols), jnp.bfloat16),
            jax.ShapeDtypeStruct((4 * W, cols), jnp.float32),
        ),
        in_specs=[SMEM] * 2 + [HBM] * (3 + len(pieces)),
        out_specs=(HBM,) * 4,
        scratch_shapes=[
            pltpu.VMEM(((blocks + 2) * W, cols), jnp.bfloat16),
            pltpu.VMEM((blocks, 2 * W, W), jnp.bfloat16),
            pltpu.VMEM((blocks, W, 3 * W), jnp.bfloat16),
            pltpu.VMEM((blocks * W, cols), jnp.bfloat16),
            pltpu.VMEM(((blocks - 2) * W, cols), jnp.bfloat16),
            pltpu.VMEM((blocks * W, cols), jnp.float32),
            pltpu.VMEM(result, jnp.bfloat16),
            pltpu.SemaphoreType.DMA((3,)),
            pltpu.SemaphoreType.DMA((len(pieces), held)),
            pltpu.SemaphoreType.DMA((result[0],)),
            pltpu.SemaphoreType.DMA((3, 2)),
        ],
        compiler_params=pltpu.CompilerParams(vmem_limit_bytes=62 * MIB),
        cost_estimate=pl.CostEstimate(flops=flops, bytes_accessed=16 * MIB, transcendentals=0),
        name="chebyshev_inner",
    )(coefficients, owners, v_low, v_mid, v_high, *pieces)


def outer_kernel(
    blocks, coef, kernel_in, v_low, v_mid, v_high, h_low, h_first, h_last, h_high,
    edge_1, edge_2, edge_total, out,
    v, hraw, hcat, cheb_1, cheb_2, total, kern, sems, osems,
):
    last = kern.shape[0] - 1
    end = out.shape[0] - 1
    stages = [
        [
            (h_low, hraw.at[pl.ds(0, 2)]),
            (v_low, v.at[0, rows_of(0, 3)]),
            (v_mid.at[rows_of(0)], v.at[0, rows_of(3)]),
            (h_high, hraw.at[pl.ds(6, 2)]),
            (v_mid.at[rows_of(blocks - 1)], v.at[1, rows_of(0)]),
            (v_high, v.at[1, rows_of(1, 3)]),
        ],
        [
            (h_first, hraw.at[pl.ds(2, 2)]),
            (h_last, hraw.at[pl.ds(4, 2)]),
            (edge_1.at[rows_of(0, 2)], cheb_1.at[0, rows_of(2, 2)]),
            (edge_1.at[rows_of(2, 2)], cheb_1.at[1, rows_of(0, 2)]),
        ],
        [
            (edge_2.at[rows_of(0, 2)], cheb_2.at[0, rows_of(2, 2)]),
            (edge_2.at[rows_of(2, 2)], cheb_2.at[1, rows_of(0, 2)]),
            (edge_total.at[rows_of(0, 2)], total.at[0]),
            (edge_total.at[rows_of(2, 2)], total.at[1]),
        ],
    ]
    at = 0
    for i, stage in enumerate(stages):
        stages[i] = [
            pltpu.make_async_copy(source, target, sems.at[at + n])
            for n, (source, target) in enumerate(stage)
        ]
        at += len(stage)
        for copy in stages[i]:
            copy.start()
    build = band_builder(hraw, hcat)

    def arrived(i):
        for copy in stages[i]:
            copy.wait()

    def band(side, j, source, row):
        return jnp.dot(
            hcat[4 * side + j], source[side, rows_of(row, 3), :], preferred_element_type=jnp.float32
        )

    arrived(0)
    for j in (0, 1, 6, 7):
        build(j, 0)
    for side, places in ((0, (0, 1)), (1, (2, 3))):
        for j in places:
            value = band(side, j, v, j - 2 * side)
            cheb_1[side, rows_of(j), :] = value.astype(jnp.bfloat16)
    arrived(1)
    for j in (2, 3, 4, 5):
        build(j, 0)
    arrived(2)
    for side, places in ((0, ((1, 0), (2, 1))), (1, ((2, 3), (1, 2)))):
        for j, place in places:
            begin = v[side, rows_of(place + 2 - 4 * side), :].astype(jnp.float32)
            value = 2.0 * band(side, j, cheb_1, j - 1) - begin
            cheb_2[side, rows_of(place), :] = value.astype(jnp.bfloat16)
            if (j, place) == places[1]:
                within = rows_of(side)
                total[side, within, :] = (
                    coef[0] * begin + (coef[1] - coef[3]) * total[side, within, :] + coef[2] * value
                )
    for side in range(2):
        for half in range(2):
            j = 2 + half if side == 0 else half
            value = total[side, rows_of(half), :] + (2.0 * coef[3]) * band(side, j, cheb_2, half)
            kern[side, :, half * W : (half + 1) * W] = value.astype(jnp.bfloat16).T
    stores = [
        pltpu.make_async_copy(kern.at[0], out.at[0], osems.at[0]),
        pltpu.make_async_copy(kern.at[last], out.at[end], osems.at[1]),
    ]
    for store in stores:
        store.start()
    for store in stores:
        store.wait()


def chebyshev_outer(coefficients, inner, v_low, v_mid, v_high, h_low, h_first, h_last, h_high):
    kernel_t, edge_1, edge_2, edge_total = inner
    blocks = v_mid.shape[0] // W
    cols = v_mid.shape[1]
    return pl.pallas_call(
        functools.partial(outer_kernel, blocks),
        out_shape=jax.ShapeDtypeStruct(kernel_t.shape, kernel_t.dtype),
        in_specs=[SMEM] + [HBM] * 11,
        out_specs=HBM,
        input_output_aliases={1: 0},
        scratch_shapes=[
            pltpu.VMEM((2, 4 * W, cols), jnp.bfloat16),
            pltpu.VMEM((8, 2 * W, W), jnp.bfloat16),
            pltpu.VMEM((8, W, 3 * W), jnp.bfloat16),
            pltpu.VMEM((2, 4 * W, cols), jnp.bfloat16),
            pltpu.VMEM((2, 4 * W, cols), jnp.bfloat16),
            pltpu.VMEM((2, 2 * W, cols), jnp.float32),
            pltpu.VMEM((2, cols, KB), jnp.bfloat16),
            pltpu.SemaphoreType.DMA((14,)),
            pltpu.SemaphoreType.DMA((2,)),
        ],
        compiler_params=pltpu.CompilerParams(vmem_limit_bytes=62 * MIB),
        name="chebyshev_outer",
    )(
        coefficients, kernel_t, v_low, v_mid, v_high, h_low, h_first, h_last, h_high,
        edge_1, edge_2, edge_total,
    )


def entry_loads(order, parts, pair, sems):
    size = parts[0].shape[0]

    def load(p):
        return pltpu.make_async_copy(parts[0].at[0], pair.at[p], sems.at[p])

    def start(p, carry):
        n = order[p]
        for t, part in enumerate(parts):
            @pl.when((n >= t * size) & (n < (t + 1) * size))
            def _():
                pltpu.make_async_copy(part.at[n - t * size], pair.at[p], sems.at[p]).start()

        return carry

    return load, start


def by_twos(first, last, load, body):
    def step(i, carry):
        p = first + 2 * i
        q = jnp.minimum(p + 1, last - 1)
        load(p).wait()

        @pl.when(q > p)
        def _():
            load(q).wait()

        body(i, p, q)
        return carry

    lax.fori_loop(0, (last - first + 1) // 2, step, 0)


def sent_rows(slots, tiles):
    return slots + tiles + -(slots + tiles) % 8


def project_kernel(blocks, plan, order, kernel_t, core, *refs):
    *parts, out, kern, pair, rows, ksems, bsems = refs
    slots = pair.shape[0]
    load, start = entry_loads(order, parts, pair, bsems)

    def fetch(b):
        return pltpu.make_async_copy(kernel_t.at[b], kern.at[b], ksems.at[b])

    def begin(b, carry):
        first, last = plan[slots + b], plan[slots + b + 1]

        @pl.when(first < last)
        def _():
            fetch(b).start()

        return lax.fori_loop(first, last, start, carry)

    lax.fori_loop(0, blocks, begin, 0)
    rows[...] = jnp.zeros_like(rows)
    rows[slots : slots + core.shape[0]] = core[...]

    def step(b, carry):
        first, last = plan[slots + b], plan[slots + b + 1]

        @pl.when(first < last)
        def _():
            fetch(b).wait()

        def body(i, p, q):
            both = jnp.concatenate([pair[p, 0], pair[q, 0]], axis=1)
            projected = jnp.dot(kern[b], both, preferred_element_type=jnp.float32)
            other = jnp.concatenate([pair[p, 1], pair[q, 1]], axis=1).astype(jnp.float32)
            value = jnp.sum(projected * other, axis=0, keepdims=True) * (1.0 / KB)
            rows[pl.ds(order[p], 1), :] = value[:, :P_SIZE]
            rows[pl.ds(order[q], 1), :] = value[:, P_SIZE:]

        by_twos(first, last, load, body)
        return carry

    lax.fori_loop(0, blocks, step, 0)
    for c in range(out.shape[0]):
        out[c] = rows[...]


def project(plan, order, kernel_t, core, parts, col_count):
    slots = col_count * CAP
    entry = parts[0].shape[1:]
    sent = sent_rows(slots, core.shape[0])
    blocks = kernel_t.shape[0]
    return pl.pallas_call(
        functools.partial(project_kernel, blocks),
        out_shape=jax.ShapeDtypeStruct((col_count, sent, P_SIZE), jnp.float32),
        in_specs=[SMEM, SMEM, HBM, VMEM] + [HBM] * len(parts),
        out_specs=VMEM,
        scratch_shapes=[
            pltpu.VMEM(kernel_t.shape, jnp.bfloat16),
            pltpu.VMEM((slots,) + entry, jnp.bfloat16),
            pltpu.VMEM((sent, P_SIZE), jnp.float32),
            pltpu.SemaphoreType.DMA((blocks,)),
            pltpu.SemaphoreType.DMA((slots,)),
        ],
        compiler_params=pltpu.CompilerParams(vmem_limit_bytes=62 * MIB),
        name="project",
    )(plan, order, kernel_t, core, *parts)


def update_kernel(
    blocks, tiles, plan, order, tile_of, contributions, collect, *refs
):
    *parts, density_out, update_out, pair, density, potential, acc, stage, sems, osems = refs
    slots = pair.shape[0]
    live = plan[slots + blocks]
    me = plan[slots + blocks + 1]
    load, start = entry_loads(order, parts, pair, sems)
    lax.fori_loop(0, live, start, 0)
    density[...] = jnp.dot(
        collect[...],
        contributions[...],
        preferred_element_type=jnp.float32,
        precision=lax.Precision.HIGHEST,
    )
    for t in range(tiles):
        density_out[pl.ds(t, 1), :] = density[pl.ds(me * tiles + t, 1), :]
    positive = jnp.maximum(density[...], 0.1)
    root = jnp.exp(jnp.log(positive) * (1.0 / 3.0))
    root = root - (root - positive / (root * root)) * (1.0 / 3.0)
    potential[...] = -exchange_factor * root
    scale = 1.0 / math.sqrt(P_SIZE)

    def store(b):
        rows = pl.ds(pl.multiple_of(b * KB, KB), KB)
        return pltpu.make_async_copy(stage.at[b], update_out.at[rows], osems.at[b])

    def step(b, carry):
        first, last = plan[slots + b], plan[slots + b + 1]

        @pl.when(first == last)
        def _():
            stage[b] = jnp.zeros(stage.shape[1:], jnp.bfloat16)

        def body(i, p, q):
            weight_p = potential[pl.ds(tile_of[order[p]], 1), :]
            weight_q = potential[pl.ds(tile_of[order[q]], 1), :] * (q - p).astype(jnp.float32)
            weighted = jnp.concatenate(
                [
                    (pair[p, 1].astype(jnp.float32) * weight_p).astype(jnp.bfloat16),
                    (pair[q, 1].astype(jnp.float32) * weight_q).astype(jnp.bfloat16),
                ],
                axis=1,
            )
            block = lax.dot_general(
                jnp.concatenate([pair[p, 0], pair[q, 0]], axis=1),
                weighted,
                (((1,), (1,)), ((), ())),
                preferred_element_type=jnp.float32,
            )

            @pl.when(last - first <= 2)
            def _():
                stage[b] = (block * scale).astype(jnp.bfloat16)

            @pl.when((last - first > 2) & (i == 0))
            def _():
                acc[...] = block

            @pl.when(i > 0)
            def _():
                acc[...] += block

        by_twos(first, last, load, body)

        @pl.when(last - first > 2)
        def _():
            stage[b] = (acc[...] * scale).astype(jnp.bfloat16)

        store(b).start()
        return carry

    lax.fori_loop(0, blocks, step, 0)
    for b in range(blocks):
        store(b).wait()


def update(plan, order, tile_of, contributions, collect, parts, tiles, blocks, cols):
    slots = len(parts) * parts[0].shape[0]
    entry = parts[0].shape[1:]
    all_tiles = (collect.shape[0], P_SIZE)
    return pl.pallas_call(
        functools.partial(update_kernel, blocks, tiles),
        out_shape=(
            jax.ShapeDtypeStruct((tiles, P_SIZE), jnp.float32),
            jax.ShapeDtypeStruct((blocks * KB, cols), jnp.bfloat16),
        ),
        in_specs=[SMEM] * 3 + [VMEM] * 2 + [HBM] * len(parts),
        out_specs=(VMEM, HBM),
        scratch_shapes=[
            pltpu.VMEM((slots,) + entry, jnp.bfloat16),
            pltpu.VMEM(all_tiles, jnp.float32),
            pltpu.VMEM(all_tiles, jnp.float32),
            pltpu.VMEM((KB, cols), jnp.float32),
            pltpu.VMEM((blocks, KB, cols), jnp.bfloat16),
            pltpu.SemaphoreType.DMA((slots,)),
            pltpu.SemaphoreType.DMA((blocks,)),
        ],
        compiler_params=pltpu.CompilerParams(vmem_limit_bytes=62 * MIB),
        name="update",
    )(plan, order, tile_of, contributions, collect, *parts)


def shift(block, axis, step):
    count = lax.axis_size(axis)
    pairs = [(i, i + step) for i in range(count) if 0 <= i + step < count]
    return lax.ppermute(block, axis, pairs)


def make_plan(lists, me, entries, tiles, col_count, blocks):
    slots = col_count * CAP
    sent = sent_rows(slots, tiles)
    lists = lists[:, : 2 * entries + tiles]
    peers, named, counts = lists[:, :entries], lists[:, entries : 2 * entries], lists[:, 2 * entries :]
    index = jnp.arange(entries, dtype=jnp.int32)
    home = jnp.arange(col_count, dtype=jnp.int32)[:, None]
    earlier = (peers[:, :, None] == peers[:, None, :]) & (index[None, :] < index[:, None])
    rank = jnp.sum(earlier.astype(jnp.int32), axis=2)
    live = (index % SLOTS)[None, :] < jnp.repeat(counts, SLOTS, axis=1)
    row = jnp.where(live, peers * sent + chunk_of(home, peers, col_count) * CAP + rank, -1).reshape(col_count, tiles, SLOTS)
    core = (home * sent + slots + jnp.arange(tiles, dtype=jnp.int32))[:, :, None]
    row = jnp.concatenate([row, core], axis=2).reshape(col_count * tiles, SLOTS + 1, 1)
    picked = row == jnp.arange(col_count * sent, dtype=jnp.int32)
    collect = jnp.sum(picked.astype(jnp.float32), axis=1)
    hit = (
        (peers == me)[:, None, :]
        & (rank[:, None, :] == jnp.arange(CAP, dtype=jnp.int32)[None, :, None])
        & live[:, None, :]
    )
    at_me = chunk_of(home, me, col_count).reshape(1, col_count) == home
    tile = home * tiles + index[None, :] // SLOTS

    def of_slots(values):
        by_home = jnp.sum(jnp.where(hit, values[:, None, :], 0), axis=2)
        return jnp.sum(jnp.where(at_me[:, :, None], by_home[None], 0), axis=1).reshape(slots)

    wanted = of_slots(named + 1) - 1
    tile_of = of_slots(tile)
    key = jnp.where(wanted < 0, blocks, wanted)
    place = jnp.arange(slots, dtype=jnp.int32)
    before = (key[None, :] < key[:, None]) | (
        (key[None, :] == key[:, None]) & (place[None, :] < place[:, None])
    )
    spot = jnp.sum(before.astype(jnp.int32), axis=1)
    order = jnp.sum(jnp.where(spot[None, :] == place[:, None], place[None, :], 0), axis=1)
    starts = jnp.sum(
        (key[None, :] < jnp.arange(blocks + 1, dtype=jnp.int32)[:, None]).astype(jnp.int32), axis=1
    )
    plan = jnp.concatenate([wanted, starts, me[None]]).astype(jnp.int32)
    return collect, plan, order.astype(jnp.int32), tile_of.astype(jnp.int32)


def shards(
    start_columns,
    hamiltonian,
    band_pattern,
    coefficients,
    tile_peer,
    tile_block,
    tile_count,
    basis_values,
    core_density,
):
    col_count = lax.axis_size("col")
    entries = tile_peer.shape[0]
    tiles = core_density.shape[0]
    cols = start_columns.shape[1]
    blocks = start_columns.shape[0] // KB
    peers = tile_peer[:, 0]
    me = lax.axis_index("col").astype(jnp.int32)

    own, lists = own_piece(
        peers, tile_block, tile_count, band_pattern, hamiltonian.reshape(-1, W), col_count
    )
    lists = lax.all_to_all(lists, "col", split_axis=0, concat_axis=0, tiled=True)
    pieces, owners, awaited = gather_pieces(own)
    v_low = shift(start_columns[-DEG * W :], "row", 1)
    v_high = shift(start_columns[: DEG * W], "row", -1)
    parts = exchange(me[None], peers, basis_values, own, awaited + [v_low, v_high, lists])

    first, last = edge_blocks(owners, pieces, col_count, DEG - 1)
    h_low = shift(last, "row", 1)
    h_high = shift(first, "row", -1)
    inner = chebyshev_inner(coefficients, owners, v_low, start_columns, v_high, pieces)
    kernel_t = chebyshev_outer(
        coefficients, inner, v_low, start_columns, v_high, h_low, first, last, h_high
    )
    collect, plan, order, tile_of = make_plan(lists[:, 0], me, entries, tiles, col_count, blocks)
    partial = project(plan, order, kernel_t, core_density, parts, col_count)
    contributions = lax.all_to_all(partial, "col", split_axis=0, concat_axis=0, tiled=True)
    contributions = contributions.reshape(-1, P_SIZE)
    return update(
        plan, order, tile_of, contributions, collect, parts, tiles, blocks, cols
    )


def solution(mesh):
    return jax.shard_map(
        shards,
        mesh=mesh,
        in_specs=(
            P("row", "col"),
            P(("row", "col"), None, None, None),
            P(("row", "col")),
            P(),
            P(("row", "col"), None),
            P(("row", "col")),
            P(("row", "col")),
            P(("row", "col"), None, None, None),
            P(("row", "col"), None),
        ),
        out_specs=(P(("row", "col"), None), P("row", "col")),
        check_vma=False,
    )
```

```python
import functools
import math

import jax
import jax.numpy as jnp
from jax import lax
from jax.experimental import pallas as pl
from jax.experimental.pallas import tpu as pltpu
from jax.sharding import PartitionSpec as P

W = 256
KB = 512
DEG = 3
SLOTS = 4
CAP = 2
P_SIZE = 128
MIB = 1 << 20
LISTS = 8

exchange_factor = (3.0 / math.pi) ** (1.0 / 3.0)
HBM = pl.BlockSpec(memory_space=pltpu.HBM)
ANY = pl.BlockSpec(memory_space=pl.ANY)
SMEM = pl.BlockSpec(memory_space=pltpu.SMEM)
VMEM = pl.BlockSpec(memory_space=pltpu.VMEM)


def partner(me, j, count):
    if count & (count - 1) == 0:
        return me ^ abs(j)
    return (me + j) % count


def piece_kernel(peers, named, counts, pattern, ham, piece, lists, blocks, sems):
    load = pltpu.make_async_copy(ham, blocks, sems.at[0])
    load.start()
    lane = lax.broadcasted_iota(jnp.int32, (LISTS, P_SIZE), 1)
    row = jnp.zeros((LISTS, P_SIZE), jnp.int32)
    at = 0
    for ref in (peers, named, counts):
        for i in range(ref.shape[0]):
            row = jnp.where(lane == at, ref[i], row)
            at += 1
    for c in range(lists.shape[0]):
        lists[c] = row
    load.wait()
    for i in range(ham.shape[0] // (2 * W)):
        coupling = slice((2 * i + 1) * W, (2 * i + 2) * W)
        blocks[coupling] = blocks[coupling] * pattern[i].astype(jnp.bfloat16)
    store = pltpu.make_async_copy(blocks, piece, sems.at[1])
    store.start()
    store.wait()


def own_piece(peers, named, counts, pattern, ham, col_count):
    return pl.pallas_call(
        piece_kernel,
        out_shape=(
            jax.ShapeDtypeStruct(ham.shape, ham.dtype),
            jax.ShapeDtypeStruct((col_count, LISTS, P_SIZE), jnp.int32),
        ),
        in_specs=[SMEM] * 4 + [HBM],
        out_specs=(HBM, VMEM),
        scratch_shapes=[pltpu.VMEM(ham.shape, ham.dtype), pltpu.SemaphoreType.DMA((2,))],
        compiler_params=pltpu.CompilerParams(vmem_limit_bytes=62 * MIB),
        name="own_piece",
    )(peers, named, counts, pattern, ham)


def lines_of(count):
    inner = max(count // 4, 1) if count & (count - 1) == 0 else 1
    return count // inner, inner


def swap_along(block, t):
    count = lax.axis_size("col")
    _, inner = lines_of(count)
    pairs = [(c, c - c % inner + partner(c % inner, t, inner)) for c in range(count)]
    return lax.ppermute(block, "col", pairs)


def chunk_of(home, owner, count):
    outer, inner = lines_of(count)
    return partner(home % inner, owner % inner, inner) * outer + home // inner


def pack_kernel(entries, col_count, wanted, me, peers, basis, first, *refs):
    outer, inner = lines_of(col_count)
    sent, (held, owner, count, in_sems, out_sems) = refs[: len(wanted)], refs[len(wanted) :]
    for c in range(col_count):
        count[c] = 0
        for k in range(CAP):
            owner[c * CAP + k] = 0
    for e in range(entries):
        p = peers[e]
        k = count[p]
        count[p] = k + 1
        owner[p * CAP + k] = e
    place = lax.rem(me[0], inner)
    tasks = []
    for target, group in zip(sent, wanted):
        for line in range(outer):
            for i, (t, k) in enumerate(group):
                n = len(tasks)
                e = owner[(line * inner + partner(place, t, inner)) * CAP + k]
                fetch = pltpu.make_async_copy(basis.at[e], held.at[n], in_sems.at[n])
                store = pltpu.make_async_copy(held.at[n], target.at[line, i], out_sems.at[n])
                tasks.append((fetch, store))
    for fetch, _ in tasks:
        fetch.start()
    for fetch, store in tasks:
        fetch.wait()
        store.start()
    for _, store in tasks:
        store.wait()


def pack(me, peers, basis, first, col_count, wanted):
    outer, _ = lines_of(col_count)
    entries = basis.shape[0]
    number = sum(len(group) for group in wanted) * outer
    return list(pl.pallas_call(
        functools.partial(pack_kernel, entries, col_count, wanted),
        out_shape=tuple(
            jax.ShapeDtypeStruct((outer, len(group)) + basis.shape[1:], basis.dtype)
            for group in wanted
        ),
        in_specs=[SMEM, SMEM, HBM, HBM],
        out_specs=(HBM,) * len(wanted),
        scratch_shapes=[
            pltpu.VMEM((number,) + basis.shape[1:], basis.dtype),
            pltpu.SMEM((col_count * CAP,), jnp.int32),
            pltpu.SMEM((col_count,), jnp.int32),
            pltpu.SemaphoreType.DMA((number,)),
            pltpu.SemaphoreType.DMA((number,)),
        ],
        compiler_params=pltpu.CompilerParams(vmem_limit_bytes=62 * MIB),
        name="pack",
    )(me, peers, basis, first))


def after(block, *others):
    return pl.pallas_call(
        lambda *refs: None,
        out_shape=jax.ShapeDtypeStruct(block.shape, block.dtype),
        in_specs=[HBM] + [ANY] * len(others),
        out_specs=HBM,
        input_output_aliases={0: 0},
        compiler_params=pltpu.CompilerParams(vmem_limit_bytes=62 * MIB),
        name="after",
    )(block, *others)


def exchange(me, peers, basis, own, awaited, handed):
    count = lax.axis_size("col")
    outer, inner = lines_of(count)
    groups = [[line * inner + place for line in range(outer)] for place in range(inner)]

    def between_lines(blocks, *others):
        block = jnp.concatenate(blocks, axis=1)
        return lax.all_to_all(
            after(block, *others), "col", split_axis=0, concat_axis=0,
            axis_index_groups=groups, tiled=True,
        )

    here = [(0, k) for k in range(CAP)]
    ahead = [[(t, 0)] for t in range(1, inner)]
    rest = [[(t, k)] for k in range(1, CAP) for t in range(1, inner)]
    sent = pack(me, peers, basis, own, count, ahead) if ahead else []
    to_lines, *later = pack(me, peers, basis, sent[0] if ahead else own, count, [here] + rest)
    swapped = {
        group[0]: swap_along(block, group[0][0]) for block, group in zip(sent + later, ahead + rest)
    }
    parts = [between_lines([to_lines], *awaited, *[swapped[group[0]] for group in ahead])]
    for t in range(1, inner):
        parts.append(between_lines([swapped[t, k] for k in range(CAP)], parts[-1], *handed))
    return [part.reshape((outer * CAP,) + part.shape[2:]) for part in parts]


def gather_pieces(own):
    count = lax.axis_size("col")
    outer, inner = lines_of(count)
    me = lax.axis_index("col").astype(jnp.int32)
    a, b = me // inner, me % inner

    def move(block, ways):
        pairs = [(x * inner + y, z * inner + y) for x, z in ways for y in range(inner)]
        return lax.ppermute(block, "col", pairs)

    if outer == 4:
        middle, outwards = [(1, 2), (2, 1)], [(1, 0), (2, 3)]
        near = move(own, [(0, 1), (1, 0), (2, 3), (3, 2)])
        across = move(own, middle)
        far = move(near, middle)
        handed = move(across, outwards)
        last = move(far, outwards)
        within = (a == 1) | (a == 2)
        lines = [
            (own, a),
            (near, a ^ 1),
            (across + handed, jnp.where(within, a ^ 3, a ^ 2)),
            (far + last, jnp.where(within, a ^ 2, a ^ 3)),
        ]
        awaited, ends = [far, handed], [last]
    else:
        lines = [(own, a)] + [
            (move(own, [(x, partner(x, t, outer)) for x in range(outer)]), partner(a, -t, outer))
            for t in range(1, outer)
        ]
        awaited, ends = [block for block, _ in lines[1:]], []
    pieces, owners = [], []
    for block, line in lines:
        pieces.append(block)
        owners.append(line * inner + b)
        for t in range(1, inner):
            pieces.append(swap_along(block, t))
            owners.append(line * inner + partner(b, -t, inner))
    ends += [piece for piece in pieces[: 2 * inner] if all(piece is not block for block, _ in lines)]
    return pieces, jnp.stack(owners).astype(jnp.int32), awaited, ends


def edge_kernel(col_count, depth, owners, *refs):
    pieces, (first, last, sems) = refs[:-3], refs[-3:]
    held = pieces[0].shape[0] // (2 * W)
    total = col_count * held

    def each(act):
        for i, piece in enumerate(pieces):
            for g in range(depth):
                for out, block, sem in ((first, g, 0), (last, total - depth + g, 1)):
                    source = piece.at[pl.ds(block % held * 2 * W, 2 * W)]
                    copy = pltpu.make_async_copy(source, out.at[g], sems.at[sem, g])

                    @pl.when(owners[i] == block // held)
                    def _():
                        act(copy)

    each(lambda copy: copy.start())
    each(lambda copy: copy.wait())


def edge_blocks(owners, pieces, col_count, depth):
    shape = jax.ShapeDtypeStruct((depth, 2 * W, W), pieces[0].dtype)
    return pl.pallas_call(
        functools.partial(edge_kernel, col_count, depth),
        out_shape=(shape, shape),
        in_specs=[SMEM] + [HBM] * len(pieces),
        out_specs=(VMEM, VMEM),
        scratch_shapes=[pltpu.SemaphoreType.DMA((2, depth))],
        compiler_params=pltpu.CompilerParams(vmem_limit_bytes=62 * MIB),
        name="edge_blocks",
    )(owners, *pieces)


def rows_of(j, count=1):
    return pl.ds(j * W if isinstance(j, int) else pl.multiple_of(j * W, W), count * W)


def band_builder(source, target):
    rows = lax.broadcasted_iota(jnp.int32, (W, W), 0)
    cols = lax.broadcasted_iota(jnp.int32, (W, W), 1)
    upper = jnp.where(rows <= cols, 1.0, 0.0).astype(jnp.bfloat16)

    def build(j, carry):
        coupling = source[j, W:]
        lower_band = coupling * upper
        target[j, :, 0:W] = lower_band
        target[j, :, W : 2 * W] = source[j, :W]
        target[j, :, 2 * W : 3 * W] = coupling - lower_band
        return carry

    return build


def inner_kernel(blocks, coef, owners, v_low, v_mid, v_high, *refs):
    (
        *pieces, out, edge_1, edge_2, edge_total,
        vext, hraw, hcat, cheb_1, cheb_2, total, kern, sems, psems, osems, esems,
    ) = refs
    held = pieces[0].shape[0] // (2 * W)
    v_copies = [
        pltpu.make_async_copy(v_low.at[rows_of(DEG - 1)], vext.at[rows_of(0)], sems.at[0]),
        pltpu.make_async_copy(v_mid, vext.at[rows_of(1, blocks)], sems.at[1]),
        pltpu.make_async_copy(v_high.at[rows_of(0)], vext.at[rows_of(blocks + 1)], sems.at[2]),
    ]

    def each_piece(act):
        for i, piece in enumerate(pieces):
            for k in range(held):
                act(pltpu.make_async_copy(
                    piece.at[pl.ds(k * 2 * W, 2 * W)],
                    hraw.at[owners[i] * held + k],
                    psems.at[i, k],
                ))

    each_piece(lambda copy: copy.start())
    for copy in v_copies:
        copy.start()
    each_piece(lambda copy: copy.wait())
    build = band_builder(hraw, hcat)
    build(0, 0)
    for copy in v_copies:
        copy.wait()

    def band(source, j, row):
        return jnp.dot(hcat[j], source[rows_of(row, 3), :], preferred_element_type=jnp.float32)

    def edges(source, target, at):
        size = source.shape[0] // W
        return [
            pltpu.make_async_copy(
                source.at[rows_of(place, 2)], target.at[rows_of(2 * i, 2)], esems.at[at, i]
            )
            for i, place in enumerate((0, size - 2))
        ]

    def first(j, carry):
        value = band(vext, j, j)
        build(jnp.minimum(j + 1, blocks - 1), 0)
        cheb_1[rows_of(j), :] = value.astype(jnp.bfloat16)
        total[rows_of(j), :] = value
        return carry

    lax.fori_loop(0, blocks, first, 0, unroll=4)

    def second(j, carry):
        begin = vext[rows_of(j + 2), :].astype(jnp.float32)
        value = 2.0 * band(cheb_1, j + 1, j) - begin
        cheb_2[rows_of(j), :] = value.astype(jnp.bfloat16)
        total[rows_of(j + 1), :] = (
            coef[0] * begin + (coef[1] - coef[3]) * total[rows_of(j + 1), :] + coef[2] * value
        )
        return carry

    lax.fori_loop(0, blocks - 2, second, 0, unroll=4)
    outgoing = (
        edges(cheb_1, edge_1, 0) + edges(cheb_2, edge_2, 1) + edges(total, edge_total, 2)
    )
    for copy in outgoing:
        copy.start()

    def store(j):
        return pltpu.make_async_copy(kern.at[j], out.at[j], osems.at[j])

    def third(j, carry):
        for half in range(KB // W):
            i = j * (KB // W) + half
            value = total[rows_of(i), :] + (2.0 * coef[3]) * band(cheb_2, i, i - 2)
            kern[j, :, half * W : (half + 1) * W] = value.astype(jnp.bfloat16).T
        store(j).start()
        return carry

    last = blocks // (KB // W) - 1
    lax.fori_loop(1, last, third, 0, unroll=2)
    for j in range(1, last):
        store(j).wait()
    for copy in outgoing:
        copy.wait()


def chebyshev_inner(coefficients, owners, v_low, v_mid, v_high, pieces):
    blocks = v_mid.shape[0] // W
    cols = v_mid.shape[1]
    flops = 2 * W * 3 * W * cols * (3 * blocks - 6)
    result = (blocks * W // KB, cols, KB)
    held = pieces[0].shape[0] // (2 * W)
    return pl.pallas_call(
        functools.partial(inner_kernel, blocks),
        out_shape=(
            jax.ShapeDtypeStruct(result, jnp.bfloat16),
            jax.ShapeDtypeStruct((4 * W, cols), jnp.bfloat16),
            jax.ShapeDtypeStruct((4 * W, cols), jnp.bfloat16),
            jax.ShapeDtypeStruct((4 * W, cols), jnp.float32),
        ),
        in_specs=[SMEM] * 2 + [HBM] * (3 + len(pieces)),
        out_specs=(HBM,) * 4,
        scratch_shapes=[
            pltpu.VMEM(((blocks + 2) * W, cols), jnp.bfloat16),
            pltpu.VMEM((blocks, 2 * W, W), jnp.bfloat16),
            pltpu.VMEM((blocks, W, 3 * W), jnp.bfloat16),
            pltpu.VMEM((blocks * W, cols), jnp.bfloat16),
            pltpu.VMEM(((blocks - 2) * W, cols), jnp.bfloat16),
            pltpu.VMEM((blocks * W, cols), jnp.float32),
            pltpu.VMEM(result, jnp.bfloat16),
            pltpu.SemaphoreType.DMA((3,)),
            pltpu.SemaphoreType.DMA((len(pieces), held)),
            pltpu.SemaphoreType.DMA((result[0],)),
            pltpu.SemaphoreType.DMA((3, 2)),
        ],
        compiler_params=pltpu.CompilerParams(vmem_limit_bytes=62 * MIB),
        cost_estimate=pl.CostEstimate(flops=flops, bytes_accessed=16 * MIB, transcendentals=0),
        name="chebyshev_inner",
    )(coefficients, owners, v_low, v_mid, v_high, *pieces)


def outer_kernel(
    blocks, coef, kernel_in, v_low, v_mid, v_high, h_low, h_first, h_last, h_high,
    edge_1, edge_2, edge_total, out,
    v, hraw, hcat, cheb_1, cheb_2, total, kern, sems, osems,
):
    last = kern.shape[0] - 1
    end = out.shape[0] - 1
    stages = [
        [
            (h_low, hraw.at[pl.ds(0, 2)]),
            (v_low, v.at[0, rows_of(0, 3)]),
            (v_mid.at[rows_of(0)], v.at[0, rows_of(3)]),
            (h_high, hraw.at[pl.ds(6, 2)]),
            (v_mid.at[rows_of(blocks - 1)], v.at[1, rows_of(0)]),
            (v_high, v.at[1, rows_of(1, 3)]),
        ],
        [
            (h_first, hraw.at[pl.ds(2, 2)]),
            (h_last, hraw.at[pl.ds(4, 2)]),
            (edge_1.at[rows_of(0, 2)], cheb_1.at[0, rows_of(2, 2)]),
            (edge_1.at[rows_of(2, 2)], cheb_1.at[1, rows_of(0, 2)]),
        ],
        [
            (edge_2.at[rows_of(0, 2)], cheb_2.at[0, rows_of(2, 2)]),
            (edge_2.at[rows_of(2, 2)], cheb_2.at[1, rows_of(0, 2)]),
            (edge_total.at[rows_of(0, 2)], total.at[0]),
            (edge_total.at[rows_of(2, 2)], total.at[1]),
        ],
    ]
    at = 0
    for i, stage in enumerate(stages):
        stages[i] = [
            pltpu.make_async_copy(source, target, sems.at[at + n])
            for n, (source, target) in enumerate(stage)
        ]
        at += len(stage)
        for copy in stages[i]:
            copy.start()
    build = band_builder(hraw, hcat)

    def arrived(i):
        for copy in stages[i]:
            copy.wait()

    def band(side, j, source, row):
        return jnp.dot(
            hcat[4 * side + j], source[side, rows_of(row, 3), :], preferred_element_type=jnp.float32
        )

    arrived(0)
    for j in (0, 1, 6, 7):
        build(j, 0)
    for side, places in ((0, (0, 1)), (1, (2, 3))):
        for j in places:
            value = band(side, j, v, j - 2 * side)
            cheb_1[side, rows_of(j), :] = value.astype(jnp.bfloat16)
    arrived(1)
    for j in (2, 3, 4, 5):
        build(j, 0)
    arrived(2)
    for side, places in ((0, ((1, 0), (2, 1))), (1, ((2, 3), (1, 2)))):
        for j, place in places:
            begin = v[side, rows_of(place + 2 - 4 * side), :].astype(jnp.float32)
            value = 2.0 * band(side, j, cheb_1, j - 1) - begin
            cheb_2[side, rows_of(place), :] = value.astype(jnp.bfloat16)
            if (j, place) == places[1]:
                within = rows_of(side)
                total[side, within, :] = (
                    coef[0] * begin + (coef[1] - coef[3]) * total[side, within, :] + coef[2] * value
                )
    for side in range(2):
        for half in range(2):
            j = 2 + half if side == 0 else half
            value = total[side, rows_of(half), :] + (2.0 * coef[3]) * band(side, j, cheb_2, half)
            kern[side, :, half * W : (half + 1) * W] = value.astype(jnp.bfloat16).T
    stores = [
        pltpu.make_async_copy(kern.at[0], out.at[0], osems.at[0]),
        pltpu.make_async_copy(kern.at[last], out.at[end], osems.at[1]),
    ]
    for store in stores:
        store.start()
    for store in stores:
        store.wait()


def chebyshev_outer(coefficients, inner, v_low, v_mid, v_high, h_low, h_first, h_last, h_high):
    kernel_t, edge_1, edge_2, edge_total = inner
    blocks = v_mid.shape[0] // W
    cols = v_mid.shape[1]
    return pl.pallas_call(
        functools.partial(outer_kernel, blocks),
        out_shape=jax.ShapeDtypeStruct(kernel_t.shape, kernel_t.dtype),
        in_specs=[SMEM] + [HBM] * 11,
        out_specs=HBM,
        input_output_aliases={1: 0},
        scratch_shapes=[
            pltpu.VMEM((2, 4 * W, cols), jnp.bfloat16),
            pltpu.VMEM((8, 2 * W, W), jnp.bfloat16),
            pltpu.VMEM((8, W, 3 * W), jnp.bfloat16),
            pltpu.VMEM((2, 4 * W, cols), jnp.bfloat16),
            pltpu.VMEM((2, 4 * W, cols), jnp.bfloat16),
            pltpu.VMEM((2, 2 * W, cols), jnp.float32),
            pltpu.VMEM((2, cols, KB), jnp.bfloat16),
            pltpu.SemaphoreType.DMA((14,)),
            pltpu.SemaphoreType.DMA((2,)),
        ],
        compiler_params=pltpu.CompilerParams(vmem_limit_bytes=62 * MIB),
        name="chebyshev_outer",
    )(
        coefficients, kernel_t, v_low, v_mid, v_high, h_low, h_first, h_last, h_high,
        edge_1, edge_2, edge_total,
    )


def entry_loads(order, parts, pair, sems):
    size = parts[0].shape[0]

    def load(p):
        return pltpu.make_async_copy(parts[0].at[0], pair.at[p], sems.at[p])

    def start(p, carry):
        n = order[p]
        for t, part in enumerate(parts):
            @pl.when((n >= t * size) & (n < (t + 1) * size))
            def _():
                pltpu.make_async_copy(part.at[n - t * size], pair.at[p], sems.at[p]).start()

        return carry

    return load, start


def by_twos(first, last, load, body):
    def step(i, carry):
        p = first + 2 * i
        q = jnp.minimum(p + 1, last - 1)
        load(p).wait()

        @pl.when(q > p)
        def _():
            load(q).wait()

        body(i, p, q)
        return carry

    lax.fori_loop(0, (last - first + 1) // 2, step, 0)


def sent_rows(slots, tiles):
    return slots + tiles + -(slots + tiles) % 8


def project_kernel(blocks, plan, order, kernel_t, core, *refs):
    *parts, out, kern, pair, rows, ksems, bsems = refs
    slots = pair.shape[0]
    load, start = entry_loads(order, parts, pair, bsems)

    def fetch(b):
        return pltpu.make_async_copy(kernel_t.at[b], kern.at[b], ksems.at[b])

    def begin(b, carry):
        first, last = plan[slots + b], plan[slots + b + 1]

        @pl.when(first < last)
        def _():
            fetch(b).start()

        return lax.fori_loop(first, last, start, carry)

    lax.fori_loop(0, blocks, begin, 0)
    rows[...] = jnp.zeros_like(rows)
    rows[slots : slots + core.shape[0]] = core[...]

    def step(b, carry):
        first, last = plan[slots + b], plan[slots + b + 1]

        @pl.when(first < last)
        def _():
            fetch(b).wait()

        def body(i, p, q):
            both = jnp.concatenate([pair[p, 0], pair[q, 0]], axis=1)
            projected = jnp.dot(kern[b], both, preferred_element_type=jnp.float32)
            other = jnp.concatenate([pair[p, 1], pair[q, 1]], axis=1).astype(jnp.float32)
            value = jnp.sum(projected * other, axis=0, keepdims=True) * (1.0 / KB)
            rows[pl.ds(order[p], 1), :] = value[:, :P_SIZE]
            rows[pl.ds(order[q], 1), :] = value[:, P_SIZE:]

        by_twos(first, last, load, body)
        return carry

    lax.fori_loop(0, blocks, step, 0)
    for c in range(out.shape[0]):
        out[c] = rows[...]


def project(plan, order, kernel_t, core, parts, col_count):
    slots = col_count * CAP
    entry = parts[0].shape[1:]
    sent = sent_rows(slots, core.shape[0])
    blocks = kernel_t.shape[0]
    return pl.pallas_call(
        functools.partial(project_kernel, blocks),
        out_shape=jax.ShapeDtypeStruct((col_count, sent, P_SIZE), jnp.float32),
        in_specs=[SMEM, SMEM, HBM, VMEM] + [HBM] * len(parts),
        out_specs=VMEM,
        scratch_shapes=[
            pltpu.VMEM(kernel_t.shape, jnp.bfloat16),
            pltpu.VMEM((slots,) + entry, jnp.bfloat16),
            pltpu.VMEM((sent, P_SIZE), jnp.float32),
            pltpu.SemaphoreType.DMA((blocks,)),
            pltpu.SemaphoreType.DMA((slots,)),
        ],
        compiler_params=pltpu.CompilerParams(vmem_limit_bytes=62 * MIB),
        name="project",
    )(plan, order, kernel_t, core, *parts)


def update_kernel(
    blocks, tiles, plan, order, tile_of, contributions, collect, *refs
):
    *parts, density_out, update_out, pair, density, potential, acc, stage, sems, osems = refs
    slots = pair.shape[0]
    live = plan[slots + blocks]
    me = plan[slots + blocks + 1]
    load, start = entry_loads(order, parts, pair, sems)
    lax.fori_loop(0, live, start, 0)
    density[...] = jnp.dot(
        collect[...],
        contributions[...],
        preferred_element_type=jnp.float32,
        precision=lax.Precision.HIGHEST,
    )
    for t in range(tiles):
        density_out[pl.ds(t, 1), :] = density[pl.ds(me * tiles + t, 1), :]
    positive = jnp.maximum(density[...], 0.1)
    root = jnp.exp(jnp.log(positive) * (1.0 / 3.0))
    root = root - (root - positive / (root * root)) * (1.0 / 3.0)
    potential[...] = -exchange_factor * root
    scale = 1.0 / math.sqrt(P_SIZE)

    def store(b):
        rows = pl.ds(pl.multiple_of(b * KB, KB), KB)
        return pltpu.make_async_copy(stage.at[b], update_out.at[rows], osems.at[b])

    def step(b, carry):
        first, last = plan[slots + b], plan[slots + b + 1]

        @pl.when(first == last)
        def _():
            stage[b] = jnp.zeros(stage.shape[1:], jnp.bfloat16)

        def body(i, p, q):
            weight_p = potential[pl.ds(tile_of[order[p]], 1), :]
            weight_q = potential[pl.ds(tile_of[order[q]], 1), :] * (q - p).astype(jnp.float32)
            weighted = jnp.concatenate(
                [
                    (pair[p, 1].astype(jnp.float32) * weight_p).astype(jnp.bfloat16),
                    (pair[q, 1].astype(jnp.float32) * weight_q).astype(jnp.bfloat16),
                ],
                axis=1,
            )
            block = lax.dot_general(
                jnp.concatenate([pair[p, 0], pair[q, 0]], axis=1),
                weighted,
                (((1,), (1,)), ((), ())),
                preferred_element_type=jnp.float32,
            )

            @pl.when(last - first <= 2)
            def _():
                stage[b] = (block * scale).astype(jnp.bfloat16)

            @pl.when((last - first > 2) & (i == 0))
            def _():
                acc[...] = block

            @pl.when(i > 0)
            def _():
                acc[...] += block

        by_twos(first, last, load, body)

        @pl.when(last - first > 2)
        def _():
            stage[b] = (acc[...] * scale).astype(jnp.bfloat16)

        store(b).start()
        return carry

    lax.fori_loop(0, blocks, step, 0)
    for b in range(blocks):
        store(b).wait()


def update(plan, order, tile_of, contributions, collect, parts, tiles, blocks, cols):
    slots = len(parts) * parts[0].shape[0]
    entry = parts[0].shape[1:]
    all_tiles = (collect.shape[0], P_SIZE)
    return pl.pallas_call(
        functools.partial(update_kernel, blocks, tiles),
        out_shape=(
            jax.ShapeDtypeStruct((tiles, P_SIZE), jnp.float32),
            jax.ShapeDtypeStruct((blocks * KB, cols), jnp.bfloat16),
        ),
        in_specs=[SMEM] * 3 + [VMEM] * 2 + [HBM] * len(parts),
        out_specs=(VMEM, HBM),
        scratch_shapes=[
            pltpu.VMEM((slots,) + entry, jnp.bfloat16),
            pltpu.VMEM(all_tiles, jnp.float32),
            pltpu.VMEM(all_tiles, jnp.float32),
            pltpu.VMEM((KB, cols), jnp.float32),
            pltpu.VMEM((blocks, KB, cols), jnp.bfloat16),
            pltpu.SemaphoreType.DMA((slots,)),
            pltpu.SemaphoreType.DMA((blocks,)),
        ],
        compiler_params=pltpu.CompilerParams(vmem_limit_bytes=62 * MIB),
        name="update",
    )(plan, order, tile_of, contributions, collect, *parts)


def shift(block, axis, step):
    count = lax.axis_size(axis)
    pairs = [(i, i + step) for i in range(count) if 0 <= i + step < count]
    return lax.ppermute(block, axis, pairs)


def make_plan(lists, me, entries, tiles, col_count, blocks):
    slots = col_count * CAP
    sent = sent_rows(slots, tiles)
    lists = lists[:, : 2 * entries + tiles]
    peers, named, counts = lists[:, :entries], lists[:, entries : 2 * entries], lists[:, 2 * entries :]
    index = jnp.arange(entries, dtype=jnp.int32)
    home = jnp.arange(col_count, dtype=jnp.int32)[:, None]
    earlier = (peers[:, :, None] == peers[:, None, :]) & (index[None, :] < index[:, None])
    rank = jnp.sum(earlier.astype(jnp.int32), axis=2)
    live = (index % SLOTS)[None, :] < jnp.repeat(counts, SLOTS, axis=1)
    row = jnp.where(live, peers * sent + chunk_of(home, peers, col_count) * CAP + rank, -1).reshape(col_count, tiles, SLOTS)
    core = (home * sent + slots + jnp.arange(tiles, dtype=jnp.int32))[:, :, None]
    row = jnp.concatenate([row, core], axis=2).reshape(col_count * tiles, SLOTS + 1, 1)
    picked = row == jnp.arange(col_count * sent, dtype=jnp.int32)
    collect = jnp.sum(picked.astype(jnp.float32), axis=1)
    hit = (
        (peers == me)[:, None, :]
        & (rank[:, None, :] == jnp.arange(CAP, dtype=jnp.int32)[None, :, None])
        & live[:, None, :]
    )
    at_me = chunk_of(home, me, col_count).reshape(1, col_count) == home
    tile = home * tiles + index[None, :] // SLOTS

    def of_slots(values):
        by_home = jnp.sum(jnp.where(hit, values[:, None, :], 0), axis=2)
        return jnp.sum(jnp.where(at_me[:, :, None], by_home[None], 0), axis=1).reshape(slots)

    wanted = of_slots(named + 1) - 1
    tile_of = of_slots(tile)
    key = jnp.where(wanted < 0, blocks, wanted)
    place = jnp.arange(slots, dtype=jnp.int32)
    before = (key[None, :] < key[:, None]) | (
        (key[None, :] == key[:, None]) & (place[None, :] < place[:, None])
    )
    spot = jnp.sum(before.astype(jnp.int32), axis=1)
    order = jnp.sum(jnp.where(spot[None, :] == place[:, None], place[None, :], 0), axis=1)
    starts = jnp.sum(
        (key[None, :] < jnp.arange(blocks + 1, dtype=jnp.int32)[:, None]).astype(jnp.int32), axis=1
    )
    plan = jnp.concatenate([wanted, starts, me[None]]).astype(jnp.int32)
    return collect, plan, order.astype(jnp.int32), tile_of.astype(jnp.int32)


def shards(
    start_columns,
    hamiltonian,
    band_pattern,
    coefficients,
    tile_peer,
    tile_block,
    tile_count,
    basis_values,
    core_density,
):
    col_count = lax.axis_size("col")
    entries = tile_peer.shape[0]
    tiles = core_density.shape[0]
    cols = start_columns.shape[1]
    blocks = start_columns.shape[0] // KB
    peers = tile_peer[:, 0]
    me = lax.axis_index("col").astype(jnp.int32)

    own, lists = own_piece(
        peers, tile_block, tile_count, band_pattern, hamiltonian.reshape(-1, W), col_count
    )
    lists = lax.all_to_all(lists, "col", split_axis=0, concat_axis=0, tiled=True)
    pieces, owners, awaited, handed = gather_pieces(own)
    v_low = shift(start_columns[-DEG * W :], "row", 1)
    v_high = shift(start_columns[: DEG * W], "row", -1)
    parts = exchange(me[None], peers, basis_values, own, awaited + [v_low, v_high, lists], handed)

    first, last = edge_blocks(owners, pieces, col_count, DEG - 1)
    h_low = shift(last, "row", 1)
    h_high = shift(first, "row", -1)
    inner = chebyshev_inner(coefficients, owners, v_low, start_columns, v_high, pieces)
    kernel_t = chebyshev_outer(
        coefficients, inner, v_low, start_columns, v_high, h_low, first, last, h_high
    )
    collect, plan, order, tile_of = make_plan(lists[:, 0], me, entries, tiles, col_count, blocks)
    partial = project(plan, order, kernel_t, core_density, parts, col_count)
    contributions = lax.all_to_all(partial, "col", split_axis=0, concat_axis=0, tiled=True)
    contributions = contributions.reshape(-1, P_SIZE)
    return update(
        plan, order, tile_of, contributions, collect, parts, tiles, blocks, cols
    )


def solution(mesh):
    return jax.shard_map(
        shards,
        mesh=mesh,
        in_specs=(
            P("row", "col"),
            P(("row", "col"), None, None, None),
            P(("row", "col")),
            P(),
            P(("row", "col"), None),
            P(("row", "col")),
            P(("row", "col")),
            P(("row", "col"), None, None, None),
            P(("row", "col"), None),
        ),
        out_specs=(P(("row", "col"), None), P("row", "col")),
        check_vma=False,
    )
```

```python
import functools
import math

import jax
import jax.numpy as jnp
from jax import lax
from jax.experimental import pallas as pl
from jax.experimental.pallas import tpu as pltpu
from jax.sharding import PartitionSpec as P

W = 256
KB = 512
DEG = 3
SLOTS = 4
CAP = 2
P_SIZE = 128
MIB = 1 << 20
LISTS = 8

exchange_factor = (3.0 / math.pi) ** (1.0 / 3.0)
HBM = pl.BlockSpec(memory_space=pltpu.HBM)
ANY = pl.BlockSpec(memory_space=pl.ANY)
SMEM = pl.BlockSpec(memory_space=pltpu.SMEM)
VMEM = pl.BlockSpec(memory_space=pltpu.VMEM)


def partner(me, j, count):
    if count & (count - 1) == 0:
        return me ^ abs(j)
    return (me + j) % count


def piece_kernel(peers, named, counts, pattern, ham, piece, lists, blocks, sems):
    load = pltpu.make_async_copy(ham, blocks, sems.at[0])
    load.start()
    lane = lax.broadcasted_iota(jnp.int32, (LISTS, P_SIZE), 1)
    row = jnp.zeros((LISTS, P_SIZE), jnp.int32)
    at = 0
    for ref in (peers, named, counts):
        for i in range(ref.shape[0]):
            row = jnp.where(lane == at, ref[i], row)
            at += 1
    for c in range(lists.shape[0]):
        lists[c] = row
    load.wait()
    for i in range(ham.shape[0] // (2 * W)):
        coupling = slice((2 * i + 1) * W, (2 * i + 2) * W)
        blocks[coupling] = blocks[coupling] * pattern[i].astype(jnp.bfloat16)
    store = pltpu.make_async_copy(blocks, piece, sems.at[1])
    store.start()
    store.wait()


def own_piece(peers, named, counts, pattern, ham, col_count):
    return pl.pallas_call(
        piece_kernel,
        out_shape=(
            jax.ShapeDtypeStruct(ham.shape, ham.dtype),
            jax.ShapeDtypeStruct((col_count, LISTS, P_SIZE), jnp.int32),
        ),
        in_specs=[SMEM] * 4 + [HBM],
        out_specs=(HBM, VMEM),
        scratch_shapes=[pltpu.VMEM(ham.shape, ham.dtype), pltpu.SemaphoreType.DMA((2,))],
        compiler_params=pltpu.CompilerParams(vmem_limit_bytes=62 * MIB),
        name="own_piece",
    )(peers, named, counts, pattern, ham)


def lines_of(count):
    inner = max(count // 4, 1) if count & (count - 1) == 0 else 1
    return count // inner, inner


def swap_along(block, t):
    count = lax.axis_size("col")
    _, inner = lines_of(count)
    pairs = [(c, c - c % inner + partner(c % inner, t, inner)) for c in range(count)]
    return lax.ppermute(block, "col", pairs)


def chunk_of(home, owner, count):
    outer, inner = lines_of(count)
    return partner(home % inner, owner % inner, inner) * outer + home // inner


def pack_kernel(entries, col_count, wanted, me, peers, basis, first, *refs):
    outer, inner = lines_of(col_count)
    sent, (held, owner, count, in_sems, out_sems) = refs[: len(wanted)], refs[len(wanted) :]
    for c in range(col_count):
        count[c] = 0
        for k in range(CAP):
            owner[c * CAP + k] = 0
    for e in range(entries):
        p = peers[e]
        k = count[p]
        count[p] = k + 1
        owner[p * CAP + k] = e
    place = lax.rem(me[0], inner)
    tasks = []
    for target, group in zip(sent, wanted):
        for line in range(outer):
            for i, (t, k) in enumerate(group):
                n = len(tasks)
                e = owner[(line * inner + partner(place, t, inner)) * CAP + k]
                fetch = pltpu.make_async_copy(basis.at[e], held.at[n], in_sems.at[n])
                store = pltpu.make_async_copy(held.at[n], target.at[line, i], out_sems.at[n])
                tasks.append((fetch, store))
    for fetch, _ in tasks:
        fetch.start()
    for fetch, store in tasks:
        fetch.wait()
        store.start()
    for _, store in tasks:
        store.wait()


def pack(me, peers, basis, first, col_count, wanted):
    outer, _ = lines_of(col_count)
    entries = basis.shape[0]
    number = sum(len(group) for group in wanted) * outer
    return list(pl.pallas_call(
        functools.partial(pack_kernel, entries, col_count, wanted),
        out_shape=tuple(
            jax.ShapeDtypeStruct((outer, len(group)) + basis.shape[1:], basis.dtype)
            for group in wanted
        ),
        in_specs=[SMEM, SMEM, HBM, HBM],
        out_specs=(HBM,) * len(wanted),
        scratch_shapes=[
            pltpu.VMEM((number,) + basis.shape[1:], basis.dtype),
            pltpu.SMEM((col_count * CAP,), jnp.int32),
            pltpu.SMEM((col_count,), jnp.int32),
            pltpu.SemaphoreType.DMA((number,)),
            pltpu.SemaphoreType.DMA((number,)),
        ],
        compiler_params=pltpu.CompilerParams(vmem_limit_bytes=62 * MIB),
        name="pack",
    )(me, peers, basis, first))


def after(block, *others):
    return pl.pallas_call(
        lambda *refs: None,
        out_shape=jax.ShapeDtypeStruct(block.shape, block.dtype),
        in_specs=[HBM] + [ANY] * len(others),
        out_specs=HBM,
        input_output_aliases={0: 0},
        compiler_params=pltpu.CompilerParams(vmem_limit_bytes=62 * MIB),
        name="after",
    )(block, *others)


def exchange(me, peers, basis, own, awaited, handed):
    count = lax.axis_size("col")
    outer, inner = lines_of(count)
    groups = [[line * inner + place for line in range(outer)] for place in range(inner)]

    def between_lines(blocks, *others):
        block = jnp.concatenate(blocks, axis=1)
        return lax.all_to_all(
            after(block, *others), "col", split_axis=0, concat_axis=0,
            axis_index_groups=groups, tiled=True,
        )

    here = [(0, k) for k in range(CAP)]
    ahead = [[(t, 0)] for t in range(1, inner)]
    rest = [[(t, k)] for k in range(1, CAP) for t in range(1, inner)]
    sent = pack(me, peers, basis, own, count, ahead) if ahead else []
    to_lines, *later = pack(me, peers, basis, sent[0] if ahead else own, count, [here] + rest)
    swapped = {
        group[0]: swap_along(block, group[0][0]) for block, group in zip(sent + later, ahead + rest)
    }
    parts = [between_lines([to_lines], *awaited, *[swapped[group[0]] for group in ahead])]
    for t in range(1, inner):
        parts.append(between_lines([swapped[t, k] for k in range(CAP)], parts[-1], *handed))
    return [part.reshape((outer * CAP,) + part.shape[2:]) for part in parts]


def gather_pieces(own):
    count = lax.axis_size("col")
    outer, inner = lines_of(count)
    me = lax.axis_index("col").astype(jnp.int32)
    a, b = me // inner, me % inner

    def move(block, ways):
        pairs = [(x * inner + y, z * inner + y) for x, z in ways for y in range(inner)]
        return lax.ppermute(block, "col", pairs)

    if outer == 4:
        middle, outwards = [(1, 2), (2, 1)], [(1, 0), (2, 3)]
        near = move(own, [(0, 1), (1, 0), (2, 3), (3, 2)])
        across = move(own, middle)
        far = move(near, middle)
        handed = move(across, outwards)
        last = move(far, outwards)
        within = (a == 1) | (a == 2)
        lines = [
            (own, a),
            (near, a ^ 1),
            (across + handed, jnp.where(within, a ^ 3, a ^ 2)),
            (far + last, jnp.where(within, a ^ 2, a ^ 3)),
        ]
        awaited, ends = [far, handed], [last]
    else:
        lines = [(own, a)] + [
            (move(own, [(x, partner(x, t, outer)) for x in range(outer)]), partner(a, -t, outer))
            for t in range(1, outer)
        ]
        awaited, ends = [block for block, _ in lines[1:]], []
    pieces, owners = [], []
    for block, line in lines:
        pieces.append(block)
        owners.append(line * inner + b)
        for t in range(1, inner):
            pieces.append(swap_along(block, t))
            owners.append(line * inner + partner(b, -t, inner))
    ends += [piece for piece in pieces[: 3 * inner] if all(piece is not block for block, _ in lines)]
    return pieces, jnp.stack(owners).astype(jnp.int32), awaited, ends


def edge_kernel(col_count, depth, owners, *refs):
    pieces, (first, last, sems) = refs[:-3], refs[-3:]
    held = pieces[0].shape[0] // (2 * W)
    total = col_count * held

    def each(act):
        for i, piece in enumerate(pieces):
            for g in range(depth):
                for out, block, sem in ((first, g, 0), (last, total - depth + g, 1)):
                    source = piece.at[pl.ds(block % held * 2 * W, 2 * W)]
                    copy = pltpu.make_async_copy(source, out.at[g], sems.at[sem, g])

                    @pl.when(owners[i] == block // held)
                    def _():
                        act(copy)

    each(lambda copy: copy.start())
    each(lambda copy: copy.wait())


def edge_blocks(owners, pieces, col_count, depth):
    shape = jax.ShapeDtypeStruct((depth, 2 * W, W), pieces[0].dtype)
    return pl.pallas_call(
        functools.partial(edge_kernel, col_count, depth),
        out_shape=(shape, shape),
        in_specs=[SMEM] + [HBM] * len(pieces),
        out_specs=(VMEM, VMEM),
        scratch_shapes=[pltpu.SemaphoreType.DMA((2, depth))],
        compiler_params=pltpu.CompilerParams(vmem_limit_bytes=62 * MIB),
        name="edge_blocks",
    )(owners, *pieces)


def rows_of(j, count=1):
    return pl.ds(j * W if isinstance(j, int) else pl.multiple_of(j * W, W), count * W)


def band_builder(source, target):
    rows = lax.broadcasted_iota(jnp.int32, (W, W), 0)
    cols = lax.broadcasted_iota(jnp.int32, (W, W), 1)
    upper = jnp.where(rows <= cols, 1.0, 0.0).astype(jnp.bfloat16)

    def build(j, carry):
        coupling = source[j, W:]
        lower_band = coupling * upper
        target[j, :, 0:W] = lower_band
        target[j, :, W : 2 * W] = source[j, :W]
        target[j, :, 2 * W : 3 * W] = coupling - lower_band
        return carry

    return build


def inner_kernel(blocks, coef, owners, v_low, v_mid, v_high, *refs):
    (
        *pieces, out, edge_1, edge_2, edge_total,
        vext, hraw, hcat, cheb_1, cheb_2, total, kern, sems, psems, osems, esems,
    ) = refs
    held = pieces[0].shape[0] // (2 * W)
    v_copies = [
        pltpu.make_async_copy(v_low.at[rows_of(DEG - 1)], vext.at[rows_of(0)], sems.at[0]),
        pltpu.make_async_copy(v_mid, vext.at[rows_of(1, blocks)], sems.at[1]),
        pltpu.make_async_copy(v_high.at[rows_of(0)], vext.at[rows_of(blocks + 1)], sems.at[2]),
    ]

    def each_piece(act):
        for i, piece in enumerate(pieces):
            for k in range(held):
                act(pltpu.make_async_copy(
                    piece.at[pl.ds(k * 2 * W, 2 * W)],
                    hraw.at[owners[i] * held + k],
                    psems.at[i, k],
                ))

    each_piece(lambda copy: copy.start())
    for copy in v_copies:
        copy.start()
    each_piece(lambda copy: copy.wait())
    build = band_builder(hraw, hcat)
    build(0, 0)
    for copy in v_copies:
        copy.wait()

    def band(source, j, row):
        return jnp.dot(hcat[j], source[rows_of(row, 3), :], preferred_element_type=jnp.float32)

    def edges(source, target, at):
        size = source.shape[0] // W
        return [
            pltpu.make_async_copy(
                source.at[rows_of(place, 2)], target.at[rows_of(2 * i, 2)], esems.at[at, i]
            )
            for i, place in enumerate((0, size - 2))
        ]

    def first(j, carry):
        value = band(vext, j, j)
        build(jnp.minimum(j + 1, blocks - 1), 0)
        cheb_1[rows_of(j), :] = value.astype(jnp.bfloat16)
        total[rows_of(j), :] = value
        return carry

    lax.fori_loop(0, blocks, first, 0, unroll=4)

    def second(j, carry):
        begin = vext[rows_of(j + 2), :].astype(jnp.float32)
        value = 2.0 * band(cheb_1, j + 1, j) - begin
        cheb_2[rows_of(j), :] = value.astype(jnp.bfloat16)
        total[rows_of(j + 1), :] = (
            coef[0] * begin + (coef[1] - coef[3]) * total[rows_of(j + 1), :] + coef[2] * value
        )
        return carry

    lax.fori_loop(0, blocks - 2, second, 0, unroll=4)
    outgoing = (
        edges(cheb_1, edge_1, 0) + edges(cheb_2, edge_2, 1) + edges(total, edge_total, 2)
    )
    for copy in outgoing:
        copy.start()

    def store(j):
        return pltpu.make_async_copy(kern.at[j], out.at[j], osems.at[j])

    def third(j, carry):
        for half in range(KB // W):
            i = j * (KB // W) + half
            value = total[rows_of(i), :] + (2.0 * coef[3]) * band(cheb_2, i, i - 2)
            kern[j, :, half * W : (half + 1) * W] = value.astype(jnp.bfloat16).T
        store(j).start()
        return carry

    last = blocks // (KB // W) - 1
    lax.fori_loop(1, last, third, 0, unroll=2)
    for j in range(1, last):
        store(j).wait()
    for copy in outgoing:
        copy.wait()


def chebyshev_inner(coefficients, owners, v_low, v_mid, v_high, pieces):
    blocks = v_mid.shape[0] // W
    cols = v_mid.shape[1]
    flops = 2 * W * 3 * W * cols * (3 * blocks - 6)
    result = (blocks * W // KB, cols, KB)
    held = pieces[0].shape[0] // (2 * W)
    return pl.pallas_call(
        functools.partial(inner_kernel, blocks),
        out_shape=(
            jax.ShapeDtypeStruct(result, jnp.bfloat16),
            jax.ShapeDtypeStruct((4 * W, cols), jnp.bfloat16),
            jax.ShapeDtypeStruct((4 * W, cols), jnp.bfloat16),
            jax.ShapeDtypeStruct((4 * W, cols), jnp.float32),
        ),
        in_specs=[SMEM] * 2 + [HBM] * (3 + len(pieces)),
        out_specs=(HBM,) * 4,
        scratch_shapes=[
            pltpu.VMEM(((blocks + 2) * W, cols), jnp.bfloat16),
            pltpu.VMEM((blocks, 2 * W, W), jnp.bfloat16),
            pltpu.VMEM((blocks, W, 3 * W), jnp.bfloat16),
            pltpu.VMEM((blocks * W, cols), jnp.bfloat16),
            pltpu.VMEM(((blocks - 2) * W, cols), jnp.bfloat16),
            pltpu.VMEM((blocks * W, cols), jnp.float32),
            pltpu.VMEM(result, jnp.bfloat16),
            pltpu.SemaphoreType.DMA((3,)),
            pltpu.SemaphoreType.DMA((len(pieces), held)),
            pltpu.SemaphoreType.DMA((result[0],)),
            pltpu.SemaphoreType.DMA((3, 2)),
        ],
        compiler_params=pltpu.CompilerParams(vmem_limit_bytes=62 * MIB),
        cost_estimate=pl.CostEstimate(flops=flops, bytes_accessed=16 * MIB, transcendentals=0),
        name="chebyshev_inner",
    )(coefficients, owners, v_low, v_mid, v_high, *pieces)


def outer_kernel(
    blocks, coef, kernel_in, v_low, v_mid, v_high, h_low, h_first, h_last, h_high,
    edge_1, edge_2, edge_total, out,
    v, hraw, hcat, cheb_1, cheb_2, total, kern, sems, osems,
):
    last = kern.shape[0] - 1
    end = out.shape[0] - 1
    stages = [
        [
            (h_low, hraw.at[pl.ds(0, 2)]),
            (v_low, v.at[0, rows_of(0, 3)]),
            (v_mid.at[rows_of(0)], v.at[0, rows_of(3)]),
            (h_high, hraw.at[pl.ds(6, 2)]),
            (v_mid.at[rows_of(blocks - 1)], v.at[1, rows_of(0)]),
            (v_high, v.at[1, rows_of(1, 3)]),
        ],
        [
            (h_first, hraw.at[pl.ds(2, 2)]),
            (h_last, hraw.at[pl.ds(4, 2)]),
            (edge_1.at[rows_of(0, 2)], cheb_1.at[0, rows_of(2, 2)]),
            (edge_1.at[rows_of(2, 2)], cheb_1.at[1, rows_of(0, 2)]),
        ],
        [
            (edge_2.at[rows_of(0, 2)], cheb_2.at[0, rows_of(2, 2)]),
            (edge_2.at[rows_of(2, 2)], cheb_2.at[1, rows_of(0, 2)]),
            (edge_total.at[rows_of(0, 2)], total.at[0]),
            (edge_total.at[rows_of(2, 2)], total.at[1]),
        ],
    ]
    at = 0
    for i, stage in enumerate(stages):
        stages[i] = [
            pltpu.make_async_copy(source, target, sems.at[at + n])
            for n, (source, target) in enumerate(stage)
        ]
        at += len(stage)
        for copy in stages[i]:
            copy.start()
    build = band_builder(hraw, hcat)

    def arrived(i):
        for copy in stages[i]:
            copy.wait()

    def band(side, j, source, row):
        return jnp.dot(
            hcat[4 * side + j], source[side, rows_of(row, 3), :], preferred_element_type=jnp.float32
        )

    arrived(0)
    for j in (0, 1, 6, 7):
        build(j, 0)
    for side, places in ((0, (0, 1)), (1, (2, 3))):
        for j in places:
            value = band(side, j, v, j - 2 * side)
            cheb_1[side, rows_of(j), :] = value.astype(jnp.bfloat16)
    arrived(1)
    for j in (2, 3, 4, 5):
        build(j, 0)
    arrived(2)
    for side, places in ((0, ((1, 0), (2, 1))), (1, ((2, 3), (1, 2)))):
        for j, place in places:
            begin = v[side, rows_of(place + 2 - 4 * side), :].astype(jnp.float32)
            value = 2.0 * band(side, j, cheb_1, j - 1) - begin
            cheb_2[side, rows_of(place), :] = value.astype(jnp.bfloat16)
            if (j, place) == places[1]:
                within = rows_of(side)
                total[side, within, :] = (
                    coef[0] * begin + (coef[1] - coef[3]) * total[side, within, :] + coef[2] * value
                )
    for side in range(2):
        for half in range(2):
            j = 2 + half if side == 0 else half
            value = total[side, rows_of(half), :] + (2.0 * coef[3]) * band(side, j, cheb_2, half)
            kern[side, :, half * W : (half + 1) * W] = value.astype(jnp.bfloat16).T
    stores = [
        pltpu.make_async_copy(kern.at[0], out.at[0], osems.at[0]),
        pltpu.make_async_copy(kern.at[last], out.at[end], osems.at[1]),
    ]
    for store in stores:
        store.start()
    for store in stores:
        store.wait()


def chebyshev_outer(coefficients, inner, v_low, v_mid, v_high, h_low, h_first, h_last, h_high):
    kernel_t, edge_1, edge_2, edge_total = inner
    blocks = v_mid.shape[0] // W
    cols = v_mid.shape[1]
    return pl.pallas_call(
        functools.partial(outer_kernel, blocks),
        out_shape=jax.ShapeDtypeStruct(kernel_t.shape, kernel_t.dtype),
        in_specs=[SMEM] + [HBM] * 11,
        out_specs=HBM,
        input_output_aliases={1: 0},
        scratch_shapes=[
            pltpu.VMEM((2, 4 * W, cols), jnp.bfloat16),
            pltpu.VMEM((8, 2 * W, W), jnp.bfloat16),
            pltpu.VMEM((8, W, 3 * W), jnp.bfloat16),
            pltpu.VMEM((2, 4 * W, cols), jnp.bfloat16),
            pltpu.VMEM((2, 4 * W, cols), jnp.bfloat16),
            pltpu.VMEM((2, 2 * W, cols), jnp.float32),
            pltpu.VMEM((2, cols, KB), jnp.bfloat16),
            pltpu.SemaphoreType.DMA((14,)),
            pltpu.SemaphoreType.DMA((2,)),
        ],
        compiler_params=pltpu.CompilerParams(vmem_limit_bytes=62 * MIB),
        name="chebyshev_outer",
    )(
        coefficients, kernel_t, v_low, v_mid, v_high, h_low, h_first, h_last, h_high,
        edge_1, edge_2, edge_total,
    )


def entry_loads(order, parts, pair, sems):
    size = parts[0].shape[0]

    def load(p):
        return pltpu.make_async_copy(parts[0].at[0], pair.at[p], sems.at[p])

    def start(p, carry):
        n = order[p]
        for t, part in enumerate(parts):
            @pl.when((n >= t * size) & (n < (t + 1) * size))
            def _():
                pltpu.make_async_copy(part.at[n - t * size], pair.at[p], sems.at[p]).start()

        return carry

    return load, start


def by_twos(first, last, load, body):
    def step(i, carry):
        p = first + 2 * i
        q = jnp.minimum(p + 1, last - 1)
        load(p).wait()

        @pl.when(q > p)
        def _():
            load(q).wait()

        body(i, p, q)
        return carry

    lax.fori_loop(0, (last - first + 1) // 2, step, 0)


def sent_rows(slots, tiles):
    return slots + tiles + -(slots + tiles) % 8


def project_kernel(blocks, plan, order, kernel_t, core, *refs):
    *parts, out, kern, pair, rows, ksems, bsems = refs
    slots = pair.shape[0]
    load, start = entry_loads(order, parts, pair, bsems)

    def fetch(b):
        return pltpu.make_async_copy(kernel_t.at[b], kern.at[b], ksems.at[b])

    def begin(b, carry):
        first, last = plan[slots + b], plan[slots + b + 1]

        @pl.when(first < last)
        def _():
            fetch(b).start()

        return lax.fori_loop(first, last, start, carry)

    lax.fori_loop(0, blocks, begin, 0)
    rows[...] = jnp.zeros_like(rows)
    rows[slots : slots + core.shape[0]] = core[...]

    def step(b, carry):
        first, last = plan[slots + b], plan[slots + b + 1]

        @pl.when(first < last)
        def _():
            fetch(b).wait()

        def body(i, p, q):
            both = jnp.concatenate([pair[p, 0], pair[q, 0]], axis=1)
            projected = jnp.dot(kern[b], both, preferred_element_type=jnp.float32)
            other = jnp.concatenate([pair[p, 1], pair[q, 1]], axis=1).astype(jnp.float32)
            value = jnp.sum(projected * other, axis=0, keepdims=True) * (1.0 / KB)
            rows[pl.ds(order[p], 1), :] = value[:, :P_SIZE]
            rows[pl.ds(order[q], 1), :] = value[:, P_SIZE:]

        by_twos(first, last, load, body)
        return carry

    lax.fori_loop(0, blocks, step, 0)
    for c in range(out.shape[0]):
        out[c] = rows[...]


def project(plan, order, kernel_t, core, parts, col_count):
    slots = col_count * CAP
    entry = parts[0].shape[1:]
    sent = sent_rows(slots, core.shape[0])
    blocks = kernel_t.shape[0]
    return pl.pallas_call(
        functools.partial(project_kernel, blocks),
        out_shape=jax.ShapeDtypeStruct((col_count, sent, P_SIZE), jnp.float32),
        in_specs=[SMEM, SMEM, HBM, VMEM] + [HBM] * len(parts),
        out_specs=VMEM,
        scratch_shapes=[
            pltpu.VMEM(kernel_t.shape, jnp.bfloat16),
            pltpu.VMEM((slots,) + entry, jnp.bfloat16),
            pltpu.VMEM((sent, P_SIZE), jnp.float32),
            pltpu.SemaphoreType.DMA((blocks,)),
            pltpu.SemaphoreType.DMA((slots,)),
        ],
        compiler_params=pltpu.CompilerParams(vmem_limit_bytes=62 * MIB),
        name="project",
    )(plan, order, kernel_t, core, *parts)


def update_kernel(
    blocks, tiles, plan, order, tile_of, contributions, collect, *refs
):
    *parts, density_out, update_out, pair, density, potential, acc, stage, sems, osems = refs
    slots = pair.shape[0]
    live = plan[slots + blocks]
    me = plan[slots + blocks + 1]
    load, start = entry_loads(order, parts, pair, sems)
    lax.fori_loop(0, live, start, 0)
    density[...] = jnp.dot(
        collect[...],
        contributions[...],
        preferred_element_type=jnp.float32,
        precision=lax.Precision.HIGHEST,
    )
    for t in range(tiles):
        density_out[pl.ds(t, 1), :] = density[pl.ds(me * tiles + t, 1), :]
    positive = jnp.maximum(density[...], 0.1)
    root = jnp.exp(jnp.log(positive) * (1.0 / 3.0))
    root = root - (root - positive / (root * root)) * (1.0 / 3.0)
    potential[...] = -exchange_factor * root
    scale = 1.0 / math.sqrt(P_SIZE)

    def store(b):
        rows = pl.ds(pl.multiple_of(b * KB, KB), KB)
        return pltpu.make_async_copy(stage.at[b], update_out.at[rows], osems.at[b])

    def step(b, carry):
        first, last = plan[slots + b], plan[slots + b + 1]

        @pl.when(first == last)
        def _():
            stage[b] = jnp.zeros(stage.shape[1:], jnp.bfloat16)

        def body(i, p, q):
            weight_p = potential[pl.ds(tile_of[order[p]], 1), :]
            weight_q = potential[pl.ds(tile_of[order[q]], 1), :] * (q - p).astype(jnp.float32)
            weighted = jnp.concatenate(
                [
                    (pair[p, 1].astype(jnp.float32) * weight_p).astype(jnp.bfloat16),
                    (pair[q, 1].astype(jnp.float32) * weight_q).astype(jnp.bfloat16),
                ],
                axis=1,
            )
            block = lax.dot_general(
                jnp.concatenate([pair[p, 0], pair[q, 0]], axis=1),
                weighted,
                (((1,), (1,)), ((), ())),
                preferred_element_type=jnp.float32,
            )

            @pl.when(last - first <= 2)
            def _():
                stage[b] = (block * scale).astype(jnp.bfloat16)

            @pl.when((last - first > 2) & (i == 0))
            def _():
                acc[...] = block

            @pl.when(i > 0)
            def _():
                acc[...] += block

        by_twos(first, last, load, body)

        @pl.when(last - first > 2)
        def _():
            stage[b] = (acc[...] * scale).astype(jnp.bfloat16)

        store(b).start()
        return carry

    lax.fori_loop(0, blocks, step, 0)
    for b in range(blocks):
        store(b).wait()


def update(plan, order, tile_of, contributions, collect, parts, tiles, blocks, cols):
    slots = len(parts) * parts[0].shape[0]
    entry = parts[0].shape[1:]
    all_tiles = (collect.shape[0], P_SIZE)
    return pl.pallas_call(
        functools.partial(update_kernel, blocks, tiles),
        out_shape=(
            jax.ShapeDtypeStruct((tiles, P_SIZE), jnp.float32),
            jax.ShapeDtypeStruct((blocks * KB, cols), jnp.bfloat16),
        ),
        in_specs=[SMEM] * 3 + [VMEM] * 2 + [HBM] * len(parts),
        out_specs=(VMEM, HBM),
        scratch_shapes=[
            pltpu.VMEM((slots,) + entry, jnp.bfloat16),
            pltpu.VMEM(all_tiles, jnp.float32),
            pltpu.VMEM(all_tiles, jnp.float32),
            pltpu.VMEM((KB, cols), jnp.float32),
            pltpu.VMEM((blocks, KB, cols), jnp.bfloat16),
            pltpu.SemaphoreType.DMA((slots,)),
            pltpu.SemaphoreType.DMA((blocks,)),
        ],
        compiler_params=pltpu.CompilerParams(vmem_limit_bytes=62 * MIB),
        name="update",
    )(plan, order, tile_of, contributions, collect, *parts)


def shift(block, axis, step):
    count = lax.axis_size(axis)
    pairs = [(i, i + step) for i in range(count) if 0 <= i + step < count]
    return lax.ppermute(block, axis, pairs)


def make_plan(lists, me, entries, tiles, col_count, blocks):
    slots = col_count * CAP
    sent = sent_rows(slots, tiles)
    lists = lists[:, : 2 * entries + tiles]
    peers, named, counts = lists[:, :entries], lists[:, entries : 2 * entries], lists[:, 2 * entries :]
    index = jnp.arange(entries, dtype=jnp.int32)
    home = jnp.arange(col_count, dtype=jnp.int32)[:, None]
    earlier = (peers[:, :, None] == peers[:, None, :]) & (index[None, :] < index[:, None])
    rank = jnp.sum(earlier.astype(jnp.int32), axis=2)
    live = (index % SLOTS)[None, :] < jnp.repeat(counts, SLOTS, axis=1)
    row = jnp.where(live, peers * sent + chunk_of(home, peers, col_count) * CAP + rank, -1).reshape(col_count, tiles, SLOTS)
    core = (home * sent + slots + jnp.arange(tiles, dtype=jnp.int32))[:, :, None]
    row = jnp.concatenate([row, core], axis=2).reshape(col_count * tiles, SLOTS + 1, 1)
    picked = row == jnp.arange(col_count * sent, dtype=jnp.int32)
    collect = jnp.sum(picked.astype(jnp.float32), axis=1)
    hit = (
        (peers == me)[:, None, :]
        & (rank[:, None, :] == jnp.arange(CAP, dtype=jnp.int32)[None, :, None])
        & live[:, None, :]
    )
    at_me = chunk_of(home, me, col_count).reshape(1, col_count) == home
    tile = home * tiles + index[None, :] // SLOTS

    def of_slots(values):
        by_home = jnp.sum(jnp.where(hit, values[:, None, :], 0), axis=2)
        return jnp.sum(jnp.where(at_me[:, :, None], by_home[None], 0), axis=1).reshape(slots)

    wanted = of_slots(named + 1) - 1
    tile_of = of_slots(tile)
    key = jnp.where(wanted < 0, blocks, wanted)
    place = jnp.arange(slots, dtype=jnp.int32)
    before = (key[None, :] < key[:, None]) | (
        (key[None, :] == key[:, None]) & (place[None, :] < place[:, None])
    )
    spot = jnp.sum(before.astype(jnp.int32), axis=1)
    order = jnp.sum(jnp.where(spot[None, :] == place[:, None], place[None, :], 0), axis=1)
    starts = jnp.sum(
        (key[None, :] < jnp.arange(blocks + 1, dtype=jnp.int32)[:, None]).astype(jnp.int32), axis=1
    )
    plan = jnp.concatenate([wanted, starts, me[None]]).astype(jnp.int32)
    return collect, plan, order.astype(jnp.int32), tile_of.astype(jnp.int32)


def shards(
    start_columns,
    hamiltonian,
    band_pattern,
    coefficients,
    tile_peer,
    tile_block,
    tile_count,
    basis_values,
    core_density,
):
    col_count = lax.axis_size("col")
    entries = tile_peer.shape[0]
    tiles = core_density.shape[0]
    cols = start_columns.shape[1]
    blocks = start_columns.shape[0] // KB
    peers = tile_peer[:, 0]
    me = lax.axis_index("col").astype(jnp.int32)

    own, lists = own_piece(
        peers, tile_block, tile_count, band_pattern, hamiltonian.reshape(-1, W), col_count
    )
    lists = lax.all_to_all(lists, "col", split_axis=0, concat_axis=0, tiled=True)
    pieces, owners, awaited, handed = gather_pieces(own)
    v_low = shift(start_columns[-DEG * W :], "row", 1)
    v_high = shift(start_columns[: DEG * W], "row", -1)
    parts = exchange(me[None], peers, basis_values, own, awaited + [v_low, v_high, lists], handed)

    first, last = edge_blocks(owners, pieces, col_count, DEG - 1)
    h_low = shift(last, "row", 1)
    h_high = shift(first, "row", -1)
    inner = chebyshev_inner(coefficients, owners, v_low, start_columns, v_high, pieces)
    kernel_t = chebyshev_outer(
        coefficients, inner, v_low, start_columns, v_high, h_low, first, last, h_high
    )
    collect, plan, order, tile_of = make_plan(lists[:, 0], me, entries, tiles, col_count, blocks)
    partial = project(plan, order, kernel_t, core_density, parts, col_count)
    contributions = lax.all_to_all(partial, "col", split_axis=0, concat_axis=0, tiled=True)
    contributions = contributions.reshape(-1, P_SIZE)
    return update(
        plan, order, tile_of, contributions, collect, parts, tiles, blocks, cols
    )


def solution(mesh):
    return jax.shard_map(
        shards,
        mesh=mesh,
        in_specs=(
            P("row", "col"),
            P(("row", "col"), None, None, None),
            P(("row", "col")),
            P(),
            P(("row", "col"), None),
            P(("row", "col")),
            P(("row", "col")),
            P(("row", "col"), None, None, None),
            P(("row", "col"), None),
        ),
        out_specs=(P(("row", "col"), None), P("row", "col")),
        check_vma=False,
    )
```

```python
import functools
import math

import jax
import jax.numpy as jnp
from jax import lax
from jax.experimental import pallas as pl
from jax.experimental.pallas import tpu as pltpu
from jax.sharding import PartitionSpec as P

W = 256
KB = 512
DEG = 3
SLOTS = 4
CAP = 2
P_SIZE = 128
MIB = 1 << 20
LISTS = 8

exchange_factor = (3.0 / math.pi) ** (1.0 / 3.0)
HBM = pl.BlockSpec(memory_space=pltpu.HBM)
ANY = pl.BlockSpec(memory_space=pl.ANY)
SMEM = pl.BlockSpec(memory_space=pltpu.SMEM)
VMEM = pl.BlockSpec(memory_space=pltpu.VMEM)


def partner(me, j, count):
    if count & (count - 1) == 0:
        return me ^ abs(j)
    return (me + j) % count


def piece_kernel(peers, named, counts, pattern, ham, piece, lists, blocks, sems):
    load = pltpu.make_async_copy(ham, blocks, sems.at[0])
    load.start()
    lane = lax.broadcasted_iota(jnp.int32, (LISTS, P_SIZE), 1)
    row = jnp.zeros((LISTS, P_SIZE), jnp.int32)
    at = 0
    for ref in (peers, named, counts):
        for i in range(ref.shape[0]):
            row = jnp.where(lane == at, ref[i], row)
            at += 1
    for c in range(lists.shape[0]):
        lists[c] = row
    load.wait()
    for i in range(ham.shape[0] // (2 * W)):
        coupling = slice((2 * i + 1) * W, (2 * i + 2) * W)
        blocks[coupling] = blocks[coupling] * pattern[i].astype(jnp.bfloat16)
    store = pltpu.make_async_copy(blocks, piece, sems.at[1])
    store.start()
    store.wait()


def own_piece(peers, named, counts, pattern, ham, col_count):
    return pl.pallas_call(
        piece_kernel,
        out_shape=(
            jax.ShapeDtypeStruct(ham.shape, ham.dtype),
            jax.ShapeDtypeStruct((col_count, LISTS, P_SIZE), jnp.int32),
        ),
        in_specs=[SMEM] * 4 + [HBM],
        out_specs=(HBM, VMEM),
        scratch_shapes=[pltpu.VMEM(ham.shape, ham.dtype), pltpu.SemaphoreType.DMA((2,))],
        compiler_params=pltpu.CompilerParams(vmem_limit_bytes=62 * MIB),
        name="own_piece",
    )(peers, named, counts, pattern, ham)


def lines_of(count):
    inner = max(count // 4, 1) if count & (count - 1) == 0 else 1
    return count // inner, inner


def swap_along(block, t):
    count = lax.axis_size("col")
    _, inner = lines_of(count)
    pairs = [(c, c - c % inner + partner(c % inner, t, inner)) for c in range(count)]
    return lax.ppermute(block, "col", pairs)


def chunk_of(home, owner, count):
    outer, inner = lines_of(count)
    return partner(home % inner, owner % inner, inner) * outer + home // inner


def pack_kernel(entries, col_count, wanted, me, peers, basis, first, *refs):
    outer, inner = lines_of(col_count)
    sent, (held, owner, count, in_sems, out_sems) = refs[: len(wanted)], refs[len(wanted) :]
    for c in range(col_count):
        count[c] = 0
        for k in range(CAP):
            owner[c * CAP + k] = 0
    for e in range(entries):
        p = peers[e]
        k = count[p]
        count[p] = k + 1
        owner[p * CAP + k] = e
    place = lax.rem(me[0], inner)
    tasks = []
    for target, group in zip(sent, wanted):
        for line in range(outer):
            for i, (t, k) in enumerate(group):
                n = len(tasks)
                e = owner[(line * inner + partner(place, t, inner)) * CAP + k]
                fetch = pltpu.make_async_copy(basis.at[e], held.at[n], in_sems.at[n])
                store = pltpu.make_async_copy(held.at[n], target.at[line, i], out_sems.at[n])
                tasks.append((fetch, store))
    for fetch, _ in tasks:
        fetch.start()
    for fetch, store in tasks:
        fetch.wait()
        store.start()
    for _, store in tasks:
        store.wait()


def pack(me, peers, basis, first, col_count, wanted):
    outer, _ = lines_of(col_count)
    entries = basis.shape[0]
    number = sum(len(group) for group in wanted) * outer
    return list(pl.pallas_call(
        functools.partial(pack_kernel, entries, col_count, wanted),
        out_shape=tuple(
            jax.ShapeDtypeStruct((outer, len(group)) + basis.shape[1:], basis.dtype)
            for group in wanted
        ),
        in_specs=[SMEM, SMEM, HBM, HBM],
        out_specs=(HBM,) * len(wanted),
        scratch_shapes=[
            pltpu.VMEM((number,) + basis.shape[1:], basis.dtype),
            pltpu.SMEM((col_count * CAP,), jnp.int32),
            pltpu.SMEM((col_count,), jnp.int32),
            pltpu.SemaphoreType.DMA((number,)),
            pltpu.SemaphoreType.DMA((number,)),
        ],
        compiler_params=pltpu.CompilerParams(vmem_limit_bytes=62 * MIB),
        name="pack",
    )(me, peers, basis, first))


def after(block, *others):
    return pl.pallas_call(
        lambda *refs: None,
        out_shape=jax.ShapeDtypeStruct(block.shape, block.dtype),
        in_specs=[HBM] + [ANY] * len(others),
        out_specs=HBM,
        input_output_aliases={0: 0},
        compiler_params=pltpu.CompilerParams(vmem_limit_bytes=62 * MIB),
        name="after",
    )(block, *others)


def exchange(me, peers, basis, own, early, awaited, handed):
    count = lax.axis_size("col")
    outer, inner = lines_of(count)
    groups = [[line * inner + place for line in range(outer)] for place in range(inner)]

    def between_lines(blocks, *others):
        block = jnp.concatenate(blocks, axis=1)
        return lax.all_to_all(
            after(block, *others), "col", split_axis=0, concat_axis=0,
            axis_index_groups=groups, tiled=True,
        )

    here = [(0, k) for k in range(CAP)]
    ahead = [[(t, 0)] for t in range(1, inner)]
    rest = [[(t, k)] for k in range(1, CAP) for t in range(1, inner)]
    sent = pack(me, peers, basis, own, count, ahead) if ahead else []
    to_lines, *later = pack(me, peers, basis, early, count, [here] + rest)
    swapped = {
        group[0]: swap_along(block, group[0][0]) for block, group in zip(sent + later, ahead + rest)
    }
    parts = [between_lines([to_lines], *awaited, *[swapped[group[0]] for group in ahead])]
    for t in range(1, inner):
        parts.append(between_lines([swapped[t, k] for k in range(CAP)], parts[-1], *handed))
    return [part.reshape((outer * CAP,) + part.shape[2:]) for part in parts]


def gather_pieces(own):
    count = lax.axis_size("col")
    outer, inner = lines_of(count)
    me = lax.axis_index("col").astype(jnp.int32)
    a, b = me // inner, me % inner

    def move(block, ways):
        pairs = [(x * inner + y, z * inner + y) for x, z in ways for y in range(inner)]
        return lax.ppermute(block, "col", pairs)

    if outer == 4:
        middle, outwards = [(1, 2), (2, 1)], [(1, 0), (2, 3)]
        near = move(own, [(0, 1), (1, 0), (2, 3), (3, 2)])
        across = move(own, middle)
        far = move(near, middle)
        handed = move(across, outwards)
        last = move(far, outwards)
        within = (a == 1) | (a == 2)
        lines = [
            (own, a),
            (near, a ^ 1),
            (across + handed, jnp.where(within, a ^ 3, a ^ 2)),
            (far + last, jnp.where(within, a ^ 2, a ^ 3)),
        ]
        awaited, ends = [far, handed], [last]
    else:
        lines = [(own, a)] + [
            (move(own, [(x, partner(x, t, outer)) for x in range(outer)]), partner(a, -t, outer))
            for t in range(1, outer)
        ]
        awaited, ends = [block for block, _ in lines[1:]], []
    pieces, owners = [], []
    for block, line in lines:
        pieces.append(block)
        owners.append(line * inner + b)
        for t in range(1, inner):
            pieces.append(swap_along(block, t))
            owners.append(line * inner + partner(b, -t, inner))
    ends += [piece for piece in pieces[: 3 * inner] if all(piece is not block for block, _ in lines)]
    return pieces, jnp.stack(owners).astype(jnp.int32), awaited, ends


def edge_kernel(col_count, depth, owners, *refs):
    pieces, (first, last, sems) = refs[:-3], refs[-3:]
    held = pieces[0].shape[0] // (2 * W)
    total = col_count * held

    def each(act):
        for i, piece in enumerate(pieces):
            for g in range(depth):
                for out, block, sem in ((first, g, 0), (last, total - depth + g, 1)):
                    source = piece.at[pl.ds(block % held * 2 * W, 2 * W)]
                    copy = pltpu.make_async_copy(source, out.at[g], sems.at[sem, g])

                    @pl.when(owners[i] == block // held)
                    def _():
                        act(copy)

    each(lambda copy: copy.start())
    each(lambda copy: copy.wait())


def edge_blocks(owners, pieces, col_count, depth):
    shape = jax.ShapeDtypeStruct((depth, 2 * W, W), pieces[0].dtype)
    return pl.pallas_call(
        functools.partial(edge_kernel, col_count, depth),
        out_shape=(shape, shape),
        in_specs=[SMEM] + [HBM] * len(pieces),
        out_specs=(VMEM, VMEM),
        scratch_shapes=[pltpu.SemaphoreType.DMA((2, depth))],
        compiler_params=pltpu.CompilerParams(vmem_limit_bytes=62 * MIB),
        name="edge_blocks",
    )(owners, *pieces)


def rows_of(j, count=1):
    return pl.ds(j * W if isinstance(j, int) else pl.multiple_of(j * W, W), count * W)


def band_builder(source, target):
    rows = lax.broadcasted_iota(jnp.int32, (W, W), 0)
    cols = lax.broadcasted_iota(jnp.int32, (W, W), 1)
    upper = jnp.where(rows <= cols, 1.0, 0.0).astype(jnp.bfloat16)

    def build(j, carry):
        coupling = source[j, W:]
        lower_band = coupling * upper
        target[j, :, 0:W] = lower_band
        target[j, :, W : 2 * W] = source[j, :W]
        target[j, :, 2 * W : 3 * W] = coupling - lower_band
        return carry

    return build


def inner_kernel(blocks, coef, owners, v_low, v_mid, v_high, *refs):
    (
        *pieces, out, edge_1, edge_2, edge_total,
        vext, hraw, hcat, cheb_1, cheb_2, total, kern, sems, psems, osems, esems,
    ) = refs
    held = pieces[0].shape[0] // (2 * W)
    v_copies = [
        pltpu.make_async_copy(v_low.at[rows_of(DEG - 1)], vext.at[rows_of(0)], sems.at[0]),
        pltpu.make_async_copy(v_mid, vext.at[rows_of(1, blocks)], sems.at[1]),
        pltpu.make_async_copy(v_high.at[rows_of(0)], vext.at[rows_of(blocks + 1)], sems.at[2]),
    ]

    def each_piece(act):
        for i, piece in enumerate(pieces):
            for k in range(held):
                act(pltpu.make_async_copy(
                    piece.at[pl.ds(k * 2 * W, 2 * W)],
                    hraw.at[owners[i] * held + k],
                    psems.at[i, k],
                ))

    each_piece(lambda copy: copy.start())
    for copy in v_copies:
        copy.start()
    each_piece(lambda copy: copy.wait())
    build = band_builder(hraw, hcat)
    build(0, 0)
    for copy in v_copies:
        copy.wait()

    def band(source, j, row):
        return jnp.dot(hcat[j], source[rows_of(row, 3), :], preferred_element_type=jnp.float32)

    def edges(source, target, at):
        size = source.shape[0] // W
        return [
            pltpu.make_async_copy(
                source.at[rows_of(place, 2)], target.at[rows_of(2 * i, 2)], esems.at[at, i]
            )
            for i, place in enumerate((0, size - 2))
        ]

    def first(j, carry):
        value = band(vext, j, j)
        build(jnp.minimum(j + 1, blocks - 1), 0)
        cheb_1[rows_of(j), :] = value.astype(jnp.bfloat16)
        total[rows_of(j), :] = value
        return carry

    lax.fori_loop(0, blocks, first, 0, unroll=4)

    def second(j, carry):
        begin = vext[rows_of(j + 2), :].astype(jnp.float32)
        value = 2.0 * band(cheb_1, j + 1, j) - begin
        cheb_2[rows_of(j), :] = value.astype(jnp.bfloat16)
        total[rows_of(j + 1), :] = (
            coef[0] * begin + (coef[1] - coef[3]) * total[rows_of(j + 1), :] + coef[2] * value
        )
        return carry

    lax.fori_loop(0, blocks - 2, second, 0, unroll=4)
    outgoing = (
        edges(cheb_1, edge_1, 0) + edges(cheb_2, edge_2, 1) + edges(total, edge_total, 2)
    )
    for copy in outgoing:
        copy.start()

    def store(j):
        return pltpu.make_async_copy(kern.at[j], out.at[j], osems.at[j])

    def third(j, carry):
        for half in range(KB // W):
            i = j * (KB // W) + half
            value = total[rows_of(i), :] + (2.0 * coef[3]) * band(cheb_2, i, i - 2)
            kern[j, :, half * W : (half + 1) * W] = value.astype(jnp.bfloat16).T
        store(j).start()
        return carry

    last = blocks // (KB // W) - 1
    lax.fori_loop(1, last, third, 0, unroll=2)
    for j in range(1, last):
        store(j).wait()
    for copy in outgoing:
        copy.wait()


def chebyshev_inner(coefficients, owners, v_low, v_mid, v_high, pieces):
    blocks = v_mid.shape[0] // W
    cols = v_mid.shape[1]
    flops = 2 * W * 3 * W * cols * (3 * blocks - 6)
    result = (blocks * W // KB, cols, KB)
    held = pieces[0].shape[0] // (2 * W)
    return pl.pallas_call(
        functools.partial(inner_kernel, blocks),
        out_shape=(
            jax.ShapeDtypeStruct(result, jnp.bfloat16),
            jax.ShapeDtypeStruct((4 * W, cols), jnp.bfloat16),
            jax.ShapeDtypeStruct((4 * W, cols), jnp.bfloat16),
            jax.ShapeDtypeStruct((4 * W, cols), jnp.float32),
        ),
        in_specs=[SMEM] * 2 + [HBM] * (3 + len(pieces)),
        out_specs=(HBM,) * 4,
        scratch_shapes=[
            pltpu.VMEM(((blocks + 2) * W, cols), jnp.bfloat16),
            pltpu.VMEM((blocks, 2 * W, W), jnp.bfloat16),
            pltpu.VMEM((blocks, W, 3 * W), jnp.bfloat16),
            pltpu.VMEM((blocks * W, cols), jnp.bfloat16),
            pltpu.VMEM(((blocks - 2) * W, cols), jnp.bfloat16),
            pltpu.VMEM((blocks * W, cols), jnp.float32),
            pltpu.VMEM(result, jnp.bfloat16),
            pltpu.SemaphoreType.DMA((3,)),
            pltpu.SemaphoreType.DMA((len(pieces), held)),
            pltpu.SemaphoreType.DMA((result[0],)),
            pltpu.SemaphoreType.DMA((3, 2)),
        ],
        compiler_params=pltpu.CompilerParams(vmem_limit_bytes=62 * MIB),
        cost_estimate=pl.CostEstimate(flops=flops, bytes_accessed=16 * MIB, transcendentals=0),
        name="chebyshev_inner",
    )(coefficients, owners, v_low, v_mid, v_high, *pieces)


def outer_kernel(
    blocks, coef, kernel_in, v_low, v_mid, v_high, h_low, h_first, h_last, h_high,
    edge_1, edge_2, edge_total, out,
    v, hraw, hcat, cheb_1, cheb_2, total, kern, sems, osems,
):
    last = kern.shape[0] - 1
    end = out.shape[0] - 1
    stages = [
        [
            (h_low, hraw.at[pl.ds(0, 2)]),
            (v_low, v.at[0, rows_of(0, 3)]),
            (v_mid.at[rows_of(0)], v.at[0, rows_of(3)]),
            (h_high, hraw.at[pl.ds(6, 2)]),
            (v_mid.at[rows_of(blocks - 1)], v.at[1, rows_of(0)]),
            (v_high, v.at[1, rows_of(1, 3)]),
        ],
        [
            (h_first, hraw.at[pl.ds(2, 2)]),
            (h_last, hraw.at[pl.ds(4, 2)]),
            (edge_1.at[rows_of(0, 2)], cheb_1.at[0, rows_of(2, 2)]),
            (edge_1.at[rows_of(2, 2)], cheb_1.at[1, rows_of(0, 2)]),
        ],
        [
            (edge_2.at[rows_of(0, 2)], cheb_2.at[0, rows_of(2, 2)]),
            (edge_2.at[rows_of(2, 2)], cheb_2.at[1, rows_of(0, 2)]),
            (edge_total.at[rows_of(0, 2)], total.at[0]),
            (edge_total.at[rows_of(2, 2)], total.at[1]),
        ],
    ]
    at = 0
    for i, stage in enumerate(stages):
        stages[i] = [
            pltpu.make_async_copy(source, target, sems.at[at + n])
            for n, (source, target) in enumerate(stage)
        ]
        at += len(stage)
        for copy in stages[i]:
            copy.start()
    build = band_builder(hraw, hcat)

    def arrived(i):
        for copy in stages[i]:
            copy.wait()

    def band(side, j, source, row):
        return jnp.dot(
            hcat[4 * side + j], source[side, rows_of(row, 3), :], preferred_element_type=jnp.float32
        )

    arrived(0)
    for j in (0, 1, 6, 7):
        build(j, 0)
    for side, places in ((0, (0, 1)), (1, (2, 3))):
        for j in places:
            value = band(side, j, v, j - 2 * side)
            cheb_1[side, rows_of(j), :] = value.astype(jnp.bfloat16)
    arrived(1)
    for j in (2, 3, 4, 5):
        build(j, 0)
    arrived(2)
    for side, places in ((0, ((1, 0), (2, 1))), (1, ((2, 3), (1, 2)))):
        for j, place in places:
            begin = v[side, rows_of(place + 2 - 4 * side), :].astype(jnp.float32)
            value = 2.0 * band(side, j, cheb_1, j - 1) - begin
            cheb_2[side, rows_of(place), :] = value.astype(jnp.bfloat16)
            if (j, place) == places[1]:
                within = rows_of(side)
                total[side, within, :] = (
                    coef[0] * begin + (coef[1] - coef[3]) * total[side, within, :] + coef[2] * value
                )
    for side in range(2):
        for half in range(2):
            j = 2 + half if side == 0 else half
            value = total[side, rows_of(half), :] + (2.0 * coef[3]) * band(side, j, cheb_2, half)
            kern[side, :, half * W : (half + 1) * W] = value.astype(jnp.bfloat16).T
    stores = [
        pltpu.make_async_copy(kern.at[0], out.at[0], osems.at[0]),
        pltpu.make_async_copy(kern.at[last], out.at[end], osems.at[1]),
    ]
    for store in stores:
        store.start()
    for store in stores:
        store.wait()


def chebyshev_outer(coefficients, inner, v_low, v_mid, v_high, h_low, h_first, h_last, h_high):
    kernel_t, edge_1, edge_2, edge_total = inner
    blocks = v_mid.shape[0] // W
    cols = v_mid.shape[1]
    return pl.pallas_call(
        functools.partial(outer_kernel, blocks),
        out_shape=jax.ShapeDtypeStruct(kernel_t.shape, kernel_t.dtype),
        in_specs=[SMEM] + [HBM] * 11,
        out_specs=HBM,
        input_output_aliases={1: 0},
        scratch_shapes=[
            pltpu.VMEM((2, 4 * W, cols), jnp.bfloat16),
            pltpu.VMEM((8, 2 * W, W), jnp.bfloat16),
            pltpu.VMEM((8, W, 3 * W), jnp.bfloat16),
            pltpu.VMEM((2, 4 * W, cols), jnp.bfloat16),
            pltpu.VMEM((2, 4 * W, cols), jnp.bfloat16),
            pltpu.VMEM((2, 2 * W, cols), jnp.float32),
            pltpu.VMEM((2, cols, KB), jnp.bfloat16),
            pltpu.SemaphoreType.DMA((14,)),
            pltpu.SemaphoreType.DMA((2,)),
        ],
        compiler_params=pltpu.CompilerParams(vmem_limit_bytes=62 * MIB),
        name="chebyshev_outer",
    )(
        coefficients, kernel_t, v_low, v_mid, v_high, h_low, h_first, h_last, h_high,
        edge_1, edge_2, edge_total,
    )


def entry_loads(order, parts, pair, sems):
    size = parts[0].shape[0]

    def load(p):
        return pltpu.make_async_copy(parts[0].at[0], pair.at[p], sems.at[p])

    def start(p, carry):
        n = order[p]
        for t, part in enumerate(parts):
            @pl.when((n >= t * size) & (n < (t + 1) * size))
            def _():
                pltpu.make_async_copy(part.at[n - t * size], pair.at[p], sems.at[p]).start()

        return carry

    return load, start


def by_twos(first, last, load, body):
    def step(i, carry):
        p = first + 2 * i
        q = jnp.minimum(p + 1, last - 1)
        load(p).wait()

        @pl.when(q > p)
        def _():
            load(q).wait()

        body(i, p, q)
        return carry

    lax.fori_loop(0, (last - first + 1) // 2, step, 0)


def sent_rows(slots, tiles):
    return slots + tiles + -(slots + tiles) % 8


def project_kernel(blocks, plan, order, kernel_t, core, *refs):
    *parts, out, kern, pair, rows, ksems, bsems = refs
    slots = pair.shape[0]
    load, start = entry_loads(order, parts, pair, bsems)

    def fetch(b):
        return pltpu.make_async_copy(kernel_t.at[b], kern.at[b], ksems.at[b])

    def begin(b, carry):
        first, last = plan[slots + b], plan[slots + b + 1]

        @pl.when(first < last)
        def _():
            fetch(b).start()

        return lax.fori_loop(first, last, start, carry)

    lax.fori_loop(0, blocks, begin, 0)
    rows[...] = jnp.zeros_like(rows)
    rows[slots : slots + core.shape[0]] = core[...]

    def step(b, carry):
        first, last = plan[slots + b], plan[slots + b + 1]

        @pl.when(first < last)
        def _():
            fetch(b).wait()

        def body(i, p, q):
            both = jnp.concatenate([pair[p, 0], pair[q, 0]], axis=1)
            projected = jnp.dot(kern[b], both, preferred_element_type=jnp.float32)
            other = jnp.concatenate([pair[p, 1], pair[q, 1]], axis=1).astype(jnp.float32)
            value = jnp.sum(projected * other, axis=0, keepdims=True) * (1.0 / KB)
            rows[pl.ds(order[p], 1), :] = value[:, :P_SIZE]
            rows[pl.ds(order[q], 1), :] = value[:, P_SIZE:]

        by_twos(first, last, load, body)
        return carry

    lax.fori_loop(0, blocks, step, 0)
    for c in range(out.shape[0]):
        out[c] = rows[...]


def project(plan, order, kernel_t, core, parts, col_count):
    slots = col_count * CAP
    entry = parts[0].shape[1:]
    sent = sent_rows(slots, core.shape[0])
    blocks = kernel_t.shape[0]
    return pl.pallas_call(
        functools.partial(project_kernel, blocks),
        out_shape=jax.ShapeDtypeStruct((col_count, sent, P_SIZE), jnp.float32),
        in_specs=[SMEM, SMEM, HBM, VMEM] + [HBM] * len(parts),
        out_specs=VMEM,
        scratch_shapes=[
            pltpu.VMEM(kernel_t.shape, jnp.bfloat16),
            pltpu.VMEM((slots,) + entry, jnp.bfloat16),
            pltpu.VMEM((sent, P_SIZE), jnp.float32),
            pltpu.SemaphoreType.DMA((blocks,)),
            pltpu.SemaphoreType.DMA((slots,)),
        ],
        compiler_params=pltpu.CompilerParams(vmem_limit_bytes=62 * MIB),
        name="project",
    )(plan, order, kernel_t, core, *parts)


def update_kernel(
    blocks, tiles, plan, order, tile_of, contributions, collect, *refs
):
    *parts, density_out, update_out, pair, density, potential, acc, stage, sems, osems = refs
    slots = pair.shape[0]
    live = plan[slots + blocks]
    me = plan[slots + blocks + 1]
    load, start = entry_loads(order, parts, pair, sems)
    lax.fori_loop(0, live, start, 0)
    density[...] = jnp.dot(
        collect[...],
        contributions[...],
        preferred_element_type=jnp.float32,
        precision=lax.Precision.HIGHEST,
    )
    for t in range(tiles):
        density_out[pl.ds(t, 1), :] = density[pl.ds(me * tiles + t, 1), :]
    positive = jnp.maximum(density[...], 0.1)
    root = jnp.exp(jnp.log(positive) * (1.0 / 3.0))
    root = root - (root - positive / (root * root)) * (1.0 / 3.0)
    potential[...] = -exchange_factor * root
    scale = 1.0 / math.sqrt(P_SIZE)

    def store(b):
        rows = pl.ds(pl.multiple_of(b * KB, KB), KB)
        return pltpu.make_async_copy(stage.at[b], update_out.at[rows], osems.at[b])

    most = jnp.maximum(live - 1, 0)

    @pl.when(live == 0)
    def _():
        pair[0] = jnp.zeros(pair.shape[1:], jnp.bfloat16)

    def arrived(p, carry):
        load(p).wait()
        return carry

    lax.fori_loop(0, live, arrived, 0)

    def two(p, last):
        sides = []
        for place in (p, p + 1):
            at = jnp.minimum(place, most)
            weight = potential[pl.ds(tile_of[order[at]], 1), :] * (place < last).astype(jnp.float32)
            sides.append((pair[at, 0], (pair[at, 1].astype(jnp.float32) * weight).astype(jnp.bfloat16)))
        return lax.dot_general(
            jnp.concatenate([rows for rows, _ in sides], axis=1),
            jnp.concatenate([weighted for _, weighted in sides], axis=1),
            (((1,), (1,)), ((), ())),
            preferred_element_type=jnp.float32,
        )

    def step(b, carry):
        first, last = plan[slots + b], plan[slots + b + 1]
        stage[b] = (two(first, last) * scale).astype(jnp.bfloat16)

        @pl.when(last - first > 2)
        def _():
            acc[...] = two(first, last)

            def more(i, carry):
                acc[...] += two(first + 2 * i, last)
                return carry

            lax.fori_loop(1, (last - first + 1) // 2, more, 0)
            stage[b] = (acc[...] * scale).astype(jnp.bfloat16)

        store(b).start()
        return carry

    lax.fori_loop(0, blocks, step, 0)
    for b in range(blocks):
        store(b).wait()


def update(plan, order, tile_of, contributions, collect, parts, tiles, blocks, cols):
    slots = len(parts) * parts[0].shape[0]
    entry = parts[0].shape[1:]
    all_tiles = (collect.shape[0], P_SIZE)
    return pl.pallas_call(
        functools.partial(update_kernel, blocks, tiles),
        out_shape=(
            jax.ShapeDtypeStruct((tiles, P_SIZE), jnp.float32),
            jax.ShapeDtypeStruct((blocks * KB, cols), jnp.bfloat16),
        ),
        in_specs=[SMEM] * 3 + [VMEM] * 2 + [HBM] * len(parts),
        out_specs=(VMEM, HBM),
        scratch_shapes=[
            pltpu.VMEM((slots,) + entry, jnp.bfloat16),
            pltpu.VMEM(all_tiles, jnp.float32),
            pltpu.VMEM(all_tiles, jnp.float32),
            pltpu.VMEM((KB, cols), jnp.float32),
            pltpu.VMEM((blocks, KB, cols), jnp.bfloat16),
            pltpu.SemaphoreType.DMA((slots,)),
            pltpu.SemaphoreType.DMA((blocks,)),
        ],
        compiler_params=pltpu.CompilerParams(vmem_limit_bytes=62 * MIB),
        name="update",
    )(plan, order, tile_of, contributions, collect, *parts)


def shift(block, axis, step):
    count = lax.axis_size(axis)
    pairs = [(i, i + step) for i in range(count) if 0 <= i + step < count]
    return lax.ppermute(block, axis, pairs)


def make_plan(lists, me, entries, tiles, col_count, blocks):
    slots = col_count * CAP
    sent = sent_rows(slots, tiles)
    lists = lists[:, : 2 * entries + tiles]
    peers, named, counts = lists[:, :entries], lists[:, entries : 2 * entries], lists[:, 2 * entries :]
    index = jnp.arange(entries, dtype=jnp.int32)
    home = jnp.arange(col_count, dtype=jnp.int32)[:, None]
    earlier = (peers[:, :, None] == peers[:, None, :]) & (index[None, :] < index[:, None])
    rank = jnp.sum(earlier.astype(jnp.int32), axis=2)
    live = (index % SLOTS)[None, :] < jnp.repeat(counts, SLOTS, axis=1)
    row = jnp.where(live, peers * sent + chunk_of(home, peers, col_count) * CAP + rank, -1).reshape(col_count, tiles, SLOTS)
    core = (home * sent + slots + jnp.arange(tiles, dtype=jnp.int32))[:, :, None]
    row = jnp.concatenate([row, core], axis=2).reshape(col_count * tiles, SLOTS + 1, 1)
    picked = row == jnp.arange(col_count * sent, dtype=jnp.int32)
    collect = jnp.sum(picked.astype(jnp.float32), axis=1)
    hit = (
        (peers == me)[:, None, :]
        & (rank[:, None, :] == jnp.arange(CAP, dtype=jnp.int32)[None, :, None])
        & live[:, None, :]
    )
    at_me = chunk_of(home, me, col_count).reshape(1, col_count) == home
    tile = home * tiles + index[None, :] // SLOTS

    def of_slots(values):
        by_home = jnp.sum(jnp.where(hit, values[:, None, :], 0), axis=2)
        return jnp.sum(jnp.where(at_me[:, :, None], by_home[None], 0), axis=1).reshape(slots)

    wanted = of_slots(named + 1) - 1
    tile_of = of_slots(tile)
    key = jnp.where(wanted < 0, blocks, wanted)
    place = jnp.arange(slots, dtype=jnp.int32)
    before = (key[None, :] < key[:, None]) | (
        (key[None, :] == key[:, None]) & (place[None, :] < place[:, None])
    )
    spot = jnp.sum(before.astype(jnp.int32), axis=1)
    order = jnp.sum(jnp.where(spot[None, :] == place[:, None], place[None, :], 0), axis=1)
    starts = jnp.sum(
        (key[None, :] < jnp.arange(blocks + 1, dtype=jnp.int32)[:, None]).astype(jnp.int32), axis=1
    )
    plan = jnp.concatenate([wanted, starts, me[None]]).astype(jnp.int32)
    return collect, plan, order.astype(jnp.int32), tile_of.astype(jnp.int32)


def shards(
    start_columns,
    hamiltonian,
    band_pattern,
    coefficients,
    tile_peer,
    tile_block,
    tile_count,
    basis_values,
    core_density,
):
    col_count = lax.axis_size("col")
    entries = tile_peer.shape[0]
    tiles = core_density.shape[0]
    cols = start_columns.shape[1]
    blocks = start_columns.shape[0] // KB
    peers = tile_peer[:, 0]
    me = lax.axis_index("col").astype(jnp.int32)

    own, lists = own_piece(
        peers, tile_block, tile_count, band_pattern, hamiltonian.reshape(-1, W), col_count
    )
    lists = lax.all_to_all(lists, "col", split_axis=0, concat_axis=0, tiled=True)
    pieces, owners, awaited, handed = gather_pieces(own)
    v_low = shift(start_columns[-DEG * W :], "row", 1)
    v_high = shift(start_columns[: DEG * W], "row", -1)
    parts = exchange(me[None], peers, basis_values, own, pieces[min(1, len(pieces) - 1)],
        awaited + [v_low, v_high, lists], handed)

    first, last = edge_blocks(owners, pieces, col_count, DEG - 1)
    h_low = shift(last, "row", 1)
    h_high = shift(first, "row", -1)
    inner = chebyshev_inner(coefficients, owners, v_low, start_columns, v_high, pieces)
    kernel_t = chebyshev_outer(
        coefficients, inner, v_low, start_columns, v_high, h_low, first, last, h_high
    )
    collect, plan, order, tile_of = make_plan(lists[:, 0], me, entries, tiles, col_count, blocks)
    partial = project(plan, order, kernel_t, core_density, parts, col_count)
    contributions = lax.all_to_all(partial, "col", split_axis=0, concat_axis=0, tiled=True)
    contributions = contributions.reshape(-1, P_SIZE)
    return update(
        plan, order, tile_of, contributions, collect, parts, tiles, blocks, cols
    )


def solution(mesh):
    return jax.shard_map(
        shards,
        mesh=mesh,
        in_specs=(
            P("row", "col"),
            P(("row", "col"), None, None, None),
            P(("row", "col")),
            P(),
            P(("row", "col"), None),
            P(("row", "col")),
            P(("row", "col")),
            P(("row", "col"), None, None, None),
            P(("row", "col"), None),
        ),
        out_specs=(P(("row", "col"), None), P("row", "col")),
        check_vma=False,
    )
```

```python
import functools
import math

import jax
import jax.numpy as jnp
from jax import lax
from jax.experimental import pallas as pl
from jax.experimental.pallas import tpu as pltpu
from jax.sharding import PartitionSpec as P

W = 256
KB = 512
DEG = 3
SLOTS = 4
CAP = 2
P_SIZE = 128
MIB = 1 << 20
LISTS = 16

exchange_factor = (3.0 / math.pi) ** (1.0 / 3.0)
HBM = pl.BlockSpec(memory_space=pltpu.HBM)
ANY = pl.BlockSpec(memory_space=pl.ANY)
SMEM = pl.BlockSpec(memory_space=pltpu.SMEM)
VMEM = pl.BlockSpec(memory_space=pltpu.VMEM)


def partner(me, j, count):
    if count & (count - 1) == 0:
        return me ^ abs(j)
    return (me + j) % count


def piece_kernel(peers, named, counts, pattern, ham, piece, blocks, sems):
    rows = ham.shape[0]
    load = pltpu.make_async_copy(ham, blocks.at[pl.ds(0, rows)], sems.at[0])
    load.start()
    lane = lax.broadcasted_iota(jnp.int32, (LISTS, W), 1)
    lists = jnp.zeros((LISTS, W), jnp.int32)
    at = 0
    for ref in (peers, named, counts):
        for i in range(ref.shape[0]):
            lists = jnp.where(lane == at, ref[i], lists)
            at += 1
    blocks[rows:] = lists.astype(jnp.float32).astype(jnp.bfloat16)
    load.wait()
    for i in range(rows // (2 * W)):
        coupling = slice((2 * i + 1) * W, (2 * i + 2) * W)
        blocks[coupling] = blocks[coupling] * pattern[i].astype(jnp.bfloat16)
    store = pltpu.make_async_copy(blocks, piece, sems.at[1])
    store.start()
    store.wait()


def own_piece(peers, named, counts, pattern, ham):
    piece = (ham.shape[0] + LISTS, W)
    return pl.pallas_call(
        piece_kernel,
        out_shape=jax.ShapeDtypeStruct(piece, ham.dtype),
        in_specs=[SMEM] * 4 + [HBM],
        out_specs=HBM,
        scratch_shapes=[pltpu.VMEM(piece, ham.dtype), pltpu.SemaphoreType.DMA((2,))],
        compiler_params=pltpu.CompilerParams(vmem_limit_bytes=62 * MIB),
        name="own_piece",
    )(peers, named, counts, pattern, ham)


def lines_of(count):
    inner = max(count // 4, 1) if count & (count - 1) == 0 else 1
    return count // inner, inner


def swap_along(block, t):
    count = lax.axis_size("col")
    _, inner = lines_of(count)
    pairs = [(c, c - c % inner + partner(c % inner, t, inner)) for c in range(count)]
    return lax.ppermute(block, "col", pairs)


def chunk_of(home, owner, count):
    outer, inner = lines_of(count)
    return partner(home % inner, owner % inner, inner) * outer + home // inner


def pack_kernel(entries, col_count, wanted, me, peers, basis, first, *refs):
    outer, inner = lines_of(col_count)
    sent, (held, owner, count, in_sems, out_sems) = refs[: len(wanted)], refs[len(wanted) :]
    for c in range(col_count):
        count[c] = 0
        for k in range(CAP):
            owner[c * CAP + k] = 0
    for e in range(entries):
        p = peers[e]
        k = count[p]
        count[p] = k + 1
        owner[p * CAP + k] = e
    place = lax.rem(me[0], inner)
    tasks = []
    for target, group in zip(sent, wanted):
        for line in range(outer):
            for i, (t, k) in enumerate(group):
                n = len(tasks)
                e = owner[(line * inner + partner(place, t, inner)) * CAP + k]
                fetch = pltpu.make_async_copy(basis.at[e], held.at[n], in_sems.at[n])
                store = pltpu.make_async_copy(held.at[n], target.at[line, i], out_sems.at[n])
                tasks.append((fetch, store))
    for fetch, _ in tasks:
        fetch.start()
    for fetch, store in tasks:
        fetch.wait()
        store.start()
    for _, store in tasks:
        store.wait()


def pack(me, peers, basis, first, col_count, wanted):
    outer, _ = lines_of(col_count)
    entries = basis.shape[0]
    number = sum(len(group) for group in wanted) * outer
    return list(pl.pallas_call(
        functools.partial(pack_kernel, entries, col_count, wanted),
        out_shape=tuple(
            jax.ShapeDtypeStruct((outer, len(group)) + basis.shape[1:], basis.dtype)
            for group in wanted
        ),
        in_specs=[SMEM, SMEM, HBM, HBM],
        out_specs=(HBM,) * len(wanted),
        scratch_shapes=[
            pltpu.VMEM((number,) + basis.shape[1:], basis.dtype),
            pltpu.SMEM((col_count * CAP,), jnp.int32),
            pltpu.SMEM((col_count,), jnp.int32),
            pltpu.SemaphoreType.DMA((number,)),
            pltpu.SemaphoreType.DMA((number,)),
        ],
        compiler_params=pltpu.CompilerParams(vmem_limit_bytes=62 * MIB),
        name="pack",
    )(me, peers, basis, first))


def after(block, *others):
    return pl.pallas_call(
        lambda *refs: None,
        out_shape=jax.ShapeDtypeStruct(block.shape, block.dtype),
        in_specs=[HBM] + [ANY] * len(others),
        out_specs=HBM,
        input_output_aliases={0: 0},
        compiler_params=pltpu.CompilerParams(vmem_limit_bytes=62 * MIB),
        name="after",
    )(block, *others)


def exchange(me, peers, basis, own, early, awaited, handed):
    count = lax.axis_size("col")
    outer, inner = lines_of(count)
    groups = [[line * inner + place for line in range(outer)] for place in range(inner)]

    def between_lines(blocks, *others):
        block = jnp.concatenate(blocks, axis=1)
        return lax.all_to_all(
            after(block, *others), "col", split_axis=0, concat_axis=0,
            axis_index_groups=groups, tiled=True,
        )

    here = [(0, k) for k in range(CAP)]
    ahead = [[(t, 0)] for t in range(1, inner)]
    rest = [[(t, k)] for k in range(1, CAP) for t in range(1, inner)]
    sent = pack(me, peers, basis, own, count, ahead) if ahead else []
    to_lines, *later = pack(me, peers, basis, early, count, [here] + rest)
    swapped = {
        group[0]: swap_along(block, group[0][0]) for block, group in zip(sent + later, ahead + rest)
    }
    parts = [between_lines([to_lines], *awaited, *[swapped[group[0]] for group in ahead])]
    for t in range(1, inner):
        parts.append(between_lines([swapped[t, k] for k in range(CAP)], parts[-1], *handed))
    return [part.reshape((outer * CAP,) + part.shape[2:]) for part in parts]


def gather_pieces(own):
    count = lax.axis_size("col")
    outer, inner = lines_of(count)
    me = lax.axis_index("col").astype(jnp.int32)
    a, b = me // inner, me % inner

    def move(block, ways):
        pairs = [(x * inner + y, z * inner + y) for x, z in ways for y in range(inner)]
        return lax.ppermute(block, "col", pairs)

    if outer == 4:
        middle, outwards = [(1, 2), (2, 1)], [(1, 0), (2, 3)]
        near = move(own, [(0, 1), (1, 0), (2, 3), (3, 2)])
        across = move(own, middle)
        far = move(near, middle)
        handed = move(across, outwards)
        last = move(far, outwards)
        within = (a == 1) | (a == 2)
        lines = [
            (own, a),
            (near, a ^ 1),
            (across + handed, jnp.where(within, a ^ 3, a ^ 2)),
            (far + last, jnp.where(within, a ^ 2, a ^ 3)),
        ]
        awaited, ends = [far, handed], [last]
    else:
        lines = [(own, a)] + [
            (move(own, [(x, partner(x, t, outer)) for x in range(outer)]), partner(a, -t, outer))
            for t in range(1, outer)
        ]
        awaited, ends = [block for block, _ in lines[1:]], []
    pieces, owners = [], []
    for block, line in lines:
        pieces.append(block)
        owners.append(line * inner + b)
        for t in range(1, inner):
            pieces.append(swap_along(block, t))
            owners.append(line * inner + partner(b, -t, inner))
    ends += [piece for piece in pieces[: 3 * inner] if all(piece is not block for block, _ in lines)]
    return pieces, jnp.stack(owners).astype(jnp.int32), awaited, ends


def edge_kernel(col_count, depth, owners, *refs):
    pieces, (first, last, lists, sems, list_sems) = refs[:-5], refs[-5:]
    rows = pieces[0].shape[0] - LISTS
    held = rows // (2 * W)
    total = col_count * held

    def each(act):
        for i, piece in enumerate(pieces):
            for g in range(depth):
                for out, block, sem in ((first, g, 0), (last, total - depth + g, 1)):
                    source = piece.at[pl.ds(block % held * 2 * W, 2 * W)]
                    copy = pltpu.make_async_copy(source, out.at[g], sems.at[sem, g])

                    @pl.when(owners[i] == block // held)
                    def _():
                        act(copy)

            @pl.when(owners[i] >= 0)
            def _():
                act(pltpu.make_async_copy(
                    piece.at[pl.ds(rows, LISTS)], lists.at[owners[i]], list_sems.at[i]
                ))

    each(lambda copy: copy.start())
    each(lambda copy: copy.wait())


def edge_blocks(owners, pieces, col_count, depth):
    shape = jax.ShapeDtypeStruct((depth, 2 * W, W), pieces[0].dtype)
    return pl.pallas_call(
        functools.partial(edge_kernel, col_count, depth),
        out_shape=(shape, shape, jax.ShapeDtypeStruct((col_count, LISTS, W), pieces[0].dtype)),
        in_specs=[SMEM] + [HBM] * len(pieces),
        out_specs=(VMEM, VMEM, VMEM),
        scratch_shapes=[
            pltpu.SemaphoreType.DMA((2, depth)),
            pltpu.SemaphoreType.DMA((len(pieces),)),
        ],
        name="edge_blocks",
    )(owners, *pieces)


def rows_of(j, count=1):
    return pl.ds(j * W if isinstance(j, int) else pl.multiple_of(j * W, W), count * W)


def band_builder(source, target):
    rows = lax.broadcasted_iota(jnp.int32, (W, W), 0)
    cols = lax.broadcasted_iota(jnp.int32, (W, W), 1)
    upper = jnp.where(rows <= cols, 1.0, 0.0).astype(jnp.bfloat16)

    def build(j, carry):
        coupling = source[j, W:]
        lower_band = coupling * upper
        target[j, :, 0:W] = lower_band
        target[j, :, W : 2 * W] = source[j, :W]
        target[j, :, 2 * W : 3 * W] = coupling - lower_band
        return carry

    return build


def inner_kernel(blocks, coef, owners, v_low, v_mid, v_high, *refs):
    (
        *pieces, out, edge_1, edge_2, edge_total,
        vext, hraw, hcat, cheb_1, cheb_2, total, kern, sems, psems, osems, esems,
    ) = refs
    held = (pieces[0].shape[0] - LISTS) // (2 * W)
    v_copies = [
        pltpu.make_async_copy(v_low.at[rows_of(DEG - 1)], vext.at[rows_of(0)], sems.at[0]),
        pltpu.make_async_copy(v_mid, vext.at[rows_of(1, blocks)], sems.at[1]),
        pltpu.make_async_copy(v_high.at[rows_of(0)], vext.at[rows_of(blocks + 1)], sems.at[2]),
    ]

    def each_piece(act):
        for i, piece in enumerate(pieces):
            for k in range(held):
                act(pltpu.make_async_copy(
                    piece.at[pl.ds(k * 2 * W, 2 * W)],
                    hraw.at[owners[i] * held + k],
                    psems.at[i, k],
                ))

    each_piece(lambda copy: copy.start())
    for copy in v_copies:
        copy.start()
    each_piece(lambda copy: copy.wait())
    build = band_builder(hraw, hcat)
    build(0, 0)
    for copy in v_copies:
        copy.wait()

    def band(source, j, row):
        return jnp.dot(hcat[j], source[rows_of(row, 3), :], preferred_element_type=jnp.float32)

    def edges(source, target, at):
        size = source.shape[0] // W
        return [
            pltpu.make_async_copy(
                source.at[rows_of(place, 2)], target.at[rows_of(2 * i, 2)], esems.at[at, i]
            )
            for i, place in enumerate((0, size - 2))
        ]

    def first(j, carry):
        value = band(vext, j, j)
        build(jnp.minimum(j + 1, blocks - 1), 0)
        cheb_1[rows_of(j), :] = value.astype(jnp.bfloat16)
        total[rows_of(j), :] = value
        return carry

    lax.fori_loop(0, blocks, first, 0, unroll=4)

    def second(j, carry):
        begin = vext[rows_of(j + 2), :].astype(jnp.float32)
        value = 2.0 * band(cheb_1, j + 1, j) - begin
        cheb_2[rows_of(j), :] = value.astype(jnp.bfloat16)
        total[rows_of(j + 1), :] = (
            coef[0] * begin + (coef[1] - coef[3]) * total[rows_of(j + 1), :] + coef[2] * value
        )
        return carry

    lax.fori_loop(0, blocks - 2, second, 0, unroll=4)
    outgoing = (
        edges(cheb_1, edge_1, 0) + edges(cheb_2, edge_2, 1) + edges(total, edge_total, 2)
    )
    for copy in outgoing:
        copy.start()

    def store(j):
        return pltpu.make_async_copy(kern.at[j], out.at[j], osems.at[j])

    def third(j, carry):
        for half in range(KB // W):
            i = j * (KB // W) + half
            value = total[rows_of(i), :] + (2.0 * coef[3]) * band(cheb_2, i, i - 2)
            kern[j, :, half * W : (half + 1) * W] = value.astype(jnp.bfloat16).T
        store(j).start()
        return carry

    last = blocks // (KB // W) - 1
    lax.fori_loop(1, last, third, 0, unroll=2)
    for j in range(1, last):
        store(j).wait()
    for copy in outgoing:
        copy.wait()


def chebyshev_inner(coefficients, owners, v_low, v_mid, v_high, pieces):
    blocks = v_mid.shape[0] // W
    cols = v_mid.shape[1]
    flops = 2 * W * 3 * W * cols * (3 * blocks - 6)
    result = (blocks * W // KB, cols, KB)
    held = (pieces[0].shape[0] - LISTS) // (2 * W)
    return pl.pallas_call(
        functools.partial(inner_kernel, blocks),
        out_shape=(
            jax.ShapeDtypeStruct(result, jnp.bfloat16),
            jax.ShapeDtypeStruct((4 * W, cols), jnp.bfloat16),
            jax.ShapeDtypeStruct((4 * W, cols), jnp.bfloat16),
            jax.ShapeDtypeStruct((4 * W, cols), jnp.float32),
        ),
        in_specs=[SMEM] * 2 + [HBM] * (3 + len(pieces)),
        out_specs=(HBM,) * 4,
        scratch_shapes=[
            pltpu.VMEM(((blocks + 2) * W, cols), jnp.bfloat16),
            pltpu.VMEM((blocks, 2 * W, W), jnp.bfloat16),
            pltpu.VMEM((blocks, W, 3 * W), jnp.bfloat16),
            pltpu.VMEM((blocks * W, cols), jnp.bfloat16),
            pltpu.VMEM(((blocks - 2) * W, cols), jnp.bfloat16),
            pltpu.VMEM((blocks * W, cols), jnp.float32),
            pltpu.VMEM(result, jnp.bfloat16),
            pltpu.SemaphoreType.DMA((3,)),
            pltpu.SemaphoreType.DMA((len(pieces), held)),
            pltpu.SemaphoreType.DMA((result[0],)),
            pltpu.SemaphoreType.DMA((3, 2)),
        ],
        compiler_params=pltpu.CompilerParams(vmem_limit_bytes=62 * MIB),
        cost_estimate=pl.CostEstimate(flops=flops, bytes_accessed=16 * MIB, transcendentals=0),
        name="chebyshev_inner",
    )(coefficients, owners, v_low, v_mid, v_high, *pieces)


def outer_kernel(
    blocks, coef, kernel_in, v_low, v_mid, v_high, h_low, h_first, h_last, h_high,
    edge_1, edge_2, edge_total, out,
    v, hraw, hcat, cheb_1, cheb_2, total, kern, sems, osems,
):
    last = kern.shape[0] - 1
    end = out.shape[0] - 1
    stages = [
        [
            (h_low, hraw.at[pl.ds(0, 2)]),
            (v_low, v.at[0, rows_of(0, 3)]),
            (v_mid.at[rows_of(0)], v.at[0, rows_of(3)]),
            (h_high, hraw.at[pl.ds(6, 2)]),
            (v_mid.at[rows_of(blocks - 1)], v.at[1, rows_of(0)]),
            (v_high, v.at[1, rows_of(1, 3)]),
        ],
        [
            (h_first, hraw.at[pl.ds(2, 2)]),
            (h_last, hraw.at[pl.ds(4, 2)]),
            (edge_1.at[rows_of(0, 2)], cheb_1.at[0, rows_of(2, 2)]),
            (edge_1.at[rows_of(2, 2)], cheb_1.at[1, rows_of(0, 2)]),
        ],
        [
            (edge_2.at[rows_of(0, 2)], cheb_2.at[0, rows_of(2, 2)]),
            (edge_2.at[rows_of(2, 2)], cheb_2.at[1, rows_of(0, 2)]),
            (edge_total.at[rows_of(0, 2)], total.at[0]),
            (edge_total.at[rows_of(2, 2)], total.at[1]),
        ],
    ]
    at = 0
    for i, stage in enumerate(stages):
        stages[i] = [
            pltpu.make_async_copy(source, target, sems.at[at + n])
            for n, (source, target) in enumerate(stage)
        ]
        at += len(stage)
        for copy in stages[i]:
            copy.start()
    build = band_builder(hraw, hcat)

    def arrived(i):
        for copy in stages[i]:
            copy.wait()

    def band(side, j, source, row):
        return jnp.dot(
            hcat[4 * side + j], source[side, rows_of(row, 3), :], preferred_element_type=jnp.float32
        )

    arrived(0)
    for j in (0, 1, 6, 7):
        build(j, 0)
    for side, places in ((0, (0, 1)), (1, (2, 3))):
        for j in places:
            value = band(side, j, v, j - 2 * side)
            cheb_1[side, rows_of(j), :] = value.astype(jnp.bfloat16)
    arrived(1)
    for j in (2, 3, 4, 5):
        build(j, 0)
    arrived(2)
    for side, places in ((0, ((1, 0), (2, 1))), (1, ((2, 3), (1, 2)))):
        for j, place in places:
            begin = v[side, rows_of(place + 2 - 4 * side), :].astype(jnp.float32)
            value = 2.0 * band(side, j, cheb_1, j - 1) - begin
            cheb_2[side, rows_of(place), :] = value.astype(jnp.bfloat16)
            if (j, place) == places[1]:
                within = rows_of(side)
                total[side, within, :] = (
                    coef[0] * begin + (coef[1] - coef[3]) * total[side, within, :] + coef[2] * value
                )
    for side in range(2):
        for half in range(2):
            j = 2 + half if side == 0 else half
            value = total[side, rows_of(half), :] + (2.0 * coef[3]) * band(side, j, cheb_2, half)
            kern[side, :, half * W : (half + 1) * W] = value.astype(jnp.bfloat16).T
    stores = [
        pltpu.make_async_copy(kern.at[0], out.at[0], osems.at[0]),
        pltpu.make_async_copy(kern.at[last], out.at[end], osems.at[1]),
    ]
    for store in stores:
        store.start()
    for store in stores:
        store.wait()


def chebyshev_outer(coefficients, inner, v_low, v_mid, v_high, h_low, h_first, h_last, h_high):
    kernel_t, edge_1, edge_2, edge_total = inner
    blocks = v_mid.shape[0] // W
    cols = v_mid.shape[1]
    return pl.pallas_call(
        functools.partial(outer_kernel, blocks),
        out_shape=jax.ShapeDtypeStruct(kernel_t.shape, kernel_t.dtype),
        in_specs=[SMEM] + [HBM] * 11,
        out_specs=HBM,
        input_output_aliases={1: 0},
        scratch_shapes=[
            pltpu.VMEM((2, 4 * W, cols), jnp.bfloat16),
            pltpu.VMEM((8, 2 * W, W), jnp.bfloat16),
            pltpu.VMEM((8, W, 3 * W), jnp.bfloat16),
            pltpu.VMEM((2, 4 * W, cols), jnp.bfloat16),
            pltpu.VMEM((2, 4 * W, cols), jnp.bfloat16),
            pltpu.VMEM((2, 2 * W, cols), jnp.float32),
            pltpu.VMEM((2, cols, KB), jnp.bfloat16),
            pltpu.SemaphoreType.DMA((14,)),
            pltpu.SemaphoreType.DMA((2,)),
        ],
        compiler_params=pltpu.CompilerParams(vmem_limit_bytes=62 * MIB),
        name="chebyshev_outer",
    )(
        coefficients, kernel_t, v_low, v_mid, v_high, h_low, h_first, h_last, h_high,
        edge_1, edge_2, edge_total,
    )


def entry_loads(order, parts, pair, sems):
    size = parts[0].shape[0]

    def load(p):
        return pltpu.make_async_copy(parts[0].at[0], pair.at[p], sems.at[p])

    def start(p, carry):
        n = order[p]
        for t, part in enumerate(parts):
            @pl.when((n >= t * size) & (n < (t + 1) * size))
            def _():
                pltpu.make_async_copy(part.at[n - t * size], pair.at[p], sems.at[p]).start()

        return carry

    return load, start


def by_twos(first, last, load, body):
    def step(i, carry):
        p = first + 2 * i
        q = jnp.minimum(p + 1, last - 1)
        load(p).wait()

        @pl.when(q > p)
        def _():
            load(q).wait()

        body(i, p, q)
        return carry

    lax.fori_loop(0, (last - first + 1) // 2, step, 0)


def sent_rows(slots, tiles):
    return slots + tiles + -(slots + tiles) % 8


def project_kernel(blocks, plan, order, kernel_t, core, *refs):
    *parts, out, kern, pair, rows, ksems, bsems = refs
    slots = pair.shape[0]
    load, start = entry_loads(order, parts, pair, bsems)

    def fetch(b):
        return pltpu.make_async_copy(kernel_t.at[b], kern.at[b], ksems.at[b])

    def begin(b, carry):
        first, last = plan[slots + b], plan[slots + b + 1]

        @pl.when(first < last)
        def _():
            fetch(b).start()

        return lax.fori_loop(first, last, start, carry)

    lax.fori_loop(0, blocks, begin, 0)
    rows[...] = jnp.zeros_like(rows)
    rows[slots : slots + core.shape[0]] = core[...]

    def step(b, carry):
        first, last = plan[slots + b], plan[slots + b + 1]

        @pl.when(first < last)
        def _():
            fetch(b).wait()

        def body(i, p, q):
            both = jnp.concatenate([pair[p, 0], pair[q, 0]], axis=1)
            projected = jnp.dot(kern[b], both, preferred_element_type=jnp.float32)
            other = jnp.concatenate([pair[p, 1], pair[q, 1]], axis=1).astype(jnp.float32)
            value = jnp.sum(projected * other, axis=0, keepdims=True) * (1.0 / KB)
            rows[pl.ds(order[p], 1), :] = value[:, :P_SIZE]
            rows[pl.ds(order[q], 1), :] = value[:, P_SIZE:]

        by_twos(first, last, load, body)
        return carry

    lax.fori_loop(0, blocks, step, 0)
    for c in range(out.shape[0]):
        out[c] = rows[...]


def project(plan, order, kernel_t, core, parts, col_count):
    slots = col_count * CAP
    entry = parts[0].shape[1:]
    sent = sent_rows(slots, core.shape[0])
    blocks = kernel_t.shape[0]
    return pl.pallas_call(
        functools.partial(project_kernel, blocks),
        out_shape=jax.ShapeDtypeStruct((col_count, sent, P_SIZE), jnp.float32),
        in_specs=[SMEM, SMEM, HBM, VMEM] + [HBM] * len(parts),
        out_specs=VMEM,
        scratch_shapes=[
            pltpu.VMEM(kernel_t.shape, jnp.bfloat16),
            pltpu.VMEM((slots,) + entry, jnp.bfloat16),
            pltpu.VMEM((sent, P_SIZE), jnp.float32),
            pltpu.SemaphoreType.DMA((blocks,)),
            pltpu.SemaphoreType.DMA((slots,)),
        ],
        compiler_params=pltpu.CompilerParams(vmem_limit_bytes=62 * MIB),
        name="project",
    )(plan, order, kernel_t, core, *parts)


def update_kernel(
    blocks, tiles, plan, order, tile_of, contributions, collect, *refs
):
    *parts, density_out, update_out, pair, density, potential, acc, stage, sems, osems = refs
    slots = pair.shape[0]
    live = plan[slots + blocks]
    me = plan[slots + blocks + 1]
    load, start = entry_loads(order, parts, pair, sems)
    lax.fori_loop(0, live, start, 0)
    density[...] = jnp.dot(
        collect[...],
        contributions[...],
        preferred_element_type=jnp.float32,
        precision=lax.Precision.HIGHEST,
    )
    for t in range(tiles):
        density_out[pl.ds(t, 1), :] = density[pl.ds(me * tiles + t, 1), :]
    positive = jnp.maximum(density[...], 0.1)
    root = jnp.exp(jnp.log(positive) * (1.0 / 3.0))
    root = root - (root - positive / (root * root)) * (1.0 / 3.0)
    potential[...] = -exchange_factor * root
    scale = 1.0 / math.sqrt(P_SIZE)

    def store(b):
        rows = pl.ds(pl.multiple_of(b * KB, KB), KB)
        return pltpu.make_async_copy(stage.at[b], update_out.at[rows], osems.at[b])

    def step(b, carry):
        first, last = plan[slots + b], plan[slots + b + 1]

        @pl.when(first == last)
        def _():
            stage[b] = jnp.zeros(stage.shape[1:], jnp.bfloat16)

        def body(i, p, q):
            weight_p = potential[pl.ds(tile_of[order[p]], 1), :]
            weight_q = potential[pl.ds(tile_of[order[q]], 1), :] * (q - p).astype(jnp.float32)
            weighted = jnp.concatenate(
                [
                    (pair[p, 1].astype(jnp.float32) * weight_p).astype(jnp.bfloat16),
                    (pair[q, 1].astype(jnp.float32) * weight_q).astype(jnp.bfloat16),
                ],
                axis=1,
            )
            block = lax.dot_general(
                jnp.concatenate([pair[p, 0], pair[q, 0]], axis=1),
                weighted,
                (((1,), (1,)), ((), ())),
                preferred_element_type=jnp.float32,
            )

            @pl.when(last - first <= 2)
            def _():
                stage[b] = (block * scale).astype(jnp.bfloat16)

            @pl.when((last - first > 2) & (i == 0))
            def _():
                acc[...] = block

            @pl.when(i > 0)
            def _():
                acc[...] += block

        by_twos(first, last, load, body)

        @pl.when(last - first > 2)
        def _():
            stage[b] = (acc[...] * scale).astype(jnp.bfloat16)

        store(b).start()
        return carry

    lax.fori_loop(0, blocks, step, 0)
    for b in range(blocks):
        store(b).wait()


def update(plan, order, tile_of, contributions, collect, parts, tiles, blocks, cols):
    slots = len(parts) * parts[0].shape[0]
    entry = parts[0].shape[1:]
    all_tiles = (collect.shape[0], P_SIZE)
    return pl.pallas_call(
        functools.partial(update_kernel, blocks, tiles),
        out_shape=(
            jax.ShapeDtypeStruct((tiles, P_SIZE), jnp.float32),
            jax.ShapeDtypeStruct((blocks * KB, cols), jnp.bfloat16),
        ),
        in_specs=[SMEM] * 3 + [VMEM] * 2 + [HBM] * len(parts),
        out_specs=(VMEM, HBM),
        scratch_shapes=[
            pltpu.VMEM((slots,) + entry, jnp.bfloat16),
            pltpu.VMEM(all_tiles, jnp.float32),
            pltpu.VMEM(all_tiles, jnp.float32),
            pltpu.VMEM((KB, cols), jnp.float32),
            pltpu.VMEM((blocks, KB, cols), jnp.bfloat16),
            pltpu.SemaphoreType.DMA((slots,)),
            pltpu.SemaphoreType.DMA((blocks,)),
        ],
        compiler_params=pltpu.CompilerParams(vmem_limit_bytes=62 * MIB),
        name="update",
    )(plan, order, tile_of, contributions, collect, *parts)


def shift(block, axis, step):
    count = lax.axis_size(axis)
    pairs = [(i, i + step) for i in range(count) if 0 <= i + step < count]
    return lax.ppermute(block, axis, pairs)


def make_plan(lists, me, entries, tiles, col_count, blocks):
    slots = col_count * CAP
    sent = sent_rows(slots, tiles)
    lists = lists[:, : 2 * entries + tiles].astype(jnp.int32)
    peers, named, counts = lists[:, :entries], lists[:, entries : 2 * entries], lists[:, 2 * entries :]
    index = jnp.arange(entries, dtype=jnp.int32)
    home = jnp.arange(col_count, dtype=jnp.int32)[:, None]
    earlier = (peers[:, :, None] == peers[:, None, :]) & (index[None, :] < index[:, None])
    rank = jnp.sum(earlier.astype(jnp.int32), axis=2)
    live = (index % SLOTS)[None, :] < jnp.repeat(counts, SLOTS, axis=1)
    row = jnp.where(live, peers * sent + chunk_of(home, peers, col_count) * CAP + rank, -1).reshape(col_count, tiles, SLOTS)
    core = (home * sent + slots + jnp.arange(tiles, dtype=jnp.int32))[:, :, None]
    row = jnp.concatenate([row, core], axis=2).reshape(col_count * tiles, SLOTS + 1, 1)
    picked = row == jnp.arange(col_count * sent, dtype=jnp.int32)
    collect = jnp.sum(picked.astype(jnp.float32), axis=1)
    hit = (
        (peers == me)[:, None, :]
        & (rank[:, None, :] == jnp.arange(CAP, dtype=jnp.int32)[None, :, None])
        & live[:, None, :]
    )
    at_me = chunk_of(home, me, col_count).reshape(1, col_count) == home
    tile = home * tiles + index[None, :] // SLOTS

    def of_slots(values):
        by_home = jnp.sum(jnp.where(hit, values[:, None, :], 0), axis=2)
        return jnp.sum(jnp.where(at_me[:, :, None], by_home[None], 0), axis=1).reshape(slots)

    wanted = of_slots(named + 1) - 1
    tile_of = of_slots(tile)
    key = jnp.where(wanted < 0, blocks, wanted)
    place = jnp.arange(slots, dtype=jnp.int32)
    before = (key[None, :] < key[:, None]) | (
        (key[None, :] == key[:, None]) & (place[None, :] < place[:, None])
    )
    spot = jnp.sum(before.astype(jnp.int32), axis=1)
    order = jnp.sum(jnp.where(spot[None, :] == place[:, None], place[None, :], 0), axis=1)
    starts = jnp.sum(
        (key[None, :] < jnp.arange(blocks + 1, dtype=jnp.int32)[:, None]).astype(jnp.int32), axis=1
    )
    plan = jnp.concatenate([wanted, starts, me[None]]).astype(jnp.int32)
    return collect, plan, order.astype(jnp.int32), tile_of.astype(jnp.int32)


def shards(
    start_columns,
    hamiltonian,
    band_pattern,
    coefficients,
    tile_peer,
    tile_block,
    tile_count,
    basis_values,
    core_density,
):
    col_count = lax.axis_size("col")
    entries = tile_peer.shape[0]
    tiles = core_density.shape[0]
    cols = start_columns.shape[1]
    blocks = start_columns.shape[0] // KB
    peers = tile_peer[:, 0]
    me = lax.axis_index("col").astype(jnp.int32)

    own = own_piece(peers, tile_block, tile_count, band_pattern, hamiltonian.reshape(-1, W))
    pieces, owners, awaited, handed = gather_pieces(own)
    v_low = shift(start_columns[-DEG * W :], "row", 1)
    v_high = shift(start_columns[: DEG * W], "row", -1)
    parts = exchange(me[None], peers, basis_values, own, pieces[min(1, len(pieces) - 1)],
        awaited + [v_low, v_high], handed)

    first, last, lists = edge_blocks(owners, pieces, col_count, DEG - 1)
    h_low = shift(last, "row", 1)
    h_high = shift(first, "row", -1)
    inner = chebyshev_inner(coefficients, owners, v_low, start_columns, v_high, pieces)
    kernel_t = chebyshev_outer(
        coefficients, inner, v_low, start_columns, v_high, h_low, first, last, h_high
    )
    collect, plan, order, tile_of = make_plan(lists[:, 0], me, entries, tiles, col_count, blocks)
    partial = project(plan, order, kernel_t, core_density, parts, col_count)
    contributions = lax.all_to_all(partial, "col", split_axis=0, concat_axis=0, tiled=True)
    contributions = contributions.reshape(-1, P_SIZE)
    return update(
        plan, order, tile_of, contributions, collect, parts, tiles, blocks, cols
    )


def solution(mesh):
    return jax.shard_map(
        shards,
        mesh=mesh,
        in_specs=(
            P("row", "col"),
            P(("row", "col"), None, None, None),
            P(("row", "col")),
            P(),
            P(("row", "col"), None),
            P(("row", "col")),
            P(("row", "col")),
            P(("row", "col"), None, None, None),
            P(("row", "col"), None),
        ),
        out_specs=(P(("row", "col"), None), P("row", "col")),
        check_vma=False,
    )
```

```python
import functools
import math

import jax
import jax.numpy as jnp
from jax import lax
from jax.experimental import pallas as pl
from jax.experimental.pallas import tpu as pltpu
from jax.sharding import PartitionSpec as P

W = 256
KB = 512
DEG = 3
SLOTS = 4
CAP = 2
P_SIZE = 128
MIB = 1 << 20
LISTS = 16

exchange_factor = (3.0 / math.pi) ** (1.0 / 3.0)
HBM = pl.BlockSpec(memory_space=pltpu.HBM)
ANY = pl.BlockSpec(memory_space=pl.ANY)
SMEM = pl.BlockSpec(memory_space=pltpu.SMEM)
VMEM = pl.BlockSpec(memory_space=pltpu.VMEM)


def partner(me, j, count):
    if count & (count - 1) == 0:
        return me ^ abs(j)
    return (me + j) % count


def piece_kernel(peers, named, counts, pattern, ham, piece, blocks, sems):
    rows = ham.shape[0]
    load = pltpu.make_async_copy(ham, blocks.at[pl.ds(0, rows)], sems.at[0])
    load.start()
    lane = lax.broadcasted_iota(jnp.int32, (LISTS, W), 1)
    lists = jnp.zeros((LISTS, W), jnp.int32)
    at = 0
    for ref in (peers, named, counts):
        for i in range(ref.shape[0]):
            lists = jnp.where(lane == at, ref[i], lists)
            at += 1
    blocks[rows:] = lists.astype(jnp.float32).astype(jnp.bfloat16)
    load.wait()
    for i in range(rows // (2 * W)):
        coupling = slice((2 * i + 1) * W, (2 * i + 2) * W)
        blocks[coupling] = blocks[coupling] * pattern[i].astype(jnp.bfloat16)
    store = pltpu.make_async_copy(blocks, piece, sems.at[1])
    store.start()
    store.wait()


def own_piece(peers, named, counts, pattern, ham):
    piece = (ham.shape[0] + LISTS, W)
    return pl.pallas_call(
        piece_kernel,
        out_shape=jax.ShapeDtypeStruct(piece, ham.dtype),
        in_specs=[SMEM] * 4 + [HBM],
        out_specs=HBM,
        scratch_shapes=[pltpu.VMEM(piece, ham.dtype), pltpu.SemaphoreType.DMA((2,))],
        compiler_params=pltpu.CompilerParams(vmem_limit_bytes=62 * MIB),
        name="own_piece",
    )(peers, named, counts, pattern, ham)


def lines_of(count):
    inner = max(count // 4, 1) if count & (count - 1) == 0 else 1
    return count // inner, inner


def swap_along(block, t):
    count = lax.axis_size("col")
    _, inner = lines_of(count)
    pairs = [(c, c - c % inner + partner(c % inner, t, inner)) for c in range(count)]
    return lax.ppermute(block, "col", pairs)


def chunk_of(home, owner, count):
    outer, inner = lines_of(count)
    return partner(home % inner, owner % inner, inner) * outer + home // inner


def pack_kernel(entries, col_count, wanted, me, peers, basis, first, *refs):
    outer, inner = lines_of(col_count)
    sent, (held, owner, count, in_sems, out_sems) = refs[: len(wanted)], refs[len(wanted) :]
    for c in range(col_count):
        count[c] = 0
        for k in range(CAP):
            owner[c * CAP + k] = 0
    for e in range(entries):
        p = peers[e]
        k = count[p]
        count[p] = k + 1
        owner[p * CAP + k] = e
    place = lax.rem(me[0], inner)
    tasks = []
    for target, group in zip(sent, wanted):
        for line in range(outer):
            for i, (t, k) in enumerate(group):
                n = len(tasks)
                e = owner[(line * inner + partner(place, t, inner)) * CAP + k]
                fetch = pltpu.make_async_copy(basis.at[e], held.at[n], in_sems.at[n])
                store = pltpu.make_async_copy(held.at[n], target.at[line, i], out_sems.at[n])
                tasks.append((fetch, store))
    for fetch, _ in tasks:
        fetch.start()
    for fetch, store in tasks:
        fetch.wait()
        store.start()
    for _, store in tasks:
        store.wait()


def pack(me, peers, basis, first, col_count, wanted):
    outer, _ = lines_of(col_count)
    entries = basis.shape[0]
    number = sum(len(group) for group in wanted) * outer
    return list(pl.pallas_call(
        functools.partial(pack_kernel, entries, col_count, wanted),
        out_shape=tuple(
            jax.ShapeDtypeStruct((outer, len(group)) + basis.shape[1:], basis.dtype)
            for group in wanted
        ),
        in_specs=[SMEM, SMEM, HBM, HBM],
        out_specs=(HBM,) * len(wanted),
        scratch_shapes=[
            pltpu.VMEM((number,) + basis.shape[1:], basis.dtype),
            pltpu.SMEM((col_count * CAP,), jnp.int32),
            pltpu.SMEM((col_count,), jnp.int32),
            pltpu.SemaphoreType.DMA((number,)),
            pltpu.SemaphoreType.DMA((number,)),
        ],
        compiler_params=pltpu.CompilerParams(vmem_limit_bytes=62 * MIB),
        name="pack",
    )(me, peers, basis, first))


def after(block, *others):
    return pl.pallas_call(
        lambda *refs: None,
        out_shape=jax.ShapeDtypeStruct(block.shape, block.dtype),
        in_specs=[HBM] + [ANY] * len(others),
        out_specs=HBM,
        input_output_aliases={0: 0},
        compiler_params=pltpu.CompilerParams(vmem_limit_bytes=62 * MIB),
        name="after",
    )(block, *others)


def stack_kernel(number, *refs):
    sources, (out, held, in_sems, out_sems) = refs[:number], refs[-4:]
    loads = [pltpu.make_async_copy(sources[i], held.at[i], in_sems.at[i]) for i in range(number)]
    stores = [
        pltpu.make_async_copy(held.at[i], out.at[:, pl.ds(i, 1)], out_sems.at[i])
        for i in range(number)
    ]
    for load in loads:
        load.start()
    for load, store in zip(loads, stores):
        load.wait()
        store.start()
    for store in stores:
        store.wait()


def stack(blocks, *others):
    block = blocks[0]
    shape = (block.shape[0], len(blocks)) + block.shape[2:]
    return pl.pallas_call(
        functools.partial(stack_kernel, len(blocks)),
        out_shape=jax.ShapeDtypeStruct(shape, block.dtype),
        in_specs=[ANY] * (len(blocks) + len(others)),
        out_specs=HBM,
        scratch_shapes=[
            pltpu.VMEM((len(blocks),) + block.shape, block.dtype),
            pltpu.SemaphoreType.DMA((len(blocks),)),
            pltpu.SemaphoreType.DMA((len(blocks),)),
        ],
        compiler_params=pltpu.CompilerParams(vmem_limit_bytes=62 * MIB),
        name="stack",
    )(*blocks, *others)


def exchange(me, peers, basis, own, early, awaited, handed):
    count = lax.axis_size("col")
    outer, inner = lines_of(count)
    groups = [[line * inner + place for line in range(outer)] for place in range(inner)]

    def between_lines(blocks, *others):
        block = stack(blocks, *others) if len(blocks) > 1 else after(blocks[0], *others)
        return lax.all_to_all(
            block, "col", split_axis=0, concat_axis=0,
            axis_index_groups=groups, tiled=True,
        )

    here = [(0, k) for k in range(CAP)]
    ahead = [[(t, 0)] for t in range(1, inner)]
    rest = [[(t, k)] for k in range(1, CAP) for t in range(1, inner)]
    sent = pack(me, peers, basis, own, count, ahead) if ahead else []
    to_lines, *later = pack(me, peers, basis, early, count, [here] + rest)
    swapped = {
        group[0]: swap_along(block, group[0][0]) for block, group in zip(sent + later, ahead + rest)
    }
    parts = [between_lines([to_lines], *awaited, *[swapped[group[0]] for group in ahead])]
    for t in range(1, inner):
        parts.append(between_lines([swapped[t, k] for k in range(CAP)], parts[-1], *handed))
    return [part.reshape((outer * CAP,) + part.shape[2:]) for part in parts]


def gather_pieces(own):
    count = lax.axis_size("col")
    outer, inner = lines_of(count)
    me = lax.axis_index("col").astype(jnp.int32)
    a, b = me // inner, me % inner

    def move(block, ways):
        pairs = [(x * inner + y, z * inner + y) for x, z in ways for y in range(inner)]
        return lax.ppermute(block, "col", pairs)

    if outer == 4:
        middle, outwards = [(1, 2), (2, 1)], [(1, 0), (2, 3)]
        near = move(own, [(0, 1), (1, 0), (2, 3), (3, 2)])
        across = move(own, middle)
        far = move(near, middle)
        handed = move(across, outwards)
        last = move(far, outwards)
        within = (a == 1) | (a == 2)
        lines = [
            (own, a),
            (near, a ^ 1),
            (across + handed, jnp.where(within, a ^ 3, a ^ 2)),
            (far + last, jnp.where(within, a ^ 2, a ^ 3)),
        ]
        awaited, ends = [far, handed], [last]
    else:
        lines = [(own, a)] + [
            (move(own, [(x, partner(x, t, outer)) for x in range(outer)]), partner(a, -t, outer))
            for t in range(1, outer)
        ]
        awaited, ends = [block for block, _ in lines[1:]], []
    pieces, owners = [], []
    for block, line in lines:
        pieces.append(block)
        owners.append(line * inner + b)
        for t in range(1, inner):
            pieces.append(swap_along(block, t))
            owners.append(line * inner + partner(b, -t, inner))
    ends += [piece for piece in pieces[: 3 * inner] if all(piece is not block for block, _ in lines)]
    return pieces, jnp.stack(owners).astype(jnp.int32), awaited, ends


def edge_kernel(col_count, depth, owners, *refs):
    pieces, (first, last, lists, sems, list_sems) = refs[:-5], refs[-5:]
    rows = pieces[0].shape[0] - LISTS
    held = rows // (2 * W)
    total = col_count * held

    def each(act):
        for i, piece in enumerate(pieces):
            for g in range(depth):
                for out, block, sem in ((first, g, 0), (last, total - depth + g, 1)):
                    source = piece.at[pl.ds(block % held * 2 * W, 2 * W)]
                    copy = pltpu.make_async_copy(source, out.at[g], sems.at[sem, g])

                    @pl.when(owners[i] == block // held)
                    def _():
                        act(copy)

            @pl.when(owners[i] >= 0)
            def _():
                act(pltpu.make_async_copy(
                    piece.at[pl.ds(rows, LISTS)], lists.at[owners[i]], list_sems.at[i]
                ))

    each(lambda copy: copy.start())
    each(lambda copy: copy.wait())


def edge_blocks(owners, pieces, col_count, depth):
    shape = jax.ShapeDtypeStruct((depth, 2 * W, W), pieces[0].dtype)
    return pl.pallas_call(
        functools.partial(edge_kernel, col_count, depth),
        out_shape=(shape, shape, jax.ShapeDtypeStruct((col_count, LISTS, W), pieces[0].dtype)),
        in_specs=[SMEM] + [HBM] * len(pieces),
        out_specs=(VMEM, VMEM, VMEM),
        scratch_shapes=[
            pltpu.SemaphoreType.DMA((2, depth)),
            pltpu.SemaphoreType.DMA((len(pieces),)),
        ],
        name="edge_blocks",
    )(owners, *pieces)


def rows_of(j, count=1):
    return pl.ds(j * W if isinstance(j, int) else pl.multiple_of(j * W, W), count * W)


def band_builder(source, target):
    rows = lax.broadcasted_iota(jnp.int32, (W, W), 0)
    cols = lax.broadcasted_iota(jnp.int32, (W, W), 1)
    upper = jnp.where(rows <= cols, 1.0, 0.0).astype(jnp.bfloat16)

    def build(j, carry):
        coupling = source[j, W:]
        lower_band = coupling * upper
        target[j, :, 0:W] = lower_band
        target[j, :, W : 2 * W] = source[j, :W]
        target[j, :, 2 * W : 3 * W] = coupling - lower_band
        return carry

    return build


def inner_kernel(blocks, coef, owners, v_low, v_mid, v_high, *refs):
    (
        *pieces, out, edge_1, edge_2, edge_total,
        vext, hraw, hcat, cheb_1, cheb_2, total, kern, sems, psems, osems, esems,
    ) = refs
    held = (pieces[0].shape[0] - LISTS) // (2 * W)
    v_copies = [
        pltpu.make_async_copy(v_low.at[rows_of(DEG - 1)], vext.at[rows_of(0)], sems.at[0]),
        pltpu.make_async_copy(v_mid, vext.at[rows_of(1, blocks)], sems.at[1]),
        pltpu.make_async_copy(v_high.at[rows_of(0)], vext.at[rows_of(blocks + 1)], sems.at[2]),
    ]

    def each_piece(act):
        for i, piece in enumerate(pieces):
            for k in range(held):
                act(pltpu.make_async_copy(
                    piece.at[pl.ds(k * 2 * W, 2 * W)],
                    hraw.at[owners[i] * held + k],
                    psems.at[i, k],
                ))

    each_piece(lambda copy: copy.start())
    for copy in v_copies:
        copy.start()
    each_piece(lambda copy: copy.wait())
    build = band_builder(hraw, hcat)
    build(0, 0)
    for copy in v_copies:
        copy.wait()

    def band(source, j, row):
        return jnp.dot(hcat[j], source[rows_of(row, 3), :], preferred_element_type=jnp.float32)

    def edges(source, target, at):
        size = source.shape[0] // W
        return [
            pltpu.make_async_copy(
                source.at[rows_of(place, 2)], target.at[rows_of(2 * i, 2)], esems.at[at, i]
            )
            for i, place in enumerate((0, size - 2))
        ]

    def first(j, carry):
        value = band(vext, j, j)
        build(jnp.minimum(j + 1, blocks - 1), 0)
        cheb_1[rows_of(j), :] = value.astype(jnp.bfloat16)
        total[rows_of(j), :] = value
        return carry

    lax.fori_loop(0, blocks, first, 0, unroll=4)

    def second(j, carry):
        begin = vext[rows_of(j + 2), :].astype(jnp.float32)
        value = 2.0 * band(cheb_1, j + 1, j) - begin
        cheb_2[rows_of(j), :] = value.astype(jnp.bfloat16)
        total[rows_of(j + 1), :] = (
            coef[0] * begin + (coef[1] - coef[3]) * total[rows_of(j + 1), :] + coef[2] * value
        )
        return carry

    lax.fori_loop(0, blocks - 2, second, 0, unroll=4)
    outgoing = (
        edges(cheb_1, edge_1, 0) + edges(cheb_2, edge_2, 1) + edges(total, edge_total, 2)
    )
    for copy in outgoing:
        copy.start()

    def store(j):
        return pltpu.make_async_copy(kern.at[j], out.at[j], osems.at[j])

    def third(j, carry):
        for half in range(KB // W):
            i = j * (KB // W) + half
            value = total[rows_of(i), :] + (2.0 * coef[3]) * band(cheb_2, i, i - 2)
            kern[j, :, half * W : (half + 1) * W] = value.astype(jnp.bfloat16).T
        store(j).start()
        return carry

    last = blocks // (KB // W) - 1
    lax.fori_loop(1, last, third, 0, unroll=2)
    for j in range(1, last):
        store(j).wait()
    for copy in outgoing:
        copy.wait()


def chebyshev_inner(coefficients, owners, v_low, v_mid, v_high, pieces):
    blocks = v_mid.shape[0] // W
    cols = v_mid.shape[1]
    flops = 2 * W * 3 * W * cols * (3 * blocks - 6)
    result = (blocks * W // KB, cols, KB)
    held = (pieces[0].shape[0] - LISTS) // (2 * W)
    return pl.pallas_call(
        functools.partial(inner_kernel, blocks),
        out_shape=(
            jax.ShapeDtypeStruct(result, jnp.bfloat16),
            jax.ShapeDtypeStruct((4 * W, cols), jnp.bfloat16),
            jax.ShapeDtypeStruct((4 * W, cols), jnp.bfloat16),
            jax.ShapeDtypeStruct((4 * W, cols), jnp.float32),
        ),
        in_specs=[SMEM] * 2 + [HBM] * (3 + len(pieces)),
        out_specs=(HBM,) * 4,
        scratch_shapes=[
            pltpu.VMEM(((blocks + 2) * W, cols), jnp.bfloat16),
            pltpu.VMEM((blocks, 2 * W, W), jnp.bfloat16),
            pltpu.VMEM((blocks, W, 3 * W), jnp.bfloat16),
            pltpu.VMEM((blocks * W, cols), jnp.bfloat16),
            pltpu.VMEM(((blocks - 2) * W, cols), jnp.bfloat16),
            pltpu.VMEM((blocks * W, cols), jnp.float32),
            pltpu.VMEM(result, jnp.bfloat16),
            pltpu.SemaphoreType.DMA((3,)),
            pltpu.SemaphoreType.DMA((len(pieces), held)),
            pltpu.SemaphoreType.DMA((result[0],)),
            pltpu.SemaphoreType.DMA((3, 2)),
        ],
        compiler_params=pltpu.CompilerParams(vmem_limit_bytes=62 * MIB),
        cost_estimate=pl.CostEstimate(flops=flops, bytes_accessed=16 * MIB, transcendentals=0),
        name="chebyshev_inner",
    )(coefficients, owners, v_low, v_mid, v_high, *pieces)


def outer_kernel(
    blocks, coef, kernel_in, v_low, v_mid, v_high, h_low, h_first, h_last, h_high,
    edge_1, edge_2, edge_total, out,
    v, hraw, hcat, cheb_1, cheb_2, total, kern, sems, osems,
):
    last = kern.shape[0] - 1
    end = out.shape[0] - 1
    stages = [
        [
            (h_low, hraw.at[pl.ds(0, 2)]),
            (v_low, v.at[0, rows_of(0, 3)]),
            (v_mid.at[rows_of(0)], v.at[0, rows_of(3)]),
            (h_high, hraw.at[pl.ds(6, 2)]),
            (v_mid.at[rows_of(blocks - 1)], v.at[1, rows_of(0)]),
            (v_high, v.at[1, rows_of(1, 3)]),
        ],
        [
            (h_first, hraw.at[pl.ds(2, 2)]),
            (h_last, hraw.at[pl.ds(4, 2)]),
            (edge_1.at[rows_of(0, 2)], cheb_1.at[0, rows_of(2, 2)]),
            (edge_1.at[rows_of(2, 2)], cheb_1.at[1, rows_of(0, 2)]),
        ],
        [
            (edge_2.at[rows_of(0, 2)], cheb_2.at[0, rows_of(2, 2)]),
            (edge_2.at[rows_of(2, 2)], cheb_2.at[1, rows_of(0, 2)]),
            (edge_total.at[rows_of(0, 2)], total.at[0]),
            (edge_total.at[rows_of(2, 2)], total.at[1]),
        ],
    ]
    at = 0
    for i, stage in enumerate(stages):
        stages[i] = [
            pltpu.make_async_copy(source, target, sems.at[at + n])
            for n, (source, target) in enumerate(stage)
        ]
        at += len(stage)
        for copy in stages[i]:
            copy.start()
    build = band_builder(hraw, hcat)

    def arrived(i):
        for copy in stages[i]:
            copy.wait()

    def band(side, j, source, row):
        return jnp.dot(
            hcat[4 * side + j], source[side, rows_of(row, 3), :], preferred_element_type=jnp.float32
        )

    arrived(0)
    for j in (0, 1, 6, 7):
        build(j, 0)
    for side, places in ((0, (0, 1)), (1, (2, 3))):
        for j in places:
            value = band(side, j, v, j - 2 * side)
            cheb_1[side, rows_of(j), :] = value.astype(jnp.bfloat16)
    arrived(1)
    for j in (2, 3, 4, 5):
        build(j, 0)
    arrived(2)
    for side, places in ((0, ((1, 0), (2, 1))), (1, ((2, 3), (1, 2)))):
        for j, place in places:
            begin = v[side, rows_of(place + 2 - 4 * side), :].astype(jnp.float32)
            value = 2.0 * band(side, j, cheb_1, j - 1) - begin
            cheb_2[side, rows_of(place), :] = value.astype(jnp.bfloat16)
            if (j, place) == places[1]:
                within = rows_of(side)
                total[side, within, :] = (
                    coef[0] * begin + (coef[1] - coef[3]) * total[side, within, :] + coef[2] * value
                )
    for side in range(2):
        for half in range(2):
            j = 2 + half if side == 0 else half
            value = total[side, rows_of(half), :] + (2.0 * coef[3]) * band(side, j, cheb_2, half)
            kern[side, :, half * W : (half + 1) * W] = value.astype(jnp.bfloat16).T
    stores = [
        pltpu.make_async_copy(kern.at[0], out.at[0], osems.at[0]),
        pltpu.make_async_copy(kern.at[last], out.at[end], osems.at[1]),
    ]
    for store in stores:
        store.start()
    for store in stores:
        store.wait()


def chebyshev_outer(coefficients, inner, v_low, v_mid, v_high, h_low, h_first, h_last, h_high):
    kernel_t, edge_1, edge_2, edge_total = inner
    blocks = v_mid.shape[0] // W
    cols = v_mid.shape[1]
    return pl.pallas_call(
        functools.partial(outer_kernel, blocks),
        out_shape=jax.ShapeDtypeStruct(kernel_t.shape, kernel_t.dtype),
        in_specs=[SMEM] + [HBM] * 11,
        out_specs=HBM,
        input_output_aliases={1: 0},
        scratch_shapes=[
            pltpu.VMEM((2, 4 * W, cols), jnp.bfloat16),
            pltpu.VMEM((8, 2 * W, W), jnp.bfloat16),
            pltpu.VMEM((8, W, 3 * W), jnp.bfloat16),
            pltpu.VMEM((2, 4 * W, cols), jnp.bfloat16),
            pltpu.VMEM((2, 4 * W, cols), jnp.bfloat16),
            pltpu.VMEM((2, 2 * W, cols), jnp.float32),
            pltpu.VMEM((2, cols, KB), jnp.bfloat16),
            pltpu.SemaphoreType.DMA((14,)),
            pltpu.SemaphoreType.DMA((2,)),
        ],
        compiler_params=pltpu.CompilerParams(vmem_limit_bytes=62 * MIB),
        name="chebyshev_outer",
    )(
        coefficients, kernel_t, v_low, v_mid, v_high, h_low, h_first, h_last, h_high,
        edge_1, edge_2, edge_total,
    )


def entry_loads(order, parts, pair, sems):
    size = parts[0].shape[0]

    def load(p):
        return pltpu.make_async_copy(parts[0].at[0], pair.at[p], sems.at[p])

    def start(p, carry):
        n = order[p]
        for t, part in enumerate(parts):
            @pl.when((n >= t * size) & (n < (t + 1) * size))
            def _():
                pltpu.make_async_copy(part.at[n - t * size], pair.at[p], sems.at[p]).start()

        return carry

    return load, start


def by_twos(first, last, load, body):
    def step(i, carry):
        p = first + 2 * i
        q = jnp.minimum(p + 1, last - 1)
        load(p).wait()

        @pl.when(q > p)
        def _():
            load(q).wait()

        body(i, p, q)
        return carry

    lax.fori_loop(0, (last - first + 1) // 2, step, 0)


def sent_rows(slots, tiles):
    return slots + tiles + -(slots + tiles) % 8


def project_kernel(blocks, plan, order, kernel_t, core, *refs):
    *parts, out, kern, pair, rows, ksems, bsems = refs
    slots = pair.shape[0]
    load, start = entry_loads(order, parts, pair, bsems)

    def fetch(b):
        return pltpu.make_async_copy(kernel_t.at[b], kern.at[b], ksems.at[b])

    def begin(b, carry):
        first, last = plan[slots + b], plan[slots + b + 1]

        @pl.when(first < last)
        def _():
            fetch(b).start()

        return lax.fori_loop(first, last, start, carry)

    lax.fori_loop(0, blocks, begin, 0)
    rows[...] = jnp.zeros_like(rows)
    rows[slots : slots + core.shape[0]] = core[...]

    def step(b, carry):
        first, last = plan[slots + b], plan[slots + b + 1]

        @pl.when(first < last)
        def _():
            fetch(b).wait()

        def body(i, p, q):
            both = jnp.concatenate([pair[p, 0], pair[q, 0]], axis=1)
            projected = jnp.dot(kern[b], both, preferred_element_type=jnp.float32)
            other = jnp.concatenate([pair[p, 1], pair[q, 1]], axis=1).astype(jnp.float32)
            value = jnp.sum(projected * other, axis=0, keepdims=True) * (1.0 / KB)
            rows[pl.ds(order[p], 1), :] = value[:, :P_SIZE]
            rows[pl.ds(order[q], 1), :] = value[:, P_SIZE:]

        by_twos(first, last, load, body)
        return carry

    lax.fori_loop(0, blocks, step, 0)
    for c in range(out.shape[0]):
        out[c] = rows[...]


def project(plan, order, kernel_t, core, parts, col_count):
    slots = col_count * CAP
    entry = parts[0].shape[1:]
    sent = sent_rows(slots, core.shape[0])
    blocks = kernel_t.shape[0]
    return pl.pallas_call(
        functools.partial(project_kernel, blocks),
        out_shape=jax.ShapeDtypeStruct((col_count, sent, P_SIZE), jnp.float32),
        in_specs=[SMEM, SMEM, HBM, VMEM] + [HBM] * len(parts),
        out_specs=VMEM,
        scratch_shapes=[
            pltpu.VMEM(kernel_t.shape, jnp.bfloat16),
            pltpu.VMEM((slots,) + entry, jnp.bfloat16),
            pltpu.VMEM((sent, P_SIZE), jnp.float32),
            pltpu.SemaphoreType.DMA((blocks,)),
            pltpu.SemaphoreType.DMA((slots,)),
        ],
        compiler_params=pltpu.CompilerParams(vmem_limit_bytes=62 * MIB),
        name="project",
    )(plan, order, kernel_t, core, *parts)


def update_kernel(
    blocks, tiles, plan, order, tile_of, contributions, collect, *refs
):
    *parts, density_out, update_out, pair, density, potential, acc, stage, sems, osems = refs
    slots = pair.shape[0]
    live = plan[slots + blocks]
    me = plan[slots + blocks + 1]
    load, start = entry_loads(order, parts, pair, sems)
    lax.fori_loop(0, live, start, 0)
    density[...] = jnp.dot(
        collect[...],
        contributions[...],
        preferred_element_type=jnp.float32,
        precision=lax.Precision.HIGHEST,
    )
    for t in range(tiles):
        density_out[pl.ds(t, 1), :] = density[pl.ds(me * tiles + t, 1), :]
    positive = jnp.maximum(density[...], 0.1)
    root = jnp.exp(jnp.log(positive) * (1.0 / 3.0))
    root = root - (root - positive / (root * root)) * (1.0 / 3.0)
    potential[...] = -exchange_factor * root
    scale = 1.0 / math.sqrt(P_SIZE)

    def store(b):
        rows = pl.ds(pl.multiple_of(b * KB, KB), KB)
        return pltpu.make_async_copy(stage.at[b], update_out.at[rows], osems.at[b])

    def step(b, carry):
        first, last = plan[slots + b], plan[slots + b + 1]

        @pl.when(first == last)
        def _():
            stage[b] = jnp.zeros(stage.shape[1:], jnp.bfloat16)

        def body(i, p, q):
            weight_p = potential[pl.ds(tile_of[order[p]], 1), :]
            weight_q = potential[pl.ds(tile_of[order[q]], 1), :] * (q - p).astype(jnp.float32)
            weighted = jnp.concatenate(
                [
                    (pair[p, 1].astype(jnp.float32) * weight_p).astype(jnp.bfloat16),
                    (pair[q, 1].astype(jnp.float32) * weight_q).astype(jnp.bfloat16),
                ],
                axis=1,
            )
            block = lax.dot_general(
                jnp.concatenate([pair[p, 0], pair[q, 0]], axis=1),
                weighted,
                (((1,), (1,)), ((), ())),
                preferred_element_type=jnp.float32,
            )

            @pl.when(last - first <= 2)
            def _():
                stage[b] = (block * scale).astype(jnp.bfloat16)

            @pl.when((last - first > 2) & (i == 0))
            def _():
                acc[...] = block

            @pl.when(i > 0)
            def _():
                acc[...] += block

        by_twos(first, last, load, body)

        @pl.when(last - first > 2)
        def _():
            stage[b] = (acc[...] * scale).astype(jnp.bfloat16)

        store(b).start()
        return carry

    lax.fori_loop(0, blocks, step, 0)
    for b in range(blocks):
        store(b).wait()


def update(plan, order, tile_of, contributions, collect, parts, tiles, blocks, cols):
    slots = len(parts) * parts[0].shape[0]
    entry = parts[0].shape[1:]
    all_tiles = (collect.shape[0], P_SIZE)
    return pl.pallas_call(
        functools.partial(update_kernel, blocks, tiles),
        out_shape=(
            jax.ShapeDtypeStruct((tiles, P_SIZE), jnp.float32),
            jax.ShapeDtypeStruct((blocks * KB, cols), jnp.bfloat16),
        ),
        in_specs=[SMEM] * 3 + [VMEM] * 2 + [HBM] * len(parts),
        out_specs=(VMEM, HBM),
        scratch_shapes=[
            pltpu.VMEM((slots,) + entry, jnp.bfloat16),
            pltpu.VMEM(all_tiles, jnp.float32),
            pltpu.VMEM(all_tiles, jnp.float32),
            pltpu.VMEM((KB, cols), jnp.float32),
            pltpu.VMEM((blocks, KB, cols), jnp.bfloat16),
            pltpu.SemaphoreType.DMA((slots,)),
            pltpu.SemaphoreType.DMA((blocks,)),
        ],
        compiler_params=pltpu.CompilerParams(vmem_limit_bytes=62 * MIB),
        name="update",
    )(plan, order, tile_of, contributions, collect, *parts)


def shift(block, axis, step):
    count = lax.axis_size(axis)
    pairs = [(i, i + step) for i in range(count) if 0 <= i + step < count]
    return lax.ppermute(block, axis, pairs)


def make_plan(lists, me, entries, tiles, col_count, blocks):
    slots = col_count * CAP
    sent = sent_rows(slots, tiles)
    lists = lists[:, : 2 * entries + tiles].astype(jnp.int32)
    peers, named, counts = lists[:, :entries], lists[:, entries : 2 * entries], lists[:, 2 * entries :]
    index = jnp.arange(entries, dtype=jnp.int32)
    home = jnp.arange(col_count, dtype=jnp.int32)[:, None]
    earlier = (peers[:, :, None] == peers[:, None, :]) & (index[None, :] < index[:, None])
    rank = jnp.sum(earlier.astype(jnp.int32), axis=2)
    live = (index % SLOTS)[None, :] < jnp.repeat(counts, SLOTS, axis=1)
    row = jnp.where(live, peers * sent + chunk_of(home, peers, col_count) * CAP + rank, -1).reshape(col_count, tiles, SLOTS)
    core = (home * sent + slots + jnp.arange(tiles, dtype=jnp.int32))[:, :, None]
    row = jnp.concatenate([row, core], axis=2).reshape(col_count * tiles, SLOTS + 1, 1)
    picked = row == jnp.arange(col_count * sent, dtype=jnp.int32)
    collect = jnp.sum(picked.astype(jnp.float32), axis=1)
    hit = (
        (peers == me)[:, None, :]
        & (rank[:, None, :] == jnp.arange(CAP, dtype=jnp.int32)[None, :, None])
        & live[:, None, :]
    )
    at_me = chunk_of(home, me, col_count).reshape(1, col_count) == home
    tile = home * tiles + index[None, :] // SLOTS

    def of_slots(values):
        by_home = jnp.sum(jnp.where(hit, values[:, None, :], 0), axis=2)
        return jnp.sum(jnp.where(at_me[:, :, None], by_home[None], 0), axis=1).reshape(slots)

    wanted = of_slots(named + 1) - 1
    tile_of = of_slots(tile)
    key = jnp.where(wanted < 0, blocks, wanted)
    place = jnp.arange(slots, dtype=jnp.int32)
    before = (key[None, :] < key[:, None]) | (
        (key[None, :] == key[:, None]) & (place[None, :] < place[:, None])
    )
    spot = jnp.sum(before.astype(jnp.int32), axis=1)
    order = jnp.sum(jnp.where(spot[None, :] == place[:, None], place[None, :], 0), axis=1)
    starts = jnp.sum(
        (key[None, :] < jnp.arange(blocks + 1, dtype=jnp.int32)[:, None]).astype(jnp.int32), axis=1
    )
    plan = jnp.concatenate([wanted, starts, me[None]]).astype(jnp.int32)
    return collect, plan, order.astype(jnp.int32), tile_of.astype(jnp.int32)


def shards(
    start_columns,
    hamiltonian,
    band_pattern,
    coefficients,
    tile_peer,
    tile_block,
    tile_count,
    basis_values,
    core_density,
):
    col_count = lax.axis_size("col")
    entries = tile_peer.shape[0]
    tiles = core_density.shape[0]
    cols = start_columns.shape[1]
    blocks = start_columns.shape[0] // KB
    peers = tile_peer[:, 0]
    me = lax.axis_index("col").astype(jnp.int32)

    own = own_piece(peers, tile_block, tile_count, band_pattern, hamiltonian.reshape(-1, W))
    pieces, owners, awaited, handed = gather_pieces(own)
    v_low = shift(start_columns[-DEG * W :], "row", 1)
    v_high = shift(start_columns[: DEG * W], "row", -1)
    parts = exchange(me[None], peers, basis_values, own, pieces[min(1, len(pieces) - 1)],
        awaited + [v_low, v_high], handed)

    first, last, lists = edge_blocks(owners, pieces, col_count, DEG - 1)
    h_low = shift(last, "row", 1)
    h_high = shift(first, "row", -1)
    inner = chebyshev_inner(coefficients, owners, v_low, start_columns, v_high, pieces)
    kernel_t = chebyshev_outer(
        coefficients, inner, v_low, start_columns, v_high, h_low, first, last, h_high
    )
    collect, plan, order, tile_of = make_plan(lists[:, 0], me, entries, tiles, col_count, blocks)
    partial = project(plan, order, kernel_t, core_density, parts, col_count)
    contributions = lax.all_to_all(partial, "col", split_axis=0, concat_axis=0, tiled=True)
    contributions = contributions.reshape(-1, P_SIZE)
    return update(
        plan, order, tile_of, contributions, collect, parts, tiles, blocks, cols
    )


def solution(mesh):
    return jax.shard_map(
        shards,
        mesh=mesh,
        in_specs=(
            P("row", "col"),
            P(("row", "col"), None, None, None),
            P(("row", "col")),
            P(),
            P(("row", "col"), None),
            P(("row", "col")),
            P(("row", "col")),
            P(("row", "col"), None, None, None),
            P(("row", "col"), None),
        ),
        out_specs=(P(("row", "col"), None), P("row", "col")),
        check_vma=False,
    )
```

```python
import functools
import math

import jax
import jax.numpy as jnp
from jax import lax
from jax.experimental import pallas as pl
from jax.experimental.pallas import tpu as pltpu
from jax.sharding import PartitionSpec as P

W = 256
KB = 512
DEG = 3
SLOTS = 4
CAP = 2
P_SIZE = 128
MIB = 1 << 20
LISTS = 16

exchange_factor = (3.0 / math.pi) ** (1.0 / 3.0)
HBM = pl.BlockSpec(memory_space=pltpu.HBM)
ANY = pl.BlockSpec(memory_space=pl.ANY)
SMEM = pl.BlockSpec(memory_space=pltpu.SMEM)
VMEM = pl.BlockSpec(memory_space=pltpu.VMEM)


def partner(me, j, count):
    if count & (count - 1) == 0:
        return me ^ abs(j)
    return (me + j) % count


def piece_kernel(peers, named, counts, pattern, ham, piece, blocks, sems):
    rows = ham.shape[0]
    load = pltpu.make_async_copy(ham, blocks.at[pl.ds(0, rows)], sems.at[0])
    load.start()
    lane = lax.broadcasted_iota(jnp.int32, (LISTS, W), 1)
    lists = jnp.zeros((LISTS, W), jnp.int32)
    at = 0
    for ref in (peers, named, counts):
        for i in range(ref.shape[0]):
            lists = jnp.where(lane == at, ref[i], lists)
            at += 1
    blocks[rows:] = lists.astype(jnp.float32).astype(jnp.bfloat16)
    load.wait()
    for i in range(rows // (2 * W)):
        coupling = slice((2 * i + 1) * W, (2 * i + 2) * W)
        blocks[coupling] = blocks[coupling] * pattern[i].astype(jnp.bfloat16)
    store = pltpu.make_async_copy(blocks, piece, sems.at[1])
    store.start()
    store.wait()


def own_piece(peers, named, counts, pattern, ham):
    piece = (ham.shape[0] + LISTS, W)
    return pl.pallas_call(
        piece_kernel,
        out_shape=jax.ShapeDtypeStruct(piece, ham.dtype),
        in_specs=[SMEM] * 4 + [HBM],
        out_specs=HBM,
        scratch_shapes=[pltpu.VMEM(piece, ham.dtype), pltpu.SemaphoreType.DMA((2,))],
        compiler_params=pltpu.CompilerParams(vmem_limit_bytes=62 * MIB),
        name="own_piece",
    )(peers, named, counts, pattern, ham)


def lines_of(count):
    inner = max(count // 4, 1) if count & (count - 1) == 0 else 1
    return count // inner, inner


def swap_along(block, t):
    count = lax.axis_size("col")
    _, inner = lines_of(count)
    pairs = [(c, c - c % inner + partner(c % inner, t, inner)) for c in range(count)]
    return lax.ppermute(block, "col", pairs)


def chunk_of(home, owner, count):
    outer, inner = lines_of(count)
    return partner(home % inner, owner % inner, inner) * outer + home // inner


def pack_kernel(entries, col_count, wanted, me, peers, basis, first, *refs):
    outer, inner = lines_of(col_count)
    sent, (held, owner, count, in_sems, out_sems) = refs[: len(wanted)], refs[len(wanted) :]
    for c in range(col_count):
        count[c] = 0
        for k in range(CAP):
            owner[c * CAP + k] = 0
    for e in range(entries):
        p = peers[e]
        k = count[p]
        count[p] = k + 1
        owner[p * CAP + k] = e
    place = lax.rem(me[0], inner)
    tasks = []
    for target, group in zip(sent, wanted):
        for line in range(outer):
            for i, (t, k) in enumerate(group):
                n = len(tasks)
                e = owner[(line * inner + partner(place, t, inner)) * CAP + k]
                fetch = pltpu.make_async_copy(basis.at[e], held.at[n], in_sems.at[n])
                store = pltpu.make_async_copy(held.at[n], target.at[line, i], out_sems.at[n])
                tasks.append((fetch, store))
    for fetch, _ in tasks:
        fetch.start()
    for fetch, store in tasks:
        fetch.wait()
        store.start()
    for _, store in tasks:
        store.wait()


def pack(me, peers, basis, first, col_count, wanted):
    outer, _ = lines_of(col_count)
    entries = basis.shape[0]
    number = sum(len(group) for group in wanted) * outer
    return list(pl.pallas_call(
        functools.partial(pack_kernel, entries, col_count, wanted),
        out_shape=tuple(
            jax.ShapeDtypeStruct((outer, len(group)) + basis.shape[1:], basis.dtype)
            for group in wanted
        ),
        in_specs=[SMEM, SMEM, HBM, HBM],
        out_specs=(HBM,) * len(wanted),
        scratch_shapes=[
            pltpu.VMEM((number,) + basis.shape[1:], basis.dtype),
            pltpu.SMEM((col_count * CAP,), jnp.int32),
            pltpu.SMEM((col_count,), jnp.int32),
            pltpu.SemaphoreType.DMA((number,)),
            pltpu.SemaphoreType.DMA((number,)),
        ],
        compiler_params=pltpu.CompilerParams(vmem_limit_bytes=62 * MIB),
        name="pack",
    )(me, peers, basis, first))


def after(block, *others):
    return pl.pallas_call(
        lambda *refs: None,
        out_shape=jax.ShapeDtypeStruct(block.shape, block.dtype),
        in_specs=[HBM] + [ANY] * len(others),
        out_specs=HBM,
        input_output_aliases={0: 0},
        compiler_params=pltpu.CompilerParams(vmem_limit_bytes=62 * MIB),
        name="after",
    )(block, *others)


def exchange(me, peers, basis, own, early, awaited, handed):
    count = lax.axis_size("col")
    outer, inner = lines_of(count)
    groups = [[line * inner + place for line in range(outer)] for place in range(inner)]

    def between_lines(blocks, *others):
        block = jnp.concatenate(blocks, axis=1)
        return lax.all_to_all(
            after(block, *others), "col", split_axis=0, concat_axis=0,
            axis_index_groups=groups, tiled=True,
        )

    here = [(0, k) for k in range(CAP)]
    ahead = [[(t, 0)] for t in range(1, inner)]
    rest = [[(t, k)] for k in range(1, CAP) for t in range(1, inner)]
    sent = pack(me, peers, basis, own, count, ahead) if ahead else []
    to_lines, *later = pack(me, peers, basis, early, count, [here] + rest)
    swapped = {
        group[0]: swap_along(block, group[0][0]) for block, group in zip(sent + later, ahead + rest)
    }
    parts = [between_lines([to_lines], *awaited, *[swapped[group[0]] for group in ahead])]
    for t in range(1, inner):
        parts.append(between_lines([swapped[t, k] for k in range(CAP)], parts[-1], *handed))
    return [part.reshape((outer * CAP,) + part.shape[2:]) for part in parts]


def gather_pieces(own):
    count = lax.axis_size("col")
    outer, inner = lines_of(count)
    me = lax.axis_index("col").astype(jnp.int32)
    a, b = me // inner, me % inner

    def move(block, ways):
        pairs = [(x * inner + y, z * inner + y) for x, z in ways for y in range(inner)]
        return lax.ppermute(block, "col", pairs)

    if outer == 4:
        middle, outwards = [(1, 2), (2, 1)], [(1, 0), (2, 3)]
        near = move(own, [(0, 1), (1, 0), (2, 3), (3, 2)])
        across = move(own, middle)
        far = move(near, middle)
        handed = move(across, outwards)
        last = move(far, outwards)
        within = (a == 1) | (a == 2)
        lines = [
            (own, a),
            (near, a ^ 1),
            (across + handed, jnp.where(within, a ^ 3, a ^ 2)),
            (far + last, jnp.where(within, a ^ 2, a ^ 3)),
        ]
        awaited, ends = [far, handed], [last]
    else:
        lines = [(own, a)] + [
            (move(own, [(x, partner(x, t, outer)) for x in range(outer)]), partner(a, -t, outer))
            for t in range(1, outer)
        ]
        awaited, ends = [block for block, _ in lines[1:]], []
    pieces, owners = [], []
    for block, line in lines:
        pieces.append(block)
        owners.append(line * inner + b)
        for t in range(1, inner):
            pieces.append(swap_along(block, t))
            owners.append(line * inner + partner(b, -t, inner))
    ends += [piece for piece in pieces[: 3 * inner] if all(piece is not block for block, _ in lines)]
    return pieces, jnp.stack(owners).astype(jnp.int32), awaited, ends


def edge_kernel(col_count, depth, owners, *refs):
    pieces, (first, last, lists, sems, list_sems) = refs[:-5], refs[-5:]
    rows = pieces[0].shape[0] - LISTS
    held = rows // (2 * W)
    total = col_count * held

    def each(act):
        for i, piece in enumerate(pieces):
            for g in range(depth):
                for out, block, sem in ((first, g, 0), (last, total - depth + g, 1)):
                    source = piece.at[pl.ds(block % held * 2 * W, 2 * W)]
                    copy = pltpu.make_async_copy(source, out.at[g], sems.at[sem, g])

                    @pl.when(owners[i] == block // held)
                    def _():
                        act(copy)

            @pl.when(owners[i] >= 0)
            def _():
                act(pltpu.make_async_copy(
                    piece.at[pl.ds(rows, LISTS)], lists.at[owners[i]], list_sems.at[i]
                ))

    each(lambda copy: copy.start())
    each(lambda copy: copy.wait())


def edge_blocks(owners, pieces, col_count, depth):
    shape = jax.ShapeDtypeStruct((depth, 2 * W, W), pieces[0].dtype)
    return pl.pallas_call(
        functools.partial(edge_kernel, col_count, depth),
        out_shape=(shape, shape, jax.ShapeDtypeStruct((col_count, LISTS, W), pieces[0].dtype)),
        in_specs=[SMEM] + [HBM] * len(pieces),
        out_specs=(VMEM, VMEM, VMEM),
        scratch_shapes=[
            pltpu.SemaphoreType.DMA((2, depth)),
            pltpu.SemaphoreType.DMA((len(pieces),)),
        ],
        name="edge_blocks",
    )(owners, *pieces)


def rows_of(j, count=1):
    return pl.ds(j * W if isinstance(j, int) else pl.multiple_of(j * W, W), count * W)


def band_builder(source, target):
    rows = lax.broadcasted_iota(jnp.int32, (W, W), 0)
    cols = lax.broadcasted_iota(jnp.int32, (W, W), 1)
    upper = jnp.where(rows <= cols, 1.0, 0.0).astype(jnp.bfloat16)

    def build(j, carry):
        coupling = source[j, W:]
        lower_band = coupling * upper
        target[j, :, 0:W] = lower_band
        target[j, :, W : 2 * W] = source[j, :W]
        target[j, :, 2 * W : 3 * W] = coupling - lower_band
        return carry

    return build


def inner_kernel(blocks, coef, owners, v_low, v_mid, v_high, *refs):
    (
        *pieces, out, edge_1, edge_2, edge_total,
        vext, hraw, hcat, cheb_1, cheb_2, total, kern, sems, psems, osems, esems,
    ) = refs
    held = (pieces[0].shape[0] - LISTS) // (2 * W)
    v_copies = [
        pltpu.make_async_copy(v_low.at[rows_of(DEG - 1)], vext.at[rows_of(0)], sems.at[0]),
        pltpu.make_async_copy(v_mid, vext.at[rows_of(1, blocks)], sems.at[1]),
        pltpu.make_async_copy(v_high.at[rows_of(0)], vext.at[rows_of(blocks + 1)], sems.at[2]),
    ]

    def each_piece(act):
        for i, piece in enumerate(pieces):
            for k in range(held):
                act(pltpu.make_async_copy(
                    piece.at[pl.ds(k * 2 * W, 2 * W)],
                    hraw.at[owners[i] * held + k],
                    psems.at[i, k],
                ))

    each_piece(lambda copy: copy.start())
    for copy in v_copies:
        copy.start()
    each_piece(lambda copy: copy.wait())
    build = band_builder(hraw, hcat)
    build(0, 0)
    for copy in v_copies:
        copy.wait()

    def band(source, j, row):
        return jnp.dot(hcat[j], source[rows_of(row, 3), :], preferred_element_type=jnp.float32)

    def edges(source, target, at):
        size = source.shape[0] // W
        return [
            pltpu.make_async_copy(
                source.at[rows_of(place, 2)], target.at[rows_of(2 * i, 2)], esems.at[at, i]
            )
            for i, place in enumerate((0, size - 2))
        ]

    def first(j, carry):
        value = band(vext, j, j)
        build(jnp.minimum(j + 1, blocks - 1), 0)
        cheb_1[rows_of(j), :] = value.astype(jnp.bfloat16)
        total[rows_of(j), :] = value
        return carry

    lax.fori_loop(0, blocks, first, 0, unroll=4)

    def second(j, carry):
        begin = vext[rows_of(j + 2), :].astype(jnp.float32)
        value = 2.0 * band(cheb_1, j + 1, j) - begin
        cheb_2[rows_of(j), :] = value.astype(jnp.bfloat16)
        total[rows_of(j + 1), :] = (
            coef[0] * begin + (coef[1] - coef[3]) * total[rows_of(j + 1), :] + coef[2] * value
        )
        return carry

    lax.fori_loop(0, blocks - 2, second, 0, unroll=4)
    outgoing = (
        edges(cheb_1, edge_1, 0) + edges(cheb_2, edge_2, 1) + edges(total, edge_total, 2)
    )
    for copy in outgoing:
        copy.start()

    def store(j):
        return pltpu.make_async_copy(kern.at[j], out.at[j], osems.at[j])

    def third(j, carry):
        for half in range(KB // W):
            i = j * (KB // W) + half
            value = total[rows_of(i), :] + (2.0 * coef[3]) * band(cheb_2, i, i - 2)
            kern[j, :, half * W : (half + 1) * W] = value.astype(jnp.bfloat16).T
        store(j).start()
        return carry

    last = blocks // (KB // W) - 1
    lax.fori_loop(1, last, third, 0, unroll=2)
    for j in range(1, last):
        store(j).wait()
    for copy in outgoing:
        copy.wait()


def chebyshev_inner(coefficients, owners, v_low, v_mid, v_high, pieces):
    blocks = v_mid.shape[0] // W
    cols = v_mid.shape[1]
    flops = 2 * W * 3 * W * cols * (3 * blocks - 6)
    result = (blocks * W // KB, cols, KB)
    held = (pieces[0].shape[0] - LISTS) // (2 * W)
    return pl.pallas_call(
        functools.partial(inner_kernel, blocks),
        out_shape=(
            jax.ShapeDtypeStruct(result, jnp.bfloat16),
            jax.ShapeDtypeStruct((4 * W, cols), jnp.bfloat16),
            jax.ShapeDtypeStruct((4 * W, cols), jnp.bfloat16),
            jax.ShapeDtypeStruct((4 * W, cols), jnp.float32),
        ),
        in_specs=[SMEM] * 2 + [HBM] * (3 + len(pieces)),
        out_specs=(HBM,) * 4,
        scratch_shapes=[
            pltpu.VMEM(((blocks + 2) * W, cols), jnp.bfloat16),
            pltpu.VMEM((blocks, 2 * W, W), jnp.bfloat16),
            pltpu.VMEM((blocks, W, 3 * W), jnp.bfloat16),
            pltpu.VMEM((blocks * W, cols), jnp.bfloat16),
            pltpu.VMEM(((blocks - 2) * W, cols), jnp.bfloat16),
            pltpu.VMEM((blocks * W, cols), jnp.float32),
            pltpu.VMEM(result, jnp.bfloat16),
            pltpu.SemaphoreType.DMA((3,)),
            pltpu.SemaphoreType.DMA((len(pieces), held)),
            pltpu.SemaphoreType.DMA((result[0],)),
            pltpu.SemaphoreType.DMA((3, 2)),
        ],
        compiler_params=pltpu.CompilerParams(vmem_limit_bytes=62 * MIB),
        cost_estimate=pl.CostEstimate(flops=flops, bytes_accessed=16 * MIB, transcendentals=0),
        name="chebyshev_inner",
    )(coefficients, owners, v_low, v_mid, v_high, *pieces)


def outer_kernel(
    blocks, coef, kernel_in, v_low, v_mid, v_high, h_low, h_first, h_last, h_high,
    edge_1, edge_2, edge_total, out,
    v, hraw, hcat, cheb_1, cheb_2, total, kern, sems, osems,
):
    last = kern.shape[0] - 1
    end = out.shape[0] - 1
    stages = [
        [
            (h_low, hraw.at[pl.ds(0, 2)]),
            (v_low, v.at[0, rows_of(0, 3)]),
            (v_mid.at[rows_of(0)], v.at[0, rows_of(3)]),
            (h_high, hraw.at[pl.ds(6, 2)]),
            (v_mid.at[rows_of(blocks - 1)], v.at[1, rows_of(0)]),
            (v_high, v.at[1, rows_of(1, 3)]),
        ],
        [
            (h_first, hraw.at[pl.ds(2, 2)]),
            (h_last, hraw.at[pl.ds(4, 2)]),
            (edge_1.at[rows_of(0, 2)], cheb_1.at[0, rows_of(2, 2)]),
            (edge_1.at[rows_of(2, 2)], cheb_1.at[1, rows_of(0, 2)]),
        ],
        [
            (edge_2.at[rows_of(0, 2)], cheb_2.at[0, rows_of(2, 2)]),
            (edge_2.at[rows_of(2, 2)], cheb_2.at[1, rows_of(0, 2)]),
            (edge_total.at[rows_of(0, 2)], total.at[0]),
            (edge_total.at[rows_of(2, 2)], total.at[1]),
        ],
    ]
    at = 0
    for i, stage in enumerate(stages):
        stages[i] = [
            pltpu.make_async_copy(source, target, sems.at[at + n])
            for n, (source, target) in enumerate(stage)
        ]
        at += len(stage)
        for copy in stages[i]:
            copy.start()
    build = band_builder(hraw, hcat)

    def arrived(i):
        for copy in stages[i]:
            copy.wait()

    def band(side, j, source, row):
        return jnp.dot(
            hcat[4 * side + j], source[side, rows_of(row, 3), :], preferred_element_type=jnp.float32
        )

    arrived(0)
    for j in (0, 1, 6, 7):
        build(j, 0)
    for side, places in ((0, (0, 1)), (1, (2, 3))):
        for j in places:
            value = band(side, j, v, j - 2 * side)
            cheb_1[side, rows_of(j), :] = value.astype(jnp.bfloat16)
    arrived(1)
    for j in (2, 3, 4, 5):
        build(j, 0)
    arrived(2)
    for side, places in ((0, ((1, 0), (2, 1))), (1, ((2, 3), (1, 2)))):
        for j, place in places:
            begin = v[side, rows_of(place + 2 - 4 * side), :].astype(jnp.float32)
            value = 2.0 * band(side, j, cheb_1, j - 1) - begin
            cheb_2[side, rows_of(place), :] = value.astype(jnp.bfloat16)
            if (j, place) == places[1]:
                within = rows_of(side)
                total[side, within, :] = (
                    coef[0] * begin + (coef[1] - coef[3]) * total[side, within, :] + coef[2] * value
                )
    for side in range(2):
        for half in range(2):
            j = 2 + half if side == 0 else half
            value = total[side, rows_of(half), :] + (2.0 * coef[3]) * band(side, j, cheb_2, half)
            kern[side, :, half * W : (half + 1) * W] = value.astype(jnp.bfloat16).T
    stores = [
        pltpu.make_async_copy(kern.at[0], out.at[0], osems.at[0]),
        pltpu.make_async_copy(kern.at[last], out.at[end], osems.at[1]),
    ]
    for store in stores:
        store.start()
    for store in stores:
        store.wait()


def chebyshev_outer(coefficients, inner, v_low, v_mid, v_high, h_low, h_first, h_last, h_high):
    kernel_t, edge_1, edge_2, edge_total = inner
    blocks = v_mid.shape[0] // W
    cols = v_mid.shape[1]
    return pl.pallas_call(
        functools.partial(outer_kernel, blocks),
        out_shape=jax.ShapeDtypeStruct(kernel_t.shape, kernel_t.dtype),
        in_specs=[SMEM] + [HBM] * 11,
        out_specs=HBM,
        input_output_aliases={1: 0},
        scratch_shapes=[
            pltpu.VMEM((2, 4 * W, cols), jnp.bfloat16),
            pltpu.VMEM((8, 2 * W, W), jnp.bfloat16),
            pltpu.VMEM((8, W, 3 * W), jnp.bfloat16),
            pltpu.VMEM((2, 4 * W, cols), jnp.bfloat16),
            pltpu.VMEM((2, 4 * W, cols), jnp.bfloat16),
            pltpu.VMEM((2, 2 * W, cols), jnp.float32),
            pltpu.VMEM((2, cols, KB), jnp.bfloat16),
            pltpu.SemaphoreType.DMA((14,)),
            pltpu.SemaphoreType.DMA((2,)),
        ],
        compiler_params=pltpu.CompilerParams(vmem_limit_bytes=62 * MIB),
        name="chebyshev_outer",
    )(
        coefficients, kernel_t, v_low, v_mid, v_high, h_low, h_first, h_last, h_high,
        edge_1, edge_2, edge_total,
    )


def entry_loads(order, parts, pair, sems):
    size = parts[0].shape[0]

    def load(p):
        return pltpu.make_async_copy(parts[0].at[0], pair.at[p], sems.at[p])

    def start(p, carry):
        n = order[p]
        for t, part in enumerate(parts):
            @pl.when((n >= t * size) & (n < (t + 1) * size))
            def _():
                pltpu.make_async_copy(part.at[n - t * size], pair.at[p], sems.at[p]).start()

        return carry

    return load, start


def by_twos(first, last, load, body):
    def step(i, carry):
        p = first + 2 * i
        q = jnp.minimum(p + 1, last - 1)
        load(p).wait()

        @pl.when(q > p)
        def _():
            load(q).wait()

        body(i, p, q)
        return carry

    lax.fori_loop(0, (last - first + 1) // 2, step, 0)


def sent_rows(slots, tiles):
    return slots + tiles + -(slots + tiles) % 8


def project_kernel(blocks, plan, order, kernel_t, core, *refs):
    *parts, out, kern, pair, rows, ksems, bsems = refs
    slots = pair.shape[0]
    load, start = entry_loads(order, parts, pair, bsems)

    def fetch(b):
        return pltpu.make_async_copy(kernel_t.at[b], kern.at[b], ksems.at[b])

    def begin(b, carry):
        first, last = plan[slots + b], plan[slots + b + 1]

        @pl.when(first < last)
        def _():
            fetch(b).start()

        return lax.fori_loop(first, last, start, carry)

    lax.fori_loop(0, blocks, begin, 0)
    rows[...] = jnp.zeros_like(rows)
    rows[slots : slots + core.shape[0]] = core[...]

    def step(b, carry):
        first, last = plan[slots + b], plan[slots + b + 1]

        @pl.when(first < last)
        def _():
            fetch(b).wait()

        def body(i, p, q):
            both = jnp.concatenate([pair[p, 0], pair[q, 0]], axis=1)
            projected = jnp.dot(kern[b], both, preferred_element_type=jnp.float32)
            other = jnp.concatenate([pair[p, 1], pair[q, 1]], axis=1).astype(jnp.float32)
            value = jnp.sum(projected * other, axis=0, keepdims=True) * (1.0 / KB)
            rows[pl.ds(order[p], 1), :] = value[:, :P_SIZE]
            rows[pl.ds(order[q], 1), :] = value[:, P_SIZE:]

        by_twos(first, last, load, body)
        return carry

    lax.fori_loop(0, blocks, step, 0)
    for c in range(out.shape[0]):
        out[c] = rows[...]


def project(plan, order, kernel_t, core, parts, col_count):
    slots = col_count * CAP
    entry = parts[0].shape[1:]
    sent = sent_rows(slots, core.shape[0])
    blocks = kernel_t.shape[0]
    return pl.pallas_call(
        functools.partial(project_kernel, blocks),
        out_shape=jax.ShapeDtypeStruct((col_count, sent, P_SIZE), jnp.float32),
        in_specs=[SMEM, SMEM, HBM, VMEM] + [HBM] * len(parts),
        out_specs=VMEM,
        scratch_shapes=[
            pltpu.VMEM(kernel_t.shape, jnp.bfloat16),
            pltpu.VMEM((slots,) + entry, jnp.bfloat16),
            pltpu.VMEM((sent, P_SIZE), jnp.float32),
            pltpu.SemaphoreType.DMA((blocks,)),
            pltpu.SemaphoreType.DMA((slots,)),
        ],
        compiler_params=pltpu.CompilerParams(vmem_limit_bytes=62 * MIB),
        name="project",
    )(plan, order, kernel_t, core, *parts)


def update_kernel(
    blocks, tiles, plan, order, tile_of, contributions, collect, *refs
):
    *parts, density_out, update_out, pair, density, potential, acc, stage, sems, osems = refs
    slots = pair.shape[0]
    live = plan[slots + blocks]
    me = plan[slots + blocks + 1]
    load, start = entry_loads(order, parts, pair, sems)
    lax.fori_loop(0, live, start, 0)
    density[...] = jnp.dot(
        collect[...],
        contributions[...],
        preferred_element_type=jnp.float32,
        precision=lax.Precision.HIGHEST,
    )
    for t in range(tiles):
        density_out[pl.ds(t, 1), :] = density[pl.ds(me * tiles + t, 1), :]
    positive = jnp.maximum(density[...], 0.1)
    root = jnp.exp(jnp.log(positive) * (1.0 / 3.0))
    root = root - (root - positive / (root * root)) * (1.0 / 3.0)
    potential[...] = -exchange_factor * root
    scale = 1.0 / math.sqrt(P_SIZE)

    def store(b):
        rows = pl.ds(pl.multiple_of(b * KB, KB), KB)
        return pltpu.make_async_copy(stage.at[b], update_out.at[rows], osems.at[b])

    def step(b, carry):
        first, last = plan[slots + b], plan[slots + b + 1]

        @pl.when(first == last)
        def _():
            stage[b] = jnp.zeros(stage.shape[1:], jnp.bfloat16)

        def body(i, p, q):
            weight_p = potential[pl.ds(tile_of[order[p]], 1), :]
            weight_q = potential[pl.ds(tile_of[order[q]], 1), :] * (q - p).astype(jnp.float32)
            weighted = jnp.concatenate(
                [
                    (pair[p, 1].astype(jnp.float32) * weight_p).astype(jnp.bfloat16),
                    (pair[q, 1].astype(jnp.float32) * weight_q).astype(jnp.bfloat16),
                ],
                axis=1,
            )
            block = lax.dot_general(
                jnp.concatenate([pair[p, 0], pair[q, 0]], axis=1),
                weighted,
                (((1,), (1,)), ((), ())),
                preferred_element_type=jnp.float32,
            )

            @pl.when(last - first <= 2)
            def _():
                stage[b] = (block * scale).astype(jnp.bfloat16)

            @pl.when((last - first > 2) & (i == 0))
            def _():
                acc[...] = block

            @pl.when(i > 0)
            def _():
                acc[...] += block

        by_twos(first, last, load, body)

        @pl.when(last - first > 2)
        def _():
            stage[b] = (acc[...] * scale).astype(jnp.bfloat16)

        store(b).start()
        return carry

    lax.fori_loop(0, blocks, step, 0)
    for b in range(blocks):
        store(b).wait()


def update(plan, order, tile_of, contributions, collect, parts, tiles, blocks, cols):
    slots = len(parts) * parts[0].shape[0]
    entry = parts[0].shape[1:]
    all_tiles = (collect.shape[0], P_SIZE)
    return pl.pallas_call(
        functools.partial(update_kernel, blocks, tiles),
        out_shape=(
            jax.ShapeDtypeStruct((tiles, P_SIZE), jnp.float32),
            jax.ShapeDtypeStruct((blocks * KB, cols), jnp.bfloat16),
        ),
        in_specs=[SMEM] * 3 + [VMEM] * 2 + [HBM] * len(parts),
        out_specs=(VMEM, HBM),
        scratch_shapes=[
            pltpu.VMEM((slots,) + entry, jnp.bfloat16),
            pltpu.VMEM(all_tiles, jnp.float32),
            pltpu.VMEM(all_tiles, jnp.float32),
            pltpu.VMEM((KB, cols), jnp.float32),
            pltpu.VMEM((blocks, KB, cols), jnp.bfloat16),
            pltpu.SemaphoreType.DMA((slots,)),
            pltpu.SemaphoreType.DMA((blocks,)),
        ],
        compiler_params=pltpu.CompilerParams(vmem_limit_bytes=24 * MIB),
        name="update",
    )(plan, order, tile_of, contributions, collect, *parts)


def shift(block, axis, step):
    count = lax.axis_size(axis)
    pairs = [(i, i + step) for i in range(count) if 0 <= i + step < count]
    return lax.ppermute(block, axis, pairs)


def make_plan(lists, me, entries, tiles, col_count, blocks):
    slots = col_count * CAP
    sent = sent_rows(slots, tiles)
    lists = lists[:, : 2 * entries + tiles].astype(jnp.int32)
    peers, named, counts = lists[:, :entries], lists[:, entries : 2 * entries], lists[:, 2 * entries :]
    index = jnp.arange(entries, dtype=jnp.int32)
    home = jnp.arange(col_count, dtype=jnp.int32)[:, None]
    earlier = (peers[:, :, None] == peers[:, None, :]) & (index[None, :] < index[:, None])
    rank = jnp.sum(earlier.astype(jnp.int32), axis=2)
    live = (index % SLOTS)[None, :] < jnp.repeat(counts, SLOTS, axis=1)
    row = jnp.where(live, peers * sent + chunk_of(home, peers, col_count) * CAP + rank, -1).reshape(col_count, tiles, SLOTS)
    core = (home * sent + slots + jnp.arange(tiles, dtype=jnp.int32))[:, :, None]
    row = jnp.concatenate([row, core], axis=2).reshape(col_count * tiles, SLOTS + 1, 1)
    picked = row == jnp.arange(col_count * sent, dtype=jnp.int32)
    collect = jnp.sum(picked.astype(jnp.float32), axis=1)
    hit = (
        (peers == me)[:, None, :]
        & (rank[:, None, :] == jnp.arange(CAP, dtype=jnp.int32)[None, :, None])
        & live[:, None, :]
    )
    at_me = chunk_of(home, me, col_count).reshape(1, col_count) == home
    tile = home * tiles + index[None, :] // SLOTS

    def of_slots(values):
        by_home = jnp.sum(jnp.where(hit, values[:, None, :], 0), axis=2)
        return jnp.sum(jnp.where(at_me[:, :, None], by_home[None], 0), axis=1).reshape(slots)

    wanted = of_slots(named + 1) - 1
    tile_of = of_slots(tile)
    key = jnp.where(wanted < 0, blocks, wanted)
    place = jnp.arange(slots, dtype=jnp.int32)
    before = (key[None, :] < key[:, None]) | (
        (key[None, :] == key[:, None]) & (place[None, :] < place[:, None])
    )
    spot = jnp.sum(before.astype(jnp.int32), axis=1)
    order = jnp.sum(jnp.where(spot[None, :] == place[:, None], place[None, :], 0), axis=1)
    starts = jnp.sum(
        (key[None, :] < jnp.arange(blocks + 1, dtype=jnp.int32)[:, None]).astype(jnp.int32), axis=1
    )
    plan = jnp.concatenate([wanted, starts, me[None]]).astype(jnp.int32)
    return collect, plan, order.astype(jnp.int32), tile_of.astype(jnp.int32)


def shards(
    start_columns,
    hamiltonian,
    band_pattern,
    coefficients,
    tile_peer,
    tile_block,
    tile_count,
    basis_values,
    core_density,
):
    col_count = lax.axis_size("col")
    entries = tile_peer.shape[0]
    tiles = core_density.shape[0]
    cols = start_columns.shape[1]
    blocks = start_columns.shape[0] // KB
    peers = tile_peer[:, 0]
    me = lax.axis_index("col").astype(jnp.int32)

    own = own_piece(peers, tile_block, tile_count, band_pattern, hamiltonian.reshape(-1, W))
    pieces, owners, awaited, handed = gather_pieces(own)
    v_low = shift(start_columns[-DEG * W :], "row", 1)
    v_high = shift(start_columns[: DEG * W], "row", -1)
    parts = exchange(me[None], peers, basis_values, own, pieces[min(1, len(pieces) - 1)],
        awaited + [v_low, v_high], handed)

    first, last, lists = edge_blocks(owners, pieces, col_count, DEG - 1)
    h_low = shift(last, "row", 1)
    h_high = shift(first, "row", -1)
    inner = chebyshev_inner(coefficients, owners, v_low, start_columns, v_high, pieces)
    kernel_t = chebyshev_outer(
        coefficients, inner, v_low, start_columns, v_high, h_low, first, last, h_high
    )
    collect, plan, order, tile_of = make_plan(lists[:, 0], me, entries, tiles, col_count, blocks)
    partial = project(plan, order, kernel_t, core_density, parts, col_count)
    contributions = lax.all_to_all(partial, "col", split_axis=0, concat_axis=0, tiled=True)
    contributions = contributions.reshape(-1, P_SIZE)
    return update(
        plan, order, tile_of, contributions, collect, parts, tiles, blocks, cols
    )


def solution(mesh):
    return jax.shard_map(
        shards,
        mesh=mesh,
        in_specs=(
            P("row", "col"),
            P(("row", "col"), None, None, None),
            P(("row", "col")),
            P(),
            P(("row", "col"), None),
            P(("row", "col")),
            P(("row", "col")),
            P(("row", "col"), None, None, None),
            P(("row", "col"), None),
        ),
        out_specs=(P(("row", "col"), None), P("row", "col")),
        check_vma=False,
    )
```

```python
import functools
import math

import jax
import jax.numpy as jnp
from jax import lax
from jax.experimental import pallas as pl
from jax.experimental.pallas import tpu as pltpu
from jax.sharding import PartitionSpec as P

W = 256
KB = 512
DEG = 3
SLOTS = 4
CAP = 2
P_SIZE = 128
MIB = 1 << 20
LISTS = 16

exchange_factor = (3.0 / math.pi) ** (1.0 / 3.0)
HBM = pl.BlockSpec(memory_space=pltpu.HBM)
ANY = pl.BlockSpec(memory_space=pl.ANY)
SMEM = pl.BlockSpec(memory_space=pltpu.SMEM)
VMEM = pl.BlockSpec(memory_space=pltpu.VMEM)


def partner(me, j, count):
    if count & (count - 1) == 0:
        return me ^ abs(j)
    return (me + j) % count


def piece_kernel(peers, named, counts, pattern, ham, piece, blocks, sems):
    rows = ham.shape[0]
    load = pltpu.make_async_copy(ham, blocks.at[pl.ds(0, rows)], sems.at[0])
    load.start()
    lane = lax.broadcasted_iota(jnp.int32, (LISTS, W), 1)
    lists = jnp.zeros((LISTS, W), jnp.int32)
    at = 0
    for ref in (peers, named, counts):
        for i in range(ref.shape[0]):
            lists = jnp.where(lane == at, ref[i], lists)
            at += 1
    blocks[rows:] = lists.astype(jnp.float32).astype(jnp.bfloat16)
    load.wait()
    for i in range(rows // (2 * W)):
        coupling = slice((2 * i + 1) * W, (2 * i + 2) * W)
        blocks[coupling] = blocks[coupling] * pattern[i].astype(jnp.bfloat16)
    store = pltpu.make_async_copy(blocks, piece, sems.at[1])
    store.start()
    store.wait()


def own_piece(peers, named, counts, pattern, ham):
    piece = (ham.shape[0] + LISTS, W)
    return pl.pallas_call(
        piece_kernel,
        out_shape=jax.ShapeDtypeStruct(piece, ham.dtype),
        in_specs=[SMEM] * 4 + [HBM],
        out_specs=HBM,
        scratch_shapes=[pltpu.VMEM(piece, ham.dtype), pltpu.SemaphoreType.DMA((2,))],
        compiler_params=pltpu.CompilerParams(vmem_limit_bytes=62 * MIB),
        name="own_piece",
    )(peers, named, counts, pattern, ham)


def lines_of(count):
    inner = max(count // 4, 1) if count & (count - 1) == 0 else 1
    return count // inner, inner


def swap_along(block, t):
    count = lax.axis_size("col")
    _, inner = lines_of(count)
    pairs = [(c, c - c % inner + partner(c % inner, t, inner)) for c in range(count)]
    return lax.ppermute(block, "col", pairs)


def chunk_of(home, owner, count):
    outer, inner = lines_of(count)
    return partner(home % inner, owner % inner, inner) * outer + home // inner


def pack_kernel(entries, col_count, wanted, me, peers, basis, first, *refs):
    outer, inner = lines_of(col_count)
    sent, (held, owner, count, in_sems, out_sems) = refs[: len(wanted)], refs[len(wanted) :]
    for c in range(col_count):
        count[c] = 0
        for k in range(CAP):
            owner[c * CAP + k] = 0
    for e in range(entries):
        p = peers[e]
        k = count[p]
        count[p] = k + 1
        owner[p * CAP + k] = e
    place = lax.rem(me[0], inner)
    tasks = []
    for target, group in zip(sent, wanted):
        for line in range(outer):
            for i, (t, k) in enumerate(group):
                n = len(tasks)
                e = owner[(line * inner + partner(place, t, inner)) * CAP + k]
                fetch = pltpu.make_async_copy(basis.at[e], held.at[n], in_sems.at[n])
                store = pltpu.make_async_copy(held.at[n], target.at[line, i], out_sems.at[n])
                tasks.append((fetch, store))
    for fetch, _ in tasks:
        fetch.start()
    for fetch, store in tasks:
        fetch.wait()
        store.start()
    for _, store in tasks:
        store.wait()


def pack(me, peers, basis, first, col_count, wanted):
    outer, _ = lines_of(col_count)
    entries = basis.shape[0]
    number = sum(len(group) for group in wanted) * outer
    return list(pl.pallas_call(
        functools.partial(pack_kernel, entries, col_count, wanted),
        out_shape=tuple(
            jax.ShapeDtypeStruct((outer, len(group)) + basis.shape[1:], basis.dtype)
            for group in wanted
        ),
        in_specs=[SMEM, SMEM, HBM, HBM],
        out_specs=(HBM,) * len(wanted),
        scratch_shapes=[
            pltpu.VMEM((number,) + basis.shape[1:], basis.dtype),
            pltpu.SMEM((col_count * CAP,), jnp.int32),
            pltpu.SMEM((col_count,), jnp.int32),
            pltpu.SemaphoreType.DMA((number,)),
            pltpu.SemaphoreType.DMA((number,)),
        ],
        compiler_params=pltpu.CompilerParams(vmem_limit_bytes=62 * MIB),
        name="pack",
    )(me, peers, basis, first))


def after(block, *others):
    return pl.pallas_call(
        lambda *refs: None,
        out_shape=jax.ShapeDtypeStruct(block.shape, block.dtype),
        in_specs=[HBM] + [ANY] * len(others),
        out_specs=HBM,
        input_output_aliases={0: 0},
        compiler_params=pltpu.CompilerParams(vmem_limit_bytes=59 * MIB),
        name="after",
    )(block, *others)


def exchange(me, peers, basis, own, early, awaited, handed):
    count = lax.axis_size("col")
    outer, inner = lines_of(count)
    groups = [[line * inner + place for line in range(outer)] for place in range(inner)]

    def between_lines(blocks, *others):
        block = jnp.concatenate(blocks, axis=1)
        return lax.all_to_all(
            after(block, *others), "col", split_axis=0, concat_axis=0,
            axis_index_groups=groups, tiled=True,
        )

    here = [(0, k) for k in range(CAP)]
    ahead = [[(t, 0)] for t in range(1, inner)]
    rest = [[(t, k)] for k in range(1, CAP) for t in range(1, inner)]
    sent = pack(me, peers, basis, own, count, ahead) if ahead else []
    to_lines, *later = pack(me, peers, basis, early, count, [here] + rest)
    swapped = {
        group[0]: swap_along(block, group[0][0]) for block, group in zip(sent + later, ahead + rest)
    }
    parts = [between_lines([to_lines], *awaited, *[swapped[group[0]] for group in ahead])]
    for t in range(1, inner):
        parts.append(between_lines([swapped[t, k] for k in range(CAP)], parts[-1], *handed))
    return [part.reshape((outer * CAP,) + part.shape[2:]) for part in parts]


def gather_pieces(own):
    count = lax.axis_size("col")
    outer, inner = lines_of(count)
    me = lax.axis_index("col").astype(jnp.int32)
    a, b = me // inner, me % inner

    def move(block, ways):
        pairs = [(x * inner + y, z * inner + y) for x, z in ways for y in range(inner)]
        return lax.ppermute(block, "col", pairs)

    if outer == 4:
        middle, outwards = [(1, 2), (2, 1)], [(1, 0), (2, 3)]
        near = move(own, [(0, 1), (1, 0), (2, 3), (3, 2)])
        across = move(own, middle)
        far = move(near, middle)
        handed = move(across, outwards)
        last = move(far, outwards)
        within = (a == 1) | (a == 2)
        lines = [
            (own, a),
            (near, a ^ 1),
            (across + handed, jnp.where(within, a ^ 3, a ^ 2)),
            (far + last, jnp.where(within, a ^ 2, a ^ 3)),
        ]
        awaited, ends = [far, handed], [last]
    else:
        lines = [(own, a)] + [
            (move(own, [(x, partner(x, t, outer)) for x in range(outer)]), partner(a, -t, outer))
            for t in range(1, outer)
        ]
        awaited, ends = [block for block, _ in lines[1:]], []
    pieces, owners = [], []
    for block, line in lines:
        pieces.append(block)
        owners.append(line * inner + b)
        for t in range(1, inner):
            pieces.append(swap_along(block, t))
            owners.append(line * inner + partner(b, -t, inner))
    ends += [piece for piece in pieces[: 3 * inner] if all(piece is not block for block, _ in lines)]
    return pieces, jnp.stack(owners).astype(jnp.int32), awaited, ends


def edge_kernel(col_count, depth, owners, *refs):
    pieces, (first, last, lists, sems, list_sems) = refs[:-5], refs[-5:]
    rows = pieces[0].shape[0] - LISTS
    held = rows // (2 * W)
    total = col_count * held

    def each(act):
        for i, piece in enumerate(pieces):
            for g in range(depth):
                for out, block, sem in ((first, g, 0), (last, total - depth + g, 1)):
                    source = piece.at[pl.ds(block % held * 2 * W, 2 * W)]
                    copy = pltpu.make_async_copy(source, out.at[g], sems.at[sem, g])

                    @pl.when(owners[i] == block // held)
                    def _():
                        act(copy)

            @pl.when(owners[i] >= 0)
            def _():
                act(pltpu.make_async_copy(
                    piece.at[pl.ds(rows, LISTS)], lists.at[owners[i]], list_sems.at[i]
                ))

    each(lambda copy: copy.start())
    each(lambda copy: copy.wait())


def edge_blocks(owners, pieces, col_count, depth):
    shape = jax.ShapeDtypeStruct((depth, 2 * W, W), pieces[0].dtype)
    return pl.pallas_call(
        functools.partial(edge_kernel, col_count, depth),
        out_shape=(shape, shape, jax.ShapeDtypeStruct((col_count, LISTS, W), pieces[0].dtype)),
        in_specs=[SMEM] + [HBM] * len(pieces),
        out_specs=(VMEM, VMEM, VMEM),
        scratch_shapes=[
            pltpu.SemaphoreType.DMA((2, depth)),
            pltpu.SemaphoreType.DMA((len(pieces),)),
        ],
        name="edge_blocks",
    )(owners, *pieces)


def rows_of(j, count=1):
    return pl.ds(j * W if isinstance(j, int) else pl.multiple_of(j * W, W), count * W)


def band_builder(source, target):
    rows = lax.broadcasted_iota(jnp.int32, (W, W), 0)
    cols = lax.broadcasted_iota(jnp.int32, (W, W), 1)
    upper = jnp.where(rows <= cols, 1.0, 0.0).astype(jnp.bfloat16)

    def build(j, carry):
        coupling = source[j, W:]
        lower_band = coupling * upper
        target[j, :, 0:W] = lower_band
        target[j, :, W : 2 * W] = source[j, :W]
        target[j, :, 2 * W : 3 * W] = coupling - lower_band
        return carry

    return build


def inner_kernel(blocks, coef, owners, v_low, v_mid, v_high, *refs):
    (
        *pieces, out, edge_1, edge_2, edge_total,
        vext, hraw, hcat, cheb_1, cheb_2, total, kern, sems, psems, osems, esems,
    ) = refs
    held = (pieces[0].shape[0] - LISTS) // (2 * W)
    v_copies = [
        pltpu.make_async_copy(v_low.at[rows_of(DEG - 1)], vext.at[rows_of(0)], sems.at[0]),
        pltpu.make_async_copy(v_mid, vext.at[rows_of(1, blocks)], sems.at[1]),
        pltpu.make_async_copy(v_high.at[rows_of(0)], vext.at[rows_of(blocks + 1)], sems.at[2]),
    ]

    def each_piece(act):
        for i, piece in enumerate(pieces):
            for k in range(held):
                act(pltpu.make_async_copy(
                    piece.at[pl.ds(k * 2 * W, 2 * W)],
                    hraw.at[owners[i] * held + k],
                    psems.at[i, k],
                ))

    each_piece(lambda copy: copy.start())
    for copy in v_copies:
        copy.start()
    each_piece(lambda copy: copy.wait())
    build = band_builder(hraw, hcat)
    build(0, 0)
    for copy in v_copies:
        copy.wait()

    def band(source, j, row):
        return jnp.dot(hcat[j], source[rows_of(row, 3), :], preferred_element_type=jnp.float32)

    def edges(source, target, at):
        size = source.shape[0] // W
        return [
            pltpu.make_async_copy(
                source.at[rows_of(place, 2)], target.at[rows_of(2 * i, 2)], esems.at[at, i]
            )
            for i, place in enumerate((0, size - 2))
        ]

    def first(j, carry):
        value = band(vext, j, j)
        build(jnp.minimum(j + 1, blocks - 1), 0)
        cheb_1[rows_of(j), :] = value.astype(jnp.bfloat16)
        total[rows_of(j), :] = value
        return carry

    lax.fori_loop(0, blocks, first, 0, unroll=4)

    def second(j, carry):
        begin = vext[rows_of(j + 2), :].astype(jnp.float32)
        value = 2.0 * band(cheb_1, j + 1, j) - begin
        cheb_2[rows_of(j), :] = value.astype(jnp.bfloat16)
        total[rows_of(j + 1), :] = (
            coef[0] * begin + (coef[1] - coef[3]) * total[rows_of(j + 1), :] + coef[2] * value
        )
        return carry

    lax.fori_loop(0, blocks - 2, second, 0, unroll=4)
    outgoing = (
        edges(cheb_1, edge_1, 0) + edges(cheb_2, edge_2, 1) + edges(total, edge_total, 2)
    )
    for copy in outgoing:
        copy.start()

    def store(j):
        return pltpu.make_async_copy(kern.at[j], out.at[j], osems.at[j])

    def third(j, carry):
        for half in range(KB // W):
            i = j * (KB // W) + half
            value = total[rows_of(i), :] + (2.0 * coef[3]) * band(cheb_2, i, i - 2)
            kern[j, :, half * W : (half + 1) * W] = value.astype(jnp.bfloat16).T
        store(j).start()
        return carry

    last = blocks // (KB // W) - 1
    lax.fori_loop(1, last, third, 0, unroll=2)
    for j in range(1, last):
        store(j).wait()
    for copy in outgoing:
        copy.wait()


def chebyshev_inner(coefficients, owners, v_low, v_mid, v_high, pieces):
    blocks = v_mid.shape[0] // W
    cols = v_mid.shape[1]
    flops = 2 * W * 3 * W * cols * (3 * blocks - 6)
    result = (blocks * W // KB, cols, KB)
    held = (pieces[0].shape[0] - LISTS) // (2 * W)
    return pl.pallas_call(
        functools.partial(inner_kernel, blocks),
        out_shape=(
            jax.ShapeDtypeStruct(result, jnp.bfloat16),
            jax.ShapeDtypeStruct((4 * W, cols), jnp.bfloat16),
            jax.ShapeDtypeStruct((4 * W, cols), jnp.bfloat16),
            jax.ShapeDtypeStruct((4 * W, cols), jnp.float32),
        ),
        in_specs=[SMEM] * 2 + [HBM] * (3 + len(pieces)),
        out_specs=(HBM,) * 4,
        scratch_shapes=[
            pltpu.VMEM(((blocks + 2) * W, cols), jnp.bfloat16),
            pltpu.VMEM((blocks, 2 * W, W), jnp.bfloat16),
            pltpu.VMEM((blocks, W, 3 * W), jnp.bfloat16),
            pltpu.VMEM((blocks * W, cols), jnp.bfloat16),
            pltpu.VMEM(((blocks - 2) * W, cols), jnp.bfloat16),
            pltpu.VMEM((blocks * W, cols), jnp.float32),
            pltpu.VMEM(result, jnp.bfloat16),
            pltpu.SemaphoreType.DMA((3,)),
            pltpu.SemaphoreType.DMA((len(pieces), held)),
            pltpu.SemaphoreType.DMA((result[0],)),
            pltpu.SemaphoreType.DMA((3, 2)),
        ],
        compiler_params=pltpu.CompilerParams(vmem_limit_bytes=62 * MIB),
        cost_estimate=pl.CostEstimate(flops=flops, bytes_accessed=16 * MIB, transcendentals=0),
        name="chebyshev_inner",
    )(coefficients, owners, v_low, v_mid, v_high, *pieces)


def outer_kernel(
    blocks, coef, kernel_in, v_low, v_mid, v_high, h_low, h_first, h_last, h_high,
    edge_1, edge_2, edge_total, out,
    v, hraw, hcat, cheb_1, cheb_2, total, kern, sems, osems,
):
    last = kern.shape[0] - 1
    end = out.shape[0] - 1
    stages = [
        [
            (h_low, hraw.at[pl.ds(0, 2)]),
            (v_low, v.at[0, rows_of(0, 3)]),
            (v_mid.at[rows_of(0)], v.at[0, rows_of(3)]),
            (h_high, hraw.at[pl.ds(6, 2)]),
            (v_mid.at[rows_of(blocks - 1)], v.at[1, rows_of(0)]),
            (v_high, v.at[1, rows_of(1, 3)]),
        ],
        [
            (h_first, hraw.at[pl.ds(2, 2)]),
            (h_last, hraw.at[pl.ds(4, 2)]),
            (edge_1.at[rows_of(0, 2)], cheb_1.at[0, rows_of(2, 2)]),
            (edge_1.at[rows_of(2, 2)], cheb_1.at[1, rows_of(0, 2)]),
        ],
        [
            (edge_2.at[rows_of(0, 2)], cheb_2.at[0, rows_of(2, 2)]),
            (edge_2.at[rows_of(2, 2)], cheb_2.at[1, rows_of(0, 2)]),
            (edge_total.at[rows_of(0, 2)], total.at[0]),
            (edge_total.at[rows_of(2, 2)], total.at[1]),
        ],
    ]
    at = 0
    for i, stage in enumerate(stages):
        stages[i] = [
            pltpu.make_async_copy(source, target, sems.at[at + n])
            for n, (source, target) in enumerate(stage)
        ]
        at += len(stage)
        for copy in stages[i]:
            copy.start()
    build = band_builder(hraw, hcat)

    def arrived(i):
        for copy in stages[i]:
            copy.wait()

    def band(side, j, source, row):
        return jnp.dot(
            hcat[4 * side + j], source[side, rows_of(row, 3), :], preferred_element_type=jnp.float32
        )

    arrived(0)
    for j in (0, 1, 6, 7):
        build(j, 0)
    for side, places in ((0, (0, 1)), (1, (2, 3))):
        for j in places:
            value = band(side, j, v, j - 2 * side)
            cheb_1[side, rows_of(j), :] = value.astype(jnp.bfloat16)
    arrived(1)
    for j in (2, 3, 4, 5):
        build(j, 0)
    arrived(2)
    for side, places in ((0, ((1, 0), (2, 1))), (1, ((2, 3), (1, 2)))):
        for j, place in places:
            begin = v[side, rows_of(place + 2 - 4 * side), :].astype(jnp.float32)
            value = 2.0 * band(side, j, cheb_1, j - 1) - begin
            cheb_2[side, rows_of(place), :] = value.astype(jnp.bfloat16)
            if (j, place) == places[1]:
                within = rows_of(side)
                total[side, within, :] = (
                    coef[0] * begin + (coef[1] - coef[3]) * total[side, within, :] + coef[2] * value
                )
    for side in range(2):
        for half in range(2):
            j = 2 + half if side == 0 else half
            value = total[side, rows_of(half), :] + (2.0 * coef[3]) * band(side, j, cheb_2, half)
            kern[side, :, half * W : (half + 1) * W] = value.astype(jnp.bfloat16).T
    stores = [
        pltpu.make_async_copy(kern.at[0], out.at[0], osems.at[0]),
        pltpu.make_async_copy(kern.at[last], out.at[end], osems.at[1]),
    ]
    for store in stores:
        store.start()
    for store in stores:
        store.wait()


def chebyshev_outer(coefficients, inner, v_low, v_mid, v_high, h_low, h_first, h_last, h_high):
    kernel_t, edge_1, edge_2, edge_total = inner
    blocks = v_mid.shape[0] // W
    cols = v_mid.shape[1]
    return pl.pallas_call(
        functools.partial(outer_kernel, blocks),
        out_shape=jax.ShapeDtypeStruct(kernel_t.shape, kernel_t.dtype),
        in_specs=[SMEM] + [HBM] * 11,
        out_specs=HBM,
        input_output_aliases={1: 0},
        scratch_shapes=[
            pltpu.VMEM((2, 4 * W, cols), jnp.bfloat16),
            pltpu.VMEM((8, 2 * W, W), jnp.bfloat16),
            pltpu.VMEM((8, W, 3 * W), jnp.bfloat16),
            pltpu.VMEM((2, 4 * W, cols), jnp.bfloat16),
            pltpu.VMEM((2, 4 * W, cols), jnp.bfloat16),
            pltpu.VMEM((2, 2 * W, cols), jnp.float32),
            pltpu.VMEM((2, cols, KB), jnp.bfloat16),
            pltpu.SemaphoreType.DMA((14,)),
            pltpu.SemaphoreType.DMA((2,)),
        ],
        compiler_params=pltpu.CompilerParams(vmem_limit_bytes=62 * MIB),
        name="chebyshev_outer",
    )(
        coefficients, kernel_t, v_low, v_mid, v_high, h_low, h_first, h_last, h_high,
        edge_1, edge_2, edge_total,
    )


def entry_loads(order, parts, pair, sems):
    size = parts[0].shape[0]

    def load(p):
        return pltpu.make_async_copy(parts[0].at[0], pair.at[p], sems.at[p])

    def start(p, carry):
        n = order[p]
        for t, part in enumerate(parts):
            @pl.when((n >= t * size) & (n < (t + 1) * size))
            def _():
                pltpu.make_async_copy(part.at[n - t * size], pair.at[p], sems.at[p]).start()

        return carry

    return load, start


def by_twos(first, last, load, body):
    def step(i, carry):
        p = first + 2 * i
        q = jnp.minimum(p + 1, last - 1)
        load(p).wait()

        @pl.when(q > p)
        def _():
            load(q).wait()

        body(i, p, q)
        return carry

    lax.fori_loop(0, (last - first + 1) // 2, step, 0)


def sent_rows(slots, tiles):
    return slots + tiles + -(slots + tiles) % 8


def project_kernel(blocks, plan, order, kernel_t, core, *refs):
    *parts, out, kern, pair, rows, ksems, bsems = refs
    slots = pair.shape[0]
    load, start = entry_loads(order, parts, pair, bsems)

    def fetch(b):
        return pltpu.make_async_copy(kernel_t.at[b], kern.at[b], ksems.at[b])

    def begin(b, carry):
        first, last = plan[slots + b], plan[slots + b + 1]

        @pl.when(first < last)
        def _():
            fetch(b).start()

        return lax.fori_loop(first, last, start, carry)

    lax.fori_loop(0, blocks, begin, 0)
    rows[...] = jnp.zeros_like(rows)
    rows[slots : slots + core.shape[0]] = core[...]

    def step(b, carry):
        first, last = plan[slots + b], plan[slots + b + 1]

        @pl.when(first < last)
        def _():
            fetch(b).wait()

        def body(i, p, q):
            both = jnp.concatenate([pair[p, 0], pair[q, 0]], axis=1)
            projected = jnp.dot(kern[b], both, preferred_element_type=jnp.float32)
            other = jnp.concatenate([pair[p, 1], pair[q, 1]], axis=1).astype(jnp.float32)
            value = jnp.sum(projected * other, axis=0, keepdims=True) * (1.0 / KB)
            rows[pl.ds(order[p], 1), :] = value[:, :P_SIZE]
            rows[pl.ds(order[q], 1), :] = value[:, P_SIZE:]

        by_twos(first, last, load, body)
        return carry

    lax.fori_loop(0, blocks, step, 0)
    for c in range(out.shape[0]):
        out[c] = rows[...]


def project(plan, order, kernel_t, core, parts, col_count):
    slots = col_count * CAP
    entry = parts[0].shape[1:]
    sent = sent_rows(slots, core.shape[0])
    blocks = kernel_t.shape[0]
    return pl.pallas_call(
        functools.partial(project_kernel, blocks),
        out_shape=jax.ShapeDtypeStruct((col_count, sent, P_SIZE), jnp.float32),
        in_specs=[SMEM, SMEM, HBM, VMEM] + [HBM] * len(parts),
        out_specs=VMEM,
        scratch_shapes=[
            pltpu.VMEM(kernel_t.shape, jnp.bfloat16),
            pltpu.VMEM((slots,) + entry, jnp.bfloat16),
            pltpu.VMEM((sent, P_SIZE), jnp.float32),
            pltpu.SemaphoreType.DMA((blocks,)),
            pltpu.SemaphoreType.DMA((slots,)),
        ],
        compiler_params=pltpu.CompilerParams(vmem_limit_bytes=62 * MIB),
        name="project",
    )(plan, order, kernel_t, core, *parts)


def update_kernel(
    blocks, tiles, plan, order, tile_of, contributions, collect, *refs
):
    *parts, density_out, update_out, pair, density, potential, acc, stage, sems, osems = refs
    slots = pair.shape[0]
    live = plan[slots + blocks]
    me = plan[slots + blocks + 1]
    load, start = entry_loads(order, parts, pair, sems)
    lax.fori_loop(0, live, start, 0)
    density[...] = jnp.dot(
        collect[...],
        contributions[...],
        preferred_element_type=jnp.float32,
        precision=lax.Precision.HIGHEST,
    )
    for t in range(tiles):
        density_out[pl.ds(t, 1), :] = density[pl.ds(me * tiles + t, 1), :]
    positive = jnp.maximum(density[...], 0.1)
    root = jnp.exp(jnp.log(positive) * (1.0 / 3.0))
    root = root - (root - positive / (root * root)) * (1.0 / 3.0)
    potential[...] = -exchange_factor * root
    scale = 1.0 / math.sqrt(P_SIZE)

    def store(b):
        rows = pl.ds(pl.multiple_of(b * KB, KB), KB)
        return pltpu.make_async_copy(stage.at[b], update_out.at[rows], osems.at[b])

    def step(b, carry):
        first, last = plan[slots + b], plan[slots + b + 1]

        @pl.when(first == last)
        def _():
            stage[b] = jnp.zeros(stage.shape[1:], jnp.bfloat16)

        def body(i, p, q):
            weight_p = potential[pl.ds(tile_of[order[p]], 1), :]
            weight_q = potential[pl.ds(tile_of[order[q]], 1), :] * (q - p).astype(jnp.float32)
            weighted = jnp.concatenate(
                [
                    (pair[p, 1].astype(jnp.float32) * weight_p).astype(jnp.bfloat16),
                    (pair[q, 1].astype(jnp.float32) * weight_q).astype(jnp.bfloat16),
                ],
                axis=1,
            )
            block = lax.dot_general(
                jnp.concatenate([pair[p, 0], pair[q, 0]], axis=1),
                weighted,
                (((1,), (1,)), ((), ())),
                preferred_element_type=jnp.float32,
            )

            @pl.when(last - first <= 2)
            def _():
                stage[b] = (block * scale).astype(jnp.bfloat16)

            @pl.when((last - first > 2) & (i == 0))
            def _():
                acc[...] = block

            @pl.when(i > 0)
            def _():
                acc[...] += block

        by_twos(first, last, load, body)

        @pl.when(last - first > 2)
        def _():
            stage[b] = (acc[...] * scale).astype(jnp.bfloat16)

        store(b).start()
        return carry

    lax.fori_loop(0, blocks, step, 0)
    for b in range(blocks):
        store(b).wait()


def update(plan, order, tile_of, contributions, collect, parts, tiles, blocks, cols):
    slots = len(parts) * parts[0].shape[0]
    entry = parts[0].shape[1:]
    all_tiles = (collect.shape[0], P_SIZE)
    return pl.pallas_call(
        functools.partial(update_kernel, blocks, tiles),
        out_shape=(
            jax.ShapeDtypeStruct((tiles, P_SIZE), jnp.float32),
            jax.ShapeDtypeStruct((blocks * KB, cols), jnp.bfloat16),
        ),
        in_specs=[SMEM] * 3 + [VMEM] * 2 + [HBM] * len(parts),
        out_specs=(VMEM, HBM),
        scratch_shapes=[
            pltpu.VMEM((slots,) + entry, jnp.bfloat16),
            pltpu.VMEM(all_tiles, jnp.float32),
            pltpu.VMEM(all_tiles, jnp.float32),
            pltpu.VMEM((KB, cols), jnp.float32),
            pltpu.VMEM((blocks, KB, cols), jnp.bfloat16),
            pltpu.SemaphoreType.DMA((slots,)),
            pltpu.SemaphoreType.DMA((blocks,)),
        ],
        compiler_params=pltpu.CompilerParams(vmem_limit_bytes=24 * MIB),
        name="update",
    )(plan, order, tile_of, contributions, collect, *parts)


def shift(block, axis, step):
    count = lax.axis_size(axis)
    pairs = [(i, i + step) for i in range(count) if 0 <= i + step < count]
    return lax.ppermute(block, axis, pairs)


def make_plan(lists, me, entries, tiles, col_count, blocks):
    slots = col_count * CAP
    sent = sent_rows(slots, tiles)
    lists = lists[:, : 2 * entries + tiles].astype(jnp.int32)
    peers, named, counts = lists[:, :entries], lists[:, entries : 2 * entries], lists[:, 2 * entries :]
    index = jnp.arange(entries, dtype=jnp.int32)
    home = jnp.arange(col_count, dtype=jnp.int32)[:, None]
    earlier = (peers[:, :, None] == peers[:, None, :]) & (index[None, :] < index[:, None])
    rank = jnp.sum(earlier.astype(jnp.int32), axis=2)
    live = (index % SLOTS)[None, :] < jnp.repeat(counts, SLOTS, axis=1)
    row = jnp.where(live, peers * sent + chunk_of(home, peers, col_count) * CAP + rank, -1).reshape(col_count, tiles, SLOTS)
    core = (home * sent + slots + jnp.arange(tiles, dtype=jnp.int32))[:, :, None]
    row = jnp.concatenate([row, core], axis=2).reshape(col_count * tiles, SLOTS + 1, 1)
    picked = row == jnp.arange(col_count * sent, dtype=jnp.int32)
    collect = jnp.sum(picked.astype(jnp.float32), axis=1)
    hit = (
        (peers == me)[:, None, :]
        & (rank[:, None, :] == jnp.arange(CAP, dtype=jnp.int32)[None, :, None])
        & live[:, None, :]
    )
    at_me = chunk_of(home, me, col_count).reshape(1, col_count) == home
    tile = home * tiles + index[None, :] // SLOTS

    def of_slots(values):
        by_home = jnp.sum(jnp.where(hit, values[:, None, :], 0), axis=2)
        return jnp.sum(jnp.where(at_me[:, :, None], by_home[None], 0), axis=1).reshape(slots)

    wanted = of_slots(named + 1) - 1
    tile_of = of_slots(tile)
    key = jnp.where(wanted < 0, blocks, wanted)
    place = jnp.arange(slots, dtype=jnp.int32)
    before = (key[None, :] < key[:, None]) | (
        (key[None, :] == key[:, None]) & (place[None, :] < place[:, None])
    )
    spot = jnp.sum(before.astype(jnp.int32), axis=1)
    order = jnp.sum(jnp.where(spot[None, :] == place[:, None], place[None, :], 0), axis=1)
    starts = jnp.sum(
        (key[None, :] < jnp.arange(blocks + 1, dtype=jnp.int32)[:, None]).astype(jnp.int32), axis=1
    )
    plan = jnp.concatenate([wanted, starts, me[None]]).astype(jnp.int32)
    return collect, plan, order.astype(jnp.int32), tile_of.astype(jnp.int32)


def shards(
    start_columns,
    hamiltonian,
    band_pattern,
    coefficients,
    tile_peer,
    tile_block,
    tile_count,
    basis_values,
    core_density,
):
    col_count = lax.axis_size("col")
    entries = tile_peer.shape[0]
    tiles = core_density.shape[0]
    cols = start_columns.shape[1]
    blocks = start_columns.shape[0] // KB
    peers = tile_peer[:, 0]
    me = lax.axis_index("col").astype(jnp.int32)

    own = own_piece(peers, tile_block, tile_count, band_pattern, hamiltonian.reshape(-1, W))
    pieces, owners, awaited, handed = gather_pieces(own)
    v_low = shift(start_columns[-DEG * W :], "row", 1)
    v_high = shift(start_columns[: DEG * W], "row", -1)
    parts = exchange(me[None], peers, basis_values, own, pieces[min(1, len(pieces) - 1)],
        awaited + [v_low, v_high], handed)

    first, last, lists = edge_blocks(owners, pieces, col_count, DEG - 1)
    h_low = shift(last, "row", 1)
    h_high = shift(first, "row", -1)
    inner = chebyshev_inner(coefficients, owners, v_low, start_columns, v_high, pieces)
    kernel_t = chebyshev_outer(
        coefficients, inner, v_low, start_columns, v_high, h_low, first, last, h_high
    )
    collect, plan, order, tile_of = make_plan(lists[:, 0], me, entries, tiles, col_count, blocks)
    partial = project(plan, order, kernel_t, core_density, parts, col_count)
    contributions = lax.all_to_all(partial, "col", split_axis=0, concat_axis=0, tiled=True)
    contributions = contributions.reshape(-1, P_SIZE)
    return update(
        plan, order, tile_of, contributions, collect, parts, tiles, blocks, cols
    )


def solution(mesh):
    return jax.shard_map(
        shards,
        mesh=mesh,
        in_specs=(
            P("row", "col"),
            P(("row", "col"), None, None, None),
            P(("row", "col")),
            P(),
            P(("row", "col"), None),
            P(("row", "col")),
            P(("row", "col")),
            P(("row", "col"), None, None, None),
            P(("row", "col"), None),
        ),
        out_specs=(P(("row", "col"), None), P("row", "col")),
        check_vma=False,
    )
```

```python
import functools
import math

import jax
import jax.numpy as jnp
from jax import lax
from jax.experimental import pallas as pl
from jax.experimental.pallas import tpu as pltpu
from jax.sharding import PartitionSpec as P

W = 256
KB = 512
DEG = 3
SLOTS = 4
CAP = 2
P_SIZE = 128
MIB = 1 << 20
LISTS = 16

exchange_factor = (3.0 / math.pi) ** (1.0 / 3.0)
HBM = pl.BlockSpec(memory_space=pltpu.HBM)
ANY = pl.BlockSpec(memory_space=pl.ANY)
SMEM = pl.BlockSpec(memory_space=pltpu.SMEM)
VMEM = pl.BlockSpec(memory_space=pltpu.VMEM)


def partner(me, j, count):
    if count & (count - 1) == 0:
        return me ^ abs(j)
    return (me + j) % count


def piece_kernel(peers, named, counts, pattern, ham, piece, blocks, sems):
    rows = ham.shape[0]
    load = pltpu.make_async_copy(ham, blocks.at[pl.ds(0, rows)], sems.at[0])
    load.start()
    lane = lax.broadcasted_iota(jnp.int32, (LISTS, W), 1)
    lists = jnp.zeros((LISTS, W), jnp.int32)
    at = 0
    for ref in (peers, named, counts):
        for i in range(ref.shape[0]):
            lists = jnp.where(lane == at, ref[i], lists)
            at += 1
    blocks[rows:] = lists.astype(jnp.float32).astype(jnp.bfloat16)
    load.wait()
    for i in range(rows // (2 * W)):
        coupling = slice((2 * i + 1) * W, (2 * i + 2) * W)
        blocks[coupling] = blocks[coupling] * pattern[i].astype(jnp.bfloat16)
    store = pltpu.make_async_copy(blocks, piece, sems.at[1])
    store.start()
    store.wait()


def own_piece(peers, named, counts, pattern, ham):
    piece = (ham.shape[0] + LISTS, W)
    return pl.pallas_call(
        piece_kernel,
        out_shape=jax.ShapeDtypeStruct(piece, ham.dtype),
        in_specs=[SMEM] * 4 + [HBM],
        out_specs=HBM,
        scratch_shapes=[pltpu.VMEM(piece, ham.dtype), pltpu.SemaphoreType.DMA((2,))],
        compiler_params=pltpu.CompilerParams(vmem_limit_bytes=62 * MIB),
        name="own_piece",
    )(peers, named, counts, pattern, ham)


def lines_of(count):
    inner = max(count // 4, 1) if count & (count - 1) == 0 else 1
    return count // inner, inner


def swap_along(block, t):
    count = lax.axis_size("col")
    _, inner = lines_of(count)
    pairs = [(c, c - c % inner + partner(c % inner, t, inner)) for c in range(count)]
    return lax.ppermute(block, "col", pairs)


def chunk_of(home, owner, count):
    outer, inner = lines_of(count)
    return partner(home % inner, owner % inner, inner) * outer + home // inner


def pack_kernel(entries, col_count, wanted, me, peers, basis, first, *refs):
    outer, inner = lines_of(col_count)
    sent, (held, owner, count, in_sems, out_sems) = refs[: len(wanted)], refs[len(wanted) :]
    for c in range(col_count):
        count[c] = 0
        for k in range(CAP):
            owner[c * CAP + k] = 0
    for e in range(entries):
        p = peers[e]
        k = count[p]
        count[p] = k + 1
        owner[p * CAP + k] = e
    place = lax.rem(me[0], inner)
    tasks = []
    for target, group in zip(sent, wanted):
        for line in range(outer):
            for i, (t, k) in enumerate(group):
                n = len(tasks)
                e = owner[(line * inner + partner(place, t, inner)) * CAP + k]
                fetch = pltpu.make_async_copy(basis.at[e], held.at[n], in_sems.at[n])
                store = pltpu.make_async_copy(held.at[n], target.at[line, i], out_sems.at[n])
                tasks.append((fetch, store))
    for fetch, _ in tasks:
        fetch.start()
    for fetch, store in tasks:
        fetch.wait()
        store.start()
    for _, store in tasks:
        store.wait()


def pack(me, peers, basis, first, col_count, wanted):
    outer, _ = lines_of(col_count)
    entries = basis.shape[0]
    number = sum(len(group) for group in wanted) * outer
    return list(pl.pallas_call(
        functools.partial(pack_kernel, entries, col_count, wanted),
        out_shape=tuple(
            jax.ShapeDtypeStruct((outer, len(group)) + basis.shape[1:], basis.dtype)
            for group in wanted
        ),
        in_specs=[SMEM, SMEM, HBM, HBM],
        out_specs=(HBM,) * len(wanted),
        scratch_shapes=[
            pltpu.VMEM((number,) + basis.shape[1:], basis.dtype),
            pltpu.SMEM((col_count * CAP,), jnp.int32),
            pltpu.SMEM((col_count,), jnp.int32),
            pltpu.SemaphoreType.DMA((number,)),
            pltpu.SemaphoreType.DMA((number,)),
        ],
        compiler_params=pltpu.CompilerParams(vmem_limit_bytes=62 * MIB),
        name="pack",
    )(me, peers, basis, first))


def after(block, *others):
    return pl.pallas_call(
        lambda *refs: None,
        out_shape=jax.ShapeDtypeStruct(block.shape, block.dtype),
        in_specs=[HBM] + [ANY] * len(others),
        out_specs=HBM,
        input_output_aliases={0: 0},
        compiler_params=pltpu.CompilerParams(vmem_limit_bytes=59 * MIB),
        name="after",
    )(block, *others)


def exchange(me, peers, basis, own, early, awaited, handed):
    count = lax.axis_size("col")
    outer, inner = lines_of(count)
    groups = [[line * inner + place for line in range(outer)] for place in range(inner)]

    def between_lines(blocks, *others):
        block = jnp.concatenate(blocks, axis=1)
        return lax.all_to_all(
            after(block, *others), "col", split_axis=0, concat_axis=0,
            axis_index_groups=groups, tiled=True,
        )

    here = [(0, k) for k in range(CAP)]
    ahead = [[(t, 0)] for t in range(1, inner)]
    rest = [[(t, k)] for k in range(1, CAP) for t in range(1, inner)]
    sent = pack(me, peers, basis, own, count, ahead) if ahead else []
    to_lines, *later = pack(me, peers, basis, early, count, [here] + rest)
    swapped = {
        group[0]: swap_along(block, group[0][0]) for block, group in zip(sent + later, ahead + rest)
    }
    parts = [between_lines([to_lines], *awaited, *[swapped[group[0]] for group in ahead])]
    for t in range(1, inner):
        parts.append(between_lines([swapped[t, k] for k in range(CAP)], parts[-1], *handed))
    return [part.reshape((outer * CAP,) + part.shape[2:]) for part in parts]


def gather_pieces(own):
    count = lax.axis_size("col")
    outer, inner = lines_of(count)
    me = lax.axis_index("col").astype(jnp.int32)
    a, b = me // inner, me % inner

    def move(block, ways):
        pairs = [(x * inner + y, z * inner + y) for x, z in ways for y in range(inner)]
        return lax.ppermute(block, "col", pairs)

    if outer == 4:
        middle, outwards = [(1, 2), (2, 1)], [(1, 0), (2, 3)]
        near = move(own, [(0, 1), (1, 0), (2, 3), (3, 2)])
        across = move(own, middle)
        far = move(near, middle)
        handed = move(across, outwards)
        last = move(far, outwards)
        within = (a == 1) | (a == 2)
        lines = [
            (own, a),
            (near, a ^ 1),
            (across + handed, jnp.where(within, a ^ 3, a ^ 2)),
            (far + last, jnp.where(within, a ^ 2, a ^ 3)),
        ]
        awaited, ends = [far, handed], [last]
    else:
        lines = [(own, a)] + [
            (move(own, [(x, partner(x, t, outer)) for x in range(outer)]), partner(a, -t, outer))
            for t in range(1, outer)
        ]
        awaited, ends = [block for block, _ in lines[1:]], []
    pieces, owners = [], []
    for block, line in lines:
        pieces.append(block)
        owners.append(line * inner + b)
        for t in range(1, inner):
            pieces.append(swap_along(block, t))
            owners.append(line * inner + partner(b, -t, inner))
    ends += [piece for piece in pieces[: 3 * inner] if all(piece is not block for block, _ in lines)]
    return pieces, jnp.stack(owners).astype(jnp.int32), awaited, ends


def edge_kernel(col_count, depth, owners, *refs):
    pieces, (first, last, lists, sems, list_sems) = refs[:-5], refs[-5:]
    rows = pieces[0].shape[0] - LISTS
    held = rows // (2 * W)
    total = col_count * held

    def each(act):
        for i, piece in enumerate(pieces):
            for g in range(depth):
                for out, block, sem in ((first, g, 0), (last, total - depth + g, 1)):
                    source = piece.at[pl.ds(block % held * 2 * W, 2 * W)]
                    copy = pltpu.make_async_copy(source, out.at[g], sems.at[sem, g])

                    @pl.when(owners[i] == block // held)
                    def _():
                        act(copy)

            @pl.when(owners[i] >= 0)
            def _():
                act(pltpu.make_async_copy(
                    piece.at[pl.ds(rows, LISTS)], lists.at[owners[i]], list_sems.at[i]
                ))

    each(lambda copy: copy.start())
    each(lambda copy: copy.wait())


def edge_blocks(owners, pieces, col_count, depth):
    shape = jax.ShapeDtypeStruct((depth, 2 * W, W), pieces[0].dtype)
    return pl.pallas_call(
        functools.partial(edge_kernel, col_count, depth),
        out_shape=(shape, shape, jax.ShapeDtypeStruct((col_count, LISTS, W), pieces[0].dtype)),
        in_specs=[SMEM] + [HBM] * len(pieces),
        out_specs=(VMEM, VMEM, VMEM),
        scratch_shapes=[
            pltpu.SemaphoreType.DMA((2, depth)),
            pltpu.SemaphoreType.DMA((len(pieces),)),
        ],
        name="edge_blocks",
    )(owners, *pieces)


def rows_of(j, count=1):
    return pl.ds(j * W if isinstance(j, int) else pl.multiple_of(j * W, W), count * W)


def band_builder(source, target):
    rows = lax.broadcasted_iota(jnp.int32, (W, W), 0)
    cols = lax.broadcasted_iota(jnp.int32, (W, W), 1)
    upper = jnp.where(rows <= cols, 1.0, 0.0).astype(jnp.bfloat16)

    def build(j, carry):
        coupling = source[j, W:]
        lower_band = coupling * upper
        target[j, :, 0:W] = lower_band
        target[j, :, W : 2 * W] = source[j, :W]
        target[j, :, 2 * W : 3 * W] = coupling - lower_band
        return carry

    return build


def inner_kernel(blocks, coef, owners, v_low, v_mid, v_high, *refs):
    (
        *pieces, out, edge_1, edge_2, edge_total,
        vext, hraw, hcat, cheb_1, cheb_2, total, kern, sems, psems, osems, esems,
    ) = refs
    held = (pieces[0].shape[0] - LISTS) // (2 * W)
    v_copies = [
        pltpu.make_async_copy(v_low.at[rows_of(DEG - 1)], vext.at[rows_of(0)], sems.at[0]),
        pltpu.make_async_copy(v_mid, vext.at[rows_of(1, blocks)], sems.at[1]),
        pltpu.make_async_copy(v_high.at[rows_of(0)], vext.at[rows_of(blocks + 1)], sems.at[2]),
    ]

    def each_piece(act):
        for i, piece in enumerate(pieces):
            for k in range(held):
                act(pltpu.make_async_copy(
                    piece.at[pl.ds(k * 2 * W, 2 * W)],
                    hraw.at[owners[i] * held + k],
                    psems.at[i, k],
                ))

    each_piece(lambda copy: copy.start())
    for copy in v_copies:
        copy.start()
    each_piece(lambda copy: copy.wait())
    build = band_builder(hraw, hcat)
    build(0, 0)
    for copy in v_copies:
        copy.wait()

    def band(source, j, row):
        return jnp.dot(hcat[j], source[rows_of(row, 3), :], preferred_element_type=jnp.float32)

    def edges(source, target, at):
        size = source.shape[0] // W
        return [
            pltpu.make_async_copy(
                source.at[rows_of(place, 2)], target.at[rows_of(2 * i, 2)], esems.at[at, i]
            )
            for i, place in enumerate((0, size - 2))
        ]

    def first(j, carry):
        value = band(vext, j, j)
        build(jnp.minimum(j + 1, blocks - 1), 0)
        cheb_1[rows_of(j), :] = value.astype(jnp.bfloat16)
        total[rows_of(j), :] = value
        return carry

    lax.fori_loop(0, blocks, first, 0, unroll=4)

    def second(j, carry):
        begin = vext[rows_of(j + 2), :].astype(jnp.float32)
        value = 2.0 * band(cheb_1, j + 1, j) - begin
        cheb_2[rows_of(j), :] = value.astype(jnp.bfloat16)
        total[rows_of(j + 1), :] = (
            coef[0] * begin + (coef[1] - coef[3]) * total[rows_of(j + 1), :] + coef[2] * value
        )
        return carry

    lax.fori_loop(0, blocks - 2, second, 0, unroll=4)
    outgoing = (
        edges(cheb_1, edge_1, 0) + edges(cheb_2, edge_2, 1) + edges(total, edge_total, 2)
    )
    for copy in outgoing:
        copy.start()

    def store(j):
        return pltpu.make_async_copy(kern.at[j], out.at[j], osems.at[j])

    def third(j, carry):
        for half in range(KB // W):
            i = j * (KB // W) + half
            value = total[rows_of(i), :] + (2.0 * coef[3]) * band(cheb_2, i, i - 2)
            kern[j, :, half * W : (half + 1) * W] = value.astype(jnp.bfloat16).T
        store(j).start()
        return carry

    last = blocks // (KB // W) - 1
    lax.fori_loop(1, last, third, 0, unroll=2)
    for j in range(1, last):
        store(j).wait()
    for copy in outgoing:
        copy.wait()


def chebyshev_inner(coefficients, owners, v_low, v_mid, v_high, pieces):
    blocks = v_mid.shape[0] // W
    cols = v_mid.shape[1]
    flops = 2 * W * 3 * W * cols * (3 * blocks - 6)
    result = (blocks * W // KB, cols, KB)
    held = (pieces[0].shape[0] - LISTS) // (2 * W)
    return pl.pallas_call(
        functools.partial(inner_kernel, blocks),
        out_shape=(
            jax.ShapeDtypeStruct(result, jnp.bfloat16),
            jax.ShapeDtypeStruct((4 * W, cols), jnp.bfloat16),
            jax.ShapeDtypeStruct((4 * W, cols), jnp.bfloat16),
            jax.ShapeDtypeStruct((4 * W, cols), jnp.float32),
        ),
        in_specs=[SMEM] * 2 + [HBM] * (3 + len(pieces)),
        out_specs=(HBM,) * 4,
        scratch_shapes=[
            pltpu.VMEM(((blocks + 2) * W, cols), jnp.bfloat16),
            pltpu.VMEM((blocks, 2 * W, W), jnp.bfloat16),
            pltpu.VMEM((blocks, W, 3 * W), jnp.bfloat16),
            pltpu.VMEM((blocks * W, cols), jnp.bfloat16),
            pltpu.VMEM(((blocks - 2) * W, cols), jnp.bfloat16),
            pltpu.VMEM((blocks * W, cols), jnp.float32),
            pltpu.VMEM(result, jnp.bfloat16),
            pltpu.SemaphoreType.DMA((3,)),
            pltpu.SemaphoreType.DMA((len(pieces), held)),
            pltpu.SemaphoreType.DMA((result[0],)),
            pltpu.SemaphoreType.DMA((3, 2)),
        ],
        compiler_params=pltpu.CompilerParams(vmem_limit_bytes=62 * MIB),
        cost_estimate=pl.CostEstimate(flops=flops, bytes_accessed=16 * MIB, transcendentals=0),
        name="chebyshev_inner",
    )(coefficients, owners, v_low, v_mid, v_high, *pieces)


def outer_kernel(
    blocks, coef, kernel_in, v_low, v_mid, v_high, h_low, h_first, h_last, h_high,
    edge_1, edge_2, edge_total, out,
    v, hraw, hcat, cheb_1, cheb_2, total, kern, sems, osems,
):
    last = kern.shape[0] - 1
    end = out.shape[0] - 1
    stages = [
        [
            (h_low, hraw.at[pl.ds(0, 2)]),
            (v_low, v.at[0, rows_of(0, 3)]),
            (v_mid.at[rows_of(0)], v.at[0, rows_of(3)]),
            (h_high, hraw.at[pl.ds(6, 2)]),
            (v_mid.at[rows_of(blocks - 1)], v.at[1, rows_of(0)]),
            (v_high, v.at[1, rows_of(1, 3)]),
        ],
        [
            (h_first, hraw.at[pl.ds(2, 2)]),
            (h_last, hraw.at[pl.ds(4, 2)]),
            (edge_1.at[rows_of(0, 2)], cheb_1.at[0, rows_of(2, 2)]),
            (edge_1.at[rows_of(2, 2)], cheb_1.at[1, rows_of(0, 2)]),
        ],
        [
            (edge_2.at[rows_of(0, 2)], cheb_2.at[0, rows_of(2, 2)]),
            (edge_2.at[rows_of(2, 2)], cheb_2.at[1, rows_of(0, 2)]),
            (edge_total.at[rows_of(0, 2)], total.at[0]),
            (edge_total.at[rows_of(2, 2)], total.at[1]),
        ],
    ]
    at = 0
    for i, stage in enumerate(stages):
        stages[i] = [
            pltpu.make_async_copy(source, target, sems.at[at + n])
            for n, (source, target) in enumerate(stage)
        ]
        at += len(stage)
        for copy in stages[i]:
            copy.start()
    build = band_builder(hraw, hcat)

    def arrived(i):
        for copy in stages[i]:
            copy.wait()

    def band(side, j, source, row):
        return jnp.dot(
            hcat[4 * side + j], source[side, rows_of(row, 3), :], preferred_element_type=jnp.float32
        )

    arrived(0)
    for j in (0, 1, 6, 7):
        build(j, 0)
    for side, places in ((0, (0, 1)), (1, (2, 3))):
        for j in places:
            value = band(side, j, v, j - 2 * side)
            cheb_1[side, rows_of(j), :] = value.astype(jnp.bfloat16)
    arrived(1)
    for j in (2, 3, 4, 5):
        build(j, 0)
    arrived(2)
    for side, places in ((0, ((1, 0), (2, 1))), (1, ((2, 3), (1, 2)))):
        for j, place in places:
            begin = v[side, rows_of(place + 2 - 4 * side), :].astype(jnp.float32)
            value = 2.0 * band(side, j, cheb_1, j - 1) - begin
            cheb_2[side, rows_of(place), :] = value.astype(jnp.bfloat16)
            if (j, place) == places[1]:
                within = rows_of(side)
                total[side, within, :] = (
                    coef[0] * begin + (coef[1] - coef[3]) * total[side, within, :] + coef[2] * value
                )
    for side in range(2):
        for half in range(2):
            j = 2 + half if side == 0 else half
            value = total[side, rows_of(half), :] + (2.0 * coef[3]) * band(side, j, cheb_2, half)
            kern[side, :, half * W : (half + 1) * W] = value.astype(jnp.bfloat16).T
    stores = [
        pltpu.make_async_copy(kern.at[0], out.at[0], osems.at[0]),
        pltpu.make_async_copy(kern.at[last], out.at[end], osems.at[1]),
    ]
    for store in stores:
        store.start()
    for store in stores:
        store.wait()


def chebyshev_outer(coefficients, inner, v_low, v_mid, v_high, h_low, h_first, h_last, h_high):
    kernel_t, edge_1, edge_2, edge_total = inner
    blocks = v_mid.shape[0] // W
    cols = v_mid.shape[1]
    return pl.pallas_call(
        functools.partial(outer_kernel, blocks),
        out_shape=jax.ShapeDtypeStruct(kernel_t.shape, kernel_t.dtype),
        in_specs=[SMEM] + [HBM] * 4 + [ANY, HBM, HBM, ANY] + [HBM] * 3,
        out_specs=HBM,
        input_output_aliases={1: 0},
        scratch_shapes=[
            pltpu.VMEM((2, 4 * W, cols), jnp.bfloat16),
            pltpu.VMEM((8, 2 * W, W), jnp.bfloat16),
            pltpu.VMEM((8, W, 3 * W), jnp.bfloat16),
            pltpu.VMEM((2, 4 * W, cols), jnp.bfloat16),
            pltpu.VMEM((2, 4 * W, cols), jnp.bfloat16),
            pltpu.VMEM((2, 2 * W, cols), jnp.float32),
            pltpu.VMEM((2, cols, KB), jnp.bfloat16),
            pltpu.SemaphoreType.DMA((14,)),
            pltpu.SemaphoreType.DMA((2,)),
        ],
        compiler_params=pltpu.CompilerParams(vmem_limit_bytes=59 * MIB),
        name="chebyshev_outer",
    )(
        coefficients, kernel_t, v_low, v_mid, v_high, h_low, h_first, h_last, h_high,
        edge_1, edge_2, edge_total,
    )


def entry_loads(order, parts, pair, sems):
    size = parts[0].shape[0]

    def load(p):
        return pltpu.make_async_copy(parts[0].at[0], pair.at[p], sems.at[p])

    def start(p, carry):
        n = order[p]
        for t, part in enumerate(parts):
            @pl.when((n >= t * size) & (n < (t + 1) * size))
            def _():
                pltpu.make_async_copy(part.at[n - t * size], pair.at[p], sems.at[p]).start()

        return carry

    return load, start


def by_twos(first, last, load, body):
    def step(i, carry):
        p = first + 2 * i
        q = jnp.minimum(p + 1, last - 1)
        load(p).wait()

        @pl.when(q > p)
        def _():
            load(q).wait()

        body(i, p, q)
        return carry

    lax.fori_loop(0, (last - first + 1) // 2, step, 0)


def sent_rows(slots, tiles):
    return slots + tiles + -(slots + tiles) % 8


def project_kernel(blocks, plan, order, kernel_t, core, *refs):
    *parts, out, kern, pair, rows, ksems, bsems = refs
    slots = pair.shape[0]
    load, start = entry_loads(order, parts, pair, bsems)

    def fetch(b):
        return pltpu.make_async_copy(kernel_t.at[b], kern.at[b], ksems.at[b])

    def begin(b, carry):
        first, last = plan[slots + b], plan[slots + b + 1]

        @pl.when(first < last)
        def _():
            fetch(b).start()

        return lax.fori_loop(first, last, start, carry)

    lax.fori_loop(0, blocks, begin, 0)
    rows[...] = jnp.zeros_like(rows)
    rows[slots : slots + core.shape[0]] = core[...]

    def step(b, carry):
        first, last = plan[slots + b], plan[slots + b + 1]

        @pl.when(first < last)
        def _():
            fetch(b).wait()

        def body(i, p, q):
            both = jnp.concatenate([pair[p, 0], pair[q, 0]], axis=1)
            projected = jnp.dot(kern[b], both, preferred_element_type=jnp.float32)
            other = jnp.concatenate([pair[p, 1], pair[q, 1]], axis=1).astype(jnp.float32)
            value = jnp.sum(projected * other, axis=0, keepdims=True) * (1.0 / KB)
            rows[pl.ds(order[p], 1), :] = value[:, :P_SIZE]
            rows[pl.ds(order[q], 1), :] = value[:, P_SIZE:]

        by_twos(first, last, load, body)
        return carry

    lax.fori_loop(0, blocks, step, 0)
    for c in range(out.shape[0]):
        out[c] = rows[...]


def project(plan, order, kernel_t, core, parts, col_count):
    slots = col_count * CAP
    entry = parts[0].shape[1:]
    sent = sent_rows(slots, core.shape[0])
    blocks = kernel_t.shape[0]
    return pl.pallas_call(
        functools.partial(project_kernel, blocks),
        out_shape=jax.ShapeDtypeStruct((col_count, sent, P_SIZE), jnp.float32),
        in_specs=[SMEM, SMEM, HBM, VMEM] + [HBM] * len(parts),
        out_specs=VMEM,
        scratch_shapes=[
            pltpu.VMEM(kernel_t.shape, jnp.bfloat16),
            pltpu.VMEM((slots,) + entry, jnp.bfloat16),
            pltpu.VMEM((sent, P_SIZE), jnp.float32),
            pltpu.SemaphoreType.DMA((blocks,)),
            pltpu.SemaphoreType.DMA((slots,)),
        ],
        compiler_params=pltpu.CompilerParams(vmem_limit_bytes=62 * MIB),
        name="project",
    )(plan, order, kernel_t, core, *parts)


def update_kernel(
    blocks, tiles, plan, order, tile_of, contributions, collect, *refs
):
    *parts, density_out, update_out, pair, density, potential, acc, stage, sems, osems = refs
    slots = pair.shape[0]
    live = plan[slots + blocks]
    me = plan[slots + blocks + 1]
    load, start = entry_loads(order, parts, pair, sems)
    lax.fori_loop(0, live, start, 0)
    density[...] = jnp.dot(
        collect[...],
        contributions[...],
        preferred_element_type=jnp.float32,
        precision=lax.Precision.HIGHEST,
    )
    for t in range(tiles):
        density_out[pl.ds(t, 1), :] = density[pl.ds(me * tiles + t, 1), :]
    positive = jnp.maximum(density[...], 0.1)
    root = jnp.exp(jnp.log(positive) * (1.0 / 3.0))
    root = root - (root - positive / (root * root)) * (1.0 / 3.0)
    potential[...] = -exchange_factor * root
    scale = 1.0 / math.sqrt(P_SIZE)

    def store(b):
        rows = pl.ds(pl.multiple_of(b * KB, KB), KB)
        return pltpu.make_async_copy(stage.at[b], update_out.at[rows], osems.at[b])

    def step(b, carry):
        first, last = plan[slots + b], plan[slots + b + 1]

        @pl.when(first == last)
        def _():
            stage[b] = jnp.zeros(stage.shape[1:], jnp.bfloat16)

        def body(i, p, q):
            weight_p = potential[pl.ds(tile_of[order[p]], 1), :]
            weight_q = potential[pl.ds(tile_of[order[q]], 1), :] * (q - p).astype(jnp.float32)
            weighted = jnp.concatenate(
                [
                    (pair[p, 1].astype(jnp.float32) * weight_p).astype(jnp.bfloat16),
                    (pair[q, 1].astype(jnp.float32) * weight_q).astype(jnp.bfloat16),
                ],
                axis=1,
            )
            block = lax.dot_general(
                jnp.concatenate([pair[p, 0], pair[q, 0]], axis=1),
                weighted,
                (((1,), (1,)), ((), ())),
                preferred_element_type=jnp.float32,
            )

            @pl.when(last - first <= 2)
            def _():
                stage[b] = (block * scale).astype(jnp.bfloat16)

            @pl.when((last - first > 2) & (i == 0))
            def _():
                acc[...] = block

            @pl.when(i > 0)
            def _():
                acc[...] += block

        by_twos(first, last, load, body)

        @pl.when(last - first > 2)
        def _():
            stage[b] = (acc[...] * scale).astype(jnp.bfloat16)

        store(b).start()
        return carry

    lax.fori_loop(0, blocks, step, 0)
    for b in range(blocks):
        store(b).wait()


def update(plan, order, tile_of, contributions, collect, parts, tiles, blocks, cols):
    slots = len(parts) * parts[0].shape[0]
    entry = parts[0].shape[1:]
    all_tiles = (collect.shape[0], P_SIZE)
    return pl.pallas_call(
        functools.partial(update_kernel, blocks, tiles),
        out_shape=(
            jax.ShapeDtypeStruct((tiles, P_SIZE), jnp.float32),
            jax.ShapeDtypeStruct((blocks * KB, cols), jnp.bfloat16),
        ),
        in_specs=[SMEM] * 3 + [VMEM] * 2 + [HBM] * len(parts),
        out_specs=(VMEM, HBM),
        scratch_shapes=[
            pltpu.VMEM((slots,) + entry, jnp.bfloat16),
            pltpu.VMEM(all_tiles, jnp.float32),
            pltpu.VMEM(all_tiles, jnp.float32),
            pltpu.VMEM((KB, cols), jnp.float32),
            pltpu.VMEM((blocks, KB, cols), jnp.bfloat16),
            pltpu.SemaphoreType.DMA((slots,)),
            pltpu.SemaphoreType.DMA((blocks,)),
        ],
        compiler_params=pltpu.CompilerParams(vmem_limit_bytes=24 * MIB),
        name="update",
    )(plan, order, tile_of, contributions, collect, *parts)


def shift(block, axis, step):
    count = lax.axis_size(axis)
    pairs = [(i, i + step) for i in range(count) if 0 <= i + step < count]
    return lax.ppermute(block, axis, pairs)


def make_plan(lists, me, entries, tiles, col_count, blocks):
    slots = col_count * CAP
    sent = sent_rows(slots, tiles)
    lists = lists[:, : 2 * entries + tiles].astype(jnp.int32)
    peers, named, counts = lists[:, :entries], lists[:, entries : 2 * entries], lists[:, 2 * entries :]
    index = jnp.arange(entries, dtype=jnp.int32)
    home = jnp.arange(col_count, dtype=jnp.int32)[:, None]
    earlier = (peers[:, :, None] == peers[:, None, :]) & (index[None, :] < index[:, None])
    rank = jnp.sum(earlier.astype(jnp.int32), axis=2)
    live = (index % SLOTS)[None, :] < jnp.repeat(counts, SLOTS, axis=1)
    row = jnp.where(live, peers * sent + chunk_of(home, peers, col_count) * CAP + rank, -1).reshape(col_count, tiles, SLOTS)
    core = (home * sent + slots + jnp.arange(tiles, dtype=jnp.int32))[:, :, None]
    row = jnp.concatenate([row, core], axis=2).reshape(col_count * tiles, SLOTS + 1, 1)
    picked = row == jnp.arange(col_count * sent, dtype=jnp.int32)
    collect = jnp.sum(picked.astype(jnp.float32), axis=1)
    hit = (
        (peers == me)[:, None, :]
        & (rank[:, None, :] == jnp.arange(CAP, dtype=jnp.int32)[None, :, None])
        & live[:, None, :]
    )
    at_me = chunk_of(home, me, col_count).reshape(1, col_count) == home
    tile = home * tiles + index[None, :] // SLOTS

    def of_slots(values):
        by_home = jnp.sum(jnp.where(hit, values[:, None, :], 0), axis=2)
        return jnp.sum(jnp.where(at_me[:, :, None], by_home[None], 0), axis=1).reshape(slots)

    wanted = of_slots(named + 1) - 1
    tile_of = of_slots(tile)
    key = jnp.where(wanted < 0, blocks, wanted)
    place = jnp.arange(slots, dtype=jnp.int32)
    before = (key[None, :] < key[:, None]) | (
        (key[None, :] == key[:, None]) & (place[None, :] < place[:, None])
    )
    spot = jnp.sum(before.astype(jnp.int32), axis=1)
    order = jnp.sum(jnp.where(spot[None, :] == place[:, None], place[None, :], 0), axis=1)
    starts = jnp.sum(
        (key[None, :] < jnp.arange(blocks + 1, dtype=jnp.int32)[:, None]).astype(jnp.int32), axis=1
    )
    plan = jnp.concatenate([wanted, starts, me[None]]).astype(jnp.int32)
    return collect, plan, order.astype(jnp.int32), tile_of.astype(jnp.int32)


def shards(
    start_columns,
    hamiltonian,
    band_pattern,
    coefficients,
    tile_peer,
    tile_block,
    tile_count,
    basis_values,
    core_density,
):
    col_count = lax.axis_size("col")
    entries = tile_peer.shape[0]
    tiles = core_density.shape[0]
    cols = start_columns.shape[1]
    blocks = start_columns.shape[0] // KB
    peers = tile_peer[:, 0]
    me = lax.axis_index("col").astype(jnp.int32)

    own = own_piece(peers, tile_block, tile_count, band_pattern, hamiltonian.reshape(-1, W))
    pieces, owners, awaited, handed = gather_pieces(own)
    v_low = shift(start_columns[-DEG * W :], "row", 1)
    v_high = shift(start_columns[: DEG * W], "row", -1)
    parts = exchange(me[None], peers, basis_values, own, pieces[min(1, len(pieces) - 1)],
        awaited + [v_low, v_high], handed)

    first, last, lists = edge_blocks(owners, pieces, col_count, DEG - 1)
    h_low = shift(last, "row", 1)
    h_high = shift(first, "row", -1)
    inner = chebyshev_inner(coefficients, owners, v_low, start_columns, v_high, pieces)
    kernel_t = chebyshev_outer(
        coefficients, inner, v_low, start_columns, v_high, h_low, first, last, h_high
    )
    collect, plan, order, tile_of = make_plan(lists[:, 0], me, entries, tiles, col_count, blocks)
    partial = project(plan, order, kernel_t, core_density, parts, col_count)
    contributions = lax.all_to_all(partial, "col", split_axis=0, concat_axis=0, tiled=True)
    contributions = contributions.reshape(-1, P_SIZE)
    return update(
        plan, order, tile_of, contributions, collect, parts, tiles, blocks, cols
    )


def solution(mesh):
    return jax.shard_map(
        shards,
        mesh=mesh,
        in_specs=(
            P("row", "col"),
            P(("row", "col"), None, None, None),
            P(("row", "col")),
            P(),
            P(("row", "col"), None),
            P(("row", "col")),
            P(("row", "col")),
            P(("row", "col"), None, None, None),
            P(("row", "col"), None),
        ),
        out_specs=(P(("row", "col"), None), P("row", "col")),
        check_vma=False,
    )
```

```python
import functools
import math

import jax
import jax.numpy as jnp
from jax import lax
from jax.experimental import pallas as pl
from jax.experimental.pallas import tpu as pltpu
from jax.sharding import PartitionSpec as P

W = 256
KB = 512
DEG = 3
SLOTS = 4
CAP = 2
P_SIZE = 128
MIB = 1 << 20
LISTS = 16

exchange_factor = (3.0 / math.pi) ** (1.0 / 3.0)
HBM = pl.BlockSpec(memory_space=pltpu.HBM)
ANY = pl.BlockSpec(memory_space=pl.ANY)
SMEM = pl.BlockSpec(memory_space=pltpu.SMEM)
VMEM = pl.BlockSpec(memory_space=pltpu.VMEM)


def partner(me, j, count):
    if count & (count - 1) == 0:
        return me ^ abs(j)
    return (me + j) % count


def piece_kernel(peers, named, counts, pattern, ham, piece, blocks, sems):
    rows = ham.shape[0]
    load = pltpu.make_async_copy(ham, blocks.at[pl.ds(0, rows)], sems.at[0])
    load.start()
    lane = lax.broadcasted_iota(jnp.int32, (LISTS, W), 1)
    lists = jnp.zeros((LISTS, W), jnp.int32)
    at = 0
    for ref in (peers, named, counts):
        for i in range(ref.shape[0]):
            lists = jnp.where(lane == at, ref[i], lists)
            at += 1
    blocks[rows:] = lists.astype(jnp.float32).astype(jnp.bfloat16)
    load.wait()
    for i in range(rows // (2 * W)):
        coupling = slice((2 * i + 1) * W, (2 * i + 2) * W)
        blocks[coupling] = blocks[coupling] * pattern[i].astype(jnp.bfloat16)
    store = pltpu.make_async_copy(blocks, piece, sems.at[1])
    store.start()
    store.wait()


def own_piece(peers, named, counts, pattern, ham):
    piece = (ham.shape[0] + LISTS, W)
    return pl.pallas_call(
        piece_kernel,
        out_shape=jax.ShapeDtypeStruct(piece, ham.dtype),
        in_specs=[SMEM] * 4 + [HBM],
        out_specs=HBM,
        scratch_shapes=[pltpu.VMEM(piece, ham.dtype), pltpu.SemaphoreType.DMA((2,))],
        compiler_params=pltpu.CompilerParams(vmem_limit_bytes=62 * MIB),
        name="own_piece",
    )(peers, named, counts, pattern, ham)


def lines_of(count):
    inner = max(count // 4, 1) if count & (count - 1) == 0 else 1
    return count // inner, inner


def swap_along(block, t):
    count = lax.axis_size("col")
    _, inner = lines_of(count)
    pairs = [(c, c - c % inner + partner(c % inner, t, inner)) for c in range(count)]
    return lax.ppermute(block, "col", pairs)


def chunk_of(home, owner, count):
    outer, inner = lines_of(count)
    return partner(home % inner, owner % inner, inner) * outer + home // inner


def pack_kernel(entries, col_count, wanted, me, peers, basis, first, *refs):
    outer, inner = lines_of(col_count)
    sent, (held, owner, count, in_sems, out_sems) = refs[: len(wanted)], refs[len(wanted) :]
    for c in range(col_count):
        count[c] = 0
        for k in range(CAP):
            owner[c * CAP + k] = 0
    for e in range(entries):
        p = peers[e]
        k = count[p]
        count[p] = k + 1
        owner[p * CAP + k] = e
    place = lax.rem(me[0], inner)
    tasks = []
    for target, group in zip(sent, wanted):
        for line in range(outer):
            for i, (t, k) in enumerate(group):
                n = len(tasks)
                e = owner[(line * inner + partner(place, t, inner)) * CAP + k]
                fetch = pltpu.make_async_copy(basis.at[e], held.at[n], in_sems.at[n])
                store = pltpu.make_async_copy(held.at[n], target.at[line, i], out_sems.at[n])
                tasks.append((fetch, store))
    for fetch, _ in tasks:
        fetch.start()
    for fetch, store in tasks:
        fetch.wait()
        store.start()
    for _, store in tasks:
        store.wait()


def pack(me, peers, basis, first, col_count, wanted):
    outer, _ = lines_of(col_count)
    entries = basis.shape[0]
    number = sum(len(group) for group in wanted) * outer
    return list(pl.pallas_call(
        functools.partial(pack_kernel, entries, col_count, wanted),
        out_shape=tuple(
            jax.ShapeDtypeStruct((outer, len(group)) + basis.shape[1:], basis.dtype)
            for group in wanted
        ),
        in_specs=[SMEM, SMEM, HBM, HBM],
        out_specs=(HBM,) * len(wanted),
        scratch_shapes=[
            pltpu.VMEM((number,) + basis.shape[1:], basis.dtype),
            pltpu.SMEM((col_count * CAP,), jnp.int32),
            pltpu.SMEM((col_count,), jnp.int32),
            pltpu.SemaphoreType.DMA((number,)),
            pltpu.SemaphoreType.DMA((number,)),
        ],
        compiler_params=pltpu.CompilerParams(vmem_limit_bytes=59 * MIB),
        name="pack",
    )(me, peers, basis, first))


def after(block, *others):
    return pl.pallas_call(
        lambda *refs: None,
        out_shape=jax.ShapeDtypeStruct(block.shape, block.dtype),
        in_specs=[HBM] + [ANY] * len(others),
        out_specs=HBM,
        input_output_aliases={0: 0},
        compiler_params=pltpu.CompilerParams(vmem_limit_bytes=59 * MIB),
        name="after",
    )(block, *others)


def exchange(me, peers, basis, own, early, awaited, handed):
    count = lax.axis_size("col")
    outer, inner = lines_of(count)
    groups = [[line * inner + place for line in range(outer)] for place in range(inner)]

    def between_lines(blocks, *others):
        block = jnp.concatenate(blocks, axis=1)
        return lax.all_to_all(
            after(block, *others), "col", split_axis=0, concat_axis=0,
            axis_index_groups=groups, tiled=True,
        )

    here = [(0, k) for k in range(CAP)]
    ahead = [[(t, 0)] for t in range(1, inner)]
    rest = [[(t, k)] for k in range(1, CAP) for t in range(1, inner)]
    sent = pack(me, peers, basis, own, count, ahead) if ahead else []
    to_lines, *later = pack(me, peers, basis, early, count, [here] + rest)
    swapped = {
        group[0]: swap_along(block, group[0][0]) for block, group in zip(sent + later, ahead + rest)
    }
    parts = [between_lines([to_lines], *awaited, *[swapped[group[0]] for group in ahead])]
    for t in range(1, inner):
        parts.append(between_lines([swapped[t, k] for k in range(CAP)], parts[-1], *handed))
    return [part.reshape((outer * CAP,) + part.shape[2:]) for part in parts]


def gather_pieces(own):
    count = lax.axis_size("col")
    outer, inner = lines_of(count)
    me = lax.axis_index("col").astype(jnp.int32)
    a, b = me // inner, me % inner

    def move(block, ways):
        pairs = [(x * inner + y, z * inner + y) for x, z in ways for y in range(inner)]
        return lax.ppermute(block, "col", pairs)

    if outer == 4:
        middle, outwards = [(1, 2), (2, 1)], [(1, 0), (2, 3)]
        near = move(own, [(0, 1), (1, 0), (2, 3), (3, 2)])
        across = move(own, middle)
        far = move(near, middle)
        handed = move(across, outwards)
        last = move(far, outwards)
        within = (a == 1) | (a == 2)
        lines = [
            (own, a),
            (near, a ^ 1),
            (across + handed, jnp.where(within, a ^ 3, a ^ 2)),
            (far + last, jnp.where(within, a ^ 2, a ^ 3)),
        ]
        awaited, ends = [far, handed], [last]
    else:
        lines = [(own, a)] + [
            (move(own, [(x, partner(x, t, outer)) for x in range(outer)]), partner(a, -t, outer))
            for t in range(1, outer)
        ]
        awaited, ends = [block for block, _ in lines[1:]], []
    pieces, owners = [], []
    for block, line in lines:
        pieces.append(block)
        owners.append(line * inner + b)
        for t in range(1, inner):
            pieces.append(swap_along(block, t))
            owners.append(line * inner + partner(b, -t, inner))
    ends += [piece for piece in pieces[: 3 * inner] if all(piece is not block for block, _ in lines)]
    return pieces, jnp.stack(owners).astype(jnp.int32), awaited, ends


def edge_kernel(col_count, depth, owners, *refs):
    pieces, (first, last, lists, sems, list_sems) = refs[:-5], refs[-5:]
    rows = pieces[0].shape[0] - LISTS
    held = rows // (2 * W)
    total = col_count * held

    def each(act):
        for i, piece in enumerate(pieces):
            for g in range(depth):
                for out, block, sem in ((first, g, 0), (last, total - depth + g, 1)):
                    source = piece.at[pl.ds(block % held * 2 * W, 2 * W)]
                    copy = pltpu.make_async_copy(source, out.at[g], sems.at[sem, g])

                    @pl.when(owners[i] == block // held)
                    def _():
                        act(copy)

            @pl.when(owners[i] >= 0)
            def _():
                act(pltpu.make_async_copy(
                    piece.at[pl.ds(rows, LISTS)], lists.at[owners[i]], list_sems.at[i]
                ))

    each(lambda copy: copy.start())
    each(lambda copy: copy.wait())


def edge_blocks(owners, pieces, col_count, depth):
    shape = jax.ShapeDtypeStruct((depth, 2 * W, W), pieces[0].dtype)
    return pl.pallas_call(
        functools.partial(edge_kernel, col_count, depth),
        out_shape=(shape, shape, jax.ShapeDtypeStruct((col_count, LISTS, W), pieces[0].dtype)),
        in_specs=[SMEM] + [ANY] * len(pieces),
        out_specs=(VMEM, VMEM, VMEM),
        scratch_shapes=[
            pltpu.SemaphoreType.DMA((2, depth)),
            pltpu.SemaphoreType.DMA((len(pieces),)),
        ],
        name="edge_blocks",
    )(owners, *pieces)


def rows_of(j, count=1):
    return pl.ds(j * W if isinstance(j, int) else pl.multiple_of(j * W, W), count * W)


def band_builder(source, target):
    rows = lax.broadcasted_iota(jnp.int32, (W, W), 0)
    cols = lax.broadcasted_iota(jnp.int32, (W, W), 1)
    upper = jnp.where(rows <= cols, 1.0, 0.0).astype(jnp.bfloat16)

    def build(j, carry):
        coupling = source[j, W:]
        lower_band = coupling * upper
        target[j, :, 0:W] = lower_band
        target[j, :, W : 2 * W] = source[j, :W]
        target[j, :, 2 * W : 3 * W] = coupling - lower_band
        return carry

    return build


def inner_kernel(blocks, coef, owners, v_low, v_mid, v_high, *refs):
    (
        *pieces, out, edge_1, edge_2, edge_total,
        vext, hraw, hcat, cheb_1, cheb_2, total, kern, sems, psems, osems, esems,
    ) = refs
    held = (pieces[0].shape[0] - LISTS) // (2 * W)
    v_copies = [
        pltpu.make_async_copy(v_low.at[rows_of(DEG - 1)], vext.at[rows_of(0)], sems.at[0]),
        pltpu.make_async_copy(v_mid, vext.at[rows_of(1, blocks)], sems.at[1]),
        pltpu.make_async_copy(v_high.at[rows_of(0)], vext.at[rows_of(blocks + 1)], sems.at[2]),
    ]

    def each_piece(act):
        for i, piece in enumerate(pieces):
            for k in range(held):
                act(pltpu.make_async_copy(
                    piece.at[pl.ds(k * 2 * W, 2 * W)],
                    hraw.at[owners[i] * held + k],
                    psems.at[i, k],
                ))

    each_piece(lambda copy: copy.start())
    for copy in v_copies:
        copy.start()
    each_piece(lambda copy: copy.wait())
    build = band_builder(hraw, hcat)
    build(0, 0)
    for copy in v_copies:
        copy.wait()

    def band(source, j, row):
        return jnp.dot(hcat[j], source[rows_of(row, 3), :], preferred_element_type=jnp.float32)

    def edges(source, target, at):
        size = source.shape[0] // W
        return [
            pltpu.make_async_copy(
                source.at[rows_of(place, 2)], target.at[rows_of(2 * i, 2)], esems.at[at, i]
            )
            for i, place in enumerate((0, size - 2))
        ]

    def first(j, carry):
        value = band(vext, j, j)
        build(jnp.minimum(j + 1, blocks - 1), 0)
        cheb_1[rows_of(j), :] = value.astype(jnp.bfloat16)
        total[rows_of(j), :] = value
        return carry

    lax.fori_loop(0, blocks, first, 0, unroll=4)

    def second(j, carry):
        begin = vext[rows_of(j + 2), :].astype(jnp.float32)
        value = 2.0 * band(cheb_1, j + 1, j) - begin
        cheb_2[rows_of(j), :] = value.astype(jnp.bfloat16)
        total[rows_of(j + 1), :] = (
            coef[0] * begin + (coef[1] - coef[3]) * total[rows_of(j + 1), :] + coef[2] * value
        )
        return carry

    lax.fori_loop(0, blocks - 2, second, 0, unroll=4)
    outgoing = (
        edges(cheb_1, edge_1, 0) + edges(cheb_2, edge_2, 1) + edges(total, edge_total, 2)
    )
    for copy in outgoing:
        copy.start()

    def store(j):
        return pltpu.make_async_copy(kern.at[j], out.at[j], osems.at[j])

    def third(j, carry):
        for half in range(KB // W):
            i = j * (KB // W) + half
            value = total[rows_of(i), :] + (2.0 * coef[3]) * band(cheb_2, i, i - 2)
            kern[j, :, half * W : (half + 1) * W] = value.astype(jnp.bfloat16).T
        store(j).start()
        return carry

    last = blocks // (KB // W) - 1
    lax.fori_loop(1, last, third, 0, unroll=2)
    for j in range(1, last):
        store(j).wait()
    for copy in outgoing:
        copy.wait()


def chebyshev_inner(coefficients, owners, v_low, v_mid, v_high, pieces):
    blocks = v_mid.shape[0] // W
    cols = v_mid.shape[1]
    flops = 2 * W * 3 * W * cols * (3 * blocks - 6)
    result = (blocks * W // KB, cols, KB)
    held = (pieces[0].shape[0] - LISTS) // (2 * W)
    return pl.pallas_call(
        functools.partial(inner_kernel, blocks),
        out_shape=(
            jax.ShapeDtypeStruct(result, jnp.bfloat16),
            jax.ShapeDtypeStruct((4 * W, cols), jnp.bfloat16),
            jax.ShapeDtypeStruct((4 * W, cols), jnp.bfloat16),
            jax.ShapeDtypeStruct((4 * W, cols), jnp.float32),
        ),
        in_specs=[SMEM] * 2 + [HBM] * (3 + len(pieces)),
        out_specs=(HBM,) * 4,
        scratch_shapes=[
            pltpu.VMEM(((blocks + 2) * W, cols), jnp.bfloat16),
            pltpu.VMEM((blocks, 2 * W, W), jnp.bfloat16),
            pltpu.VMEM((blocks, W, 3 * W), jnp.bfloat16),
            pltpu.VMEM((blocks * W, cols), jnp.bfloat16),
            pltpu.VMEM(((blocks - 2) * W, cols), jnp.bfloat16),
            pltpu.VMEM((blocks * W, cols), jnp.float32),
            pltpu.VMEM(result, jnp.bfloat16),
            pltpu.SemaphoreType.DMA((3,)),
            pltpu.SemaphoreType.DMA((len(pieces), held)),
            pltpu.SemaphoreType.DMA((result[0],)),
            pltpu.SemaphoreType.DMA((3, 2)),
        ],
        compiler_params=pltpu.CompilerParams(vmem_limit_bytes=62 * MIB),
        cost_estimate=pl.CostEstimate(flops=flops, bytes_accessed=16 * MIB, transcendentals=0),
        name="chebyshev_inner",
    )(coefficients, owners, v_low, v_mid, v_high, *pieces)


def outer_kernel(
    blocks, coef, kernel_in, v_low, v_mid, v_high, h_low, h_first, h_last, h_high,
    edge_1, edge_2, edge_total, out,
    v, hraw, hcat, cheb_1, cheb_2, total, kern, sems, osems,
):
    last = kern.shape[0] - 1
    end = out.shape[0] - 1
    stages = [
        [
            (h_low, hraw.at[pl.ds(0, 2)]),
            (v_low, v.at[0, rows_of(0, 3)]),
            (v_mid.at[rows_of(0)], v.at[0, rows_of(3)]),
            (h_high, hraw.at[pl.ds(6, 2)]),
            (v_mid.at[rows_of(blocks - 1)], v.at[1, rows_of(0)]),
            (v_high, v.at[1, rows_of(1, 3)]),
        ],
        [
            (h_first, hraw.at[pl.ds(2, 2)]),
            (h_last, hraw.at[pl.ds(4, 2)]),
            (edge_1.at[rows_of(0, 2)], cheb_1.at[0, rows_of(2, 2)]),
            (edge_1.at[rows_of(2, 2)], cheb_1.at[1, rows_of(0, 2)]),
        ],
        [
            (edge_2.at[rows_of(0, 2)], cheb_2.at[0, rows_of(2, 2)]),
            (edge_2.at[rows_of(2, 2)], cheb_2.at[1, rows_of(0, 2)]),
            (edge_total.at[rows_of(0, 2)], total.at[0]),
            (edge_total.at[rows_of(2, 2)], total.at[1]),
        ],
    ]
    at = 0
    for i, stage in enumerate(stages):
        stages[i] = [
            pltpu.make_async_copy(source, target, sems.at[at + n])
            for n, (source, target) in enumerate(stage)
        ]
        at += len(stage)
        for copy in stages[i]:
            copy.start()
    build = band_builder(hraw, hcat)

    def arrived(i):
        for copy in stages[i]:
            copy.wait()

    def band(side, j, source, row):
        return jnp.dot(
            hcat[4 * side + j], source[side, rows_of(row, 3), :], preferred_element_type=jnp.float32
        )

    arrived(0)
    for j in (0, 1, 6, 7):
        build(j, 0)
    for side, places in ((0, (0, 1)), (1, (2, 3))):
        for j in places:
            value = band(side, j, v, j - 2 * side)
            cheb_1[side, rows_of(j), :] = value.astype(jnp.bfloat16)
    arrived(1)
    for j in (2, 3, 4, 5):
        build(j, 0)
    arrived(2)
    for side, places in ((0, ((1, 0), (2, 1))), (1, ((2, 3), (1, 2)))):
        for j, place in places:
            begin = v[side, rows_of(place + 2 - 4 * side), :].astype(jnp.float32)
            value = 2.0 * band(side, j, cheb_1, j - 1) - begin
            cheb_2[side, rows_of(place), :] = value.astype(jnp.bfloat16)
            if (j, place) == places[1]:
                within = rows_of(side)
                total[side, within, :] = (
                    coef[0] * begin + (coef[1] - coef[3]) * total[side, within, :] + coef[2] * value
                )
    for side in range(2):
        for half in range(2):
            j = 2 + half if side == 0 else half
            value = total[side, rows_of(half), :] + (2.0 * coef[3]) * band(side, j, cheb_2, half)
            kern[side, :, half * W : (half + 1) * W] = value.astype(jnp.bfloat16).T
    stores = [
        pltpu.make_async_copy(kern.at[0], out.at[0], osems.at[0]),
        pltpu.make_async_copy(kern.at[last], out.at[end], osems.at[1]),
    ]
    for store in stores:
        store.start()
    for store in stores:
        store.wait()


def chebyshev_outer(coefficients, inner, v_low, v_mid, v_high, h_low, h_first, h_last, h_high):
    kernel_t, edge_1, edge_2, edge_total = inner
    blocks = v_mid.shape[0] // W
    cols = v_mid.shape[1]
    return pl.pallas_call(
        functools.partial(outer_kernel, blocks),
        out_shape=jax.ShapeDtypeStruct(kernel_t.shape, kernel_t.dtype),
        in_specs=[SMEM] + [HBM] * 4 + [ANY, HBM, HBM, ANY] + [HBM] * 3,
        out_specs=HBM,
        input_output_aliases={1: 0},
        scratch_shapes=[
            pltpu.VMEM((2, 4 * W, cols), jnp.bfloat16),
            pltpu.VMEM((8, 2 * W, W), jnp.bfloat16),
            pltpu.VMEM((8, W, 3 * W), jnp.bfloat16),
            pltpu.VMEM((2, 4 * W, cols), jnp.bfloat16),
            pltpu.VMEM((2, 4 * W, cols), jnp.bfloat16),
            pltpu.VMEM((2, 2 * W, cols), jnp.float32),
            pltpu.VMEM((2, cols, KB), jnp.bfloat16),
            pltpu.SemaphoreType.DMA((14,)),
            pltpu.SemaphoreType.DMA((2,)),
        ],
        compiler_params=pltpu.CompilerParams(vmem_limit_bytes=59 * MIB),
        name="chebyshev_outer",
    )(
        coefficients, kernel_t, v_low, v_mid, v_high, h_low, h_first, h_last, h_high,
        edge_1, edge_2, edge_total,
    )


def entry_loads(order, parts, pair, sems):
    size = parts[0].shape[0]

    def load(p):
        return pltpu.make_async_copy(parts[0].at[0], pair.at[p], sems.at[p])

    def start(p, carry):
        n = order[p]
        for t, part in enumerate(parts):
            @pl.when((n >= t * size) & (n < (t + 1) * size))
            def _():
                pltpu.make_async_copy(part.at[n - t * size], pair.at[p], sems.at[p]).start()

        return carry

    return load, start


def by_twos(first, last, load, body):
    def step(i, carry):
        p = first + 2 * i
        q = jnp.minimum(p + 1, last - 1)
        load(p).wait()

        @pl.when(q > p)
        def _():
            load(q).wait()

        body(i, p, q)
        return carry

    lax.fori_loop(0, (last - first + 1) // 2, step, 0)


def sent_rows(slots, tiles):
    return slots + tiles + -(slots + tiles) % 8


def project_kernel(blocks, plan, order, kernel_t, core, *refs):
    *parts, out, kern, pair, rows, ksems, bsems = refs
    slots = pair.shape[0]
    load, start = entry_loads(order, parts, pair, bsems)

    def fetch(b):
        return pltpu.make_async_copy(kernel_t.at[b], kern.at[b], ksems.at[b])

    def begin(b, carry):
        first, last = plan[slots + b], plan[slots + b + 1]

        @pl.when(first < last)
        def _():
            fetch(b).start()

        return lax.fori_loop(first, last, start, carry)

    lax.fori_loop(0, blocks, begin, 0)
    rows[...] = jnp.zeros_like(rows)
    rows[slots : slots + core.shape[0]] = core[...]

    def step(b, carry):
        first, last = plan[slots + b], plan[slots + b + 1]

        @pl.when(first < last)
        def _():
            fetch(b).wait()

        def body(i, p, q):
            both = jnp.concatenate([pair[p, 0], pair[q, 0]], axis=1)
            projected = jnp.dot(kern[b], both, preferred_element_type=jnp.float32)
            other = jnp.concatenate([pair[p, 1], pair[q, 1]], axis=1).astype(jnp.float32)
            value = jnp.sum(projected * other, axis=0, keepdims=True) * (1.0 / KB)
            rows[pl.ds(order[p], 1), :] = value[:, :P_SIZE]
            rows[pl.ds(order[q], 1), :] = value[:, P_SIZE:]

        by_twos(first, last, load, body)
        return carry

    lax.fori_loop(0, blocks, step, 0)
    for c in range(out.shape[0]):
        out[c] = rows[...]


def project(plan, order, kernel_t, core, parts, col_count):
    slots = col_count * CAP
    entry = parts[0].shape[1:]
    sent = sent_rows(slots, core.shape[0])
    blocks = kernel_t.shape[0]
    return pl.pallas_call(
        functools.partial(project_kernel, blocks),
        out_shape=jax.ShapeDtypeStruct((col_count, sent, P_SIZE), jnp.float32),
        in_specs=[SMEM, SMEM, HBM, VMEM] + [HBM] * len(parts),
        out_specs=VMEM,
        scratch_shapes=[
            pltpu.VMEM(kernel_t.shape, jnp.bfloat16),
            pltpu.VMEM((slots,) + entry, jnp.bfloat16),
            pltpu.VMEM((sent, P_SIZE), jnp.float32),
            pltpu.SemaphoreType.DMA((blocks,)),
            pltpu.SemaphoreType.DMA((slots,)),
        ],
        compiler_params=pltpu.CompilerParams(vmem_limit_bytes=62 * MIB),
        name="project",
    )(plan, order, kernel_t, core, *parts)


def update_kernel(
    blocks, tiles, plan, order, tile_of, contributions, collect, *refs
):
    *parts, density_out, update_out, pair, density, potential, acc, stage, sems, osems = refs
    slots = pair.shape[0]
    live = plan[slots + blocks]
    me = plan[slots + blocks + 1]
    load, start = entry_loads(order, parts, pair, sems)
    lax.fori_loop(0, live, start, 0)
    density[...] = jnp.dot(
        collect[...],
        contributions[...],
        preferred_element_type=jnp.float32,
        precision=lax.Precision.HIGHEST,
    )
    for t in range(tiles):
        density_out[pl.ds(t, 1), :] = density[pl.ds(me * tiles + t, 1), :]
    positive = jnp.maximum(density[...], 0.1)
    root = jnp.exp(jnp.log(positive) * (1.0 / 3.0))
    root = root - (root - positive / (root * root)) * (1.0 / 3.0)
    potential[...] = -exchange_factor * root
    scale = 1.0 / math.sqrt(P_SIZE)

    def store(b):
        rows = pl.ds(pl.multiple_of(b * KB, KB), KB)
        return pltpu.make_async_copy(stage.at[b], update_out.at[rows], osems.at[b])

    def step(b, carry):
        first, last = plan[slots + b], plan[slots + b + 1]

        @pl.when(first == last)
        def _():
            stage[b] = jnp.zeros(stage.shape[1:], jnp.bfloat16)

        def body(i, p, q):
            weight_p = potential[pl.ds(tile_of[order[p]], 1), :]
            weight_q = potential[pl.ds(tile_of[order[q]], 1), :] * (q - p).astype(jnp.float32)
            weighted = jnp.concatenate(
                [
                    (pair[p, 1].astype(jnp.float32) * weight_p).astype(jnp.bfloat16),
                    (pair[q, 1].astype(jnp.float32) * weight_q).astype(jnp.bfloat16),
                ],
                axis=1,
            )
            block = lax.dot_general(
                jnp.concatenate([pair[p, 0], pair[q, 0]], axis=1),
                weighted,
                (((1,), (1,)), ((), ())),
                preferred_element_type=jnp.float32,
            )

            @pl.when(last - first <= 2)
            def _():
                stage[b] = (block * scale).astype(jnp.bfloat16)

            @pl.when((last - first > 2) & (i == 0))
            def _():
                acc[...] = block

            @pl.when(i > 0)
            def _():
                acc[...] += block

        by_twos(first, last, load, body)

        @pl.when(last - first > 2)
        def _():
            stage[b] = (acc[...] * scale).astype(jnp.bfloat16)

        store(b).start()
        return carry

    lax.fori_loop(0, blocks, step, 0)
    for b in range(blocks):
        store(b).wait()


def update(plan, order, tile_of, contributions, collect, parts, tiles, blocks, cols):
    slots = len(parts) * parts[0].shape[0]
    entry = parts[0].shape[1:]
    all_tiles = (collect.shape[0], P_SIZE)
    return pl.pallas_call(
        functools.partial(update_kernel, blocks, tiles),
        out_shape=(
            jax.ShapeDtypeStruct((tiles, P_SIZE), jnp.float32),
            jax.ShapeDtypeStruct((blocks * KB, cols), jnp.bfloat16),
        ),
        in_specs=[SMEM] * 3 + [VMEM] * 2 + [HBM] * len(parts),
        out_specs=(VMEM, HBM),
        scratch_shapes=[
            pltpu.VMEM((slots,) + entry, jnp.bfloat16),
            pltpu.VMEM(all_tiles, jnp.float32),
            pltpu.VMEM(all_tiles, jnp.float32),
            pltpu.VMEM((KB, cols), jnp.float32),
            pltpu.VMEM((blocks, KB, cols), jnp.bfloat16),
            pltpu.SemaphoreType.DMA((slots,)),
            pltpu.SemaphoreType.DMA((blocks,)),
        ],
        compiler_params=pltpu.CompilerParams(vmem_limit_bytes=24 * MIB),
        name="update",
    )(plan, order, tile_of, contributions, collect, *parts)


def shift(block, axis, step):
    count = lax.axis_size(axis)
    pairs = [(i, i + step) for i in range(count) if 0 <= i + step < count]
    return lax.ppermute(block, axis, pairs)


def make_plan(lists, me, entries, tiles, col_count, blocks):
    slots = col_count * CAP
    sent = sent_rows(slots, tiles)
    lists = lists[:, : 2 * entries + tiles].astype(jnp.int32)
    peers, named, counts = lists[:, :entries], lists[:, entries : 2 * entries], lists[:, 2 * entries :]
    index = jnp.arange(entries, dtype=jnp.int32)
    home = jnp.arange(col_count, dtype=jnp.int32)[:, None]
    earlier = (peers[:, :, None] == peers[:, None, :]) & (index[None, :] < index[:, None])
    rank = jnp.sum(earlier.astype(jnp.int32), axis=2)
    live = (index % SLOTS)[None, :] < jnp.repeat(counts, SLOTS, axis=1)
    row = jnp.where(live, peers * sent + chunk_of(home, peers, col_count) * CAP + rank, -1).reshape(col_count, tiles, SLOTS)
    core = (home * sent + slots + jnp.arange(tiles, dtype=jnp.int32))[:, :, None]
    row = jnp.concatenate([row, core], axis=2).reshape(col_count * tiles, SLOTS + 1, 1)
    picked = row == jnp.arange(col_count * sent, dtype=jnp.int32)
    collect = jnp.sum(picked.astype(jnp.float32), axis=1)
    hit = (
        (peers == me)[:, None, :]
        & (rank[:, None, :] == jnp.arange(CAP, dtype=jnp.int32)[None, :, None])
        & live[:, None, :]
    )
    at_me = chunk_of(home, me, col_count).reshape(1, col_count) == home
    tile = home * tiles + index[None, :] // SLOTS

    def of_slots(values):
        by_home = jnp.sum(jnp.where(hit, values[:, None, :], 0), axis=2)
        return jnp.sum(jnp.where(at_me[:, :, None], by_home[None], 0), axis=1).reshape(slots)

    wanted = of_slots(named + 1) - 1
    tile_of = of_slots(tile)
    key = jnp.where(wanted < 0, blocks, wanted)
    place = jnp.arange(slots, dtype=jnp.int32)
    before = (key[None, :] < key[:, None]) | (
        (key[None, :] == key[:, None]) & (place[None, :] < place[:, None])
    )
    spot = jnp.sum(before.astype(jnp.int32), axis=1)
    order = jnp.sum(jnp.where(spot[None, :] == place[:, None], place[None, :], 0), axis=1)
    starts = jnp.sum(
        (key[None, :] < jnp.arange(blocks + 1, dtype=jnp.int32)[:, None]).astype(jnp.int32), axis=1
    )
    plan = jnp.concatenate([wanted, starts, me[None]]).astype(jnp.int32)
    return collect, plan, order.astype(jnp.int32), tile_of.astype(jnp.int32)


def shards(
    start_columns,
    hamiltonian,
    band_pattern,
    coefficients,
    tile_peer,
    tile_block,
    tile_count,
    basis_values,
    core_density,
):
    col_count = lax.axis_size("col")
    entries = tile_peer.shape[0]
    tiles = core_density.shape[0]
    cols = start_columns.shape[1]
    blocks = start_columns.shape[0] // KB
    peers = tile_peer[:, 0]
    me = lax.axis_index("col").astype(jnp.int32)

    own = own_piece(peers, tile_block, tile_count, band_pattern, hamiltonian.reshape(-1, W))
    pieces, owners, awaited, handed = gather_pieces(own)
    v_low = shift(start_columns[-DEG * W :], "row", 1)
    v_high = shift(start_columns[: DEG * W], "row", -1)
    parts = exchange(me[None], peers, basis_values, own, pieces[min(1, len(pieces) - 1)],
        awaited + [v_low, v_high], handed)

    first, last, lists = edge_blocks(owners, pieces, col_count, DEG - 1)
    h_low = shift(last, "row", 1)
    h_high = shift(first, "row", -1)
    inner = chebyshev_inner(coefficients, owners, v_low, start_columns, v_high, pieces)
    kernel_t = chebyshev_outer(
        coefficients, inner, v_low, start_columns, v_high, h_low, first, last, h_high
    )
    collect, plan, order, tile_of = make_plan(lists[:, 0], me, entries, tiles, col_count, blocks)
    partial = project(plan, order, kernel_t, core_density, parts, col_count)
    contributions = lax.all_to_all(partial, "col", split_axis=0, concat_axis=0, tiled=True)
    contributions = contributions.reshape(-1, P_SIZE)
    return update(
        plan, order, tile_of, contributions, collect, parts, tiles, blocks, cols
    )


def solution(mesh):
    return jax.shard_map(
        shards,
        mesh=mesh,
        in_specs=(
            P("row", "col"),
            P(("row", "col"), None, None, None),
            P(("row", "col")),
            P(),
            P(("row", "col"), None),
            P(("row", "col")),
            P(("row", "col")),
            P(("row", "col"), None, None, None),
            P(("row", "col"), None),
        ),
        out_specs=(P(("row", "col"), None), P("row", "col")),
        check_vma=False,
    )
```
